32 devices in a mesh: shard: 8 (over z, core), ctx: 2 (over x), tp: 2 (over y).
Axes of the slice: x: 2, y: 2, z: 4, core: 2. Of those that a mesh axis runs over, the one named last changes fastest.
Arguments:
- tokens: bfloat16 [16, 1032, 1024], P('shard', 'ctx'), may hold values from -6 to 6
- cotangent: bfloat16 [16, 1032, 1024], P('shard', 'ctx'), may hold values from -6 to 6
- valid_tokens: int32 [16, 1032], P('shard'), may hold values from 0 to 1, as said below
- places: int32 [2, 16, 1032], P(None, 'shard', 'ctx'), may hold values from 0 to 31, as said below
- qkv_weight: bfloat16 [3, 1024, 1024], P(None, 'shard', 'tp'), may hold values from -0.1875 to 0.1875
- head_biases: bfloat16 [3, 16, 64], P(None, 'tp', 'shard'), may hold values from -1.1953125 to 1.1953125
- head_gain: bfloat16 [16, 64], P('tp', 'shard'), may hold values from 0.5 to 1.5
- out_weight: bfloat16 [1024, 1024], P('tp', 'shard'), may hold values from -0.1875 to 0.1875
- norm_gains: bfloat16 [2, 1024], P(None, 'shard'), may hold values from 0.5 to 1.5
- width_biases: bfloat16 [4, 1024], P(None, 'shard'), may hold values from -1.1953125 to 1.1953125
- gate_up: bfloat16 [2, 1024, 2730], P(None, 'shard', 'tp'), may hold values from -0.1875 to 0.1875
- hidden_biases: bfloat16 [3, 2730], P(None, 'tp'), may hold values from -1.1953125 to 1.1953125
- hidden_gain: bfloat16 [2730], P('tp'), may hold values from 0.5 to 1.5
- down_weight: bfloat16 [2730, 1024], P('tp', 'shard'), may hold values from -0.109375 to 0.109375
Outputs:
- output: bfloat16 [16, 1032, 1024], P('shard', 'ctx')
- tokens_grad: float32 [16, 1032, 1024], P('shard', 'ctx')
- qkv_grad: float32 [3, 1024, 1024], P(None, 'shard', 'tp')
- head_biases_grad: float32 [3, 16, 64], P(None, 'tp', 'shard')
- head_gain_grad: float32 [16, 64], P('tp', 'shard')
- out_weight_grad: float32 [1024, 1024], P('tp', 'shard')
- norm_gains_grad: float32 [2, 1024], P(None, 'shard')
- width_biases_grad: float32 [4, 1024], P(None, 'shard')
- gate_up_grad: float32 [2, 1024, 2730], P(None, 'shard', 'tp')
- hidden_biases_grad: float32 [3, 2730], P(None, 'tp')
- hidden_gain_grad: float32 [2730], P('tp')
- down_weight_grad: float32 [2730, 1024], P('tp', 'shard')
The draws below stay inside these ranges and needn't reach their ends.
Inputs may be any that keep to these rules, and one draw needn't show every extreme that they name: `valid_tokens`: valid slots of each image form a prefix: the class token at slot 0 and 32 * w patch tokens after it, where w is 31 or 32; among the 2 images of each index of shard, one has w = 32. `places`: for a valid slot t >= 1 of an image with w columns the row is (t - 1) // w and the column (t - 1) % w; slot 0 and padding slots hold 0 and 0.
All inputs are finite; a program needn't handle non-finite values.
Results may differ from the reference program's by a relative error of at most 0.02.
Values may be sent and summed in bfloat16 or wider, within the bound.
A program may use at most 256 MiB of HBM per device.

```python
import math
import jax
import jax.numpy as jnp
from jax import lax

D = 1024
H = 16
HD = 64
FF = 2730
G = 32
MB = 2
SEQ = 1032
IMAGES = 16


def image_widths(key):
    groups = IMAGES // MB
    narrow = jax.random.randint(jax.random.fold_in(key, 11), (groups, MB), 0, 2)
    chosen = jax.random.randint(jax.random.fold_in(key, 12), (groups, 1), 0, MB)
    slot_ids = jnp.arange(MB)[None, :]
    widths = jnp.where(slot_ids == chosen, G, G - narrow)
    return widths.reshape(IMAGES).astype(jnp.int32)


def draw_valid_tokens(key, part):
    widths = image_widths(key)
    position = jnp.arange(SEQ, dtype=jnp.int32)[None, :]
    return (position <= G * widths[:, None]).astype(jnp.int32)


def draw_places(key, part):
    widths = image_widths(key)[:, None]
    position = jnp.arange(SEQ, dtype=jnp.int32)[None, :]
    offset = jnp.maximum(position - 1, 0)
    live_slot = (position >= 1) & (position <= G * widths)
    row_ids = jnp.where(live_slot, offset // widths, 0)
    col_ids = jnp.where(live_slot, offset % widths, 0)
    return jnp.stack([row_ids, col_ids]).astype(jnp.int32)


def levels(stream_key, shape, shards, low, top_value):
    def one(dim, parts):
        draws = jax.random.uniform(jax.random.fold_in(jax.random.fold_in(stream_key, 6), dim), (parts,), jnp.float32, low / len(shards), top_value / len(shards))
        return jnp.repeat(jnp.exp(draws), shape[dim] // parts).reshape((-1,) + (1,) * (len(shape) - dim - 1))

    gain = one(*shards[0])
    for cut in shards[1:]:
        gain = gain * one(*cut)
    return gain


def bell_draw(rng, extent, scale, reach, pieces=(), held_as=jnp.bfloat16):
    array = scale * jax.random.normal(rng, extent, jnp.float32)
    if pieces:
        array = array * levels(rng, extent, pieces, -0.22, 0.18)
    return jnp.clip(array, -reach, reach).astype(held_as)


def setup_inputs(seed: int = 0) -> dict:
    key_list = jax.random.split(jax.random.key(seed), 15)
    tokens = bell_draw(key_list[0], (IMAGES, SEQ, D), 1.0, 6.0, ((0, 8), (1, 2)))
    cotangent = bell_draw(key_list[1], (IMAGES, SEQ, D), 1.0, 6.0, ((0, 8), (1, 2)))
    valid_tokens = draw_valid_tokens(jax.random.fold_in(key_list[14], 71), 0)
    places = draw_places(jax.random.fold_in(key_list[14], 71), 0)
    qkv_weight = bell_draw(key_list[4], (3, D, D), D ** -0.5, 0.1875, ((1, 8), (2, 2)))
    head_biases = bell_draw(key_list[5], (3, H, HD), 0.2, 1.1953125, ((1, 2), (2, 8)))
    head_gain = jnp.clip(1.0 + 0.1 * jax.random.normal(key_list[6], (H, HD), jnp.float32), 0.5, 1.5).astype(jnp.bfloat16)
    out_weight = bell_draw(key_list[7], (D, D), D ** -0.5, 0.1875, ((0, 2), (1, 8)))
    norm_gains = jnp.clip(1.0 + 0.1 * jax.random.normal(key_list[8], (2, D), jnp.float32), 0.5, 1.5).astype(jnp.bfloat16)
    width_biases = bell_draw(key_list[9], (4, D), 0.2, 1.1953125, ((1, 8),))
    gate_up = bell_draw(key_list[10], (2, D, FF), D ** -0.5, 0.1875, ((1, 8), (2, 2)))
    hidden_biases = bell_draw(key_list[11], (3, FF), 0.2, 1.1953125, ((1, 2),))
    hidden_gain = jnp.clip(1.0 + 0.1 * jax.random.normal(key_list[12], (FF,), jnp.float32), 0.5, 1.5).astype(jnp.bfloat16)
    down_weight = bell_draw(key_list[13], (FF, D), FF ** -0.5, 0.109375, ((0, 2), (1, 8)))
    return dict(tokens=tokens, cotangent=cotangent, valid_tokens=valid_tokens, places=places, qkv_weight=qkv_weight, head_biases=head_biases, head_gain=head_gain, out_weight=out_weight, norm_gains=norm_gains, width_biases=width_biases, gate_up=gate_up, hidden_biases=hidden_biases, hidden_gain=hidden_gain, down_weight=down_weight)


EPS = 1e-06
HIGH = lax.Precision.HIGHEST

@jax.custom_vjp
def low(v):
    return lax.optimization_barrier(v.astype(jnp.bfloat16)).astype(jnp.float32)

@jax.custom_vjp
def low_back(v):
    return v

def low_keep(v):
    return (low(v), None)

def low_pass(kept, grad):
    return (grad,)

def back_keep(v):
    return (v, None)

def back_low(kept, grad):
    return (low(grad),)
low.defvjp(low_keep, low_pass)
low_back.defvjp(back_keep, back_low)

def layer_norm(values, gain_vec, bias_vec):
    average = lax.optimization_barrier(jnp.mean(values, axis=-1, keepdims=True))
    centred = values - average
    variance = lax.optimization_barrier(jnp.mean(centred * centred, axis=-1, keepdims=True))
    return centred * lax.rsqrt(variance + EPS) * gain_vec + bias_vec

def angle_table(row_ids, col_ids, head_size):
    quarter = head_size // 4
    frequency = 10000.0 ** (-jnp.arange(quarter, dtype=jnp.float32) / quarter)
    row_part = row_ids.astype(jnp.float32)[:, None] * frequency[None, :]
    col_part = col_ids.astype(jnp.float32)[:, None] * frequency[None, :]
    return jnp.concatenate([row_part, row_part, col_part, col_part], axis=1)

def turn_half(values):
    quarter = values.shape[-1] // 4
    part_one = values[..., :quarter]
    part_two = values[..., quarter:2 * quarter]
    part_three = values[..., 2 * quarter:3 * quarter]
    part_four = values[..., 3 * quarter:]
    return jnp.concatenate([-part_two, part_one, -part_four, part_three], axis=-1)

def rotate(values, angles):
    return values * jnp.cos(angles)[:, None, :] + turn_half(values) * jnp.sin(angles)[:, None, :]

def product(left, right):
    return jnp.dot(left, right, precision=HIGH)

def reference(tokens, cotangent, valid_tokens, places, qkv_weight, head_biases, head_gain, out_weight, norm_gains, width_biases, gate_up, hidden_biases, hidden_gain, down_weight):
    score_scale = 1.0 / math.sqrt(HD)
    weights_in = (qkv_weight, head_biases, head_gain, out_weight, norm_gains, width_biases, gate_up, hidden_biases, hidden_gain, down_weight)
    weights_f = tuple((item.astype(jnp.float32) for item in weights_in))

    def forward(token_all, qkv_matrix, head_bias, head_scale, out_matrix, norm_scale, width_bias, gate_matrix, hidden_bias, hidden_scale, down_matrix):

        def one_image(items):
            token_rows, valid_row, row_ids, col_ids = items
            normed_one = low(layer_norm(token_rows, norm_scale[0], width_bias[0]))
            query_pre = low_back(product(normed_one, qkv_matrix[0]) + head_bias[0].reshape(-1))
            key_pre = low_back(product(normed_one, qkv_matrix[1]))
            value_pre = low_back(product(normed_one, qkv_matrix[2]) + head_bias[1].reshape(-1))
            angles = angle_table(row_ids, col_ids, HD)
            queries = low(rotate(query_pre.reshape(SEQ, H, HD), angles))
            keys_rot = low(rotate(key_pre.reshape(SEQ, H, HD), angles))
            values = low(value_pre).reshape(SEQ, H, HD)
            scores = low_back(jnp.einsum('thd,shd->hts', queries, keys_rot, precision=HIGH) * score_scale)
            scores = jnp.where(valid_row[None, None, :] > 0, scores, -1e+30)
            row_top = lax.optimization_barrier(jnp.max(scores, axis=-1, keepdims=True))
            shifted = jnp.exp(scores - row_top)
            weights_soft = low(shifted / lax.optimization_barrier(jnp.sum(shifted, axis=-1, keepdims=True)))
            mixed = low_back(jnp.einsum('hts,shd->thd', weights_soft, values, precision=HIGH).reshape(SEQ, D))
            mix_in = low(layer_norm(mixed, head_scale.reshape(-1), head_bias[2].reshape(-1)))
            resid = token_rows + low_back(product(mix_in, out_matrix) + width_bias[2])
            second_in = low(layer_norm(resid, norm_scale[1], width_bias[1]))
            gate_pre = low_back(product(second_in, gate_matrix[0]) + hidden_bias[0])
            up_pre = low_back(product(second_in, gate_matrix[1]) + hidden_bias[1])
            down_in = low(layer_norm(jax.nn.silu(gate_pre) * up_pre, hidden_scale, hidden_bias[2]))
            return resid + low_back(product(down_in, down_matrix) + width_bias[3])
        return lax.map(jax.checkpoint(one_image), (token_all, valid_tokens, places[0], places[1]))
    output_f, pullback = jax.vjp(forward, tokens.astype(jnp.float32), *weights_f)
    gradients = pullback(cotangent.astype(jnp.float32))
    return (output_f.astype(jnp.bfloat16), gradients[0], gradients[1], gradients[2], gradients[3], gradients[4], gradients[5], gradients[6], gradients[7], gradients[8], gradients[9], gradients[10])
```

```python
import functools
import math

import jax
import jax.numpy as jnp
from jax import lax
from jax.experimental import pallas as pl
from jax.experimental.pallas import tpu as pltpu
from jax.sharding import PartitionSpec as P

SHARD, CTX, TP = "shard", "ctx", "tp"


EPS = 1e-06


def standardize(values):
    average = jnp.mean(values, axis=-1, keepdims=True)
    centred = values - average
    spread = lax.rsqrt(jnp.mean(centred * centred, axis=-1, keepdims=True) + EPS)
    return (centred * spread, spread)


def norm_back(grad_hat, normed, spread):
    mean_one = jnp.mean(grad_hat, axis=-1, keepdims=True)
    mean_two = jnp.mean(grad_hat * normed, axis=-1, keepdims=True)
    return (grad_hat - mean_one - normed * mean_two) * spread


def angle_table(row_ids, col_ids, head_size):
    quarter = head_size // 4
    frequency = 10000.0 ** (-jnp.arange(quarter, dtype=jnp.float32) / quarter)
    row_part = row_ids.astype(jnp.float32)[:, None] * frequency[None, :]
    col_part = col_ids.astype(jnp.float32)[:, None] * frequency[None, :]
    return jnp.concatenate([row_part, row_part, col_part, col_part], axis=1)


def turn_half(values):
    quarter = values.shape[-1] // 4
    part_one = values[..., :quarter]
    part_two = values[..., quarter : 2 * quarter]
    part_three = values[..., 2 * quarter : 3 * quarter]
    part_four = values[..., 3 * quarter :]
    return jnp.concatenate([-part_two, part_one, -part_four, part_three], axis=-1)


def rotate(values, angles):
    return values * jnp.cos(angles)[None, :, :] + turn_half(values) * jnp.sin(angles)[None, :, :]


def unrotate(values, angles):
    return values * jnp.cos(angles)[None, :, :] - turn_half(values) * jnp.sin(angles)[None, :, :]


def head_major(values, heads, head_size):
    return values.reshape(values.shape[0], heads, head_size).transpose(1, 0, 2)


def column_sum(values):
    return jnp.sum(values.astype(jnp.float32), axis=0)


def general_plan(
    tokens,
    cotangent,
    valid_tokens,
    places,
    qkv_weight,
    head_biases,
    head_gain,
    out_weight,
    norm_gains,
    width_biases,
    gate_up,
    hidden_biases,
    hidden_gain,
    down_weight,
):
    micro = tokens.shape[0]
    width = tokens.shape[2]
    local_dim = qkv_weight.shape[2]
    local_heads = head_biases.shape[1]
    head_size = local_dim // local_heads
    local_hidden = hidden_gain.shape[0]
    FF = local_hidden * lax.axis_size(TP)
    score_scale = 1.0 / math.sqrt(head_size)
    f32 = jnp.float32
    bf16 = jnp.bfloat16

    def one_batch(batch_idx, carried):
        gathered = (
            lax.all_gather(qkv_weight, SHARD, axis=1, tiled=True),
            lax.all_gather(head_biases, SHARD, axis=2, tiled=True),
            lax.all_gather(head_gain, SHARD, axis=1, tiled=True),
            lax.all_gather(out_weight, SHARD, axis=1, tiled=True),
            lax.all_gather(norm_gains, SHARD, axis=1, tiled=True),
            lax.all_gather(width_biases, SHARD, axis=1, tiled=True),
            lax.all_gather(gate_up, SHARD, axis=1, tiled=True),
            lax.all_gather(down_weight, SHARD, axis=1, tiled=True),
        )
        qkv_full, head_bias, head_scale, out_full, norm_scale, width_bias, gate_full, down_full = (
            gathered
        )
        head_bias_f = head_bias.astype(f32)
        head_scale_f = head_scale.astype(f32)[:, None, :]
        norm_scale = norm_scale.astype(f32)
        width_bias = width_bias.astype(f32)
        hidden_bias = hidden_biases.astype(f32)
        hidden_scale = hidden_gain.astype(f32)
        out_heads = out_full.reshape(local_heads, head_size, width)
        token_rows = lax.dynamic_index_in_dim(tokens, batch_idx, 0, keepdims=False).astype(f32)
        cot_rows = lax.dynamic_index_in_dim(cotangent, batch_idx, 0, keepdims=False).astype(f32)
        valid_row = lax.dynamic_index_in_dim(valid_tokens, batch_idx, 0, keepdims=False) > 0
        row_ids = lax.dynamic_index_in_dim(places[0], batch_idx, 0, keepdims=False)
        col_ids = lax.dynamic_index_in_dim(places[1], batch_idx, 0, keepdims=False)
        angles = angle_table(row_ids, col_ids, head_size)
        normed_one, spread_one = standardize(token_rows)
        first_in = (normed_one * norm_scale[0] + width_bias[0]).astype(bf16)
        query_flat = jnp.dot(first_in, qkv_full[0], preferred_element_type=f32)
        key_flat = jnp.dot(first_in, qkv_full[1], preferred_element_type=f32)
        value_flat = jnp.dot(first_in, qkv_full[2], preferred_element_type=f32)
        query_pre = head_major(query_flat, local_heads, head_size) + head_bias_f[0][:, None, :]
        key_pre = head_major(key_flat, local_heads, head_size)
        value_local = (
            head_major(value_flat, local_heads, head_size) + head_bias_f[1][:, None, :]
        ).astype(bf16)
        queries = rotate(query_pre, angles).astype(bf16)
        key_local = rotate(key_pre, angles).astype(bf16)
        key_heads, value_heads = (
            lax.all_gather(key_local, CTX, axis=1, tiled=True),
            lax.all_gather(value_local, CTX, axis=1, tiled=True),
        )

        def score_block():
            raw = (
                jnp.einsum("htd,hsd->hts", queries, key_heads, preferred_element_type=f32)
                * score_scale
            )
            return jnp.where(valid_row[None, None, :], raw, -1e30)

        scores = score_block()
        row_top = jnp.max(scores, axis=-1, keepdims=True)
        row_total = jnp.sum(jnp.exp(scores - row_top), axis=-1, keepdims=True)
        soft_low = (jnp.exp(scores - row_top) / row_total).astype(bf16)
        mixed = jnp.einsum("hts,hsd->htd", soft_low, value_heads, preferred_element_type=f32)
        mix_sums = lax.psum(
            (
                jnp.sum(mixed, axis=(0, 2), keepdims=True),
                jnp.sum(mixed * mixed, axis=(0, 2), keepdims=True),
            ),
            TP,
        )
        mix_mean = mix_sums[0] / width
        spread_mix = lax.rsqrt(mix_sums[1] / width - mix_mean * mix_mean + EPS)
        mix_hat = (mixed - mix_mean) * spread_mix
        mix_in = (mix_hat * head_scale_f + head_bias_f[2][:, None, :]).astype(bf16)
        branch = lax.psum(
            jnp.einsum("htd,hdn->tn", mix_in, out_heads, preferred_element_type=f32), TP
        )
        resid = token_rows + (branch + width_bias[2])
        normed_two, spread_two = standardize(resid)
        second_in = (normed_two * norm_scale[1] + width_bias[1]).astype(bf16)
        gate_pre = jnp.dot(second_in, gate_full[0], preferred_element_type=f32) + hidden_bias[0]
        up_pre = jnp.dot(second_in, gate_full[1], preferred_element_type=f32) + hidden_bias[1]
        sigmoid_gate = jax.nn.sigmoid(gate_pre)
        silu_gate = gate_pre * sigmoid_gate
        hidden = silu_gate * up_pre
        hidden_sums = lax.psum(
            (
                jnp.sum(hidden, axis=-1, keepdims=True),
                jnp.sum(hidden * hidden, axis=-1, keepdims=True),
            ),
            TP,
        )
        hidden_mean = hidden_sums[0] / FF
        spread_hid = lax.rsqrt(hidden_sums[1] / FF - hidden_mean * hidden_mean + EPS)
        hidden_hat = (hidden - hidden_mean) * spread_hid
        down_in = (hidden_hat * hidden_scale + hidden_bias[2]).astype(bf16)
        ffn_out = lax.psum(
            jnp.dot(down_in, down_full, preferred_element_type=f32).astype(jnp.bfloat16), TP
        ).astype(jnp.float32)
        result = (resid + (ffn_out + width_bias[3])).astype(bf16)
        d_ffn_low = cot_rows.astype(bf16)
        g_down = jnp.einsum("tf,td->fd", down_in, d_ffn_low, preferred_element_type=f32)
        d_down_in = jnp.einsum("td,fd->tf", d_ffn_low, down_full, preferred_element_type=f32)
        grad_hid = d_down_in * hidden_scale
        hid_back = lax.psum(
            (
                jnp.sum(grad_hid, axis=-1, keepdims=True),
                jnp.sum(grad_hid * hidden_hat, axis=-1, keepdims=True),
            ),
            TP,
        )
        d_hidden = (grad_hid - hid_back[0] / FF - hidden_hat * (hid_back[1] / FF)) * spread_hid
        d_gate = (
            d_hidden * up_pre * sigmoid_gate * (1.0 + gate_pre * (1.0 - sigmoid_gate))
        ).astype(bf16)
        d_up = (d_hidden * silu_gate).astype(bf16)
        g_gate_one = jnp.einsum("td,tf->df", second_in, d_gate, preferred_element_type=f32)
        g_up_one = jnp.einsum("td,tf->df", second_in, d_up, preferred_element_type=f32)
        d_second_part = jnp.einsum(
            "tf,df->td", d_gate, gate_full[0], preferred_element_type=f32
        ) + jnp.einsum("tf,df->td", d_up, gate_full[1], preferred_element_type=f32)
        d_second = lax.psum(d_second_part, TP)
        d_resid = cot_rows + norm_back(d_second * norm_scale[1], normed_two, spread_two)
        d_branch_low = d_resid.astype(bf16)
        g_out = jnp.einsum("htd,tn->hdn", mix_in, d_branch_low, preferred_element_type=f32).reshape(
            local_dim, width
        )
        d_mix_in = jnp.einsum("tn,hdn->htd", d_branch_low, out_heads, preferred_element_type=f32)
        grad_mix = d_mix_in * head_scale_f
        mix_back = lax.psum(
            (
                jnp.sum(grad_mix, axis=(0, 2), keepdims=True),
                jnp.sum(grad_mix * mix_hat, axis=(0, 2), keepdims=True),
            ),
            TP,
        )
        d_mixed = (
            (grad_mix - mix_back[0] / width - mix_hat * (mix_back[1] / width)) * spread_mix
        ).astype(bf16)
        again = score_block()
        weights_soft = jnp.exp(again - row_top) / row_total
        d_soft = jnp.einsum("htd,hsd->hts", d_mixed, value_heads, preferred_element_type=f32)
        row_dot = jnp.sum(weights_soft * d_soft, axis=-1, keepdims=True)
        d_scores = (weights_soft * (d_soft - row_dot)).astype(bf16)
        d_query = (
            jnp.einsum("hts,hsd->htd", d_scores, key_heads, preferred_element_type=f32)
            * score_scale
        )
        soft_again = weights_soft.astype(bf16)
        d_key_all = (
            jnp.einsum("hts,htd->hsd", d_scores, queries, preferred_element_type=f32) * score_scale
        )
        d_value_all = jnp.einsum("hts,htd->hsd", soft_again, d_mixed, preferred_element_type=f32)
        d_key_heads, d_value_loc = (
            lax.psum_scatter(
                d_key_all.astype(jnp.bfloat16), CTX, scatter_dimension=1, tiled=True
            ).astype(jnp.float32),
            lax.psum_scatter(
                d_value_all.astype(jnp.bfloat16), CTX, scatter_dimension=1, tiled=True
            ).astype(jnp.float32),
        )
        d_query_low = unrotate(d_query, angles).astype(bf16)
        d_key_low = unrotate(d_key_heads, angles).astype(bf16)
        d_value_low = d_value_loc.astype(bf16)
        g_query = jnp.einsum(
            "tn,htd->nhd", first_in, d_query_low, preferred_element_type=f32
        ).reshape(width, local_dim)
        g_key = jnp.einsum("tn,htd->nhd", first_in, d_key_low, preferred_element_type=f32).reshape(
            width, local_dim
        )
        g_value = jnp.einsum(
            "tn,htd->nhd", first_in, d_value_low, preferred_element_type=f32
        ).reshape(width, local_dim)
        d_first_part = jnp.einsum(
            "htd,nhd->tn",
            d_query_low,
            qkv_full[0].reshape(width, local_heads, head_size),
            preferred_element_type=f32,
        )
        d_first_part = d_first_part + jnp.einsum(
            "htd,nhd->tn",
            d_key_low,
            qkv_full[1].reshape(width, local_heads, head_size),
            preferred_element_type=f32,
        )
        d_first_part = d_first_part + jnp.einsum(
            "htd,nhd->tn",
            d_value_low,
            qkv_full[2].reshape(width, local_heads, head_size),
            preferred_element_type=f32,
        )
        d_first = lax.psum(d_first_part.astype(jnp.bfloat16), TP).astype(jnp.float32)
        d_tokens = d_resid + norm_back(d_first * norm_scale[0], normed_one, spread_one)
        g_head_bias = jnp.stack(
            [
                jnp.sum(d_query_low.astype(f32), axis=1),
                jnp.sum(d_value_low.astype(f32), axis=1),
                jnp.sum(d_mix_in, axis=1),
            ]
        )
        g_head_scale = jnp.sum(d_mix_in * mix_hat, axis=1)
        g_norm = jnp.stack([column_sum(d_first * normed_one), column_sum(d_second * normed_two)])
        g_width = jnp.stack(
            [
                column_sum(d_first),
                column_sum(d_second),
                column_sum(d_branch_low),
                column_sum(d_ffn_low),
            ]
        )
        g_hidden_bias = jnp.stack([column_sum(d_gate), column_sum(d_up), column_sum(d_down_in)])
        g_hidden_scale = column_sum(d_down_in * hidden_hat)
        out_all = lax.dynamic_update_index_in_dim(carried[0], result, batch_idx, 0)
        grad_all = lax.dynamic_update_index_in_dim(carried[1], d_tokens, batch_idx, 0)
        updates = (
            g_query,
            g_key,
            g_value,
            g_head_bias,
            g_head_scale,
            g_out,
            g_norm,
            g_width,
            g_gate_one,
            g_up_one,
            g_down,
            g_hidden_bias,
            g_hidden_scale,
        )
        return (
            out_all,
            grad_all,
            tuple((before + added for before, added in zip(carried[2], updates))),
        )

    zeros_acc = (
        jnp.zeros((width, local_dim), f32),
        jnp.zeros((width, local_dim), f32),
        jnp.zeros((width, local_dim), f32),
        jnp.zeros((3, local_heads, head_size), f32),
        jnp.zeros((local_heads, head_size), f32),
        jnp.zeros((local_dim, width), f32),
        jnp.zeros((2, width), f32),
        jnp.zeros((4, width), f32),
        jnp.zeros((width, local_hidden), f32),
        jnp.zeros((width, local_hidden), f32),
        jnp.zeros((local_hidden, width), f32),
        jnp.zeros((3, local_hidden), f32),
        jnp.zeros((local_hidden,), f32),
    )
    start = (jnp.zeros(tokens.shape, bf16), jnp.zeros(tokens.shape, f32), zeros_acc)
    out_all, grad_all, summed = lax.fori_loop(0, micro, one_batch, start)
    (
        acc_query,
        acc_key,
        acc_value,
        acc_head_bias,
        acc_head_scale,
        acc_out,
        acc_norm,
        acc_width,
        acc_gate_one,
        acc_up_one,
        acc_down,
        acc_hidden_bias,
        acc_hidden_scale,
    ) = summed
    acc_qkv = jnp.stack([acc_query, acc_key, acc_value])
    acc_gate = jnp.stack([acc_gate_one, acc_up_one])
    sharded = (
        acc_qkv,
        acc_head_bias,
        acc_head_scale,
        acc_out,
        acc_norm,
        acc_width,
        acc_gate,
        acc_down,
    )
    hidden_done = lax.psum((acc_hidden_bias, acc_hidden_scale), (SHARD, CTX))
    return (
        out_all,
        grad_all,
        lax.psum_scatter(
            lax.psum(sharded[0].astype(jnp.bfloat16), CTX),
            SHARD,
            scatter_dimension=1,
            tiled=True,
        ).astype(jnp.float32),
        lax.psum_scatter(
            lax.psum(sharded[1].astype(jnp.bfloat16), CTX),
            SHARD,
            scatter_dimension=2,
            tiled=True,
        ).astype(jnp.float32),
        lax.psum_scatter(
            lax.psum(sharded[2].astype(jnp.bfloat16), CTX),
            SHARD,
            scatter_dimension=1,
            tiled=True,
        ).astype(jnp.float32),
        lax.psum_scatter(
            lax.psum(sharded[3].astype(jnp.bfloat16), CTX),
            SHARD,
            scatter_dimension=1,
            tiled=True,
        ).astype(jnp.float32),
        lax.psum_scatter(
            lax.psum(sharded[4].astype(jnp.bfloat16), CTX),
            SHARD,
            scatter_dimension=1,
            tiled=True,
        ).astype(jnp.float32),
        lax.psum_scatter(
            lax.psum(sharded[5].astype(jnp.bfloat16), CTX),
            SHARD,
            scatter_dimension=1,
            tiled=True,
        ).astype(jnp.float32),
        lax.psum_scatter(
            lax.psum(sharded[6].astype(jnp.bfloat16), CTX),
            SHARD,
            scatter_dimension=1,
            tiled=True,
        ).astype(jnp.float32),
        hidden_done[0],
        hidden_done[1],
        lax.psum_scatter(
            lax.psum(sharded[7].astype(jnp.bfloat16), CTX),
            SHARD,
            scatter_dimension=1,
            tiled=True,
        ).astype(jnp.float32),
    )


MESH = pl.DeviceIdType.MESH
LIMIT = 56 * 1024 * 1024
ANY = pl.BlockSpec(memory_space=pl.ANY)
IN_VMEM = pl.BlockSpec(memory_space=pltpu.VMEM)
CORE, ACROSS, BESIDE, UP, DOWN, SWAP, FAR = range(7)
ROW, COL = range(2)


def place_of():
    index = lax.axis_index(SHARD)
    return (lax.div(index, 2), lax.rem(index, 2), lax.axis_index(CTX), lax.axis_index(TP))


def when(condition, action):
    if condition is None:
        action()
    else:
        pl.when(condition)(action)


def both(first, second):
    return jnp.logical_and(first, second)


def device(place, way):
    z, k, x, y = place
    return {
        CORE: {SHARD: 2 * z + 1 - k},
        ACROSS: {CTX: 1 - x},
        BESIDE: {TP: 1 - y},
        UP: {SHARD: 2 * z + 2 + k},
        DOWN: {SHARD: 2 * z - 2 + k},
        SWAP: {SHARD: 2 * z + 1 - k, CTX: 1 - x},
        FAR: {SHARD: 2 * z + 1 - k, CTX: 1 - x, TP: 1 - y},
    }[way]


def greet(layers, place, diagonals):
    z, k, x, y = place
    barrier = pltpu.get_barrier_semaphore()

    def hello(way):
        pl.semaphore_signal(barrier, inc=1, device_id=device(place, way), device_id_type=MESH)

    hello(CORE)
    hello(ACROSS)
    hello(BESIDE)
    pl.when(z > 0)(lambda: hello(DOWN))
    pl.when(z < layers - 1)(lambda: hello(UP))
    count = 3 + jnp.where(z > 0, 1, 0) + jnp.where(z < layers - 1, 1, 0)
    for way in diagonals:
        pl.when(k != x)(lambda way=way: hello(way))
        count = count + jnp.where(k != x, 1, 0)
    pl.semaphore_wait(barrier, count)


class Links:
    def __init__(self, place, send_sem, recv_sem):
        self.place, self.send_sem, self.recv_sem = place, send_sem, recv_sem
        self.used = 0
        self.sent = []

    def take(self, count):
        first = self.used
        self.used += count
        return first

    def copy(self, way, at, source, target):
        return pltpu.make_async_remote_copy(
            src_ref=source,
            dst_ref=target,
            send_sem=self.send_sem.at[at],
            recv_sem=self.recv_sem.at[at],
            device_id=device(self.place, way),
            device_id_type=MESH,
        )

    def send(self, condition, copy):
        when(condition, copy.start)
        self.sent.append((condition, copy))

    def finish(self):
        for condition, copy in self.sent:
            when(condition, copy.wait_send)


def piece_view(kind, rows, cols, ref, y, s, first, size):
    if kind == ROW:
        at_row, at_col = s * rows + first, y * cols
    else:
        at_row, at_col = y * rows + first, s * cols
    at_row, at_col = pl.multiple_of(at_row, 16), pl.multiple_of(at_col, 128)
    return ref.at[pl.ds(at_row, size), pl.ds(at_col, cols)]


def cut_rows(ref, first, size):
    return ref.at[pl.ds(pl.multiple_of(first, 16), size), :]


class Gather:
    def __init__(self, layers, links, kind, own, full, split, local_sem):
        self.layers, self.links, self.kind, self.own, self.full = layers, links, kind, own, full
        self.rows, self.cols = own.shape
        self.split, self.half = split, split // 2
        self.local_sem = local_sem
        n = layers
        self.z_a = links.take(2 * n)
        self.z_b = links.take(2 * n)
        self.x_a, self.x_b = links.take(n), links.take(n)
        self.y_a, self.y_b = links.take(n), links.take(1)
        self.core_a, self.core_b = links.take(2 * n), links.take(2 * n)

    @staticmethod
    def sem_count(layers):
        return 11 * layers + 1

    def copy(self, way, at, y, z, first, size, from_own=False, other_core=False):
        k = self.links.place[1]
        s = 2 * z + (1 - k if other_core else k)
        there = piece_view(self.kind, self.rows, self.cols, self.full, y, s, first, size)
        here = cut_rows(self.own, first, size) if from_own else there
        return self.links.copy(way, at, here, there)

    def half_a(self, way, at, y, z, which, from_own=False):
        return self.copy(way, at, y, z, which * self.half, self.half, from_own)

    def part_a(self, way, at, y, z, from_own=False, other_core=False):
        return self.copy(way, at, y, z, 0, self.split, from_own, other_core)

    def part_b(self, way, at, y, z, from_own=False, other_core=False):
        return self.copy(
            way, at, y, z, self.split, self.rows - self.split, from_own, other_core
        )

    def z_at(self, base, way, z):
        return base + (0 if way == UP else self.layers) + z

    def core_at(self, base, y, z):
        return base + 2 * z + y

    def begin(self):
        z, k, x, y = self.links.place
        send = self.links.send
        low, high = z > 0, z < self.layers - 1
        own_view = piece_view(
            self.kind, self.rows, self.cols, self.full, y, 2 * z + k, 0, self.rows
        )
        self.local = pltpu.make_async_copy(self.own, own_view, self.local_sem)
        if self.split < self.rows:
            send(None, self.part_b(BESIDE, self.y_b, y, z, True))
            same = x == y
            send(both(same, high), self.part_b(UP, self.z_at(self.z_b, UP, z), y, z, True))
            send(both(same, low), self.part_b(DOWN, self.z_at(self.z_b, DOWN, z), y, z, True))
        if self.split:
            send(high, self.half_a(UP, self.z_at(self.z_a, UP, z), y, z, x, True))
            send(low, self.half_a(DOWN, self.z_at(self.z_a, DOWN, z), y, z, x, True))
            send(None, self.part_a(BESIDE, self.y_a + z, y, z, True))
            send(None, self.part_a(CORE, self.core_at(self.core_a, y, z), y, z, True))
        if self.split < self.rows:
            send(None, self.part_b(CORE, self.core_at(self.core_b, y, z), y, z, True))
        self.local.start()

    def cross_y(self):
        if self.split == self.rows:
            return
        z, k, x, y = self.links.place
        send = self.links.send
        self.part_b(BESIDE, self.y_b, 1 - y, z).wait_recv()
        other = x != y
        low, high = z > 0, z < self.layers - 1
        send(both(other, high), self.part_b(UP, self.z_at(self.z_b, UP, z), 1 - y, z))
        send(both(other, low), self.part_b(DOWN, self.z_at(self.z_b, DOWN, z), 1 - y, z))
        send(None, self.part_b(CORE, self.core_at(self.core_b, 1 - y, z), 1 - y, z))

    def steps(self, step):
        z = self.links.place[0]
        below, above = z - 1 - step, z + 1 + step
        return (
            (UP, below, below >= 0, z < self.layers - 1),
            (DOWN, above, above <= self.layers - 1, z > 0),
        )

    def along_z(self, step):
        z, k, x, y = self.links.place
        send = self.links.send
        for way, origin, there, further in self.steps(step):
            if self.split < self.rows:
                came = self.part_b(way, self.z_at(self.z_b, way, origin), x, origin)
                when(there, came.wait_recv)
                send(both(there, further), came)
                send(there, self.part_b(ACROSS, self.x_b + origin, x, origin))
                send(there, self.part_b(CORE, self.core_at(self.core_b, x, origin), x, origin))
            if self.split:
                came = self.half_a(way, self.z_at(self.z_a, way, origin), y, origin, x)
                when(there, came.wait_recv)
                send(both(there, further), came)
                send(there, self.half_a(ACROSS, self.x_a + origin, y, origin, x))

    def along_x(self, step):
        z, k, x, y = self.links.place
        send = self.links.send
        for way, origin, there, further in self.steps(step):
            if self.split:
                when(there, self.half_a(ACROSS, self.x_a + origin, y, origin, 1 - x).wait_recv)
                send(there, self.part_a(BESIDE, self.y_a + origin, y, origin))
                send(there, self.part_a(CORE, self.core_at(self.core_a, y, origin), y, origin))
            if self.split < self.rows:
                when(there, self.part_b(ACROSS, self.x_b + origin, 1 - x, origin).wait_recv)
                at = self.core_at(self.core_b, 1 - x, origin)
                send(there, self.part_b(CORE, at, 1 - x, origin))

    def along_y(self, step):
        if not self.split:
            return
        z, k, x, y = self.links.place
        send = self.links.send
        todo = ((None, z, None, None),) if step < 0 else self.steps(step)
        for way, origin, there, further in todo:
            when(there, self.part_a(BESIDE, self.y_a + origin, 1 - y, origin).wait_recv)
            at = self.core_at(self.core_a, 1 - y, origin)
            send(there, self.part_a(CORE, at, 1 - y, origin))

    def stages(self):
        found = [[self.begin], [self.cross_y]]
        for step in range(self.layers + 1):
            now = []
            if step < self.layers - 1:
                now.append(functools.partial(self.along_z, step))
            if step == 0:
                now.append(functools.partial(self.along_y, -1))
            if 0 <= step - 1 < self.layers - 1:
                now.append(functools.partial(self.along_x, step - 1))
            if 0 <= step - 2 < self.layers - 1:
                now.append(functools.partial(self.along_y, step - 2))
            found.append(now)
        return found

    def arrived(self):
        self.local.wait()
        for layer in range(self.layers):
            for y in range(2):
                if self.split:
                    at = self.core_at(self.core_a, y, layer)
                    self.part_a(CORE, at, y, layer, other_core=True).wait_recv()
                if self.split < self.rows:
                    at = self.core_at(self.core_b, y, layer)
                    self.part_b(CORE, at, y, layer, other_core=True).wait_recv()


def ticks_of(jobs, lead):
    plans = [job.stages() for job in jobs]
    ticks = [[] for _ in range(len(jobs) + max([len(plan) for plan in plans]))]
    for number, plan in enumerate(plans):
        for stage, actions in enumerate(plan):
            at = max(0, number - lead) if stage == 0 else number + stage
            ticks[at] += actions
    return [tick for tick in ticks if tick]


class Swap:
    def __init__(self, links, source, target, local_sem):
        z, k, x, y = links.place
        self.same, self.other = k == x, k != x
        self.here = pltpu.make_async_copy(source, target, local_sem)
        self.there = links.copy(SWAP, links.take(1), source, target)

    def begin(self):
        pl.when(self.same)(self.here.start)
        pl.when(self.other)(self.there.start)

    def arrived(self):
        pl.when(self.same)(self.here.wait)
        pl.when(self.other)(self.there.wait)


class Cross:
    def __init__(self, links, source, target, local_sem):
        y = links.place[3]
        at = links.take(1)
        self.here = pltpu.make_async_copy(source, target.at[y], local_sem)
        self.out = links.copy(BESIDE, at, source, target.at[y])
        self.back = links.copy(BESIDE, at, source, target.at[1 - y])

    def begin(self):
        self.here.start()
        self.out.start()

    def arrived(self):
        self.here.wait()
        self.out.wait_send()
        self.back.wait_recv()


class Spread:
    def __init__(self, links, block, both_images, local_sem):
        z, k, x, y = links.place
        self.same, self.other = k == x, k != x
        here, first, second = links.take(1), links.take(1), 0
        target = both_images.at[y]
        self.keep = pltpu.make_async_copy(block, target, local_sem)
        self.beside = links.copy(BESIDE, here, block, target)
        self.swap = links.copy(SWAP, first, block, target)
        self.far = links.copy(FAR, here, block, target)
        self.came = links.copy(BESIDE, here, block, both_images.at[1 - y])

    def begin(self):
        def same():
            self.keep.start()
            self.beside.start()

        def other():
            self.swap.start()
            self.far.start()

        pl.when(self.same)(same)
        pl.when(self.other)(other)

    def arrived(self):
        def same():
            self.keep.wait()
            self.beside.wait_send()

        def other():
            self.swap.wait()
            self.far.wait_send()

        pl.when(self.same)(same)
        pl.when(self.other)(other)
        self.came.wait_recv()


def gather_kernel(layers, jobs, swaps, crosses, mats, *refs):
    own, refs = refs[:mats], refs[mats:]
    swap_in, refs = refs[:swaps], refs[swaps:]
    cross_in, refs = refs[:crosses], refs[crosses:]
    full, refs = refs[:mats], refs[mats:]
    swap_out, refs = refs[:swaps], refs[swaps:]
    cross_out, refs = refs[:crosses], refs[crosses:]
    send_sem, recv_sem, local_sem = refs
    place = place_of()
    greet(layers, place, (SWAP,) if swaps else ())
    links = Links(place, send_sem, recv_sem)
    y = place[3]
    extras = []
    for source, target in zip(swap_in, swap_out):
        if len(source.shape) > len(target.shape):
            source = source.at[y]
        extras.append(Swap(links, source, target, local_sem.at[len(extras)]))
    for source, target in zip(cross_in, cross_out):
        extras.append(Cross(links, source, target, local_sem.at[len(extras)]))
    for extra in extras:
        extra.begin()
    todo = []
    for mat, lead, kind, split in jobs:
        piece, whole = own[mat], full[mat]
        if lead is not None:
            piece, whole = piece.at[lead], whole.at[lead]
        at = local_sem.at[len(extras) + len(todo)]
        todo.append(Gather(layers, links, kind, piece, whole, split, at))
    for tick in ticks_of(todo, 1):
        for action in tick:
            action()
    for job in todo + extras:
        job.arrived()
    links.finish()


def full_shape(layers, kind, piece):
    if kind == ROW:
        return piece[:-2] + (piece[-2] * layers * 2, piece[-1] * 2)
    return (piece[-2] * 2, piece[-1] * layers * 2)


def gather(layers, number, jobs, own, swap_in=(), cross_in=()):
    kinds = {job[0]: job[2] for job in jobs}
    shapes = [
        jax.ShapeDtypeStruct(full_shape(layers, kinds[i], piece.shape), piece.dtype)
        for i, piece in enumerate(own)
    ]
    for item in swap_in:
        big = item.dtype == jnp.bfloat16
        shapes.append(jax.ShapeDtypeStruct(item.shape[1:] if big else item.shape, item.dtype))
    for item in cross_in:
        shapes.append(jax.ShapeDtypeStruct((2,) + item.shape, item.dtype))
    extra = len(swap_in) + len(cross_in)
    sems = len(jobs) * Gather.sem_count(layers) + extra
    given = list(own) + list(swap_in) + list(cross_in)
    return pl.pallas_call(
        functools.partial(gather_kernel, layers, jobs, len(swap_in), len(cross_in), len(own)),
        out_shape=shapes,
        in_specs=[ANY] * len(given),
        out_specs=[ANY] * len(shapes),
        scratch_shapes=[
            pltpu.SemaphoreType.DMA((sems,)),
            pltpu.SemaphoreType.DMA((sems,)),
            pltpu.SemaphoreType.DMA((len(jobs) + extra,)),
        ],
        compiler_params=pltpu.CompilerParams(collective_id=number, has_side_effects=True),
    )(*given)


def by_chunks(shape, body):
    rows, cols = shape
    chunk = 16
    while rows % (2 * chunk) == 0 and 2 * chunk * cols <= 16384:
        chunk *= 2

    def step(i, nothing):
        body((pl.ds(pl.multiple_of(i * chunk, 16), chunk), slice(None)))
        return nothing

    lax.fori_loop(0, rows // chunk, step, 0)


def add_into(target, term):
    def body(where):
        total = target[where].astype(jnp.float32) + term[where].astype(jnp.float32)
        target[where] = total.astype(target.dtype)

    by_chunks(target.shape, body)


def store_sum(out, *terms):
    def body(where):
        total = terms[0][where].astype(jnp.float32)
        for term in terms[1:]:
            total = total + term[where].astype(jnp.float32)
        out[where] = total

    by_chunks(out.shape, body)


class Reduce:
    def __init__(self, layers, links, kind, grad, out, split, scratch, local_sem, local_base):
        self.layers, self.links, self.kind, self.grad, self.out = layers, links, kind, grad, out
        self.mine, self.core_in, self.y_in, self.x_in, self.up_in, self.down_in, self.last = scratch
        self.rows, self.cols = self.mine.shape[-2:]
        self.split = split
        self.local_sem, self.local_base = local_sem, local_base
        n = layers
        self.core = links.take(2 * n)
        self.y_a, self.x_b = links.take(n), links.take(n)
        self.z_a, self.z_b = links.take(2 * n), links.take(2 * n)
        self.end_a, self.end_b, self.end_c = links.take(1), links.take(1), links.take(1)
        self.order = []
        low, high = 0, layers - 1
        while low <= high:
            self.order.append(high)
            if low < high:
                self.order.append(low)
            low, high = low + 1, high - 1

    @staticmethod
    def sem_count(layers):
        return 8 * layers + 3

    def part_a(self, ref):
        return cut_rows(ref, 0, self.split)

    def part_b(self, ref):
        return cut_rows(ref, self.split, self.rows - self.split)

    def grad_piece(self, y, s):
        return piece_view(self.kind, self.rows, self.cols, self.grad, y, s, 0, self.rows)

    def local(self, y, layer):
        k = self.links.place[1]
        return pltpu.make_async_copy(
            self.grad_piece(y, 2 * layer + k),
            self.mine.at[y, layer],
            self.local_sem.at[self.local_base + 2 * layer + y],
        )

    def to_core(self, y, layer):
        k = self.links.place[1]
        return self.links.copy(
            CORE,
            self.core + 2 * layer + y,
            self.grad_piece(y, 2 * layer + 1 - k),
            self.core_in.at[y, layer],
        )

    def begin(self):
        for layer in self.order:
            for y in range(2):
                self.links.send(None, self.to_core(y, layer))
                self.local(y, layer).start()

    def to_y(self, layer):
        y = self.links.place[3]
        source = self.part_a(self.mine.at[1 - y, layer])
        return self.links.copy(BESIDE, self.y_a + layer, source, self.y_in.at[layer])

    def to_x(self, layer):
        x = self.links.place[2]
        source = self.part_b(self.mine.at[1 - x, layer])
        return self.links.copy(ACROSS, self.x_b + layer, source, self.x_in.at[layer])

    def chip_sum(self):
        for layer in self.order:
            for side in range(2):
                self.local(side, layer).wait()
                self.to_core(side, layer).wait_recv()
                add_into(self.mine.at[side, layer], self.core_in.at[side, layer])
            self.links.send(None, self.to_y(layer))
            self.links.send(None, self.to_x(layer))

    def plane_sum(self):
        z, k, x, y = self.links.place
        for layer in self.order:
            self.to_y(layer).wait_recv()
            add_into(self.part_a(self.mine.at[y, layer]), self.y_in.at[layer])
            self.to_x(layer).wait_recv()
            add_into(self.part_b(self.mine.at[x, layer]), self.x_in.at[layer])

    def chain(self, way, layer):
        z, k, x, y = self.links.place
        inbox = self.up_in if way == UP else self.down_in
        add = 0 if way == UP else self.layers
        found = []
        for base, part, side in ((self.z_a, self.part_a, y), (self.z_b, self.part_b, x)):
            total, box = part(self.mine.at[side, layer]), part(inbox.at[layer])
            found.append((total, box, self.links.copy(way, base + add + layer, total, box)))
        return found

    def take(self, way, layer):
        for total, box, copy in self.chain(way, layer):
            copy.wait_recv()
            add_into(total, box)

    def along_z(self, depth):
        z = self.links.place[0]
        top = self.layers - 1
        for way, here, goals in (
            (UP, z == depth, range(top, depth, -1)),
            (DOWN, z == top - depth, range(0, top - depth)),
        ):
            for layer in goals:
                if depth:
                    pl.when(here)(functools.partial(self.take, way, layer))
                for total, box, copy in self.chain(way, layer):
                    self.links.send(here, copy)

    def ending(self):
        z, k, x, y = self.links.place
        pl.when(z > 0)(functools.partial(self.take, UP, z))
        pl.when(z < self.layers - 1)(functools.partial(self.take, DOWN, z))
        self.sum_a, self.sum_b = self.part_a(self.mine.at[y, z]), self.part_b(self.mine.at[x, z])
        self.got_a, self.got_b = self.part_a(self.last.at[0]), self.part_b(self.last.at[0])
        self.got_y = self.part_b(self.last.at[1])
        self.x_end = self.links.copy(ACROSS, self.end_a, self.sum_a, self.got_a)
        self.y_end = self.links.copy(BESIDE, self.end_b, self.sum_b, self.got_y)
        self.x_last = self.links.copy(ACROSS, self.end_c, self.sum_b, self.got_b)
        self.links.send(y != x, self.y_end)
        self.links.send(None, self.x_end)

    def owner(self):
        z, k, x, y = self.links.place

        def own():
            self.y_end.wait_recv()
            add_into(self.sum_b, self.got_y)

        pl.when(y == x)(own)
        self.links.send(y == x, self.x_last)
        self.x_end.wait_recv()
        store_sum(self.part_a(self.out), self.sum_a, self.got_a)

    def write(self):
        z, k, x, y = self.links.place
        out_b = self.part_b(self.out)

        def received():
            self.x_last.wait_recv()
            store_sum(out_b, self.got_b)

        pl.when(y != x)(received)
        pl.when(y == x)(lambda: store_sum(out_b, self.sum_b))

    def stages(self):
        chains = [[functools.partial(self.along_z, depth)] for depth in range(self.layers - 1)]
        return [
            [self.begin], [self.chip_sum], [self.plane_sum], *chains,
            [self.ending], [self.owner], [self.write],
        ]


class Total:
    def __init__(self, layers, links, given, out, boxes, layer_boxes):
        self.layers, self.links, self.given, self.out = layers, links, given, out
        self.boxes, self.layer_boxes = boxes, layer_boxes
        self.pair = [links.take(1) for _ in range(3)]
        self.z_up, self.z_down = links.take(layers), links.take(layers)

    @staticmethod
    def sem_count(layers):
        return 3 + 2 * layers

    def exchange(self, number):
        way = (CORE, ACROSS, BESIDE)[number]
        source = self.given if number == 0 else self.boxes.at[2 + number]
        return self.links.copy(way, self.pair[number], source, self.boxes.at[number])

    def begin(self):
        self.links.send(None, self.exchange(0))

    def join(self, number):
        z = self.links.place[0]
        self.exchange(number).wait_recv()
        mine = self.given if number == 0 else self.boxes.at[2 + number]
        result = self.layer_boxes.at[z] if number == 2 else self.boxes.at[3 + number]
        store_sum(result, mine, self.boxes.at[number])
        if number < 2:
            self.links.send(None, self.exchange(number + 1))
        else:
            self.links.send(z < self.layers - 1, self.pass_on(UP, z))
            self.links.send(z > 0, self.pass_on(DOWN, z))

    def pass_on(self, way, layer):
        box = self.layer_boxes.at[layer]
        return self.links.copy(way, (self.z_up if way == UP else self.z_down) + layer, box, box)

    def along_z(self, step):
        z = self.links.place[0]
        top = self.layers - 1
        below, above = z - 1 - step, z + 1 + step
        for way, origin, there, further in (
            (UP, below, below >= 0, z < top),
            (DOWN, above, above <= top, z > 0),
        ):
            copy = self.pass_on(way, origin)
            when(there, copy.wait_recv)
            self.links.send(both(there, further), copy)

    def write(self):
        store_sum(self.out, *[self.layer_boxes.at[layer] for layer in range(self.layers)])

    def stages(self):
        joins = [[functools.partial(self.join, number)] for number in range(3)]
        moves = [[functools.partial(self.along_z, step)] for step in range(self.layers - 1)]
        return [[self.begin], *joins, *moves, [self.write]]


def reduce_kernel(layers, jobs, mats, blocks, *refs):
    grads, refs = refs[:mats], refs[mats:]
    total_in, refs = refs[0], refs[1:]
    block_in, refs = refs[:blocks], refs[blocks:]
    outs, refs = refs[:mats], refs[mats:]
    total_out, refs = refs[0], refs[1:]
    block_out, refs = refs[:blocks], refs[blocks:]
    scratch = refs[: 7 * len(jobs)]
    boxes, layer_boxes, send_sem, recv_sem, local_sem = refs[7 * len(jobs) :]
    place = place_of()
    greet(layers, place, (SWAP, FAR))
    links = Links(place, send_sem, recv_sem)
    todo = []
    for number, (mat, lead, kind, split) in enumerate(jobs):
        grad, out = grads[mat], outs[mat]
        if lead is not None:
            grad, out = grad.at[lead], out.at[lead]
        own = scratch[7 * number : 7 * number + 7]
        at = number * 2 * layers
        todo.append(Reduce(layers, links, kind, grad, out, split, own, local_sem, at))
    todo.insert(1, Total(layers, links, total_in, total_out, boxes, layer_boxes))
    extras = [
        Spread(links, source, target, local_sem.at[len(jobs) * 2 * layers + i])
        for i, (source, target) in enumerate(zip(block_in, block_out))
    ]
    for number, tick in enumerate(ticks_of(todo, 1)):
        for action in tick:
            action()
        if number == 2:
            for extra in extras:
                extra.begin()
    for extra in extras:
        extra.arrived()
    links.finish()


def piece_shape(layers, kind, full):
    if kind == ROW:
        return full[:-2] + (full[-2] // (2 * layers), full[-1] // 2)
    return (full[-2] // 2, full[-1] // (2 * layers))


def reduce_grads(layers, number, jobs, grads, total, blocks):
    kinds = {job[0]: job[2] for job in jobs}
    pieces = [piece_shape(layers, kinds[i], g.shape) for i, g in enumerate(grads)]
    scratch = []
    for mat, lead, kind, split in jobs:
        rows, cols = pieces[mat][-2:]
        for lead_shape, here in (
            ((2, layers), rows), ((2, layers), rows), ((layers,), split), ((layers,), rows - split),
            ((layers,), rows), ((layers,), rows), ((2,), rows),
        ):
            scratch.append(pltpu.VMEM(lead_shape + (here, cols), jnp.bfloat16))
    sems = len(jobs) * Reduce.sem_count(layers) + Total.sem_count(layers) + 2 * len(blocks)
    images = [jax.ShapeDtypeStruct((2,) + block.shape, block.dtype) for block in blocks]
    return pl.pallas_call(
        functools.partial(reduce_kernel, layers, jobs, len(grads), len(blocks)),
        out_shape=[jax.ShapeDtypeStruct(piece, jnp.float32) for piece in pieces]
        + [jax.ShapeDtypeStruct(total.shape, total.dtype)]
        + images,
        in_specs=[ANY] * len(grads) + [IN_VMEM] + [ANY] * len(blocks),
        out_specs=[IN_VMEM] * len(pieces) + [IN_VMEM] + [ANY] * len(blocks),
        scratch_shapes=scratch
        + [
            pltpu.VMEM((5,) + total.shape, jnp.float32),
            pltpu.VMEM((layers,) + total.shape, jnp.float32),
            pltpu.SemaphoreType.DMA((sems,)),
            pltpu.SemaphoreType.DMA((sems,)),
            pltpu.SemaphoreType.DMA((len(jobs) * 2 * layers + len(blocks),)),
        ],
        compiler_params=pltpu.CompilerParams(
            collective_id=number, has_side_effects=True, vmem_limit_bytes=LIMIT
        ),
    )(*grads, total, *blocks)


def pair_lanes(shape, head_size):
    lane = lax.broadcasted_iota(jnp.int32, shape, len(shape) - 1)
    return lane < head_size


def dot_last(left, right):
    return lax.dot_general(left, right, (((1,), (1,)), ((), ())), preferred_element_type=jnp.float32)


def dot_first(left, right):
    return lax.dot_general(left, right, (((0,), (0,)), ((), ())), preferred_element_type=jnp.float32)


def dot(left, right):
    return lax.dot_general(left, right, (((1,), (0,)), ((), ())), preferred_element_type=jnp.float32)


def only_head(values, head, head_size):
    lane = lax.broadcasted_iota(jnp.int32, (1, values.shape[1]), 1)
    keep = (lane < head_size) if head == 0 else (lane >= head_size)
    return values * jnp.where(keep, 1.0, 0.0).astype(values.dtype)


LOG2_E = 1.4426950408889634


def mix_kernel(head_size, q_ref, k_ref, v_ref, bias_ref, o_ref, stat_ref):
    scale = LOG2_E / math.sqrt(head_size)
    q, k, v = q_ref[...], k_ref[...], v_ref[...]
    bias = bias_ref[...]
    parts = []
    for head in range(2):
        s = dot_last(only_head(q, head, head_size), k) * scale + bias
        top = jnp.max(s, axis=1, keepdims=True)
        e = jnp.exp2(s - top)
        total = jnp.sum(e, axis=1, keepdims=True)
        parts.append(dot(e.astype(jnp.bfloat16), v) * (1.0 / total))
        level = jnp.broadcast_to(top + jnp.log2(total), (q.shape[0], 128))
        stat_ref[0, head : head + 1, :] = jnp.transpose(level)[0:1, :]
    o_ref[...] = jnp.where(pair_lanes(o_ref.shape, head_size), parts[0], parts[1])


def mix_forward(q, k, v, bias, head_size):
    rows, width = q.shape
    keys = k.shape[0]
    pairs = width // (2 * head_size)
    lanes = 2 * head_size
    return pl.pallas_call(
        functools.partial(mix_kernel, head_size),
        grid=(pairs,),
        out_shape=[
            jax.ShapeDtypeStruct((rows, width), jnp.float32),
            jax.ShapeDtypeStruct((pairs, 2, rows), jnp.float32),
        ],
        in_specs=[
            pl.BlockSpec((rows, lanes), lambda i: (0, i)),
            pl.BlockSpec((keys, lanes), lambda i: (0, i)),
            pl.BlockSpec((keys, lanes), lambda i: (0, i)),
            pl.BlockSpec((1, keys), lambda i: (0, 0)),
        ],
        out_specs=[
            pl.BlockSpec((rows, lanes), lambda i: (0, i)),
            pl.BlockSpec((1, 2, rows), lambda i: (i, 0, 0)),
        ],
        compiler_params=pltpu.CompilerParams(vmem_limit_bytes=LIMIT),
    )(q, k, v, bias)


def mix_back_kernel(
    head_size, q_ref, k_ref, v_ref, do_ref, stat_ref, dot_ref, bias_ref, dq_ref, dk_ref, dv_ref
):
    scale = 1.0 / math.sqrt(head_size)
    q, k, v, do = q_ref[...], k_ref[...], v_ref[...], do_ref[...]
    bias = bias_ref[...]
    found = []
    for head in range(2):
        s = dot_last(k, only_head(q, head, head_size)) * (scale * LOG2_E) + bias
        p = jnp.exp2(s - stat_ref[0, head : head + 1, :])
        dp = dot_last(v, only_head(do, head, head_size))
        ds = (p * (dp - dot_ref[0, head : head + 1, :])).astype(jnp.bfloat16)
        dv = dot(p.astype(jnp.bfloat16), do)
        dk = dot(ds, q) * scale
        dq = dot_first(ds, k) * scale
        found.append((dq, dk, dv))
    for ref, first, second in zip((dq_ref, dk_ref, dv_ref), *found):
        ref[...] = jnp.where(pair_lanes(ref.shape, head_size), first, second).astype(ref.dtype)


def mix_backward(q, k, v, do, stats, row_dots, bias, head_size):
    rows, width = q.shape
    keys = k.shape[0]
    pairs = width // (2 * head_size)
    lanes = 2 * head_size
    of_rows = pl.BlockSpec((rows, lanes), lambda i: (0, i))
    of_keys = pl.BlockSpec((keys, lanes), lambda i: (0, i))
    of_stats = pl.BlockSpec((1, 2, rows), lambda i: (i, 0, 0))
    return pl.pallas_call(
        functools.partial(mix_back_kernel, head_size),
        grid=(pairs,),
        out_shape=[
            jax.ShapeDtypeStruct((rows, width), jnp.float32),
            jax.ShapeDtypeStruct((keys, width), jnp.bfloat16),
            jax.ShapeDtypeStruct((keys, width), jnp.bfloat16),
        ],
        in_specs=[
            of_rows, of_keys, of_keys, of_rows, of_stats, of_stats,
            pl.BlockSpec((keys, 1), lambda i: (0, 0)),
        ],
        out_specs=[of_rows, of_keys, of_keys],
        compiler_params=pltpu.CompilerParams(vmem_limit_bytes=LIMIT),
    )(q, k, v, do, stats, row_dots, bias)


def turn_lanes(values, quarter):
    width = values.shape[-1]
    lane = lax.broadcasted_iota(jnp.int32, (1, width), 1)
    even = lax.rem(lax.div(lane, quarter), 2) == 0
    after = pltpu.roll(values, width - quarter, 1)
    before = pltpu.roll(values, quarter, 1)
    return jnp.where(even, -after, before)


def project_kernel(quarter, tiles, x_ref, norm_ref, w_ref, bias_ref, cos_ref, sin_ref, out_ref, n_ref):
    step = pl.program_id(0)

    @pl.when(step == 0)
    def _():
        hat, spread = standardize(x_ref[...].astype(jnp.float32))
        n_ref[...] = (hat * norm_ref[0:1, :] + norm_ref[1:2, :]).astype(jnp.bfloat16)

    raw = dot(n_ref[...], w_ref[0]) + bias_ref[0]

    @pl.when(step < 2 * tiles)
    def _():
        turned = turn_lanes(raw, quarter)
        out_ref[0] = (raw * cos_ref[...] + turned * sin_ref[...]).astype(jnp.bfloat16)

    @pl.when(step >= 2 * tiles)
    def _():
        out_ref[0] = raw.astype(jnp.bfloat16)


def project(x, norm, weights, bias, cos, sin, head_size, tile=256):
    rows, width = x.shape
    tiles = width // tile
    fixed = lambda i: (0, 0)
    return pl.pallas_call(
        functools.partial(project_kernel, head_size // 4, tiles),
        grid=(3 * tiles,),
        out_shape=[
            jax.ShapeDtypeStruct((3, rows, width), jnp.bfloat16),
            jax.ShapeDtypeStruct((rows, width), jnp.bfloat16),
        ],
        in_specs=[
            pl.BlockSpec((rows, width), fixed),
            pl.BlockSpec((2, width), fixed),
            pl.BlockSpec((1, width, tile), lambda i: (i // tiles, 0, i % tiles)),
            pl.BlockSpec((1, 1, tile), lambda i: (i // tiles, 0, i % tiles)),
            pl.BlockSpec((rows, tile), fixed),
            pl.BlockSpec((rows, tile), fixed),
        ],
        out_specs=[
            pl.BlockSpec((1, rows, tile), lambda i: (i // tiles, 0, i % tiles)),
            pl.BlockSpec((rows, width), fixed),
        ],
        compiler_params=pltpu.CompilerParams(vmem_limit_bytes=LIMIT),
    )(x, norm, weights, bias, cos, sin)


def pad_to(values, axis, size):
    pads = [(0, 0)] * values.ndim
    pads[axis] = (0, size - values.shape[axis])
    return jnp.pad(values, pads)


def round_up(size, step):
    return (size + step - 1) // step * step


def image_per_chip(
    layers,
    tokens,
    cotangent,
    valid_tokens,
    places,
    qkv_weight,
    head_biases,
    head_gain,
    out_weight,
    norm_gains,
    width_biases,
    gate_up,
    hidden_biases,
    hidden_gain,
    down_weight,
):
    f32 = jnp.float32
    bf16 = jnp.bfloat16
    z, k, x, y = place_of()
    s = 2 * z + k
    shards = 2 * layers
    width = tokens.shape[2]
    rows = tokens.shape[1]
    heads_here = head_gain.shape[0]
    heads = 2 * heads_here
    dims_here = head_gain.shape[1]
    head_size = dims_here * shards
    real_here = hidden_gain.shape[0]
    hidden_here = round_up(real_here, 128)
    real = 2 * real_here
    hidden_size = 2 * hidden_here
    score_scale = 1.0 / math.sqrt(head_size)

    heads_flat = jnp.concatenate([head_biases, head_gain[None]], axis=0).reshape(-1, 128)
    head_rows = heads_flat.shape[0]
    vectors = jnp.concatenate([norm_gains, width_biases, heads_flat], axis=0)
    vectors = pad_to(vectors, 0, 16)
    hidden_vectors = jnp.concatenate([hidden_biases, hidden_gain[None]], axis=0)
    hidden_vectors = pad_to(pad_to(hidden_vectors, 1, hidden_here), 0, 16)
    gate_pad = pad_to(gate_up, 2, hidden_here)
    down_pad = pad_to(down_weight, 0, hidden_here)

    jobs = (
        (0, 0, ROW, 64), (0, 1, ROW, 64), (0, 2, ROW, 64), (1, None, COL, 0),
        (2, None, COL, 256), (3, 0, ROW, 64), (3, 1, ROW, 64), (4, None, COL, hidden_here // 2),
    )
    (
        qkv_full, vector_full, out_full, gate_full, down_full,
        token_block, cot_block, valid_both, place_both, hidden_full,
    ) = gather(
        layers, 0, jobs, (qkv_weight, vectors, out_weight, gate_pad, down_pad),
        (tokens, cotangent, valid_tokens, places), (hidden_vectors,),
    )
    norm_scale = vector_full[0:2].astype(f32)
    width_bias = vector_full[2:6].astype(f32)
    head_part = jnp.stack([vector_full[6 : 6 + head_rows], vector_full[22 : 22 + head_rows]])
    head_part = head_part.reshape(2, head_rows, shards, 128).transpose(0, 2, 1, 3)
    head_part = head_part.reshape(2, shards, 4, heads_here, dims_here).transpose(2, 0, 3, 1, 4)
    head_part = head_part.reshape(4, heads * head_size).astype(f32)
    hidden_part = jnp.concatenate([hidden_full[0, :4], hidden_full[1, :4]], axis=1).astype(f32)

    padded = round_up(rows, 16)
    token_block = pad_to(token_block, 0, padded)
    cot_block = pad_to(cot_block, 0, padded)
    token_rows = token_block.astype(f32)
    cot_rows = cot_block.astype(f32)
    valid_row = lax.dynamic_index_in_dim(valid_both, y, 0, keepdims=False)
    row_ids = pad_to(lax.dynamic_index_in_dim(place_both[0], y, 0, keepdims=False), 0, padded)
    col_ids = pad_to(lax.dynamic_index_in_dim(place_both[1], y, 0, keepdims=False), 0, padded)
    key_bias = jnp.where(pad_to(valid_row.reshape(2, rows), 1, padded) > 0, 0.0, -1e30)
    key_bias = key_bias.astype(f32).reshape(1, 2 * padded)
    angles = angle_table(row_ids, col_ids, head_size)
    tile = 512
    cos, sin = [jnp.tile(turn(angles), (1, tile // head_size)) for turn in (jnp.cos, jnp.sin)]
    norm_one = jnp.stack([norm_scale[0], width_bias[0]])
    qkv_bias = jnp.stack([head_part[0], jnp.zeros_like(head_part[0]), head_part[1]])[:, None]
    qkv, first_in = project(token_block, norm_one, qkv_full, qkv_bias, cos, sin, head_size, tile)
    pairs = [(i, i ^ 1) for i in range(shards)]
    own = qkv[1:]
    other = lax.ppermute(own, SHARD, pairs)
    halves = jnp.stack([jnp.where(k == 0, own, other), jnp.where(k == 0, other, own)], axis=1)
    keys = halves[0].reshape(2 * padded, width)
    values = halves[1].reshape(2 * padded, width)
    mixed, stats = mix_forward(qkv[0], keys, values, key_bias, head_size)
    mix_hat, spread_mix = standardize(mixed)
    mix_in = (mix_hat * head_part[3] + head_part[2]).astype(bf16)
    branch = jnp.dot(mix_in, out_full, preferred_element_type=f32)
    resid = token_rows + (branch + width_bias[2])
    normed_two, spread_two = standardize(resid)
    second_in = (normed_two * norm_scale[1] + width_bias[1]).astype(bf16)
    gate_pre = jnp.dot(second_in, gate_full[0], preferred_element_type=f32) + hidden_part[0]
    up_pre = jnp.dot(second_in, gate_full[1], preferred_element_type=f32) + hidden_part[1]
    sigmoid_gate = jax.nn.sigmoid(gate_pre)
    silu_gate = gate_pre * sigmoid_gate
    hidden = silu_gate * up_pre
    hidden_mean = jnp.sum(hidden, axis=-1, keepdims=True) / real
    centred = hidden - hidden_mean
    extra = (hidden_size - real) * hidden_mean * hidden_mean
    hidden_var = (jnp.sum(centred * centred, axis=-1, keepdims=True) - extra) / real
    spread_hid = lax.rsqrt(jnp.maximum(hidden_var, 0.0) + EPS)
    hidden_hat = centred * spread_hid
    down_in = (hidden_hat * hidden_part[3] + hidden_part[2]).astype(bf16)
    ffn_out = jnp.dot(down_in, down_full, preferred_element_type=f32)
    result = (resid + (ffn_out + width_bias[3])).astype(bf16)

    g_down = jnp.einsum("tf,td->fd", down_in, cot_block, preferred_element_type=f32)
    d_down_in = jnp.einsum("td,fd->tf", cot_block, down_full, preferred_element_type=f32)
    grad_hid = d_down_in * hidden_part[3]
    hid_back_one = jnp.sum(grad_hid, axis=-1, keepdims=True) / real
    hid_back_two = jnp.sum(grad_hid * hidden_hat, axis=-1, keepdims=True) / real
    d_hidden = (grad_hid - hid_back_one - hidden_hat * hid_back_two) * spread_hid
    d_gate = (d_hidden * up_pre * sigmoid_gate * (1.0 + gate_pre * (1.0 - sigmoid_gate))).astype(
        bf16
    )
    d_up = (d_hidden * silu_gate).astype(bf16)
    g_gate_up = jnp.stack(
        [
            jnp.einsum("td,tf->df", second_in, d_gate, preferred_element_type=f32).astype(bf16),
            jnp.einsum("td,tf->df", second_in, d_up, preferred_element_type=f32).astype(bf16),
        ]
    )
    d_second = jnp.einsum("tf,df->td", d_gate, gate_full[0], preferred_element_type=f32)
    d_second = d_second + jnp.einsum("tf,df->td", d_up, gate_full[1], preferred_element_type=f32)
    d_resid = cot_rows + norm_back(d_second * norm_scale[1], normed_two, spread_two)
    d_branch_low = d_resid.astype(bf16)
    g_out = jnp.einsum("tm,tn->mn", mix_in, d_branch_low, preferred_element_type=f32)
    d_mix_in = jnp.einsum("tn,mn->tm", d_branch_low, out_full, preferred_element_type=f32)
    d_mixed = norm_back(d_mix_in * head_part[3], mix_hat, spread_mix).astype(bf16)
    row_dots = jnp.sum((d_mixed.astype(f32) * mixed).reshape(padded, heads // 2, 2, head_size), axis=-1)
    row_dots = row_dots.transpose(1, 2, 0)
    d_query, d_keys, d_values = mix_backward(
        qkv[0], keys, values, d_mixed, stats, row_dots, key_bias.reshape(-1, 1), head_size
    )

    def pair_sum(parts):
        mine = lax.dynamic_slice_in_dim(parts, k * padded, padded, axis=0)
        yours = lax.dynamic_slice_in_dim(parts, (1 - k) * padded, padded, axis=0)
        return mine.astype(f32) + lax.ppermute(yours, SHARD, pairs).astype(f32)

    cos, sin = jnp.cos(angles), jnp.sin(angles)

    def turn_back(values):
        values = values.reshape(padded, heads, head_size)
        turned = values * cos[:, None] - turn_half(values) * sin[:, None]
        return turned.reshape(padded, width).astype(bf16)

    d_query_low = turn_back(d_query)
    d_key_low = turn_back(pair_sum(d_keys))
    d_value_low = pair_sum(d_values).astype(bf16)
    g_qkv = jnp.stack(
        [
            jnp.einsum("tn,tm->nm", first_in, part, preferred_element_type=f32).astype(bf16)
            for part in (d_query_low, d_key_low, d_value_low)
        ]
    )
    d_first = jnp.einsum("tm,nm->tn", d_query_low, qkv_full[0], preferred_element_type=f32)
    d_first = d_first + jnp.einsum("tm,nm->tn", d_key_low, qkv_full[1], preferred_element_type=f32)
    d_first = d_first + jnp.einsum(
        "tm,nm->tn", d_value_low, qkv_full[2], preferred_element_type=f32
    )
    normed_one, spread_one = standardize(token_rows)
    d_tokens = d_resid + norm_back(d_first * norm_scale[0], normed_one, spread_one)

    vector_grads = jnp.concatenate(
        [
            column_sum(d_query_low),
            column_sum(d_value_low),
            column_sum(d_mix_in),
            column_sum(d_mix_in * mix_hat),
            column_sum(d_first * normed_one),
            column_sum(d_second * normed_two),
            column_sum(d_first),
            column_sum(d_second),
            column_sum(d_branch_low),
            column_sum(cot_block),
            column_sum(d_gate),
            column_sum(d_up),
            column_sum(d_down_in),
            column_sum(d_down_in * hidden_hat),
        ]
    ).reshape(-1, 128)
    vector_grads = pad_to(vector_grads, 0, round_up(vector_grads.shape[0], 16))
    grad_jobs = (
        (0, None, COL, hidden_here // 2), (1, 0, ROW, 64), (1, 1, ROW, 64), (2, None, COL, 256),
        (3, 0, ROW, 64), (3, 1, ROW, 64), (3, 2, ROW, 64),
    )
    down_piece, gate_piece, out_piece, qkv_piece, vector_grads, result, d_tokens = reduce_grads(
        layers, 1, grad_jobs, (g_down.astype(bf16), g_gate_up, g_out.astype(bf16), g_qkv),
        vector_grads, (result[:rows], d_tokens[:rows].astype(bf16)),
    )
    vector_grads = vector_grads.reshape(-1)
    head_sums = vector_grads[: 4 * width].reshape(4, heads, head_size)
    head_sums = lax.dynamic_slice(
        head_sums, (0, y * heads_here, s * dims_here), (4, heads_here, dims_here)
    )
    width_sums = vector_grads[4 * width : 10 * width].reshape(6, width)
    width_sums = lax.dynamic_slice(width_sums, (0, s * 128), (6, width // shards))
    hidden_sums = vector_grads[10 * width : 10 * width + 4 * hidden_size]
    hidden_sums = hidden_sums.reshape(4, hidden_size)
    hidden_sums = lax.dynamic_slice(hidden_sums, (0, y * hidden_here), (4, hidden_here))
    hidden_sums = hidden_sums[:, :real_here]

    return (
        result,
        d_tokens.astype(f32),
        qkv_piece,
        head_sums[:3],
        head_sums[3],
        out_piece,
        width_sums[:2],
        width_sums[2:],
        gate_piece[:, :, :real_here],
        hidden_sums[:3],
        hidden_sums[3],
        down_piece[:real_here],
    )


def solution(mesh):
    small = mesh.shape[CTX] == 2 and mesh.shape[TP] == 2
    body = functools.partial(image_per_chip, mesh.shape[SHARD] // 2) if small else general_plan

    return jax.shard_map(
        body,
        mesh=mesh,
        in_specs=(
            P(SHARD, CTX, None),
            P(SHARD, CTX, None),
            P(SHARD, None),
            P(None, SHARD, CTX),
            P(None, SHARD, TP),
            P(None, TP, SHARD),
            P(TP, SHARD),
            P(TP, SHARD),
            P(None, SHARD),
            P(None, SHARD),
            P(None, SHARD, TP),
            P(None, TP),
            P(TP),
            P(TP, SHARD),
        ),
        out_specs=(
            P(SHARD, CTX, None),
            P(SHARD, CTX, None),
            P(None, SHARD, TP),
            P(None, TP, SHARD),
            P(TP, SHARD),
            P(TP, SHARD),
            P(None, SHARD),
            P(None, SHARD),
            P(None, SHARD, TP),
            P(None, TP),
            P(TP),
            P(TP, SHARD),
        ),
        check_vma=False,
    )
```

```python
import functools
import math

import jax
import jax.numpy as jnp
from jax import lax
from jax.experimental import pallas as pl
from jax.experimental.pallas import tpu as pltpu
from jax.sharding import PartitionSpec as P

SHARD, CTX, TP = "shard", "ctx", "tp"


EPS = 1e-06


def standardize(values):
    average = jnp.mean(values, axis=-1, keepdims=True)
    centred = values - average
    spread = lax.rsqrt(jnp.mean(centred * centred, axis=-1, keepdims=True) + EPS)
    return (centred * spread, spread)


def norm_back(grad_hat, normed, spread):
    mean_one = jnp.mean(grad_hat, axis=-1, keepdims=True)
    mean_two = jnp.mean(grad_hat * normed, axis=-1, keepdims=True)
    return (grad_hat - mean_one - normed * mean_two) * spread


def angle_table(row_ids, col_ids, head_size):
    quarter = head_size // 4
    frequency = 10000.0 ** (-jnp.arange(quarter, dtype=jnp.float32) / quarter)
    row_part = row_ids.astype(jnp.float32)[:, None] * frequency[None, :]
    col_part = col_ids.astype(jnp.float32)[:, None] * frequency[None, :]
    return jnp.concatenate([row_part, row_part, col_part, col_part], axis=1)


def turn_half(values):
    quarter = values.shape[-1] // 4
    part_one = values[..., :quarter]
    part_two = values[..., quarter : 2 * quarter]
    part_three = values[..., 2 * quarter : 3 * quarter]
    part_four = values[..., 3 * quarter :]
    return jnp.concatenate([-part_two, part_one, -part_four, part_three], axis=-1)


def rotate(values, angles):
    return values * jnp.cos(angles)[None, :, :] + turn_half(values) * jnp.sin(angles)[None, :, :]


def unrotate(values, angles):
    return values * jnp.cos(angles)[None, :, :] - turn_half(values) * jnp.sin(angles)[None, :, :]


def head_major(values, heads, head_size):
    return values.reshape(values.shape[0], heads, head_size).transpose(1, 0, 2)


def column_sum(values):
    return jnp.sum(values.astype(jnp.float32), axis=0)


def general_plan(
    tokens,
    cotangent,
    valid_tokens,
    places,
    qkv_weight,
    head_biases,
    head_gain,
    out_weight,
    norm_gains,
    width_biases,
    gate_up,
    hidden_biases,
    hidden_gain,
    down_weight,
):
    micro = tokens.shape[0]
    width = tokens.shape[2]
    local_dim = qkv_weight.shape[2]
    local_heads = head_biases.shape[1]
    head_size = local_dim // local_heads
    local_hidden = hidden_gain.shape[0]
    FF = local_hidden * lax.axis_size(TP)
    score_scale = 1.0 / math.sqrt(head_size)
    f32 = jnp.float32
    bf16 = jnp.bfloat16

    def one_batch(batch_idx, carried):
        gathered = (
            lax.all_gather(qkv_weight, SHARD, axis=1, tiled=True),
            lax.all_gather(head_biases, SHARD, axis=2, tiled=True),
            lax.all_gather(head_gain, SHARD, axis=1, tiled=True),
            lax.all_gather(out_weight, SHARD, axis=1, tiled=True),
            lax.all_gather(norm_gains, SHARD, axis=1, tiled=True),
            lax.all_gather(width_biases, SHARD, axis=1, tiled=True),
            lax.all_gather(gate_up, SHARD, axis=1, tiled=True),
            lax.all_gather(down_weight, SHARD, axis=1, tiled=True),
        )
        qkv_full, head_bias, head_scale, out_full, norm_scale, width_bias, gate_full, down_full = (
            gathered
        )
        head_bias_f = head_bias.astype(f32)
        head_scale_f = head_scale.astype(f32)[:, None, :]
        norm_scale = norm_scale.astype(f32)
        width_bias = width_bias.astype(f32)
        hidden_bias = hidden_biases.astype(f32)
        hidden_scale = hidden_gain.astype(f32)
        out_heads = out_full.reshape(local_heads, head_size, width)
        token_rows = lax.dynamic_index_in_dim(tokens, batch_idx, 0, keepdims=False).astype(f32)
        cot_rows = lax.dynamic_index_in_dim(cotangent, batch_idx, 0, keepdims=False).astype(f32)
        valid_row = lax.dynamic_index_in_dim(valid_tokens, batch_idx, 0, keepdims=False) > 0
        row_ids = lax.dynamic_index_in_dim(places[0], batch_idx, 0, keepdims=False)
        col_ids = lax.dynamic_index_in_dim(places[1], batch_idx, 0, keepdims=False)
        angles = angle_table(row_ids, col_ids, head_size)
        normed_one, spread_one = standardize(token_rows)
        first_in = (normed_one * norm_scale[0] + width_bias[0]).astype(bf16)
        query_flat = jnp.dot(first_in, qkv_full[0], preferred_element_type=f32)
        key_flat = jnp.dot(first_in, qkv_full[1], preferred_element_type=f32)
        value_flat = jnp.dot(first_in, qkv_full[2], preferred_element_type=f32)
        query_pre = head_major(query_flat, local_heads, head_size) + head_bias_f[0][:, None, :]
        key_pre = head_major(key_flat, local_heads, head_size)
        value_local = (
            head_major(value_flat, local_heads, head_size) + head_bias_f[1][:, None, :]
        ).astype(bf16)
        queries = rotate(query_pre, angles).astype(bf16)
        key_local = rotate(key_pre, angles).astype(bf16)
        key_heads, value_heads = (
            lax.all_gather(key_local, CTX, axis=1, tiled=True),
            lax.all_gather(value_local, CTX, axis=1, tiled=True),
        )

        def score_block():
            raw = (
                jnp.einsum("htd,hsd->hts", queries, key_heads, preferred_element_type=f32)
                * score_scale
            )
            return jnp.where(valid_row[None, None, :], raw, -1e30)

        scores = score_block()
        row_top = jnp.max(scores, axis=-1, keepdims=True)
        row_total = jnp.sum(jnp.exp(scores - row_top), axis=-1, keepdims=True)
        soft_low = (jnp.exp(scores - row_top) / row_total).astype(bf16)
        mixed = jnp.einsum("hts,hsd->htd", soft_low, value_heads, preferred_element_type=f32)
        mix_sums = lax.psum(
            (
                jnp.sum(mixed, axis=(0, 2), keepdims=True),
                jnp.sum(mixed * mixed, axis=(0, 2), keepdims=True),
            ),
            TP,
        )
        mix_mean = mix_sums[0] / width
        spread_mix = lax.rsqrt(mix_sums[1] / width - mix_mean * mix_mean + EPS)
        mix_hat = (mixed - mix_mean) * spread_mix
        mix_in = (mix_hat * head_scale_f + head_bias_f[2][:, None, :]).astype(bf16)
        branch = lax.psum(
            jnp.einsum("htd,hdn->tn", mix_in, out_heads, preferred_element_type=f32), TP
        )
        resid = token_rows + (branch + width_bias[2])
        normed_two, spread_two = standardize(resid)
        second_in = (normed_two * norm_scale[1] + width_bias[1]).astype(bf16)
        gate_pre = jnp.dot(second_in, gate_full[0], preferred_element_type=f32) + hidden_bias[0]
        up_pre = jnp.dot(second_in, gate_full[1], preferred_element_type=f32) + hidden_bias[1]
        sigmoid_gate = jax.nn.sigmoid(gate_pre)
        silu_gate = gate_pre * sigmoid_gate
        hidden = silu_gate * up_pre
        hidden_sums = lax.psum(
            (
                jnp.sum(hidden, axis=-1, keepdims=True),
                jnp.sum(hidden * hidden, axis=-1, keepdims=True),
            ),
            TP,
        )
        hidden_mean = hidden_sums[0] / FF
        spread_hid = lax.rsqrt(hidden_sums[1] / FF - hidden_mean * hidden_mean + EPS)
        hidden_hat = (hidden - hidden_mean) * spread_hid
        down_in = (hidden_hat * hidden_scale + hidden_bias[2]).astype(bf16)
        ffn_out = lax.psum(
            jnp.dot(down_in, down_full, preferred_element_type=f32).astype(jnp.bfloat16), TP
        ).astype(jnp.float32)
        result = (resid + (ffn_out + width_bias[3])).astype(bf16)
        d_ffn_low = cot_rows.astype(bf16)
        g_down = jnp.einsum("tf,td->fd", down_in, d_ffn_low, preferred_element_type=f32)
        d_down_in = jnp.einsum("td,fd->tf", d_ffn_low, down_full, preferred_element_type=f32)
        grad_hid = d_down_in * hidden_scale
        hid_back = lax.psum(
            (
                jnp.sum(grad_hid, axis=-1, keepdims=True),
                jnp.sum(grad_hid * hidden_hat, axis=-1, keepdims=True),
            ),
            TP,
        )
        d_hidden = (grad_hid - hid_back[0] / FF - hidden_hat * (hid_back[1] / FF)) * spread_hid
        d_gate = (
            d_hidden * up_pre * sigmoid_gate * (1.0 + gate_pre * (1.0 - sigmoid_gate))
        ).astype(bf16)
        d_up = (d_hidden * silu_gate).astype(bf16)
        g_gate_one = jnp.einsum("td,tf->df", second_in, d_gate, preferred_element_type=f32)
        g_up_one = jnp.einsum("td,tf->df", second_in, d_up, preferred_element_type=f32)
        d_second_part = jnp.einsum(
            "tf,df->td", d_gate, gate_full[0], preferred_element_type=f32
        ) + jnp.einsum("tf,df->td", d_up, gate_full[1], preferred_element_type=f32)
        d_second = lax.psum(d_second_part, TP)
        d_resid = cot_rows + norm_back(d_second * norm_scale[1], normed_two, spread_two)
        d_branch_low = d_resid.astype(bf16)
        g_out = jnp.einsum("htd,tn->hdn", mix_in, d_branch_low, preferred_element_type=f32).reshape(
            local_dim, width
        )
        d_mix_in = jnp.einsum("tn,hdn->htd", d_branch_low, out_heads, preferred_element_type=f32)
        grad_mix = d_mix_in * head_scale_f
        mix_back = lax.psum(
            (
                jnp.sum(grad_mix, axis=(0, 2), keepdims=True),
                jnp.sum(grad_mix * mix_hat, axis=(0, 2), keepdims=True),
            ),
            TP,
        )
        d_mixed = (
            (grad_mix - mix_back[0] / width - mix_hat * (mix_back[1] / width)) * spread_mix
        ).astype(bf16)
        again = score_block()
        weights_soft = jnp.exp(again - row_top) / row_total
        d_soft = jnp.einsum("htd,hsd->hts", d_mixed, value_heads, preferred_element_type=f32)
        row_dot = jnp.sum(weights_soft * d_soft, axis=-1, keepdims=True)
        d_scores = (weights_soft * (d_soft - row_dot)).astype(bf16)
        d_query = (
            jnp.einsum("hts,hsd->htd", d_scores, key_heads, preferred_element_type=f32)
            * score_scale
        )
        soft_again = weights_soft.astype(bf16)
        d_key_all = (
            jnp.einsum("hts,htd->hsd", d_scores, queries, preferred_element_type=f32) * score_scale
        )
        d_value_all = jnp.einsum("hts,htd->hsd", soft_again, d_mixed, preferred_element_type=f32)
        d_key_heads, d_value_loc = (
            lax.psum_scatter(
                d_key_all.astype(jnp.bfloat16), CTX, scatter_dimension=1, tiled=True
            ).astype(jnp.float32),
            lax.psum_scatter(
                d_value_all.astype(jnp.bfloat16), CTX, scatter_dimension=1, tiled=True
            ).astype(jnp.float32),
        )
        d_query_low = unrotate(d_query, angles).astype(bf16)
        d_key_low = unrotate(d_key_heads, angles).astype(bf16)
        d_value_low = d_value_loc.astype(bf16)
        g_query = jnp.einsum(
            "tn,htd->nhd", first_in, d_query_low, preferred_element_type=f32
        ).reshape(width, local_dim)
        g_key = jnp.einsum("tn,htd->nhd", first_in, d_key_low, preferred_element_type=f32).reshape(
            width, local_dim
        )
        g_value = jnp.einsum(
            "tn,htd->nhd", first_in, d_value_low, preferred_element_type=f32
        ).reshape(width, local_dim)
        d_first_part = jnp.einsum(
            "htd,nhd->tn",
            d_query_low,
            qkv_full[0].reshape(width, local_heads, head_size),
            preferred_element_type=f32,
        )
        d_first_part = d_first_part + jnp.einsum(
            "htd,nhd->tn",
            d_key_low,
            qkv_full[1].reshape(width, local_heads, head_size),
            preferred_element_type=f32,
        )
        d_first_part = d_first_part + jnp.einsum(
            "htd,nhd->tn",
            d_value_low,
            qkv_full[2].reshape(width, local_heads, head_size),
            preferred_element_type=f32,
        )
        d_first = lax.psum(d_first_part.astype(jnp.bfloat16), TP).astype(jnp.float32)
        d_tokens = d_resid + norm_back(d_first * norm_scale[0], normed_one, spread_one)
        g_head_bias = jnp.stack(
            [
                jnp.sum(d_query_low.astype(f32), axis=1),
                jnp.sum(d_value_low.astype(f32), axis=1),
                jnp.sum(d_mix_in, axis=1),
            ]
        )
        g_head_scale = jnp.sum(d_mix_in * mix_hat, axis=1)
        g_norm = jnp.stack([column_sum(d_first * normed_one), column_sum(d_second * normed_two)])
        g_width = jnp.stack(
            [
                column_sum(d_first),
                column_sum(d_second),
                column_sum(d_branch_low),
                column_sum(d_ffn_low),
            ]
        )
        g_hidden_bias = jnp.stack([column_sum(d_gate), column_sum(d_up), column_sum(d_down_in)])
        g_hidden_scale = column_sum(d_down_in * hidden_hat)
        out_all = lax.dynamic_update_index_in_dim(carried[0], result, batch_idx, 0)
        grad_all = lax.dynamic_update_index_in_dim(carried[1], d_tokens, batch_idx, 0)
        updates = (
            g_query,
            g_key,
            g_value,
            g_head_bias,
            g_head_scale,
            g_out,
            g_norm,
            g_width,
            g_gate_one,
            g_up_one,
            g_down,
            g_hidden_bias,
            g_hidden_scale,
        )
        return (
            out_all,
            grad_all,
            tuple((before + added for before, added in zip(carried[2], updates))),
        )

    zeros_acc = (
        jnp.zeros((width, local_dim), f32),
        jnp.zeros((width, local_dim), f32),
        jnp.zeros((width, local_dim), f32),
        jnp.zeros((3, local_heads, head_size), f32),
        jnp.zeros((local_heads, head_size), f32),
        jnp.zeros((local_dim, width), f32),
        jnp.zeros((2, width), f32),
        jnp.zeros((4, width), f32),
        jnp.zeros((width, local_hidden), f32),
        jnp.zeros((width, local_hidden), f32),
        jnp.zeros((local_hidden, width), f32),
        jnp.zeros((3, local_hidden), f32),
        jnp.zeros((local_hidden,), f32),
    )
    start = (jnp.zeros(tokens.shape, bf16), jnp.zeros(tokens.shape, f32), zeros_acc)
    out_all, grad_all, summed = lax.fori_loop(0, micro, one_batch, start)
    (
        acc_query,
        acc_key,
        acc_value,
        acc_head_bias,
        acc_head_scale,
        acc_out,
        acc_norm,
        acc_width,
        acc_gate_one,
        acc_up_one,
        acc_down,
        acc_hidden_bias,
        acc_hidden_scale,
    ) = summed
    acc_qkv = jnp.stack([acc_query, acc_key, acc_value])
    acc_gate = jnp.stack([acc_gate_one, acc_up_one])
    sharded = (
        acc_qkv,
        acc_head_bias,
        acc_head_scale,
        acc_out,
        acc_norm,
        acc_width,
        acc_gate,
        acc_down,
    )
    hidden_done = lax.psum((acc_hidden_bias, acc_hidden_scale), (SHARD, CTX))
    return (
        out_all,
        grad_all,
        lax.psum_scatter(
            lax.psum(sharded[0].astype(jnp.bfloat16), CTX),
            SHARD,
            scatter_dimension=1,
            tiled=True,
        ).astype(jnp.float32),
        lax.psum_scatter(
            lax.psum(sharded[1].astype(jnp.bfloat16), CTX),
            SHARD,
            scatter_dimension=2,
            tiled=True,
        ).astype(jnp.float32),
        lax.psum_scatter(
            lax.psum(sharded[2].astype(jnp.bfloat16), CTX),
            SHARD,
            scatter_dimension=1,
            tiled=True,
        ).astype(jnp.float32),
        lax.psum_scatter(
            lax.psum(sharded[3].astype(jnp.bfloat16), CTX),
            SHARD,
            scatter_dimension=1,
            tiled=True,
        ).astype(jnp.float32),
        lax.psum_scatter(
            lax.psum(sharded[4].astype(jnp.bfloat16), CTX),
            SHARD,
            scatter_dimension=1,
            tiled=True,
        ).astype(jnp.float32),
        lax.psum_scatter(
            lax.psum(sharded[5].astype(jnp.bfloat16), CTX),
            SHARD,
            scatter_dimension=1,
            tiled=True,
        ).astype(jnp.float32),
        lax.psum_scatter(
            lax.psum(sharded[6].astype(jnp.bfloat16), CTX),
            SHARD,
            scatter_dimension=1,
            tiled=True,
        ).astype(jnp.float32),
        hidden_done[0],
        hidden_done[1],
        lax.psum_scatter(
            lax.psum(sharded[7].astype(jnp.bfloat16), CTX),
            SHARD,
            scatter_dimension=1,
            tiled=True,
        ).astype(jnp.float32),
    )


MESH = pl.DeviceIdType.MESH
LIMIT = 56 * 1024 * 1024
ANY = pl.BlockSpec(memory_space=pl.ANY)
IN_VMEM = pl.BlockSpec(memory_space=pltpu.VMEM)
CORE, ACROSS, BESIDE, UP, DOWN, SWAP, FAR = range(7)
ROW, COL = range(2)


def place_of():
    index = lax.axis_index(SHARD)
    return (lax.div(index, 2), lax.rem(index, 2), lax.axis_index(CTX), lax.axis_index(TP))


def when(condition, action):
    if condition is None:
        action()
    else:
        pl.when(condition)(action)


def both(first, second):
    return jnp.logical_and(first, second)


def device(place, way):
    z, k, x, y = place
    return {
        CORE: {SHARD: 2 * z + 1 - k},
        ACROSS: {CTX: 1 - x},
        BESIDE: {TP: 1 - y},
        UP: {SHARD: 2 * z + 2 + k},
        DOWN: {SHARD: 2 * z - 2 + k},
        SWAP: {SHARD: 2 * z + 1 - k, CTX: 1 - x},
        FAR: {SHARD: 2 * z + 1 - k, CTX: 1 - x, TP: 1 - y},
    }[way]


def greet(layers, place, diagonals):
    z, k, x, y = place
    barrier = pltpu.get_barrier_semaphore()

    def hello(way):
        pl.semaphore_signal(barrier, inc=1, device_id=device(place, way), device_id_type=MESH)

    hello(CORE)
    hello(ACROSS)
    hello(BESIDE)
    pl.when(z > 0)(lambda: hello(DOWN))
    pl.when(z < layers - 1)(lambda: hello(UP))
    count = 3 + jnp.where(z > 0, 1, 0) + jnp.where(z < layers - 1, 1, 0)
    for way in diagonals:
        pl.when(k != x)(lambda way=way: hello(way))
        count = count + jnp.where(k != x, 1, 0)
    pl.semaphore_wait(barrier, count)


class Links:
    def __init__(self, place, send_sem, recv_sem):
        self.place, self.send_sem, self.recv_sem = place, send_sem, recv_sem
        self.used = 0
        self.sent = []
        self.noted = None

    def take(self, count):
        first = self.used
        self.used += count
        return first

    def copy(self, way, at, source, target):
        return pltpu.make_async_remote_copy(
            src_ref=source,
            dst_ref=target,
            send_sem=self.send_sem.at[at],
            recv_sem=self.recv_sem.at[at],
            device_id=device(self.place, way),
            device_id_type=MESH,
        )

    def do(self, condition, action):
        if self.noted is None:
            when(condition, action)
        else:
            self.noted.append((condition, action))

    def record(self, actions):
        self.noted = []
        for action in actions:
            action()
        found, self.noted = self.noted, None
        return found

    def send(self, condition, copy):
        self.do(condition, copy.start)
        self.sent.append((condition, copy))

    def finish(self):
        for condition, copy in self.sent:
            when(condition, copy.wait_send)


def run(noted):
    for condition, action in noted:
        when(condition, action)


def piece_view(kind, rows, cols, ref, y, s, first, size):
    if kind == ROW:
        at_row, at_col = s * rows + first, y * cols
    else:
        at_row, at_col = y * rows + first, s * cols
    at_row, at_col = pl.multiple_of(at_row, 16), pl.multiple_of(at_col, 128)
    return ref.at[pl.ds(at_row, size), pl.ds(at_col, cols)]


def cut_rows(ref, first, size):
    return ref.at[pl.ds(pl.multiple_of(first, 16), size), :]


class Gather:
    def __init__(self, layers, links, kind, own, full, split, local_sem):
        self.layers, self.links, self.kind, self.own, self.full = layers, links, kind, own, full
        self.rows, self.cols = own.shape
        self.split, self.half = split, split // 2
        self.local_sem = local_sem
        n = layers
        self.z_a = links.take(2 * n)
        self.z_b = links.take(2 * n)
        self.x_a, self.x_b = links.take(n), links.take(n)
        self.y_a, self.y_b = links.take(n), links.take(1)
        self.core_a, self.core_b = links.take(2 * n), links.take(2 * n)

    @staticmethod
    def sem_count(layers):
        return 11 * layers + 1

    def copy(self, way, at, y, z, first, size, from_own=False, other_core=False):
        k = self.links.place[1]
        s = 2 * z + (1 - k if other_core else k)
        there = piece_view(self.kind, self.rows, self.cols, self.full, y, s, first, size)
        here = cut_rows(self.own, first, size) if from_own else there
        return self.links.copy(way, at, here, there)

    def half_a(self, way, at, y, z, which, from_own=False):
        return self.copy(way, at, y, z, which * self.half, self.half, from_own)

    def part_a(self, way, at, y, z, from_own=False, other_core=False):
        return self.copy(way, at, y, z, 0, self.split, from_own, other_core)

    def part_b(self, way, at, y, z, from_own=False, other_core=False):
        return self.copy(
            way, at, y, z, self.split, self.rows - self.split, from_own, other_core
        )

    def z_at(self, base, way, z):
        return base + (0 if way == UP else self.layers) + z

    def core_at(self, base, y, z):
        return base + 2 * z + y

    def begin(self):
        z, k, x, y = self.links.place
        send = self.links.send
        low, high = z > 0, z < self.layers - 1
        own_view = piece_view(
            self.kind, self.rows, self.cols, self.full, y, 2 * z + k, 0, self.rows
        )
        self.local = pltpu.make_async_copy(self.own, own_view, self.local_sem)
        if self.split < self.rows:
            send(None, self.part_b(BESIDE, self.y_b, y, z, True))
            same = x == y
            send(both(same, high), self.part_b(UP, self.z_at(self.z_b, UP, z), y, z, True))
            send(both(same, low), self.part_b(DOWN, self.z_at(self.z_b, DOWN, z), y, z, True))
        if self.split:
            send(high, self.half_a(UP, self.z_at(self.z_a, UP, z), y, z, x, True))
            send(low, self.half_a(DOWN, self.z_at(self.z_a, DOWN, z), y, z, x, True))
            send(None, self.part_a(BESIDE, self.y_a + z, y, z, True))
            send(None, self.part_a(CORE, self.core_at(self.core_a, y, z), y, z, True))
        if self.split < self.rows:
            send(None, self.part_b(CORE, self.core_at(self.core_b, y, z), y, z, True))
        self.links.do(None, self.local.start)

    def cross_y(self):
        if self.split == self.rows:
            return
        z, k, x, y = self.links.place
        send = self.links.send
        self.links.do(None, self.part_b(BESIDE, self.y_b, 1 - y, z).wait_recv)
        other = x != y
        low, high = z > 0, z < self.layers - 1
        send(both(other, high), self.part_b(UP, self.z_at(self.z_b, UP, z), 1 - y, z))
        send(both(other, low), self.part_b(DOWN, self.z_at(self.z_b, DOWN, z), 1 - y, z))
        send(None, self.part_b(CORE, self.core_at(self.core_b, 1 - y, z), 1 - y, z))

    def steps(self, step):
        z = self.links.place[0]
        below, above = z - 1 - step, z + 1 + step
        return (
            (UP, below, below >= 0, z < self.layers - 1),
            (DOWN, above, above <= self.layers - 1, z > 0),
        )

    def along_z(self, step):
        z, k, x, y = self.links.place
        send = self.links.send
        for way, origin, there, further in self.steps(step):
            if self.split < self.rows:
                came = self.part_b(way, self.z_at(self.z_b, way, origin), x, origin)
                self.links.do(there, came.wait_recv)
                send(both(there, further), came)
                send(there, self.part_b(ACROSS, self.x_b + origin, x, origin))
                send(there, self.part_b(CORE, self.core_at(self.core_b, x, origin), x, origin))
            if self.split:
                came = self.half_a(way, self.z_at(self.z_a, way, origin), y, origin, x)
                self.links.do(there, came.wait_recv)
                send(both(there, further), came)
                send(there, self.half_a(ACROSS, self.x_a + origin, y, origin, x))

    def along_x(self, step):
        z, k, x, y = self.links.place
        send = self.links.send
        for way, origin, there, further in self.steps(step):
            if self.split:
                self.links.do(there, self.half_a(ACROSS, self.x_a + origin, y, origin, 1 - x).wait_recv)
                send(there, self.part_a(BESIDE, self.y_a + origin, y, origin))
                send(there, self.part_a(CORE, self.core_at(self.core_a, y, origin), y, origin))
            if self.split < self.rows:
                self.links.do(there, self.part_b(ACROSS, self.x_b + origin, 1 - x, origin).wait_recv)
                at = self.core_at(self.core_b, 1 - x, origin)
                send(there, self.part_b(CORE, at, 1 - x, origin))

    def along_y(self, step):
        if not self.split:
            return
        z, k, x, y = self.links.place
        send = self.links.send
        todo = ((None, z, None, None),) if step < 0 else self.steps(step)
        for way, origin, there, further in todo:
            self.links.do(there, self.part_a(BESIDE, self.y_a + origin, 1 - y, origin).wait_recv)
            at = self.core_at(self.core_a, 1 - y, origin)
            send(there, self.part_a(CORE, at, 1 - y, origin))

    def stages(self):
        found = [[self.begin], [self.cross_y]]
        for step in range(self.layers + 1):
            now = []
            if step < self.layers - 1:
                now.append(functools.partial(self.along_z, step))
            if step == 0:
                now.append(functools.partial(self.along_y, -1))
            if 0 <= step - 1 < self.layers - 1:
                now.append(functools.partial(self.along_x, step - 1))
            if 0 <= step - 2 < self.layers - 1:
                now.append(functools.partial(self.along_y, step - 2))
            found.append(now)
        return found

    def arrived(self):
        self.links.do(None, self.local.wait)
        for layer in range(self.layers):
            for y in range(2):
                if self.split:
                    at = self.core_at(self.core_a, y, layer)
                    self.links.do(None, self.part_a(CORE, at, y, layer, other_core=True).wait_recv)
                if self.split < self.rows:
                    at = self.core_at(self.core_b, y, layer)
                    self.links.do(None, self.part_b(CORE, at, y, layer, other_core=True).wait_recv)


def ticks_of(links, jobs, lead):
    plans = [job.stages() for job in jobs]
    ticks = [[] for _ in range(len(jobs) + max([len(plan) for plan in plans]))]
    for number, plan in enumerate(plans):
        for stage, actions in enumerate(plan):
            at = max(0, number - lead) if stage == 0 else number + stage
            ticks[at] += actions
    return [links.record(tick) for tick in ticks if tick]


class Swap:
    def __init__(self, links, source, target, local_sem):
        z, k, x, y = links.place
        self.same, self.other = k == x, k != x
        self.here = pltpu.make_async_copy(source, target, local_sem)
        self.there = links.copy(SWAP, links.take(1), source, target)

    def begin(self):
        pl.when(self.same)(self.here.start)
        pl.when(self.other)(self.there.start)

    def arrived(self):
        pl.when(self.same)(self.here.wait)
        pl.when(self.other)(self.there.wait)


class Cross:
    def __init__(self, links, source, target, local_sem):
        y = links.place[3]
        at = links.take(1)
        self.here = pltpu.make_async_copy(source, target.at[y], local_sem)
        self.out = links.copy(BESIDE, at, source, target.at[y])
        self.back = links.copy(BESIDE, at, source, target.at[1 - y])

    def begin(self):
        self.here.start()
        self.out.start()

    def arrived(self):
        self.here.wait()
        self.out.wait_send()
        self.back.wait_recv()


class Spread:
    def __init__(self, links, block, both_images, local_sem):
        z, k, x, y = links.place
        self.same, self.other = k == x, k != x
        here, first, second = links.take(1), links.take(1), 0
        target = both_images.at[y]
        self.keep = pltpu.make_async_copy(block, target, local_sem)
        self.beside = links.copy(BESIDE, here, block, target)
        self.swap = links.copy(SWAP, first, block, target)
        self.far = links.copy(FAR, here, block, target)
        self.came = links.copy(BESIDE, here, block, both_images.at[1 - y])

    def begin(self):
        def same():
            self.keep.start()
            self.beside.start()

        def other():
            self.swap.start()
            self.far.start()

        pl.when(self.same)(same)
        pl.when(self.other)(other)

    def arrived(self):
        def same():
            self.keep.wait()
            self.beside.wait_send()

        def other():
            self.swap.wait()
            self.far.wait_send()

        pl.when(self.same)(same)
        pl.when(self.other)(other)
        self.came.wait_recv()


def full_shape(layers, kind, piece):
    if kind == ROW:
        return piece[:-2] + (piece[-2] * layers * 2, piece[-1] * 2)
    return (piece[-2] * 2, piece[-1] * layers * 2)


def by_chunks(shape, body):
    rows, cols = shape
    chunk = 16
    while rows % (2 * chunk) == 0 and 2 * chunk * cols <= 16384:
        chunk *= 2

    def step(i, nothing):
        body((pl.ds(pl.multiple_of(i * chunk, 16), chunk), slice(None)))
        return nothing

    lax.fori_loop(0, rows // chunk, step, 0)


def add_into(target, term):
    def body(where):
        total = target[where].astype(jnp.float32) + term[where].astype(jnp.float32)
        target[where] = total.astype(target.dtype)

    by_chunks(target.shape, body)


def store_sum(out, *terms):
    def body(where):
        total = terms[0][where].astype(jnp.float32)
        for term in terms[1:]:
            total = total + term[where].astype(jnp.float32)
        out[where] = total

    by_chunks(out.shape, body)


class Reduce:
    def __init__(self, layers, links, kind, grad, out, split, scratch, local_sem, local_base):
        self.layers, self.links, self.kind, self.grad, self.out = layers, links, kind, grad, out
        self.mine, self.core_in, self.y_in, self.x_in, self.z_in, self.last = scratch
        self.rows, self.cols = self.mine.shape[-2:]
        self.split = split
        self.local_sem, self.local_base = local_sem, local_base
        n = layers
        self.core = links.take(2 * n)
        self.y_a, self.x_b = links.take(n), links.take(n)
        self.z_a, self.z_b = links.take(2 * n), links.take(2 * n)
        self.end_a, self.end_b, self.end_c = links.take(1), links.take(1), links.take(1)
        self.order = []
        low, high = 0, layers - 1
        while low <= high:
            self.order.append(high)
            if low < high:
                self.order.append(low)
            low, high = low + 1, high - 1

    @staticmethod
    def sem_count(layers):
        return 8 * layers + 3

    def part_a(self, ref):
        return cut_rows(ref, 0, self.split)

    def part_b(self, ref):
        return cut_rows(ref, self.split, self.rows - self.split)

    def add(self, condition, target, term):
        self.links.do(condition, functools.partial(add_into, target, term))

    def grad_piece(self, y, s):
        return piece_view(self.kind, self.rows, self.cols, self.grad, y, s, 0, self.rows)

    def local(self, y, layer):
        k = self.links.place[1]
        return pltpu.make_async_copy(
            self.grad_piece(y, 2 * layer + k),
            self.mine.at[y, layer],
            self.local_sem.at[self.local_base + 2 * layer + y],
        )

    def to_core(self, y, layer):
        k = self.links.place[1]
        return self.links.copy(
            CORE,
            self.core + 2 * layer + y,
            self.grad_piece(y, 2 * layer + 1 - k),
            self.core_in.at[y, layer],
        )

    def begin(self):
        for layer in self.order:
            for y in range(2):
                self.links.send(None, self.to_core(y, layer))
                self.links.do(None, self.local(y, layer).start)

    def to_y(self, layer):
        y = self.links.place[3]
        source = self.part_a(self.mine.at[1 - y, layer])
        return self.links.copy(BESIDE, self.y_a + layer, source, self.y_in.at[layer])

    def to_x(self, layer):
        x = self.links.place[2]
        source = self.part_b(self.mine.at[1 - x, layer])
        return self.links.copy(ACROSS, self.x_b + layer, source, self.x_in.at[layer])

    def chip_sum(self):
        for layer in self.order:
            for side in range(2):
                self.links.do(None, self.local(side, layer).wait)
                self.links.do(None, self.to_core(side, layer).wait_recv)
                self.add(None, self.mine.at[side, layer], self.core_in.at[side, layer])
            self.links.send(None, self.to_y(layer))
            self.links.send(None, self.to_x(layer))

    def plane_sum(self):
        z, k, x, y = self.links.place
        for layer in self.order:
            self.links.do(None, self.to_y(layer).wait_recv)
            self.add(None, self.part_a(self.mine.at[y, layer]), self.y_in.at[layer])
            self.links.do(None, self.to_x(layer).wait_recv)
            self.add(None, self.part_b(self.mine.at[x, layer]), self.x_in.at[layer])

    def chain(self, way, layer, receiver):
        z, k, x, y = self.links.place
        slot = layer if way == UP else jnp.where(receiver == layer, self.layers, layer)
        add = 0 if way == UP else self.layers
        found = []
        for base, part, side in ((self.z_a, self.part_a, y), (self.z_b, self.part_b, x)):
            total, box = part(self.mine.at[side, layer]), part(self.z_in.at[slot])
            found.append((total, box, self.links.copy(way, base + add + layer, total, box)))
        return found

    def take(self, condition, way, layer):
        for total, box, copy in self.chain(way, layer, self.links.place[0]):
            self.links.do(condition, copy.wait_recv)
            self.add(condition, total, box)

    def along_z(self, depth):
        z = self.links.place[0]
        top = self.layers - 1
        for way, here, goals in (
            (UP, z == depth, range(top, depth, -1)),
            (DOWN, z == top - depth, range(0, top - depth)),
        ):
            for layer in goals:
                if depth:
                    self.take(here, way, layer)
                for total, box, copy in self.chain(way, layer, z + 1 if way == UP else z - 1):
                    self.links.send(here, copy)

    def ending(self):
        z, k, x, y = self.links.place
        self.take(z > 0, UP, z)
        self.take(z < self.layers - 1, DOWN, z)
        self.sum_a, self.sum_b = self.part_a(self.mine.at[y, z]), self.part_b(self.mine.at[x, z])
        self.got_a, self.got_b = self.part_a(self.last.at[0]), self.part_b(self.last.at[0])
        self.got_y = self.part_b(self.last.at[1])
        self.x_end = self.links.copy(ACROSS, self.end_a, self.sum_a, self.got_a)
        self.y_end = self.links.copy(BESIDE, self.end_b, self.sum_b, self.got_y)
        self.x_last = self.links.copy(ACROSS, self.end_c, self.sum_b, self.got_b)
        self.links.send(y != x, self.y_end)
        self.links.send(None, self.x_end)

    def owner(self):
        z, k, x, y = self.links.place

        self.links.do(y == x, self.y_end.wait_recv)
        self.add(y == x, self.sum_b, self.got_y)
        self.links.send(y == x, self.x_last)
        self.links.do(None, self.x_end.wait_recv)
        out_a = self.part_a(self.out)
        self.links.do(None, functools.partial(store_sum, out_a, self.sum_a, self.got_a))

    def write(self):
        z, k, x, y = self.links.place
        out_b = self.part_b(self.out)

        self.links.do(y != x, self.x_last.wait_recv)
        self.links.do(y != x, functools.partial(store_sum, out_b, self.got_b))
        self.links.do(y == x, functools.partial(store_sum, out_b, self.sum_b))

    def stages(self):
        chains = [[functools.partial(self.along_z, depth)] for depth in range(self.layers - 1)]
        return [
            [self.begin], [self.chip_sum], [self.plane_sum], *chains,
            [self.ending], [self.owner], [self.write],
        ]


class Total:
    def __init__(self, layers, links, given, out, boxes, layer_boxes):
        self.layers, self.links, self.given, self.out = layers, links, given, out
        self.boxes, self.layer_boxes = boxes, layer_boxes
        self.pair = [links.take(1) for _ in range(3)]
        self.z_up, self.z_down = links.take(layers), links.take(layers)

    @staticmethod
    def sem_count(layers):
        return 3 + 2 * layers

    def exchange(self, number):
        way = (CORE, ACROSS, BESIDE)[number]
        source = self.given if number == 0 else self.boxes.at[2 + number]
        return self.links.copy(way, self.pair[number], source, self.boxes.at[number])

    def begin(self):
        self.links.send(None, self.exchange(0))

    def join(self, number):
        z = self.links.place[0]
        self.links.do(None, self.exchange(number).wait_recv)
        mine = self.given if number == 0 else self.boxes.at[2 + number]
        result = self.layer_boxes.at[z] if number == 2 else self.boxes.at[3 + number]
        self.links.do(None, functools.partial(store_sum, result, mine, self.boxes.at[number]))
        if number < 2:
            self.links.send(None, self.exchange(number + 1))
        else:
            self.links.send(z < self.layers - 1, self.pass_on(UP, z))
            self.links.send(z > 0, self.pass_on(DOWN, z))

    def pass_on(self, way, layer):
        box = self.layer_boxes.at[layer]
        return self.links.copy(way, (self.z_up if way == UP else self.z_down) + layer, box, box)

    def along_z(self, step):
        z = self.links.place[0]
        top = self.layers - 1
        below, above = z - 1 - step, z + 1 + step
        for way, origin, there, further in (
            (UP, below, below >= 0, z < top),
            (DOWN, above, above <= top, z > 0),
        ):
            copy = self.pass_on(way, origin)
            self.links.do(there, copy.wait_recv)
            self.links.send(both(there, further), copy)

    def write(self):
        layers = [self.layer_boxes.at[layer] for layer in range(self.layers)]
        self.links.do(None, functools.partial(store_sum, self.out, *layers))

    def stages(self):
        joins = [[functools.partial(self.join, number)] for number in range(3)]
        moves = [[functools.partial(self.along_z, step)] for step in range(self.layers - 1)]
        return [[self.begin], *joins, *moves, [self.write]]


def reduce_jobs(layers, links, jobs, grads, outs, scratch, local_sem):
    todo = []
    for number, (mat, lead, kind, split) in enumerate(jobs):
        grad, out = grads[mat], outs[mat]
        if lead is not None:
            grad, out = grad.at[lead], out.at[lead]
        own = scratch[6 * number : 6 * number + 6]
        at = number * 2 * layers
        todo.append(Reduce(layers, links, kind, grad, out, split, own, local_sem, at))
    return todo


def reduce_scratch(layers, jobs, pieces):
    scratch = []
    for mat, lead, kind, split in jobs:
        rows, cols = pieces[mat][-2:]
        for lead_shape, here in (
            ((2, layers), rows), ((2, layers), rows), ((layers,), split), ((layers,), rows - split),
            ((layers + 1,), rows), ((2,), rows),
        ):
            scratch.append(pltpu.VMEM(lead_shape + (here, cols), jnp.bfloat16))
    return scratch


def reduce_kernel(layers, jobs, mats, blocks, *refs):
    grads, refs = refs[:mats], refs[mats:]
    total_in, refs = refs[0], refs[1:]
    block_in, refs = refs[:blocks], refs[blocks:]
    outs, refs = refs[:mats], refs[mats:]
    total_out, refs = refs[0], refs[1:]
    block_out, refs = refs[:blocks], refs[blocks:]
    scratch = refs[: 6 * len(jobs)]
    boxes, layer_boxes, send_sem, recv_sem, local_sem = refs[6 * len(jobs) :]
    place = place_of()
    greet(layers, place, (SWAP, FAR))
    links = Links(place, send_sem, recv_sem)
    todo = reduce_jobs(layers, links, jobs, grads, outs, scratch, local_sem)
    todo.insert(1, Total(layers, links, total_in, total_out, boxes, layer_boxes))
    extras = [
        Spread(links, source, target, local_sem.at[len(jobs) * 2 * layers + i])
        for i, (source, target) in enumerate(zip(block_in, block_out))
    ]
    for number, tick in enumerate(ticks_of(links, todo, 1)):
        run(tick)
        if number == 0:
            for extra in extras:
                extra.begin()
    for extra in extras:
        extra.arrived()
    links.finish()


def piece_shape(layers, kind, full):
    if kind == ROW:
        return full[:-2] + (full[-2] // (2 * layers), full[-1] // 2)
    return (full[-2] // 2, full[-1] // (2 * layers))


def reduce_grads(layers, number, jobs, grads, total, blocks):
    kinds = {job[0]: job[2] for job in jobs}
    pieces = [piece_shape(layers, kinds[i], g.shape) for i, g in enumerate(grads)]
    scratch = reduce_scratch(layers, jobs, pieces)
    sems = len(jobs) * Reduce.sem_count(layers) + Total.sem_count(layers) + 2 * len(blocks)
    images = [jax.ShapeDtypeStruct((2,) + block.shape, block.dtype) for block in blocks]
    return pl.pallas_call(
        functools.partial(reduce_kernel, layers, jobs, len(grads), len(blocks)),
        out_shape=[jax.ShapeDtypeStruct(piece, jnp.float32) for piece in pieces]
        + [jax.ShapeDtypeStruct(total.shape, total.dtype)]
        + images,
        in_specs=[ANY] * len(grads) + [IN_VMEM] + [ANY] * len(blocks),
        out_specs=[IN_VMEM] * len(pieces) + [IN_VMEM] + [ANY] * len(blocks),
        scratch_shapes=scratch
        + [
            pltpu.VMEM((5,) + total.shape, jnp.float32),
            pltpu.VMEM((layers,) + total.shape, jnp.float32),
            pltpu.SemaphoreType.DMA((sems,)),
            pltpu.SemaphoreType.DMA((sems,)),
            pltpu.SemaphoreType.DMA((len(jobs) * 2 * layers + len(blocks),)),
        ],
        compiler_params=pltpu.CompilerParams(
            collective_id=number, has_side_effects=True, vmem_limit_bytes=LIMIT
        ),
    )(*grads, total, *blocks)


def pair_lanes(shape, head_size):
    lane = lax.broadcasted_iota(jnp.int32, shape, len(shape) - 1)
    return lane < head_size


def dot_last(left, right):
    return lax.dot_general(left, right, (((1,), (1,)), ((), ())), preferred_element_type=jnp.float32)


def dot_first(left, right):
    return lax.dot_general(left, right, (((0,), (0,)), ((), ())), preferred_element_type=jnp.float32)


def dot(left, right):
    return lax.dot_general(left, right, (((1,), (0,)), ((), ())), preferred_element_type=jnp.float32)


def only_head(values, head, head_size):
    lane = lax.broadcasted_iota(jnp.int32, (1, values.shape[1]), 1)
    keep = (lane < head_size) if head == 0 else (lane >= head_size)
    return values * jnp.where(keep, 1.0, 0.0).astype(values.dtype)


LOG2_E = 1.4426950408889634


def turn_lanes(values, quarter):
    width = values.shape[-1]
    lane = lax.broadcasted_iota(jnp.int32, (1, width), 1)
    even = lax.rem(lax.div(lane, quarter), 2) == 0
    after = pltpu.roll(values, width - quarter, 1)
    before = pltpu.roll(values, quarter, 1)
    return jnp.where(even, -after, before)


def front_kernel(layers, head_size, grid_side, *refs):
    (
        vec_own, qkv_own, out_own, gate_own, down_own, tokens, valid, hidden_own,
        vec_full, qkv_full, out_full, gate_full, down_full, hidden_full,
        x_out, n_out, q_out, k_out, v_out, o_out, stat_out, vec_out, count_out,
        x, valid_both, vec, weight, hat, normed, q, keys, values, cos, sin, bias,
        send_sem, recv_sem, local_sem,
    ) = refs
    f32, bf16 = jnp.float32, jnp.bfloat16
    place = place_of()
    z, k, me_x, y = place
    greet(layers, place, (SWAP,))
    links = Links(place, send_sem, recv_sem)
    rows, width = x.shape
    tokens_here = valid.shape[1] // 2
    tile = weight.shape[2]
    quarter = head_size // 4
    lanes = 2 * head_size
    locals_used = [0]

    def local_at():
        locals_used[0] += 1
        return local_sem.at[locals_used[0] - 1]

    block = Swap(links, tokens.at[y], x, local_at())
    valid_swap = Swap(links, valid, valid_both, local_at())
    cross = Cross(links, hidden_own, hidden_full, local_at())
    half = out_own.shape[0] // 2
    down_half = down_own.shape[0] // 2
    todo = [
        (ROW, vec_own, vec_full, 0),
        (ROW, qkv_own.at[0], qkv_full.at[0], 64),
        (ROW, qkv_own.at[1], qkv_full.at[1], 64),
        (ROW, qkv_own.at[2], qkv_full.at[2], 64),
        (COL, out_own, out_full, half),
        (ROW, gate_own.at[0], gate_full.at[0], 64),
        (ROW, gate_own.at[1], gate_full.at[1], 64),
        (COL, down_own, down_full, down_half),
    ]
    jobs = [
        Gather(layers, links, kind, own, full, split, local_at())
        for kind, own, full, split in todo
    ]
    ticks = ticks_of(links, jobs, 1)
    weight_loads = []
    for mat in range(3):
        for part in range(width // tile):
            slot = len(weight_loads) % 2
            weight_loads.append(
                pltpu.make_async_copy(
                    qkv_full.at[mat, :, pl.ds(part * tile, tile)], weight.at[slot], local_at()
                )
            )
    vec_load = pltpu.make_async_copy(vec_full, vec, local_at())
    keeps = [
        pltpu.make_async_copy(source, target, local_at())
        for source, target in ((x, x_out), (normed, n_out), (q, q_out), (keys, k_out), (values, v_out))
    ]
    shares = []
    my_rows = pl.ds(pl.multiple_of(k * rows, 16), rows)
    other_rows = pl.ds(pl.multiple_of((1 - k) * rows, 16), rows)
    for store in (keys, values):
        for part in range(width // tile):
            at = links.take(1)
            cols = pl.ds(part * tile, tile)
            out_going = links.copy(CORE, at, store.at[my_rows, cols], store.at[my_rows, cols])
            coming = links.copy(CORE, at, store.at[other_rows, cols], store.at[other_rows, cols])
            shares.append((out_going, coming))

    block.begin()
    valid_swap.begin()
    run(ticks[0])
    cross.begin()
    run(ticks[1])

    block.arrived()
    valid_swap.arrived()
    keeps[0].start()
    chunk = rows // 3

    def normalise(i, nothing):
        at = pl.ds(pl.multiple_of(i * chunk, 16), chunk)
        value, spread = standardize(x[at, :].astype(f32))
        hat[at, :] = value
        return nothing

    lax.fori_loop(0, 3, normalise, 0)
    flags = jnp.where(y == 0, valid_both[0:1, :], valid_both[1:2, :]).astype(f32)
    count = jnp.sum(flags, axis=1, keepdims=True)
    count_out[...] = jnp.broadcast_to(count, count_out.shape)
    columns = (count - 1.0) * (1.0 / grid_side)
    token = lax.broadcasted_iota(jnp.int32, (rows, lanes), 0).astype(f32)
    token = token + (k * tokens_here).astype(f32)
    lane = lax.broadcasted_iota(jnp.int32, (rows, lanes), 1)
    live = jnp.logical_and(token >= 1.0, token < count)
    row_id = jnp.floor((token - 0.5) / columns)
    col_id = token - 1.0 - row_id * columns
    where_at = jnp.where(lax.rem(lane, head_size) < 2 * quarter, row_id, col_id)
    where_at = jnp.where(live, where_at, 0.0)
    power = lax.rem(lane, quarter).astype(f32) * (-math.log(10000.0) / quarter)
    angle = where_at * jnp.exp(power)
    cos[...] = jnp.cos(angle)
    sin[...] = jnp.sin(angle)
    key = lax.broadcasted_iota(jnp.int32, bias.shape, 1)
    second = key >= rows
    within = jnp.where(second, key - rows, key)
    key_token = jnp.where(second, within + tokens_here, within).astype(f32)
    seen = jnp.logical_and(within < tokens_here, key_token < count)
    bias[...] = jnp.where(seen, 0.0, -1e30)

    for tick in ticks[2:8]:
        run(tick)
    jobs[0].arrived()
    vec_load.start()
    vec_load.wait()
    piece_rows = vec_own.shape[0]
    summed = vec[0:piece_rows, :].astype(f32)
    for s in range(1, 2 * layers):
        summed = summed + vec[s * piece_rows : (s + 1) * piece_rows, :].astype(f32)
    vec_out[...] = summed

    def scale(i, nothing):
        at = pl.ds(pl.multiple_of(i * chunk, 16), chunk)
        normed[at, :] = (hat[at, :] * vec_out[4:5, :] + vec_out[6:7, :]).astype(bf16)
        return nothing

    lax.fori_loop(0, 3, scale, 0)
    keeps[1].start()
    run(ticks[8])
    repeat = tile // lanes
    per = width // tile
    for mat in range(3):
        jobs[1 + mat].arrived()
        for part in range(per):
            weight_loads[mat * per + part].start()
        for part in range(per):
            load = weight_loads[mat * per + part]
            load.wait()
            cols = pl.ds(part * tile, tile)
            raw = dot(normed[...], weight[(mat * per + part) % 2])
            if mat != 1:
                raw = raw + vec_out[0 if mat == 0 else 1 : 1 if mat == 0 else 2, cols]
            if mat < 2:
                turned = turn_lanes(raw, quarter)
                wide_cos = jnp.concatenate([cos[...]] * repeat, axis=1)
                wide_sin = jnp.concatenate([sin[...]] * repeat, axis=1)
                raw = raw * wide_cos + turned * wide_sin
            if mat == 0:
                q[:, cols] = raw.astype(bf16)
            else:
                (keys if mat == 1 else values)[my_rows, cols] = raw.astype(bf16)
                shares[(mat - 1) * per + part][0].start()
        run(ticks[9 + mat])
    keeps[2].start()
    for out_going, coming in shares:
        out_going.wait_send()
        coming.wait_recv()
    keeps[3].start()
    keeps[4].start()

    late = ticks[12:]
    score_scale = LOG2_E / math.sqrt(head_size)
    pairs = width // lanes

    def mix(i, nothing):
        for number, tick in enumerate(late):
            pl.when(i == number)(functools.partial(run, tick))
        cols = pl.ds(pl.multiple_of(i * lanes, lanes), lanes)
        queries, near_keys, near_values = q[:, cols], keys[:, cols], values[:, cols]
        parts = []
        for head in range(2):
            s = dot_last(only_head(queries, head, head_size), near_keys) * score_scale + bias[...]
            top = jnp.max(s, axis=1, keepdims=True)
            e = jnp.exp2(s - top)
            total = jnp.sum(e, axis=1, keepdims=True)
            parts.append(dot(e.astype(bf16), near_values) * (1.0 / total))
            level = jnp.broadcast_to(top + jnp.log2(total), (rows, 128))
            stat_out[i, head : head + 1, :] = jnp.transpose(level)[0:1, :]
        o_out[:, cols] = jnp.where(pair_lanes((rows, lanes), head_size), parts[0], parts[1])
        return nothing

    lax.fori_loop(0, pairs, mix, 0)
    for tick in late[8:]:
        run(tick)
    for job in jobs[4:]:
        job.arrived()
    cross.arrived()
    for keep in keeps:
        keep.wait()
    links.finish()


def front(layers, number, head_size, grid_side, vec, qkv, out, gate, down, tokens, valid, hidden):
    bf16, f32 = jnp.bfloat16, jnp.float32
    rows, width = tokens.shape[1:]
    pairs = width // (2 * head_size)
    tile = 512
    fulls = [
        full_shape(layers, kind, piece.shape)
        for kind, piece in ((ROW, vec), (ROW, qkv), (COL, out), (ROW, gate), (COL, down))
    ]
    shapes = [jax.ShapeDtypeStruct(shape, bf16) for shape in fulls]
    shapes += [jax.ShapeDtypeStruct((2,) + hidden.shape, bf16)]
    shapes += [jax.ShapeDtypeStruct((n * rows, width), bf16) for n in (1, 1, 1, 2, 2)]
    shapes += [
        jax.ShapeDtypeStruct((rows, width), f32),
        jax.ShapeDtypeStruct((pairs, 2, rows), f32),
        jax.ShapeDtypeStruct((vec.shape[0], width), f32),
        jax.ShapeDtypeStruct((8, 128), f32),
    ]
    sems = 8 * Gather.sem_count(layers) + 7
    return pl.pallas_call(
        functools.partial(front_kernel, layers, head_size, grid_side),
        out_shape=shapes,
        in_specs=[ANY] * 8,
        out_specs=[ANY] * 11 + [IN_VMEM] * 4,
        scratch_shapes=[
            pltpu.VMEM((rows, width), bf16),
            pltpu.VMEM(valid.shape, valid.dtype),
            pltpu.VMEM(fulls[0], bf16),
            pltpu.VMEM((2, width, tile), bf16),
            pltpu.VMEM((rows, width), f32),
            pltpu.VMEM((rows, width), bf16),
            pltpu.VMEM((rows, width), bf16),
            pltpu.VMEM((2 * rows, width), bf16),
            pltpu.VMEM((2 * rows, width), bf16),
            pltpu.VMEM((rows, 2 * head_size), f32),
            pltpu.VMEM((rows, 2 * head_size), f32),
            pltpu.VMEM((1, 2 * rows), f32),
            pltpu.SemaphoreType.DMA((sems,)),
            pltpu.SemaphoreType.DMA((sems,)),
            pltpu.SemaphoreType.DMA((32,)),
        ],
        compiler_params=pltpu.CompilerParams(
            collective_id=number, has_side_effects=True, vmem_limit_bytes=LIMIT
        ),
    )(vec, qkv, out, gate, down, tokens, valid, hidden)


def back_kernel(layers, head_size, jobs, mats, *refs):
    grads, refs = refs[:mats], refs[mats:]
    q, keys, values, do, stats, row_dots, bias, cos, sin = refs[:9]
    outs, refs = refs[9 : 9 + mats], refs[9 + mats :]
    dq_out, dk_out, dv_out = refs[:3]
    scratch, refs = refs[3 : 3 + 6 * len(jobs)], refs[3 + 6 * len(jobs) :]
    k_box, v_box, k_sum, v_sum, send_sem, recv_sem, local_sem = refs
    f32, bf16 = jnp.float32, jnp.bfloat16
    place = place_of()
    z, k, x, y = place
    greet(layers, place, ())
    links = Links(place, send_sem, recv_sem)
    todo = reduce_jobs(layers, links, jobs, grads, outs, scratch, local_sem)
    ticks = ticks_of(links, todo, 1)
    rows, width = q.shape
    lanes = 2 * head_size
    pairs = width // lanes
    scale = 1.0 / math.sqrt(head_size)
    quarter = head_size // 4
    my_rows = pl.ds(pl.multiple_of(k * rows, 16), rows)
    other_rows = pl.ds(pl.multiple_of((1 - k) * rows, 16), rows)
    first = links.take(2 * pairs)

    def share(i):
        cols = pl.ds(pl.multiple_of(i * lanes, lanes), lanes)
        return (
            links.copy(CORE, first + 2 * i, k_sum.at[other_rows, cols], k_box.at[:, cols]),
            links.copy(CORE, first + 2 * i + 1, v_sum.at[other_rows, cols], v_box.at[:, cols]),
        )

    def turn_back(grad):
        return grad * cos[...] - turn_lanes(grad, quarter) * sin[...]

    lead = 2
    for tick in ticks[:lead]:
        run(tick)
    late = ticks[lead:]

    def step(i, nothing):
        for number, tick in enumerate(late[:pairs]):
            pl.when(i == number)(functools.partial(run, tick))
        cols = pl.ds(pl.multiple_of(i * lanes, lanes), lanes)
        queries, near_keys, near_values, grad = q[:, cols], keys[:, cols], values[:, cols], do[:, cols]
        found = []
        for head in range(2):
            s = dot_last(near_keys, only_head(queries, head, head_size)) * (scale * LOG2_E)
            p = jnp.exp2(s + bias[...] - stats[i, head : head + 1, :])
            dp = dot_last(near_values, only_head(grad, head, head_size))
            ds = (p * (dp - row_dots[i, head : head + 1, :])).astype(bf16)
            found.append(
                (dot_first(near_keys, ds) * scale, dot(ds, queries) * scale, dot(p.astype(bf16), grad))
            )
        dq = jnp.concatenate([found[0][0][:head_size], found[1][0][head_size:]], axis=0)
        dq_out[:, cols] = turn_back(jnp.transpose(dq)).astype(bf16)
        in_first = pair_lanes((2 * rows, lanes), head_size)
        k_sum[:, cols] = jnp.where(in_first, found[0][1], found[1][1]).astype(bf16)
        v_sum[:, cols] = jnp.where(in_first, found[0][2], found[1][2]).astype(bf16)
        for copy in share(i):
            copy.start()
        return nothing

    lax.fori_loop(0, pairs, step, 0)

    def join(i, nothing):
        cols = pl.ds(pl.multiple_of(i * lanes, lanes), lanes)
        for copy in share(i):
            copy.wait()
        dk = k_sum[my_rows, cols].astype(f32) + k_box[:, cols].astype(f32)
        dk_out[:, cols] = turn_back(dk).astype(bf16)
        dv = v_sum[my_rows, cols].astype(f32) + v_box[:, cols].astype(f32)
        dv_out[:, cols] = dv.astype(bf16)
        return nothing

    for tick in late[pairs : pairs + 1]:
        run(tick)
    lax.fori_loop(0, pairs, join, 0)
    for tick in late[pairs + 1 :]:
        run(tick)
    links.finish()


def back(layers, number, head_size, jobs, grads, q, keys, values, do, stats, row_dots, bias, cos, sin):
    bf16, f32 = jnp.bfloat16, jnp.float32
    kinds = {job[0]: job[2] for job in jobs}
    pieces = [piece_shape(layers, kinds[i], g.shape) for i, g in enumerate(grads)]
    rows, width = q.shape
    pairs = width // (2 * head_size)
    sems = len(jobs) * Reduce.sem_count(layers) + 2 * pairs
    return pl.pallas_call(
        functools.partial(back_kernel, layers, head_size, jobs, len(grads)),
        out_shape=[jax.ShapeDtypeStruct(piece, f32) for piece in pieces]
        + [jax.ShapeDtypeStruct((rows, width), bf16) for _ in range(3)],
        in_specs=[ANY] * len(grads) + [IN_VMEM] * 9,
        out_specs=[IN_VMEM] * (len(pieces) + 3),
        scratch_shapes=reduce_scratch(layers, jobs, pieces)
        + [
            pltpu.VMEM((rows, width), bf16),
            pltpu.VMEM((rows, width), bf16),
            pltpu.VMEM((2 * rows, width), bf16),
            pltpu.VMEM((2 * rows, width), bf16),
            pltpu.SemaphoreType.DMA((sems,)),
            pltpu.SemaphoreType.DMA((sems,)),
            pltpu.SemaphoreType.DMA((len(jobs) * 2 * layers,)),
        ],
        compiler_params=pltpu.CompilerParams(
            collective_id=number, has_side_effects=True, vmem_limit_bytes=62 * 1024 * 1024
        ),
    )(*grads, q, keys, values, do, stats, row_dots, bias, cos, sin)


def pad_to(values, axis, size):
    pads = [(0, 0)] * values.ndim
    pads[axis] = (0, size - values.shape[axis])
    return jnp.pad(values, pads)


def round_up(size, step):
    return (size + step - 1) // step * step


def tables(count, k, tokens_here, rows, head_size, grid_side):
    columns = (count - 1.0) / grid_side
    token = (k * tokens_here + jnp.arange(rows)).astype(jnp.float32)
    live = jnp.logical_and(token >= 1.0, token < count)
    row_id = jnp.floor((token - 0.5) / columns)
    col_id = token - 1.0 - row_id * columns
    angles = angle_table(jnp.where(live, row_id, 0.0), jnp.where(live, col_id, 0.0), head_size)
    within = jnp.arange(rows)
    seen = jnp.stack([within, within + tokens_here]).astype(jnp.float32) < count
    seen = jnp.logical_and(seen, within < tokens_here)
    return angles, jnp.where(seen, 0.0, -1e30).astype(jnp.float32).reshape(-1, 1)


def image_per_chip(
    layers,
    tokens,
    cotangent,
    valid_tokens,
    places,
    qkv_weight,
    head_biases,
    head_gain,
    out_weight,
    norm_gains,
    width_biases,
    gate_up,
    hidden_biases,
    hidden_gain,
    down_weight,
):
    f32 = jnp.float32
    bf16 = jnp.bfloat16
    z, k, x, y = place_of()
    s = 2 * z + k
    shards = 2 * layers
    width = tokens.shape[2]
    rows = tokens.shape[1]
    heads_here = head_gain.shape[0]
    heads = 2 * heads_here
    dims_here = head_gain.shape[1]
    head_size = dims_here * shards
    real_here = hidden_gain.shape[0]
    hidden_here = round_up(real_here, 128)
    real = 2 * real_here
    hidden_size = 2 * hidden_here
    score_scale = 1.0 / math.sqrt(head_size)

    padded = round_up(rows, 16)
    heads_own = jnp.concatenate([head_biases, head_gain[None]], axis=0)
    spot = jnp.zeros((4, heads_here, head_size), bf16)
    spot = lax.dynamic_update_slice(spot, heads_own, (0, 0, s * dims_here)).reshape(4, -1)
    width_own = jnp.concatenate([norm_gains, width_biases], axis=0)
    lane_at = s * width_own.shape[1] - y * spot.shape[1]
    inside = both(lane_at >= 0, lane_at < spot.shape[1])
    width_own = jnp.where(inside, width_own, jnp.zeros_like(width_own))
    at = jnp.where(inside, lane_at, 0)
    lanes_own = lax.dynamic_update_slice(jnp.zeros((6, spot.shape[1]), bf16), width_own, (0, at))
    vectors = pad_to(jnp.concatenate([spot, lanes_own], axis=0), 0, 16)
    hidden_vectors = jnp.concatenate([hidden_biases, hidden_gain[None]], axis=0)
    hidden_vectors = pad_to(pad_to(hidden_vectors, 1, hidden_here), 0, 16)
    gate_pad = pad_to(gate_up, 2, hidden_here)
    down_pad = pad_to(down_weight, 0, hidden_here)
    swaps = []
    for layer in range(layers):
        swaps += [(4 * layer + 1, 4 * layer + 2), (4 * layer + 2, 4 * layer + 1)]
    (
        vec_full, qkv_full, out_full, gate_full, down_full, hidden_full,
        token_block, first_in, queries, keys, values, mixed, stats, vec, count,
    ) = front(
        layers, 0, head_size, 32, vectors, qkv_weight, out_weight, gate_pad, down_pad,
        pad_to(tokens, 1, padded), valid_tokens, hidden_vectors,
    )
    cot_own = lax.dynamic_index_in_dim(cotangent, y, 0, keepdims=False)
    cot_own = pad_to(cot_own, 0, padded)
    cot_other = lax.ppermute(cot_own, (SHARD, CTX), swaps)
    cot_block = jnp.where(k == x, cot_own, cot_other)
    head_part, norm_scale, width_bias = vec[0:4], vec[4:6], vec[6:10]
    hidden_part = jnp.concatenate([hidden_full[0, :4], hidden_full[1, :4]], axis=1).astype(f32)
    token_rows = token_block.astype(f32)
    cot_rows = cot_block.astype(f32)
    mix_hat, spread_mix = standardize(mixed)
    mix_in = (mix_hat * head_part[3] + head_part[2]).astype(bf16)
    branch = jnp.dot(mix_in, out_full, preferred_element_type=f32)
    resid = token_rows + (branch + width_bias[2])
    normed_two, spread_two = standardize(resid)
    second_in = (normed_two * norm_scale[1] + width_bias[1]).astype(bf16)
    gate_pre = jnp.dot(second_in, gate_full[0], preferred_element_type=f32) + hidden_part[0]
    up_pre = jnp.dot(second_in, gate_full[1], preferred_element_type=f32) + hidden_part[1]
    sigmoid_gate = jax.nn.sigmoid(gate_pre)
    silu_gate = gate_pre * sigmoid_gate
    hidden = silu_gate * up_pre
    hidden_mean = jnp.sum(hidden, axis=-1, keepdims=True) / real
    centred = hidden - hidden_mean
    extra = (hidden_size - real) * hidden_mean * hidden_mean
    hidden_var = (jnp.sum(centred * centred, axis=-1, keepdims=True) - extra) / real
    spread_hid = lax.rsqrt(jnp.maximum(hidden_var, 0.0) + EPS)
    hidden_hat = centred * spread_hid
    down_in = (hidden_hat * hidden_part[3] + hidden_part[2]).astype(bf16)
    ffn_out = jnp.dot(down_in, down_full, preferred_element_type=f32)
    result = (resid + (ffn_out + width_bias[3])).astype(bf16)

    g_down = jnp.einsum("tf,td->fd", down_in, cot_block, preferred_element_type=f32)
    d_down_in = jnp.einsum("td,fd->tf", cot_block, down_full, preferred_element_type=f32)
    grad_hid = d_down_in * hidden_part[3]
    hid_back_one = jnp.sum(grad_hid, axis=-1, keepdims=True) / real
    hid_back_two = jnp.sum(grad_hid * hidden_hat, axis=-1, keepdims=True) / real
    d_hidden = (grad_hid - hid_back_one - hidden_hat * hid_back_two) * spread_hid
    d_gate = (d_hidden * up_pre * sigmoid_gate * (1.0 + gate_pre * (1.0 - sigmoid_gate))).astype(
        bf16
    )
    d_up = (d_hidden * silu_gate).astype(bf16)
    g_gate = jnp.einsum("td,tf->df", second_in, d_gate, preferred_element_type=f32).astype(bf16)
    g_up = jnp.einsum("td,tf->df", second_in, d_up, preferred_element_type=f32).astype(bf16)
    d_second = jnp.einsum("tf,df->td", d_gate, gate_full[0], preferred_element_type=f32)
    d_second = d_second + jnp.einsum("tf,df->td", d_up, gate_full[1], preferred_element_type=f32)
    d_resid = cot_rows + norm_back(d_second * norm_scale[1], normed_two, spread_two)
    d_branch_low = d_resid.astype(bf16)
    g_out = jnp.einsum("tm,tn->mn", mix_in, d_branch_low, preferred_element_type=f32)
    d_mix_in = jnp.einsum("tn,mn->tm", d_branch_low, out_full, preferred_element_type=f32)
    d_mixed = norm_back(d_mix_in * head_part[3], mix_hat, spread_mix).astype(bf16)
    row_dots = jnp.sum((d_mixed.astype(f32) * mixed).reshape(padded, heads // 2, 2, head_size), axis=-1)
    row_dots = row_dots.transpose(1, 2, 0)
    angles, key_bias = tables(count[0, 0], k, rows, padded, head_size, 32)
    cos, sin = [jnp.tile(turn(angles), (1, 2)) for turn in (jnp.cos, jnp.sin)]
    grad_jobs = (
        (0, None, COL, hidden_here // 2), (1, None, ROW, 64), (2, None, ROW, 64), (3, None, COL, 256),
    )
    (
        down_piece, gate_piece, up_piece, out_piece, d_query_low, d_key_low, d_value_low,
    ) = back(
        layers, 1, head_size, grad_jobs, (g_down.astype(bf16), g_gate, g_up, g_out.astype(bf16)),
        queries, keys, values, d_mixed, stats, row_dots, key_bias, cos, sin,
    )
    g_query, g_key, g_value = [
        jnp.einsum("tn,tm->nm", first_in, part, preferred_element_type=f32).astype(bf16)
        for part in (d_query_low, d_key_low, d_value_low)
    ]
    d_first = jnp.einsum("tm,nm->tn", d_query_low, qkv_full[0], preferred_element_type=f32)
    d_first = d_first + jnp.einsum("tm,nm->tn", d_key_low, qkv_full[1], preferred_element_type=f32)
    d_first = d_first + jnp.einsum(
        "tm,nm->tn", d_value_low, qkv_full[2], preferred_element_type=f32
    )
    normed_one, spread_one = standardize(token_rows)
    d_tokens = d_resid + norm_back(d_first * norm_scale[0], normed_one, spread_one)

    vector_grads = jnp.concatenate(
        [
            column_sum(d_query_low),
            column_sum(d_value_low),
            column_sum(d_mix_in),
            column_sum(d_mix_in * mix_hat),
            column_sum(d_first * normed_one),
            column_sum(d_second * normed_two),
            column_sum(d_first),
            column_sum(d_second),
            column_sum(d_branch_low),
            column_sum(cot_block),
            column_sum(d_gate),
            column_sum(d_up),
            column_sum(d_down_in),
            column_sum(d_down_in * hidden_hat),
        ]
    ).reshape(-1, 128)
    vector_grads = pad_to(vector_grads, 0, round_up(vector_grads.shape[0], 16))
    late_jobs = ((0, None, ROW, 64), (1, None, ROW, 64), (2, None, ROW, 64))
    query_piece, key_piece, value_piece, vector_grads, result, d_tokens = reduce_grads(
        layers, 2, late_jobs, (g_query, g_key, g_value),
        vector_grads, (result[:rows], d_tokens[:rows].astype(bf16)),
    )
    vector_grads = vector_grads.reshape(-1)
    head_sums = vector_grads[: 4 * width].reshape(4, heads, head_size)
    head_sums = lax.dynamic_slice(
        head_sums, (0, y * heads_here, s * dims_here), (4, heads_here, dims_here)
    )
    width_sums = vector_grads[4 * width : 10 * width].reshape(6, width)
    width_sums = lax.dynamic_slice(width_sums, (0, s * 128), (6, width // shards))
    hidden_sums = vector_grads[10 * width : 10 * width + 4 * hidden_size]
    hidden_sums = hidden_sums.reshape(4, hidden_size)
    hidden_sums = lax.dynamic_slice(hidden_sums, (0, y * hidden_here), (4, hidden_here))
    hidden_sums = hidden_sums[:, :real_here]

    return (
        result,
        d_tokens.astype(f32),
        jnp.stack([query_piece, key_piece, value_piece]),
        head_sums[:3],
        head_sums[3],
        out_piece,
        width_sums[:2],
        width_sums[2:],
        jnp.stack([gate_piece[:, :real_here], up_piece[:, :real_here]]),
        hidden_sums[:3],
        hidden_sums[3],
        down_piece[:real_here],
    )


def solution(mesh):
    small = mesh.shape[CTX] == 2 and mesh.shape[TP] == 2
    body = functools.partial(image_per_chip, mesh.shape[SHARD] // 2) if small else general_plan

    return jax.shard_map(
        body,
        mesh=mesh,
        in_specs=(
            P(SHARD, CTX, None),
            P(SHARD, CTX, None),
            P(SHARD, None),
            P(None, SHARD, CTX),
            P(None, SHARD, TP),
            P(None, TP, SHARD),
            P(TP, SHARD),
            P(TP, SHARD),
            P(None, SHARD),
            P(None, SHARD),
            P(None, SHARD, TP),
            P(None, TP),
            P(TP),
            P(TP, SHARD),
        ),
        out_specs=(
            P(SHARD, CTX, None),
            P(SHARD, CTX, None),
            P(None, SHARD, TP),
            P(None, TP, SHARD),
            P(TP, SHARD),
            P(TP, SHARD),
            P(None, SHARD),
            P(None, SHARD),
            P(None, SHARD, TP),
            P(None, TP),
            P(TP),
            P(TP, SHARD),
        ),
        check_vma=False,
    )
```

```python
import functools
import math

import jax
import jax.numpy as jnp
from jax import lax
from jax.experimental import pallas as pl
from jax.experimental.pallas import tpu as pltpu
from jax.sharding import PartitionSpec as P

SHARD, CTX, TP = "shard", "ctx", "tp"


EPS = 1e-06


def standardize(values):
    average = jnp.mean(values, axis=-1, keepdims=True)
    centred = values - average
    spread = lax.rsqrt(jnp.mean(centred * centred, axis=-1, keepdims=True) + EPS)
    return (centred * spread, spread)


def norm_back(grad_hat, normed, spread):
    mean_one = jnp.mean(grad_hat, axis=-1, keepdims=True)
    mean_two = jnp.mean(grad_hat * normed, axis=-1, keepdims=True)
    return (grad_hat - mean_one - normed * mean_two) * spread


def angle_table(row_ids, col_ids, head_size):
    quarter = head_size // 4
    frequency = 10000.0 ** (-jnp.arange(quarter, dtype=jnp.float32) / quarter)
    row_part = row_ids.astype(jnp.float32)[:, None] * frequency[None, :]
    col_part = col_ids.astype(jnp.float32)[:, None] * frequency[None, :]
    return jnp.concatenate([row_part, row_part, col_part, col_part], axis=1)


def turn_half(values):
    quarter = values.shape[-1] // 4
    part_one = values[..., :quarter]
    part_two = values[..., quarter : 2 * quarter]
    part_three = values[..., 2 * quarter : 3 * quarter]
    part_four = values[..., 3 * quarter :]
    return jnp.concatenate([-part_two, part_one, -part_four, part_three], axis=-1)


def rotate(values, angles):
    return values * jnp.cos(angles)[None, :, :] + turn_half(values) * jnp.sin(angles)[None, :, :]


def unrotate(values, angles):
    return values * jnp.cos(angles)[None, :, :] - turn_half(values) * jnp.sin(angles)[None, :, :]


def head_major(values, heads, head_size):
    return values.reshape(values.shape[0], heads, head_size).transpose(1, 0, 2)


def column_sum(values):
    return jnp.sum(values.astype(jnp.float32), axis=0)


def general_plan(
    tokens,
    cotangent,
    valid_tokens,
    places,
    qkv_weight,
    head_biases,
    head_gain,
    out_weight,
    norm_gains,
    width_biases,
    gate_up,
    hidden_biases,
    hidden_gain,
    down_weight,
):
    micro = tokens.shape[0]
    width = tokens.shape[2]
    local_dim = qkv_weight.shape[2]
    local_heads = head_biases.shape[1]
    head_size = local_dim // local_heads
    local_hidden = hidden_gain.shape[0]
    FF = local_hidden * lax.axis_size(TP)
    score_scale = 1.0 / math.sqrt(head_size)
    f32 = jnp.float32
    bf16 = jnp.bfloat16

    def one_batch(batch_idx, carried):
        gathered = (
            lax.all_gather(qkv_weight, SHARD, axis=1, tiled=True),
            lax.all_gather(head_biases, SHARD, axis=2, tiled=True),
            lax.all_gather(head_gain, SHARD, axis=1, tiled=True),
            lax.all_gather(out_weight, SHARD, axis=1, tiled=True),
            lax.all_gather(norm_gains, SHARD, axis=1, tiled=True),
            lax.all_gather(width_biases, SHARD, axis=1, tiled=True),
            lax.all_gather(gate_up, SHARD, axis=1, tiled=True),
            lax.all_gather(down_weight, SHARD, axis=1, tiled=True),
        )
        qkv_full, head_bias, head_scale, out_full, norm_scale, width_bias, gate_full, down_full = (
            gathered
        )
        head_bias_f = head_bias.astype(f32)
        head_scale_f = head_scale.astype(f32)[:, None, :]
        norm_scale = norm_scale.astype(f32)
        width_bias = width_bias.astype(f32)
        hidden_bias = hidden_biases.astype(f32)
        hidden_scale = hidden_gain.astype(f32)
        out_heads = out_full.reshape(local_heads, head_size, width)
        token_rows = lax.dynamic_index_in_dim(tokens, batch_idx, 0, keepdims=False).astype(f32)
        cot_rows = lax.dynamic_index_in_dim(cotangent, batch_idx, 0, keepdims=False).astype(f32)
        valid_row = lax.dynamic_index_in_dim(valid_tokens, batch_idx, 0, keepdims=False) > 0
        row_ids = lax.dynamic_index_in_dim(places[0], batch_idx, 0, keepdims=False)
        col_ids = lax.dynamic_index_in_dim(places[1], batch_idx, 0, keepdims=False)
        angles = angle_table(row_ids, col_ids, head_size)
        normed_one, spread_one = standardize(token_rows)
        first_in = (normed_one * norm_scale[0] + width_bias[0]).astype(bf16)
        query_flat = jnp.dot(first_in, qkv_full[0], preferred_element_type=f32)
        key_flat = jnp.dot(first_in, qkv_full[1], preferred_element_type=f32)
        value_flat = jnp.dot(first_in, qkv_full[2], preferred_element_type=f32)
        query_pre = head_major(query_flat, local_heads, head_size) + head_bias_f[0][:, None, :]
        key_pre = head_major(key_flat, local_heads, head_size)
        value_local = (
            head_major(value_flat, local_heads, head_size) + head_bias_f[1][:, None, :]
        ).astype(bf16)
        queries = rotate(query_pre, angles).astype(bf16)
        key_local = rotate(key_pre, angles).astype(bf16)
        key_heads, value_heads = (
            lax.all_gather(key_local, CTX, axis=1, tiled=True),
            lax.all_gather(value_local, CTX, axis=1, tiled=True),
        )

        def score_block():
            raw = (
                jnp.einsum("htd,hsd->hts", queries, key_heads, preferred_element_type=f32)
                * score_scale
            )
            return jnp.where(valid_row[None, None, :], raw, -1e30)

        scores = score_block()
        row_top = jnp.max(scores, axis=-1, keepdims=True)
        row_total = jnp.sum(jnp.exp(scores - row_top), axis=-1, keepdims=True)
        soft_low = (jnp.exp(scores - row_top) / row_total).astype(bf16)
        mixed = jnp.einsum("hts,hsd->htd", soft_low, value_heads, preferred_element_type=f32)
        mix_sums = lax.psum(
            (
                jnp.sum(mixed, axis=(0, 2), keepdims=True),
                jnp.sum(mixed * mixed, axis=(0, 2), keepdims=True),
            ),
            TP,
        )
        mix_mean = mix_sums[0] / width
        spread_mix = lax.rsqrt(mix_sums[1] / width - mix_mean * mix_mean + EPS)
        mix_hat = (mixed - mix_mean) * spread_mix
        mix_in = (mix_hat * head_scale_f + head_bias_f[2][:, None, :]).astype(bf16)
        branch = lax.psum(
            jnp.einsum("htd,hdn->tn", mix_in, out_heads, preferred_element_type=f32), TP
        )
        resid = token_rows + (branch + width_bias[2])
        normed_two, spread_two = standardize(resid)
        second_in = (normed_two * norm_scale[1] + width_bias[1]).astype(bf16)
        gate_pre = jnp.dot(second_in, gate_full[0], preferred_element_type=f32) + hidden_bias[0]
        up_pre = jnp.dot(second_in, gate_full[1], preferred_element_type=f32) + hidden_bias[1]
        sigmoid_gate = jax.nn.sigmoid(gate_pre)
        silu_gate = gate_pre * sigmoid_gate
        hidden = silu_gate * up_pre
        hidden_sums = lax.psum(
            (
                jnp.sum(hidden, axis=-1, keepdims=True),
                jnp.sum(hidden * hidden, axis=-1, keepdims=True),
            ),
            TP,
        )
        hidden_mean = hidden_sums[0] / FF
        spread_hid = lax.rsqrt(hidden_sums[1] / FF - hidden_mean * hidden_mean + EPS)
        hidden_hat = (hidden - hidden_mean) * spread_hid
        down_in = (hidden_hat * hidden_scale + hidden_bias[2]).astype(bf16)
        ffn_out = lax.psum(
            jnp.dot(down_in, down_full, preferred_element_type=f32).astype(jnp.bfloat16), TP
        ).astype(jnp.float32)
        result = (resid + (ffn_out + width_bias[3])).astype(bf16)
        d_ffn_low = cot_rows.astype(bf16)
        g_down = jnp.einsum("tf,td->fd", down_in, d_ffn_low, preferred_element_type=f32)
        d_down_in = jnp.einsum("td,fd->tf", d_ffn_low, down_full, preferred_element_type=f32)
        grad_hid = d_down_in * hidden_scale
        hid_back = lax.psum(
            (
                jnp.sum(grad_hid, axis=-1, keepdims=True),
                jnp.sum(grad_hid * hidden_hat, axis=-1, keepdims=True),
            ),
            TP,
        )
        d_hidden = (grad_hid - hid_back[0] / FF - hidden_hat * (hid_back[1] / FF)) * spread_hid
        d_gate = (
            d_hidden * up_pre * sigmoid_gate * (1.0 + gate_pre * (1.0 - sigmoid_gate))
        ).astype(bf16)
        d_up = (d_hidden * silu_gate).astype(bf16)
        g_gate_one = jnp.einsum("td,tf->df", second_in, d_gate, preferred_element_type=f32)
        g_up_one = jnp.einsum("td,tf->df", second_in, d_up, preferred_element_type=f32)
        d_second_part = jnp.einsum(
            "tf,df->td", d_gate, gate_full[0], preferred_element_type=f32
        ) + jnp.einsum("tf,df->td", d_up, gate_full[1], preferred_element_type=f32)
        d_second = lax.psum(d_second_part, TP)
        d_resid = cot_rows + norm_back(d_second * norm_scale[1], normed_two, spread_two)
        d_branch_low = d_resid.astype(bf16)
        g_out = jnp.einsum("htd,tn->hdn", mix_in, d_branch_low, preferred_element_type=f32).reshape(
            local_dim, width
        )
        d_mix_in = jnp.einsum("tn,hdn->htd", d_branch_low, out_heads, preferred_element_type=f32)
        grad_mix = d_mix_in * head_scale_f
        mix_back = lax.psum(
            (
                jnp.sum(grad_mix, axis=(0, 2), keepdims=True),
                jnp.sum(grad_mix * mix_hat, axis=(0, 2), keepdims=True),
            ),
            TP,
        )
        d_mixed = (
            (grad_mix - mix_back[0] / width - mix_hat * (mix_back[1] / width)) * spread_mix
        ).astype(bf16)
        again = score_block()
        weights_soft = jnp.exp(again - row_top) / row_total
        d_soft = jnp.einsum("htd,hsd->hts", d_mixed, value_heads, preferred_element_type=f32)
        row_dot = jnp.sum(weights_soft * d_soft, axis=-1, keepdims=True)
        d_scores = (weights_soft * (d_soft - row_dot)).astype(bf16)
        d_query = (
            jnp.einsum("hts,hsd->htd", d_scores, key_heads, preferred_element_type=f32)
            * score_scale
        )
        soft_again = weights_soft.astype(bf16)
        d_key_all = (
            jnp.einsum("hts,htd->hsd", d_scores, queries, preferred_element_type=f32) * score_scale
        )
        d_value_all = jnp.einsum("hts,htd->hsd", soft_again, d_mixed, preferred_element_type=f32)
        d_key_heads, d_value_loc = (
            lax.psum_scatter(
                d_key_all.astype(jnp.bfloat16), CTX, scatter_dimension=1, tiled=True
            ).astype(jnp.float32),
            lax.psum_scatter(
                d_value_all.astype(jnp.bfloat16), CTX, scatter_dimension=1, tiled=True
            ).astype(jnp.float32),
        )
        d_query_low = unrotate(d_query, angles).astype(bf16)
        d_key_low = unrotate(d_key_heads, angles).astype(bf16)
        d_value_low = d_value_loc.astype(bf16)
        g_query = jnp.einsum(
            "tn,htd->nhd", first_in, d_query_low, preferred_element_type=f32
        ).reshape(width, local_dim)
        g_key = jnp.einsum("tn,htd->nhd", first_in, d_key_low, preferred_element_type=f32).reshape(
            width, local_dim
        )
        g_value = jnp.einsum(
            "tn,htd->nhd", first_in, d_value_low, preferred_element_type=f32
        ).reshape(width, local_dim)
        d_first_part = jnp.einsum(
            "htd,nhd->tn",
            d_query_low,
            qkv_full[0].reshape(width, local_heads, head_size),
            preferred_element_type=f32,
        )
        d_first_part = d_first_part + jnp.einsum(
            "htd,nhd->tn",
            d_key_low,
            qkv_full[1].reshape(width, local_heads, head_size),
            preferred_element_type=f32,
        )
        d_first_part = d_first_part + jnp.einsum(
            "htd,nhd->tn",
            d_value_low,
            qkv_full[2].reshape(width, local_heads, head_size),
            preferred_element_type=f32,
        )
        d_first = lax.psum(d_first_part.astype(jnp.bfloat16), TP).astype(jnp.float32)
        d_tokens = d_resid + norm_back(d_first * norm_scale[0], normed_one, spread_one)
        g_head_bias = jnp.stack(
            [
                jnp.sum(d_query_low.astype(f32), axis=1),
                jnp.sum(d_value_low.astype(f32), axis=1),
                jnp.sum(d_mix_in, axis=1),
            ]
        )
        g_head_scale = jnp.sum(d_mix_in * mix_hat, axis=1)
        g_norm = jnp.stack([column_sum(d_first * normed_one), column_sum(d_second * normed_two)])
        g_width = jnp.stack(
            [
                column_sum(d_first),
                column_sum(d_second),
                column_sum(d_branch_low),
                column_sum(d_ffn_low),
            ]
        )
        g_hidden_bias = jnp.stack([column_sum(d_gate), column_sum(d_up), column_sum(d_down_in)])
        g_hidden_scale = column_sum(d_down_in * hidden_hat)
        out_all = lax.dynamic_update_index_in_dim(carried[0], result, batch_idx, 0)
        grad_all = lax.dynamic_update_index_in_dim(carried[1], d_tokens, batch_idx, 0)
        updates = (
            g_query,
            g_key,
            g_value,
            g_head_bias,
            g_head_scale,
            g_out,
            g_norm,
            g_width,
            g_gate_one,
            g_up_one,
            g_down,
            g_hidden_bias,
            g_hidden_scale,
        )
        return (
            out_all,
            grad_all,
            tuple((before + added for before, added in zip(carried[2], updates))),
        )

    zeros_acc = (
        jnp.zeros((width, local_dim), f32),
        jnp.zeros((width, local_dim), f32),
        jnp.zeros((width, local_dim), f32),
        jnp.zeros((3, local_heads, head_size), f32),
        jnp.zeros((local_heads, head_size), f32),
        jnp.zeros((local_dim, width), f32),
        jnp.zeros((2, width), f32),
        jnp.zeros((4, width), f32),
        jnp.zeros((width, local_hidden), f32),
        jnp.zeros((width, local_hidden), f32),
        jnp.zeros((local_hidden, width), f32),
        jnp.zeros((3, local_hidden), f32),
        jnp.zeros((local_hidden,), f32),
    )
    start = (jnp.zeros(tokens.shape, bf16), jnp.zeros(tokens.shape, f32), zeros_acc)
    out_all, grad_all, summed = lax.fori_loop(0, micro, one_batch, start)
    (
        acc_query,
        acc_key,
        acc_value,
        acc_head_bias,
        acc_head_scale,
        acc_out,
        acc_norm,
        acc_width,
        acc_gate_one,
        acc_up_one,
        acc_down,
        acc_hidden_bias,
        acc_hidden_scale,
    ) = summed
    acc_qkv = jnp.stack([acc_query, acc_key, acc_value])
    acc_gate = jnp.stack([acc_gate_one, acc_up_one])
    sharded = (
        acc_qkv,
        acc_head_bias,
        acc_head_scale,
        acc_out,
        acc_norm,
        acc_width,
        acc_gate,
        acc_down,
    )
    hidden_done = lax.psum((acc_hidden_bias, acc_hidden_scale), (SHARD, CTX))
    return (
        out_all,
        grad_all,
        lax.psum_scatter(
            lax.psum(sharded[0].astype(jnp.bfloat16), CTX),
            SHARD,
            scatter_dimension=1,
            tiled=True,
        ).astype(jnp.float32),
        lax.psum_scatter(
            lax.psum(sharded[1].astype(jnp.bfloat16), CTX),
            SHARD,
            scatter_dimension=2,
            tiled=True,
        ).astype(jnp.float32),
        lax.psum_scatter(
            lax.psum(sharded[2].astype(jnp.bfloat16), CTX),
            SHARD,
            scatter_dimension=1,
            tiled=True,
        ).astype(jnp.float32),
        lax.psum_scatter(
            lax.psum(sharded[3].astype(jnp.bfloat16), CTX),
            SHARD,
            scatter_dimension=1,
            tiled=True,
        ).astype(jnp.float32),
        lax.psum_scatter(
            lax.psum(sharded[4].astype(jnp.bfloat16), CTX),
            SHARD,
            scatter_dimension=1,
            tiled=True,
        ).astype(jnp.float32),
        lax.psum_scatter(
            lax.psum(sharded[5].astype(jnp.bfloat16), CTX),
            SHARD,
            scatter_dimension=1,
            tiled=True,
        ).astype(jnp.float32),
        lax.psum_scatter(
            lax.psum(sharded[6].astype(jnp.bfloat16), CTX),
            SHARD,
            scatter_dimension=1,
            tiled=True,
        ).astype(jnp.float32),
        hidden_done[0],
        hidden_done[1],
        lax.psum_scatter(
            lax.psum(sharded[7].astype(jnp.bfloat16), CTX),
            SHARD,
            scatter_dimension=1,
            tiled=True,
        ).astype(jnp.float32),
    )


MESH = pl.DeviceIdType.MESH
LIMIT = 56 * 1024 * 1024
ANY = pl.BlockSpec(memory_space=pl.ANY)
IN_VMEM = pl.BlockSpec(memory_space=pltpu.VMEM)
CORE, ACROSS, BESIDE, UP, DOWN, SWAP, FAR = range(7)
ROW, COL = range(2)


def place_of():
    index = lax.axis_index(SHARD)
    return (lax.div(index, 2), lax.rem(index, 2), lax.axis_index(CTX), lax.axis_index(TP))


def when(condition, action):
    if condition is None:
        action()
    else:
        pl.when(condition)(action)


def both(first, second):
    return jnp.logical_and(first, second)


def device(place, way):
    z, k, x, y = place
    return {
        CORE: {SHARD: 2 * z + 1 - k},
        ACROSS: {CTX: 1 - x},
        BESIDE: {TP: 1 - y},
        UP: {SHARD: 2 * z + 2 + k},
        DOWN: {SHARD: 2 * z - 2 + k},
        SWAP: {SHARD: 2 * z + 1 - k, CTX: 1 - x},
        FAR: {SHARD: 2 * z + 1 - k, CTX: 1 - x, TP: 1 - y},
    }[way]


def greet(layers, place, diagonals):
    z, k, x, y = place
    barrier = pltpu.get_barrier_semaphore()

    def hello(way):
        pl.semaphore_signal(barrier, inc=1, device_id=device(place, way), device_id_type=MESH)

    hello(CORE)
    hello(ACROSS)
    hello(BESIDE)
    pl.when(z > 0)(lambda: hello(DOWN))
    pl.when(z < layers - 1)(lambda: hello(UP))
    count = 3 + jnp.where(z > 0, 1, 0) + jnp.where(z < layers - 1, 1, 0)
    for way in diagonals:
        pl.when(k != x)(lambda way=way: hello(way))
        count = count + jnp.where(k != x, 1, 0)
    pl.semaphore_wait(barrier, count)


class Links:
    def __init__(self, place, send_sem, recv_sem):
        self.place, self.send_sem, self.recv_sem = place, send_sem, recv_sem
        self.used = 0
        self.sent = []
        self.noted = None

    def take(self, count):
        first = self.used
        self.used += count
        return first

    def copy(self, way, at, source, target):
        return pltpu.make_async_remote_copy(
            src_ref=source,
            dst_ref=target,
            send_sem=self.send_sem.at[at],
            recv_sem=self.recv_sem.at[at],
            device_id=device(self.place, way),
            device_id_type=MESH,
        )

    def do(self, condition, action):
        if self.noted is None:
            when(condition, action)
        else:
            self.noted.append((condition, action))

    def record(self, actions):
        self.noted = []
        for action in actions:
            action()
        found, self.noted = self.noted, None
        return found

    def send(self, condition, copy):
        self.do(condition, copy.start)
        self.sent.append((condition, copy))

    def finish(self):
        for condition, copy in self.sent:
            when(condition, copy.wait_send)


def run(noted):
    for condition, action in noted:
        when(condition, action)


def piece_view(kind, rows, cols, ref, y, s, first, size):
    if kind == ROW:
        at_row, at_col = s * rows + first, y * cols
    else:
        at_row, at_col = y * rows + first, s * cols
    at_row, at_col = pl.multiple_of(at_row, 16), pl.multiple_of(at_col, 128)
    return ref.at[pl.ds(at_row, size), pl.ds(at_col, cols)]


def cut_rows(ref, first, size):
    return ref.at[pl.ds(pl.multiple_of(first, 16), size), :]


class Gather:
    def __init__(self, layers, links, kind, own, full, low, rows, split, local_sem):
        self.layers, self.links, self.kind, self.own, self.full = layers, links, kind, own, full
        self.piece_rows, self.cols = own.shape
        self.low, self.rows = low, rows
        self.split, self.half = split, split // 2
        self.local_sem = local_sem
        n = layers
        self.z_a = links.take(2 * n)
        self.z_b = links.take(2 * n)
        self.x_a, self.x_b = links.take(n), links.take(n)
        self.y_a, self.y_b = links.take(n), links.take(1)
        self.core = links.take(2 * n)

    @staticmethod
    def sem_count(layers):
        return 9 * layers + 1

    def copy(self, way, at, y, z, first, size, from_own=False, other_core=False):
        k = self.links.place[1]
        s = 2 * z + (1 - k if other_core else k)
        first = first + self.low
        there = piece_view(self.kind, self.piece_rows, self.cols, self.full, y, s, first, size)
        here = cut_rows(self.own, first, size) if from_own else there
        return self.links.copy(way, at, here, there)

    def half_a(self, way, at, y, z, which, from_own=False):
        return self.copy(way, at, y, z, which * self.half, self.half, from_own)

    def part_a(self, way, at, y, z, from_own=False):
        return self.copy(way, at, y, z, 0, self.split, from_own)

    def part_b(self, way, at, y, z, from_own=False):
        return self.copy(way, at, y, z, self.split, self.rows - self.split, from_own)

    def to_core(self, y, z, from_own=False, other_core=False):
        return self.copy(CORE, self.core + 2 * z + y, y, z, 0, self.rows, from_own, other_core)

    def z_at(self, base, way, z):
        return base + (0 if way == UP else self.layers) + z

    def begin(self):
        z, k, x, y = self.links.place
        send = self.links.send
        low, high = z > 0, z < self.layers - 1
        own_view = piece_view(
            self.kind, self.piece_rows, self.cols, self.full, y, 2 * z + k, self.low, self.rows
        )
        own = cut_rows(self.own, self.low, self.rows)
        self.local = pltpu.make_async_copy(own, own_view, self.local_sem)
        if self.split < self.rows:
            send(None, self.part_b(BESIDE, self.y_b, y, z, True))
            same = x == y
            send(both(same, high), self.part_b(UP, self.z_at(self.z_b, UP, z), y, z, True))
            send(both(same, low), self.part_b(DOWN, self.z_at(self.z_b, DOWN, z), y, z, True))
        if self.split:
            send(high, self.half_a(UP, self.z_at(self.z_a, UP, z), y, z, x, True))
            send(low, self.half_a(DOWN, self.z_at(self.z_a, DOWN, z), y, z, x, True))
            send(None, self.part_a(BESIDE, self.y_a + z, y, z, True))
        send(None, self.to_core(y, z, True))
        self.links.do(None, self.local.start)

    def cross_y(self):
        if self.split == self.rows:
            return
        z, k, x, y = self.links.place
        send = self.links.send
        self.links.do(None, self.part_b(BESIDE, self.y_b, 1 - y, z).wait_recv)
        other = x != y
        low, high = z > 0, z < self.layers - 1
        send(both(other, high), self.part_b(UP, self.z_at(self.z_b, UP, z), 1 - y, z))
        send(both(other, low), self.part_b(DOWN, self.z_at(self.z_b, DOWN, z), 1 - y, z))

    def steps(self, step):
        z = self.links.place[0]
        below, above = z - 1 - step, z + 1 + step
        return (
            (UP, below, below >= 0, z < self.layers - 1),
            (DOWN, above, above <= self.layers - 1, z > 0),
        )

    def along_z(self, step):
        z, k, x, y = self.links.place
        send = self.links.send
        for way, origin, there, further in self.steps(step):
            if self.split < self.rows:
                came = self.part_b(way, self.z_at(self.z_b, way, origin), x, origin)
                self.links.do(there, came.wait_recv)
                send(both(there, further), came)
                send(there, self.part_b(ACROSS, self.x_b + origin, x, origin))
            if self.split:
                came = self.half_a(way, self.z_at(self.z_a, way, origin), y, origin, x)
                self.links.do(there, came.wait_recv)
                send(both(there, further), came)
                send(there, self.half_a(ACROSS, self.x_a + origin, y, origin, x))

    def along_x(self, step):
        z, k, x, y = self.links.place
        send = self.links.send
        for way, origin, there, further in self.steps(step):
            if self.split:
                self.links.do(there, self.half_a(ACROSS, self.x_a + origin, y, origin, 1 - x).wait_recv)
                send(there, self.part_a(BESIDE, self.y_a + origin, y, origin))
            if self.split < self.rows:
                self.links.do(there, self.part_b(ACROSS, self.x_b + origin, 1 - x, origin).wait_recv)
            send(there, self.to_core(y, origin))

    def along_y(self, step):
        z, k, x, y = self.links.place
        todo = ((None, z, None, None),) if step < 0 else self.steps(step)
        for way, origin, there, further in todo:
            if self.split:
                self.links.do(there, self.part_a(BESIDE, self.y_a + origin, 1 - y, origin).wait_recv)
            self.links.send(there, self.to_core(1 - y, origin))

    def stages(self):
        found = [[self.begin], [self.cross_y]]
        for step in range(self.layers + 1):
            now = []
            if step < self.layers - 1:
                now.append(functools.partial(self.along_z, step))
            if step == 0:
                now.append(functools.partial(self.along_y, -1))
            if 0 <= step - 1 < self.layers - 1:
                now.append(functools.partial(self.along_x, step - 1))
            if 0 <= step - 2 < self.layers - 1:
                now.append(functools.partial(self.along_y, step - 2))
            found.append(now)
        return found

    def arrived(self):
        self.links.do(None, self.local.wait)
        for layer in range(self.layers):
            for y in range(2):
                self.links.do(None, self.to_core(y, layer, other_core=True).wait_recv)


def ticks_of(links, jobs, starts, begins):
    plans = [job.stages() for job in jobs]
    ticks = [[] for _ in range(max([at + len(plan) for at, plan in zip(starts, plans)]))]
    for start, begin, plan in zip(starts, begins, plans):
        for stage, actions in enumerate(plan):
            ticks[start + stage if stage else begin] += actions
    return [links.record(tick) for tick in ticks]


class Swap:
    def __init__(self, links, source, target, local_sem):
        z, k, x, y = links.place
        self.same, self.other = k == x, k != x
        self.here = pltpu.make_async_copy(source, target, local_sem)
        self.there = links.copy(SWAP, links.take(1), source, target)

    def begin(self):
        pl.when(self.same)(self.here.start)
        pl.when(self.other)(self.there.start)

    def arrived(self):
        pl.when(self.same)(self.here.wait)
        pl.when(self.other)(self.there.wait)


class Cross:
    def __init__(self, links, source, target, local_sem):
        y = links.place[3]
        at = links.take(1)
        self.here = pltpu.make_async_copy(source, target.at[y], local_sem)
        self.out = links.copy(BESIDE, at, source, target.at[y])
        self.back = links.copy(BESIDE, at, source, target.at[1 - y])

    def begin(self):
        self.here.start()
        self.out.start()

    def arrived(self):
        self.here.wait()
        self.out.wait_send()
        self.back.wait_recv()


class Spread:
    def __init__(self, links, block, both_images, local_sem):
        z, k, x, y = links.place
        self.same, self.other = k == x, k != x
        here, first, second = links.take(1), links.take(1), 0
        target = both_images.at[y]
        self.keep = pltpu.make_async_copy(block, target, local_sem)
        self.beside = links.copy(BESIDE, here, block, target)
        self.swap = links.copy(SWAP, first, block, target)
        self.far = links.copy(FAR, here, block, target)
        self.came = links.copy(BESIDE, here, block, both_images.at[1 - y])

    def begin(self):
        def same():
            self.keep.start()
            self.beside.start()

        def other():
            self.swap.start()
            self.far.start()

        pl.when(self.same)(same)
        pl.when(self.other)(other)

    def arrived(self):
        def same():
            self.keep.wait()
            self.beside.wait_send()

        def other():
            self.swap.wait()
            self.far.wait_send()

        pl.when(self.same)(same)
        pl.when(self.other)(other)
        self.came.wait_recv()


def full_shape(layers, kind, piece):
    if kind == ROW:
        return piece[:-2] + (piece[-2] * layers * 2, piece[-1] * 2)
    return (piece[-2] * 2, piece[-1] * layers * 2)


def by_chunks(shape, body):
    rows, cols = shape
    chunk = 16
    while rows % (2 * chunk) == 0 and 2 * chunk * cols <= 16384:
        chunk *= 2

    def step(i, nothing):
        body((pl.ds(pl.multiple_of(i * chunk, 16), chunk), slice(None)))
        return nothing

    lax.fori_loop(0, rows // chunk, step, 0)


def add_into(target, term):
    def body(where):
        target[where] = target[where] + term[where]

    by_chunks(target.shape, body)


def store_sum(out, *terms):
    def body(where):
        total = terms[0][where].astype(jnp.float32)
        for term in terms[1:]:
            total = total + term[where].astype(jnp.float32)
        out[where] = total

    by_chunks(out.shape, body)


class Reduce:
    def __init__(self, layers, links, kind, grad, out, low, split, scratch, local_sem, local_base):
        self.layers, self.links, self.kind, self.grad = layers, links, kind, grad
        self.mine, self.load, self.y_in, self.x_in, self.z_in, self.last = scratch
        self.sent = []
        self.rows, self.cols = self.mine.shape[-2:]
        self.low, self.piece_rows = low, out.shape[0]
        self.out = cut_rows(out, low, self.rows)
        self.split = split
        self.local_sem, self.local_base = local_sem, local_base
        n = layers
        self.core = links.take(2 * n)
        self.y_a, self.x_b = links.take(n), links.take(n)
        self.z_a, self.z_b = links.take(2 * n), links.take(2 * n)
        self.end_a, self.end_b, self.end_c = links.take(1), links.take(1), links.take(1)
        self.order = []
        low, high = 0, layers - 1
        while low <= high:
            self.order.append(high)
            if low < high:
                self.order.append(low)
            low, high = low + 1, high - 1

    @staticmethod
    def sem_count(layers):
        return 8 * layers + 3

    def part_a(self, ref):
        return cut_rows(ref, 0, self.split)

    def part_b(self, ref):
        return cut_rows(ref, self.split, self.rows - self.split)

    def send(self, condition, copy):
        self.links.do(condition, copy.start)
        self.sent.append((condition, copy))

    def finish(self):
        for condition, copy in self.sent:
            when(condition, copy.wait_send)

    def add(self, condition, target, term):
        self.links.do(condition, functools.partial(add_into, target, term))

    def grad_piece(self, y, s):
        return piece_view(
            self.kind, self.piece_rows, self.cols, self.grad, y, s, self.low, self.rows
        )

    def local(self, number):
        k = self.links.place[1]
        layer, y = self.order[number // 2], number % 2
        return pltpu.make_async_copy(
            self.grad_piece(y, 2 * layer + k),
            self.load.at[number % 2],
            self.local_sem.at[self.local_base + number],
        )

    def to_core(self, y, layer):
        k = self.links.place[1]
        return self.links.copy(
            CORE,
            self.core + 2 * layer + y,
            self.grad_piece(y, 2 * layer + 1 - k),
            self.mine.at[y, layer],
        )

    def begin(self):
        for layer in self.order:
            for y in range(2):
                self.send(None, self.to_core(y, layer))
        for number in range(2):
            self.links.do(None, self.local(number).start)

    def to_y(self, layer):
        y = self.links.place[3]
        source = self.part_a(self.mine.at[1 - y, layer])
        return self.links.copy(BESIDE, self.y_a + layer, source, self.y_in.at[layer])

    def to_x(self, layer):
        x = self.links.place[2]
        source = self.part_b(self.mine.at[1 - x, layer])
        return self.links.copy(ACROSS, self.x_b + layer, source, self.x_in.at[layer])

    def chip_sum(self):
        for number in range(2 * self.layers):
            layer, side = self.order[number // 2], number % 2
            self.links.do(None, self.local(number).wait)
            self.links.do(None, self.to_core(side, layer).wait_recv)
            self.add(None, self.mine.at[side, layer], self.load.at[number % 2])
            if number + 2 < 2 * self.layers:
                self.links.do(None, self.local(number + 2).start)
            if side:
                self.send(None, self.to_y(layer))
                self.send(None, self.to_x(layer))

    def plane_sum(self):
        z, k, x, y = self.links.place
        for layer in self.order:
            self.links.do(None, self.to_y(layer).wait_recv)
            self.add(None, self.part_a(self.mine.at[y, layer]), self.y_in.at[layer])
            self.links.do(None, self.to_x(layer).wait_recv)
            self.add(None, self.part_b(self.mine.at[x, layer]), self.x_in.at[layer])

    def chain(self, way, layer, receiver):
        z, k, x, y = self.links.place
        slot = layer if way == UP else jnp.where(receiver == layer, self.layers, layer)
        add = 0 if way == UP else self.layers
        found = []
        for base, part, side in ((self.z_a, self.part_a, y), (self.z_b, self.part_b, x)):
            total, box = part(self.mine.at[side, layer]), part(self.z_in.at[slot])
            found.append((total, box, self.links.copy(way, base + add + layer, total, box)))
        return found

    def take(self, condition, way, layer):
        for total, box, copy in self.chain(way, layer, self.links.place[0]):
            self.links.do(condition, copy.wait_recv)
            self.add(condition, total, box)

    def along_z(self, depth):
        z = self.links.place[0]
        top = self.layers - 1
        for way, here, goals in (
            (UP, z == depth, range(top, depth, -1)),
            (DOWN, z == top - depth, range(0, top - depth)),
        ):
            for layer in goals:
                if depth:
                    self.take(here, way, layer)
                for total, box, copy in self.chain(way, layer, z + 1 if way == UP else z - 1):
                    self.send(here, copy)

    def ending(self):
        z, k, x, y = self.links.place
        self.take(z > 0, UP, z)
        self.take(z < self.layers - 1, DOWN, z)
        self.sum_a, self.sum_b = self.part_a(self.mine.at[y, z]), self.part_b(self.mine.at[x, z])
        self.got_a, self.got_b = self.part_a(self.last.at[0]), self.part_b(self.last.at[0])
        self.got_y = self.part_b(self.last.at[1])
        self.x_end = self.links.copy(ACROSS, self.end_a, self.sum_a, self.got_a)
        self.y_end = self.links.copy(BESIDE, self.end_b, self.sum_b, self.got_y)
        self.x_last = self.links.copy(ACROSS, self.end_c, self.sum_b, self.got_b)
        self.send(y != x, self.y_end)
        self.send(None, self.x_end)

    def owner(self):
        z, k, x, y = self.links.place

        self.links.do(y == x, self.y_end.wait_recv)
        self.add(y == x, self.sum_b, self.got_y)
        self.send(y == x, self.x_last)
        self.links.do(None, self.x_end.wait_recv)
        out_a = self.part_a(self.out)
        self.links.do(None, functools.partial(store_sum, out_a, self.sum_a, self.got_a))

    def write(self):
        z, k, x, y = self.links.place
        out_b = self.part_b(self.out)

        self.links.do(y != x, self.x_last.wait_recv)
        self.links.do(y != x, functools.partial(store_sum, out_b, self.got_b))
        self.links.do(y == x, functools.partial(store_sum, out_b, self.sum_b))

    def stages(self):
        chains = [[functools.partial(self.along_z, depth)] for depth in range(self.layers - 1)]
        return [
            [self.begin], [self.chip_sum], [self.plane_sum], *chains,
            [self.ending], [self.owner], [self.write],
        ]


class Total:
    def __init__(self, layers, links, given, out, boxes, layer_boxes):
        self.layers, self.links, self.given, self.out = layers, links, given, out
        self.boxes, self.layer_boxes = boxes, layer_boxes
        self.pair = [links.take(1) for _ in range(3)]
        self.z_up, self.z_down = links.take(layers), links.take(layers)

    @staticmethod
    def sem_count(layers):
        return 3 + 2 * layers

    def exchange(self, number):
        way = (CORE, ACROSS, BESIDE)[number]
        source = self.given if number == 0 else self.boxes.at[2 + number]
        return self.links.copy(way, self.pair[number], source, self.boxes.at[number])

    def begin(self):
        self.links.send(None, self.exchange(0))

    def join(self, number):
        z = self.links.place[0]
        self.links.do(None, self.exchange(number).wait_recv)
        mine = self.given if number == 0 else self.boxes.at[2 + number]
        result = self.layer_boxes.at[z] if number == 2 else self.boxes.at[3 + number]
        self.links.do(None, functools.partial(store_sum, result, mine, self.boxes.at[number]))
        if number < 2:
            self.links.send(None, self.exchange(number + 1))
        else:
            self.links.send(z < self.layers - 1, self.pass_on(UP, z))
            self.links.send(z > 0, self.pass_on(DOWN, z))

    def pass_on(self, way, layer):
        box = self.layer_boxes.at[layer]
        return self.links.copy(way, (self.z_up if way == UP else self.z_down) + layer, box, box)

    def along_z(self, step):
        z = self.links.place[0]
        top = self.layers - 1
        below, above = z - 1 - step, z + 1 + step
        for way, origin, there, further in (
            (UP, below, below >= 0, z < top),
            (DOWN, above, above <= top, z > 0),
        ):
            copy = self.pass_on(way, origin)
            self.links.do(there, copy.wait_recv)
            self.links.send(both(there, further), copy)

    def write(self):
        layers = [self.layer_boxes.at[layer] for layer in range(self.layers)]
        self.links.do(None, functools.partial(store_sum, self.out, *layers))

    def stages(self):
        joins = [[functools.partial(self.join, number)] for number in range(3)]
        moves = [[functools.partial(self.along_z, step)] for step in range(self.layers - 1)]
        return [[self.begin], *joins, *moves, [self.write]]


def reduce_jobs(layers, links, jobs, grads, outs, scratch, local_sem):
    todo = []
    for number, (mat, kind, low, rows, split) in enumerate(jobs):
        own = scratch[6 * number : 6 * number + 6]
        at = number * 2 * layers
        grad, out = grads[mat], outs[mat]
        todo.append(Reduce(layers, links, kind, grad, out, low, split, own, local_sem, at))
    return todo


def reduce_shapes(layers, rows, cols, split):
    return [
        (2, layers, rows, cols), (2, rows, cols), (layers, split, cols),
        (layers, rows - split, cols), (layers + 1, rows, cols), (2, rows, cols),
    ]


def piece_shape(layers, kind, full):
    if kind == ROW:
        return full[:-2] + (full[-2] // (2 * layers), full[-1] // 2)
    return (full[-2] // 2, full[-1] // (2 * layers))


def pair_lanes(shape, head_size):
    lane = lax.broadcasted_iota(jnp.int32, shape, len(shape) - 1)
    return lane < head_size


def dot_last(left, right):
    return lax.dot_general(left, right, (((1,), (1,)), ((), ())), preferred_element_type=jnp.float32)


def dot_first(left, right):
    return lax.dot_general(left, right, (((0,), (0,)), ((), ())), preferred_element_type=jnp.float32)


def dot(left, right):
    return lax.dot_general(left, right, (((1,), (0,)), ((), ())), preferred_element_type=jnp.float32)


def only_head(values, head, head_size):
    lane = lax.broadcasted_iota(jnp.int32, (1, values.shape[1]), 1)
    keep = (lane < head_size) if head == 0 else (lane >= head_size)
    return values * jnp.where(keep, 1.0, 0.0).astype(values.dtype)


LOG2_E = 1.4426950408889634


def turn_lanes(values, quarter):
    width = values.shape[-1]
    lane = lax.broadcasted_iota(jnp.int32, (1, width), 1)
    even = lax.rem(lax.div(lane, quarter), 2) == 0
    after = pltpu.roll(values, width - quarter, 1)
    before = pltpu.roll(values, quarter, 1)
    return jnp.where(even, -after, before)


def slot_bias(shape, axis, rows, tokens_here, count):
    slot = lax.broadcasted_iota(jnp.int32, shape, axis)
    second = slot >= rows
    within = jnp.where(second, slot - rows, slot)
    token = jnp.where(second, within + tokens_here, within).astype(jnp.float32)
    return jnp.where(jnp.logical_and(within < tokens_here, token < count), 0.0, -1e30)


def front_kernel(layers, head_size, grid_side, *refs):
    (
        vec_own, qkv_own, out_own, gate_own, down_own, tokens, valid, hidden_own,
        vec_full, qkv_full, out_full, gate_full, down_full, hidden_full,
        x_out, n_out, q_out, k_out, v_out, o_out, stat_out, vec_out, count_out, cos, sin,
        x, valid_both, vec, weight, hat, normed, q, keys, values, bias,
        send_sem, recv_sem, local_sem,
    ) = refs
    f32, bf16 = jnp.float32, jnp.bfloat16
    place = place_of()
    z, k, me_x, y = place
    greet(layers, place, (SWAP,))
    links = Links(place, send_sem, recv_sem)
    rows, width = x.shape
    tokens_here = valid.shape[1] // 2
    tile = weight.shape[2]
    quarter = head_size // 4
    lanes = 2 * head_size
    locals_used = [0]

    def local_at():
        locals_used[0] += 1
        return local_sem.at[locals_used[0] - 1]

    block = Swap(links, tokens.at[y], x, local_at())
    valid_swap = Swap(links, valid, valid_both, local_at())
    cross = Cross(links, hidden_own, hidden_full, local_at())
    out_rows, down_rows = out_own.shape[0], down_own.shape[0] // 2
    todo = [
        (ROW, vec_own, vec_full, 0, vec_own.shape[0], 0),
        (ROW, qkv_own.at[0], qkv_full.at[0], 0, 128, 64),
        (ROW, qkv_own.at[1], qkv_full.at[1], 0, 128, 64),
        (ROW, qkv_own.at[2], qkv_full.at[2], 0, 128, 64),
        (ROW, gate_own.at[0], gate_full.at[0], 0, 64, 32),
        (ROW, gate_own.at[0], gate_full.at[0], 64, 64, 32),
        (ROW, gate_own.at[1], gate_full.at[1], 0, 64, 32),
        (ROW, gate_own.at[1], gate_full.at[1], 64, 64, 32),
        (COL, down_own, down_full, 0, down_rows, down_rows // 2),
        (COL, down_own, down_full, down_rows, down_rows, down_rows // 2),
        (COL, out_own, out_full, 0, out_rows, out_rows // 2),
    ]
    starts = (0, 1, 2, 3, 4, 5, 6, 7, 8, 9, 10)
    begins = (0, 0, 1, 2, 3, 4, 5, 6, 7, 8, 9)
    jobs = [
        Gather(layers, links, kind, own, full, low, size, split, local_at())
        for kind, own, full, low, size, split in todo
    ]
    ticks = ticks_of(links, jobs, starts, begins)
    weight_loads = []
    for mat in range(3):
        for part in range(width // tile):
            slot = len(weight_loads) % 2
            weight_loads.append(
                pltpu.make_async_copy(
                    qkv_full.at[mat, :, pl.ds(part * tile, tile)], weight.at[slot], local_at()
                )
            )
    vec_load = pltpu.make_async_copy(vec_full, vec, local_at())
    keeps = [
        pltpu.make_async_copy(source, target, local_at())
        for source, target in ((x, x_out), (normed, n_out), (q, q_out), (keys, k_out), (values, v_out))
    ]
    shares = []
    my_rows = pl.ds(pl.multiple_of(k * rows, 16), rows)
    other_rows = pl.ds(pl.multiple_of((1 - k) * rows, 16), rows)
    for store in (keys, values):
        for part in range(width // tile):
            at = links.take(1)
            cols = pl.ds(part * tile, tile)
            out_going = links.copy(CORE, at, store.at[my_rows, cols], store.at[my_rows, cols])
            coming = links.copy(CORE, at, store.at[other_rows, cols], store.at[other_rows, cols])
            shares.append((out_going, coming))

    block.begin()
    valid_swap.begin()
    run(ticks[0])
    cross.begin()
    run(ticks[1])

    block.arrived()
    valid_swap.arrived()
    keeps[0].start()
    chunk = rows // 3

    def normalise(i, nothing):
        at = pl.ds(pl.multiple_of(i * chunk, 16), chunk)
        value, spread = standardize(x[at, :].astype(f32))
        hat[at, :] = value
        return nothing

    lax.fori_loop(0, 3, normalise, 0)
    flags = jnp.where(y == 0, valid_both[0:1, :], valid_both[1:2, :]).astype(f32)
    count = jnp.sum(flags, axis=1, keepdims=True)
    count_out[...] = jnp.broadcast_to(count, count_out.shape)
    columns = (count - 1.0) * (1.0 / grid_side)
    token = lax.broadcasted_iota(jnp.int32, (rows, lanes), 0).astype(f32)
    token = token + (k * tokens_here).astype(f32)
    lane = lax.broadcasted_iota(jnp.int32, (rows, lanes), 1)
    live = jnp.logical_and(token >= 1.0, token < count)
    row_id = jnp.floor((token - 0.5) / columns)
    col_id = token - 1.0 - row_id * columns
    where_at = jnp.where(lax.rem(lane, head_size) < 2 * quarter, row_id, col_id)
    where_at = jnp.where(live, where_at, 0.0)
    power = lax.rem(lane, quarter).astype(f32) * (-math.log(10000.0) / quarter)
    angle = where_at * jnp.exp(power)
    cos[...] = jnp.cos(angle)
    sin[...] = jnp.sin(angle)
    bias[...] = slot_bias(bias.shape, 1, rows, tokens_here, count)

    for tick in ticks[2:8]:
        run(tick)
    jobs[0].arrived()
    vec_load.start()
    vec_load.wait()
    piece_rows = vec_own.shape[0]
    summed = vec[0:piece_rows, :].astype(f32)
    for s in range(1, 2 * layers):
        summed = summed + vec[s * piece_rows : (s + 1) * piece_rows, :].astype(f32)
    vec_out[...] = summed

    def scale(i, nothing):
        at = pl.ds(pl.multiple_of(i * chunk, 16), chunk)
        normed[at, :] = (hat[at, :] * vec_out[4:5, :] + vec_out[6:7, :]).astype(bf16)
        return nothing

    lax.fori_loop(0, 3, scale, 0)
    keeps[1].start()
    repeat = tile // lanes
    per = width // tile
    for mat in range(3):
        run(ticks[8 + mat])
        jobs[1 + mat].arrived()
        for part in range(per):
            weight_loads[mat * per + part].start()
        for part in range(per):
            load = weight_loads[mat * per + part]
            load.wait()
            cols = pl.ds(part * tile, tile)
            raw = dot(normed[...], weight[(mat * per + part) % 2])
            if mat != 1:
                raw = raw + vec_out[0 if mat == 0 else 1 : 1 if mat == 0 else 2, cols]
            if mat < 2:
                turned = turn_lanes(raw, quarter)
                wide_cos = jnp.concatenate([cos[...]] * repeat, axis=1)
                wide_sin = jnp.concatenate([sin[...]] * repeat, axis=1)
                raw = raw * wide_cos + turned * wide_sin
            if mat == 0:
                q[:, cols] = raw.astype(bf16)
            else:
                (keys if mat == 1 else values)[my_rows, cols] = raw.astype(bf16)
                shares[(mat - 1) * per + part][0].start()
    keeps[2].start()
    for out_going, coming in shares:
        out_going.wait_send()
        coming.wait_recv()
    keeps[3].start()
    keeps[4].start()

    late = ticks[11:]
    score_scale = LOG2_E / math.sqrt(head_size)
    pairs = width // lanes

    def mix(i, nothing):
        for number, tick in enumerate(late):
            pl.when(i == number)(functools.partial(run, tick))
        cols = pl.ds(pl.multiple_of(i * lanes, lanes), lanes)
        queries, near_keys, near_values = q[:, cols], keys[:, cols], values[:, cols]
        parts = []
        for head in range(2):
            s = dot_last(only_head(queries, head, head_size), near_keys) * score_scale + bias[...]
            top = jnp.max(s, axis=1, keepdims=True)
            e = jnp.exp2(s - top)
            total = jnp.sum(e, axis=1, keepdims=True)
            parts.append(dot(e.astype(bf16), near_values) * (1.0 / total))
            level = jnp.broadcast_to(top + jnp.log2(total), (rows, 128))
            stat_out[i, head : head + 1, :] = jnp.transpose(level)[0:1, :]
        o_out[:, cols] = jnp.where(pair_lanes((rows, lanes), head_size), parts[0], parts[1])
        return nothing

    lax.fori_loop(0, pairs, mix, 0)
    for tick in late[8:]:
        run(tick)
    for job in jobs[4:]:
        job.arrived()
    cross.arrived()
    for keep in keeps:
        keep.wait()
    links.finish()


def front(layers, number, head_size, grid_side, vec, qkv, out, gate, down, tokens, valid, hidden):
    bf16, f32 = jnp.bfloat16, jnp.float32
    rows, width = tokens.shape[1:]
    pairs = width // (2 * head_size)
    tile = 512
    fulls = [
        full_shape(layers, kind, piece.shape)
        for kind, piece in ((ROW, vec), (ROW, qkv), (COL, out), (ROW, gate), (COL, down))
    ]
    shapes = [jax.ShapeDtypeStruct(shape, bf16) for shape in fulls]
    shapes += [jax.ShapeDtypeStruct((2,) + hidden.shape, bf16)]
    shapes += [jax.ShapeDtypeStruct((n * rows, width), bf16) for n in (1, 1, 1, 2, 2)]
    shapes += [
        jax.ShapeDtypeStruct((rows, width), f32),
        jax.ShapeDtypeStruct((pairs, 2, rows), f32),
        jax.ShapeDtypeStruct((vec.shape[0], width), f32),
        jax.ShapeDtypeStruct((8, 128), f32),
        jax.ShapeDtypeStruct((rows, 2 * head_size), f32),
        jax.ShapeDtypeStruct((rows, 2 * head_size), f32),
    ]
    sems = 11 * Gather.sem_count(layers) + 7
    return pl.pallas_call(
        functools.partial(front_kernel, layers, head_size, grid_side),
        out_shape=shapes,
        in_specs=[ANY] * 8,
        out_specs=[ANY] * 11 + [IN_VMEM] * 6,
        scratch_shapes=[
            pltpu.VMEM((rows, width), bf16),
            pltpu.VMEM(valid.shape, valid.dtype),
            pltpu.VMEM(fulls[0], bf16),
            pltpu.VMEM((2, width, tile), bf16),
            pltpu.VMEM((rows, width), f32),
            pltpu.VMEM((rows, width), bf16),
            pltpu.VMEM((rows, width), bf16),
            pltpu.VMEM((2 * rows, width), bf16),
            pltpu.VMEM((2 * rows, width), bf16),
            pltpu.VMEM((1, 2 * rows), f32),
            pltpu.SemaphoreType.DMA((sems,)),
            pltpu.SemaphoreType.DMA((sems,)),
            pltpu.SemaphoreType.DMA((32,)),
        ],
        compiler_params=pltpu.CompilerParams(
            collective_id=number, has_side_effects=True, vmem_limit_bytes=LIMIT
        ),
    )(vec, qkv, out, gate, down, tokens, valid, hidden)


def back_kernel(layers, head_size, tokens_here, jobs, late_jobs, mats, *refs):
    grads, refs = refs[:mats], refs[mats:]
    given_arrays, refs = refs[:9], refs[9:]
    q_in, keys_in, values_in, do_in, mixed_in, n_in, x_in, resid_in, weights = given_arrays
    stats, count, cos, sin, vec, total_in = refs[:6]
    outs, refs = refs[6 : 6 + mats], refs[6 + mats :]
    late_outs, total_out, tokens_out, late_grads = refs[:3], refs[3], refs[4], refs[5:8]
    scratch, refs = refs[8 : 8 + 6 * len(jobs)], refs[8 + 6 * len(jobs) :]
    (
        q, keys, values, do, mixed, k_sum, v_sum, dq_low, dk_low, dv_low, normed_t, d_first,
        d_tokens, bias, total, boxes, layer_boxes, send_sem, recv_sem, local_sem, ready,
    ) = refs
    f32, bf16 = jnp.float32, jnp.bfloat16
    place = place_of()
    z, k, x, y = place
    greet(layers, place, (SWAP, FAR))
    links = Links(place, send_sem, recv_sem)
    first_jobs = reduce_jobs(layers, links, jobs, grads, outs, scratch, local_sem)
    locals_used = [len(jobs) * 2 * layers]

    def local_at():
        locals_used[0] += 1
        return local_sem.at[locals_used[0] - 1]

    second_jobs = []
    for mat, low, rows_here, split, host, first_col in late_jobs:
        cols_here = pl.ds(first_col, late_outs[mat].shape[-1])
        own = []
        for ref in scratch[6 * host : 6 * host + 6]:
            own.append(ref.at[(slice(None),) * (len(ref.shape) - 1) + (cols_here,)])
        second_jobs.append(
            Reduce(
                layers, links, ROW, late_grads[mat], late_outs[mat], low, split, own,
                local_sem, locals_used[0],
            )
        )
        locals_used[0] += 2 * layers
    sums = Total(layers, links, total, total_out, boxes, layer_boxes)
    early, n_late = len(jobs), len(second_jobs)
    handover = early + 5
    late_starts = [handover + number // 2 for number in range(n_late)]
    starts = list(range(early)) + late_starts + [handover + 3]
    begins = [max(0, number - 1) for number in range(early)] + late_starts + [handover + 3]
    ticks = ticks_of(links, first_jobs + second_jobs + [sums], starts, begins)
    spread = Spread(links, d_tokens, tokens_out, local_at())

    rows, width = q.shape
    lanes = 2 * head_size
    pairs = width // lanes
    scale = 1.0 / math.sqrt(head_size)
    quarter = head_size // 4
    my_rows = pl.ds(pl.multiple_of(k * rows, 16), rows)
    other_rows = pl.ds(pl.multiple_of((1 - k) * rows, 16), rows)
    first = links.take(2 * pairs)

    def share(i):
        cols = pl.ds(pl.multiple_of(i * lanes, lanes), lanes)
        return (
            links.copy(CORE, first + 2 * i, k_sum.at[other_rows, cols], dk_low.at[:, cols]),
            links.copy(CORE, first + 2 * i + 1, v_sum.at[other_rows, cols], dv_low.at[:, cols]),
        )

    def turn_back(grad):
        return grad * cos[...] - turn_lanes(grad, quarter) * sin[...]

    def load(source, target):
        copy = pltpu.make_async_copy(source, target, local_at())
        copy.start()
        return copy

    run(ticks[0])
    loads = [
        load(source, target)
        for source, target in (
            (q_in, q), (keys_in, keys), (values_in, values), (do_in, do), (mixed_in, mixed)
        )
    ]
    bias[...] = slot_bias(bias.shape, 0, rows, tokens_here, count[0:1, 0:1])
    total[...] = total_in[...]
    run(ticks[1])
    for copy in loads:
        copy.wait()
    beside = ticks[2 : 2 + pairs]

    def step(i, nothing):
        for number, tick in enumerate(beside):
            pl.when(i == number)(functools.partial(run, tick))
        cols = pl.ds(pl.multiple_of(i * lanes, lanes), lanes)
        queries, near_keys, near_values, grad = q[:, cols], keys[:, cols], values[:, cols], do[:, cols]
        products = jnp.transpose(grad.astype(f32) * mixed[:, cols])
        found = []
        for head in range(2):
            row_dot = products[head * head_size : (head + 1) * head_size]
            row_dot = jnp.sum(row_dot, axis=0, keepdims=True)
            s = dot_last(near_keys, only_head(queries, head, head_size)) * (scale * LOG2_E)
            p = jnp.exp2(s + bias[...] - stats[i, head : head + 1, :])
            dp = dot_last(near_values, only_head(grad, head, head_size))
            ds = (p * (dp - row_dot)).astype(bf16)
            found.append(
                (dot_first(near_keys, ds) * scale, dot(ds, queries) * scale, dot(p.astype(bf16), grad))
            )
        dq = jnp.concatenate([found[0][0][:head_size], found[1][0][head_size:]], axis=0)
        dq = turn_back(jnp.transpose(dq)).astype(bf16)
        dq_low[:, cols] = dq
        total[pl.ds(i, 1), :] = jnp.sum(dq.astype(f32), axis=0, keepdims=True)
        in_first = pair_lanes((2 * rows, lanes), head_size)
        k_sum[:, cols] = jnp.where(in_first, found[0][1], found[1][1]).astype(bf16)
        v_sum[:, cols] = jnp.where(in_first, found[0][2], found[1][2]).astype(bf16)
        for copy in share(i):
            copy.start()
        return nothing

    lax.fori_loop(0, pairs, step, 0)
    normed_load = load(n_in, q)
    loads = [load(weights.at[0], keys.at[pl.ds(0, width)]), load(weights.at[1], values.at[pl.ds(0, width)])]
    loads += [load(x_in, do), load(resid_in, mixed)]
    at_tick = [2 + pairs]

    def advance():
        run(ticks[at_tick[0]])
        at_tick[0] += 1

    def join(i, nothing):
        cols = pl.ds(pl.multiple_of(i * lanes, lanes), lanes)
        for copy in share(i):
            copy.wait()
        dk = k_sum[my_rows, cols].astype(f32) + dk_low[:, cols].astype(f32)
        dk_low[:, cols] = turn_back(dk).astype(bf16)
        dv = v_sum[my_rows, cols].astype(f32) + dv_low[:, cols].astype(f32)
        dv = dv.astype(bf16)
        dv_low[:, cols] = dv
        total[pl.ds(pairs + i, 1), :] = jnp.sum(dv.astype(f32), axis=0, keepdims=True)
        return nothing

    advance()
    lax.fori_loop(0, pairs, join, 0)
    normed_load.wait()
    last_weight = load(weights.at[2], k_sum.at[pl.ds(0, width)])

    def flip(i, nothing):
        at = pl.ds(pl.multiple_of(i * lanes, lanes), lanes)
        normed_t[at, :] = jnp.transpose(q[:, at])
        return nothing

    lax.fori_loop(0, width // lanes, flip, 0)
    while at_tick[0] < handover:
        advance()
    tile = 256
    stores = []

    def weight_grad(mat):
        low_grad = (dq_low, dk_low, dv_low)[mat]
        def part(i, nothing):
            at = pl.ds(pl.multiple_of(i * tile, tile), tile)
            v_sum[at, :] = dot(normed_t[at, :], low_grad[...]).astype(bf16)
            return nothing

        lax.fori_loop(0, width // tile, part, 0)
        stores.append(load(v_sum.at[pl.ds(0, width)], late_grads[mat]))

    weight_grad(0)
    for job in first_jobs[:4]:
        job.finish()
    near = [(None, CORE), (None, ACROSS), (None, BESIDE), (z > 0, DOWN), (z < layers - 1, UP)]
    for condition, way in near:

        def hello(way=way):
            pl.semaphore_signal(
                ready, inc=1, device_id=device(place, way), device_id_type=MESH
            )

        when(condition, hello)
    expected = 3 + jnp.where(z > 0, 1, 0) + jnp.where(z < layers - 1, 1, 0)
    pl.semaphore_wait(ready, expected)
    stores[-1].wait()
    advance()
    for mat in (1, 2):
        weight_grad(mat)
        stores[-1].wait()
        advance()
    for copy in loads + [last_weight]:
        copy.wait()

    def project_back(i, nothing):
        at = pl.ds(pl.multiple_of(i * tile, tile), tile)
        result = dot_last(dq_low[...], keys[at, :])
        result = result + dot_last(dk_low[...], values[at, :])
        d_first[:, at] = result + dot_last(dv_low[...], k_sum[at, :])
        return nothing

    lax.fori_loop(0, width // tile, project_back, 0)
    chunk = rows // 3
    gain = vec[4:5, :]
    gain_sum = jnp.zeros((1, width), f32)
    bias_sum = jnp.zeros((1, width), f32)
    for number in range(3):
        at = pl.ds(number * chunk, chunk)
        hat, inverse = standardize(do[at, :].astype(f32))
        dn = d_first[at, :]
        d_tokens[at, :] = (mixed[at, :] + norm_back(dn * gain, hat, inverse)).astype(bf16)
        gain_sum = gain_sum + jnp.sum(dn * hat, axis=0, keepdims=True)
        bias_sum = bias_sum + jnp.sum(dn, axis=0, keepdims=True)
    for i in range(width // 128):
        cols = slice(i * 128, (i + 1) * 128)
        at = 4 * width // 128 + i
        total[at : at + 1, :] = gain_sum[:, cols]
        at = 6 * width // 128 + i
        total[at : at + 1, :] = bias_sum[:, cols]
    spread.begin()
    while at_tick[0] < len(ticks):
        advance()
    spread.arrived()
    for job in first_jobs[4:] + second_jobs:
        job.finish()
    links.finish()


def back(layers, number, head_size, tokens_here, jobs, late_jobs, grads, given, small, total):
    bf16, f32 = jnp.bfloat16, jnp.float32
    pieces = [piece_shape(layers, kind, g.shape) for kind, g in grads]
    rows, width = given[0].shape
    pairs = width // (2 * head_size)
    sems = (len(jobs) + len(late_jobs)) * Reduce.sem_count(layers) + 2 * pairs
    sems += Total.sem_count(layers) + 2
    late_piece = (width // (2 * layers), width // 2)
    scratch = []
    for mat, kind, low, job_rows, split in jobs:
        shapes = reduce_shapes(layers, job_rows, pieces[mat][-1], split)
        scratch += [pltpu.VMEM(shape, bf16) for shape in shapes]
    half, whole = (rows, width), (2 * rows, width)
    buffers = [(half, bf16), (whole, bf16), (whole, bf16), (half, bf16), (half, f32)]
    buffers += [(whole, bf16)] * 2 + [(half, bf16)] * 3 + [((width, rows), bf16), (half, f32)]
    buffers += [(half, bf16), ((2 * rows, 1), f32), (total.shape, f32)]
    buffers += [((5,) + total.shape, f32), ((layers,) + total.shape, f32)]
    return pl.pallas_call(
        functools.partial(
            back_kernel, layers, head_size, tokens_here, jobs, late_jobs, len(grads)
        ),
        out_shape=[jax.ShapeDtypeStruct(piece, f32) for piece in pieces]
        + [jax.ShapeDtypeStruct(late_piece, f32)] * 3
        + [jax.ShapeDtypeStruct(total.shape, f32)]
        + [jax.ShapeDtypeStruct((2, rows, width), bf16)]
        + [jax.ShapeDtypeStruct((width, width), bf16)] * 3,
        in_specs=[ANY] * (len(grads) + len(given)) + [IN_VMEM] * (len(small) + 1),
        out_specs=[IN_VMEM] * (len(pieces) + 4) + [ANY] * 4,
        scratch_shapes=scratch
        + [pltpu.VMEM(shape, dtype) for shape, dtype in buffers]
        + [
            pltpu.SemaphoreType.DMA((sems,)),
            pltpu.SemaphoreType.DMA((sems,)),
            pltpu.SemaphoreType.DMA(((len(jobs) + len(late_jobs)) * 2 * layers + 16,)),
            pltpu.SemaphoreType.REGULAR,
        ],
        compiler_params=pltpu.CompilerParams(
            collective_id=number, has_side_effects=True, vmem_limit_bytes=62 * 1024 * 1024
        ),
    )(*[g for kind, g in grads], *given, *small, total)


def pad_to(values, axis, size):
    pads = [(0, 0)] * values.ndim
    pads[axis] = (0, size - values.shape[axis])
    return jnp.pad(values, pads)


def round_up(size, step):
    return (size + step - 1) // step * step


def image_per_chip(
    layers,
    tokens,
    cotangent,
    valid_tokens,
    places,
    qkv_weight,
    head_biases,
    head_gain,
    out_weight,
    norm_gains,
    width_biases,
    gate_up,
    hidden_biases,
    hidden_gain,
    down_weight,
):
    f32 = jnp.float32
    bf16 = jnp.bfloat16
    z, k, x, y = place_of()
    s = 2 * z + k
    shards = 2 * layers
    width = tokens.shape[2]
    rows = tokens.shape[1]
    heads_here = head_gain.shape[0]
    heads = 2 * heads_here
    dims_here = head_gain.shape[1]
    head_size = dims_here * shards
    real_here = hidden_gain.shape[0]
    hidden_here = round_up(real_here, 128)
    real = 2 * real_here
    hidden_size = 2 * hidden_here
    score_scale = 1.0 / math.sqrt(head_size)

    padded = round_up(rows, 16)
    heads_own = jnp.concatenate([head_biases, head_gain[None]], axis=0)
    spot = jnp.zeros((4, heads_here, head_size), bf16)
    spot = lax.dynamic_update_slice(spot, heads_own, (0, 0, s * dims_here)).reshape(4, -1)
    width_own = jnp.concatenate([norm_gains, width_biases], axis=0)
    lane_at = s * width_own.shape[1] - y * spot.shape[1]
    inside = both(lane_at >= 0, lane_at < spot.shape[1])
    width_own = jnp.where(inside, width_own, jnp.zeros_like(width_own))
    at = jnp.where(inside, lane_at, 0)
    lanes_own = lax.dynamic_update_slice(jnp.zeros((6, spot.shape[1]), bf16), width_own, (0, at))
    vectors = pad_to(jnp.concatenate([spot, lanes_own], axis=0), 0, 16)
    hidden_vectors = jnp.concatenate([hidden_biases, hidden_gain[None]], axis=0)
    hidden_vectors = pad_to(pad_to(hidden_vectors, 1, hidden_here), 0, 16)
    gate_pad = pad_to(gate_up, 2, hidden_here)
    down_pad = pad_to(down_weight, 0, hidden_here)
    swaps = []
    for layer in range(layers):
        swaps += [(4 * layer + 1, 4 * layer + 2), (4 * layer + 2, 4 * layer + 1)]
    (
        vec_full, qkv_full, out_full, gate_full, down_full, hidden_full,
        token_block, first_in, queries, keys, values, mixed, stats, vec, count, cos, sin,
    ) = front(
        layers, 0, head_size, 32, vectors, qkv_weight, out_weight, gate_pad, down_pad,
        pad_to(tokens, 1, padded), valid_tokens, hidden_vectors,
    )
    cotangent, token_block = lax.optimization_barrier((cotangent, token_block))
    cot_own = lax.dynamic_index_in_dim(cotangent, y, 0, keepdims=False)
    cot_own = pad_to(cot_own, 0, padded)
    cot_other = lax.ppermute(cot_own, (SHARD, CTX), swaps)
    cot_block = jnp.where(k == x, cot_own, cot_other)
    head_part, norm_scale, width_bias = vec[0:4], vec[4:6], vec[6:10]
    hidden_part = jnp.concatenate([hidden_full[0, :4], hidden_full[1, :4]], axis=1).astype(f32)
    token_rows = token_block.astype(f32)
    cot_rows = cot_block.astype(f32)
    mix_hat, spread_mix = standardize(mixed)
    mix_in = (mix_hat * head_part[3] + head_part[2]).astype(bf16)
    branch = jnp.dot(mix_in, out_full, preferred_element_type=f32)
    resid = token_rows + (branch + width_bias[2])
    normed_two, spread_two = standardize(resid)
    second_in = (normed_two * norm_scale[1] + width_bias[1]).astype(bf16)
    gate_pre = jnp.dot(second_in, gate_full[0], preferred_element_type=f32) + hidden_part[0]
    up_pre = jnp.dot(second_in, gate_full[1], preferred_element_type=f32) + hidden_part[1]
    sigmoid_gate = jax.nn.sigmoid(gate_pre)
    silu_gate = gate_pre * sigmoid_gate
    hidden = silu_gate * up_pre
    hidden_mean = jnp.sum(hidden, axis=-1, keepdims=True) / real
    centred = hidden - hidden_mean
    extra = (hidden_size - real) * hidden_mean * hidden_mean
    hidden_var = (jnp.sum(centred * centred, axis=-1, keepdims=True) - extra) / real
    spread_hid = lax.rsqrt(jnp.maximum(hidden_var, 0.0) + EPS)
    hidden_hat = centred * spread_hid
    down_in = (hidden_hat * hidden_part[3] + hidden_part[2]).astype(bf16)
    ffn_out = jnp.dot(down_in, down_full, preferred_element_type=f32)
    result = (resid + (ffn_out + width_bias[3])).astype(bf16)[:rows]
    result = jnp.where(k == x, result, lax.ppermute(result, (SHARD, CTX), swaps))
    result_other = lax.ppermute(result, TP, [(0, 1), (1, 0)])
    result = jnp.where(y == 0, jnp.stack([result, result_other]), jnp.stack([result_other, result]))

    g_down = jnp.einsum("tf,td->fd", down_in, cot_block, preferred_element_type=f32)
    d_down_in = jnp.einsum("td,fd->tf", cot_block, down_full, preferred_element_type=f32)
    grad_hid = d_down_in * hidden_part[3]
    hid_back_one = jnp.sum(grad_hid, axis=-1, keepdims=True) / real
    hid_back_two = jnp.sum(grad_hid * hidden_hat, axis=-1, keepdims=True) / real
    d_hidden = (grad_hid - hid_back_one - hidden_hat * hid_back_two) * spread_hid
    d_gate = (d_hidden * up_pre * sigmoid_gate * (1.0 + gate_pre * (1.0 - sigmoid_gate))).astype(
        bf16
    )
    d_up = (d_hidden * silu_gate).astype(bf16)
    g_gate = jnp.einsum("td,tf->df", second_in, d_gate, preferred_element_type=f32).astype(bf16)
    g_up = jnp.einsum("td,tf->df", second_in, d_up, preferred_element_type=f32).astype(bf16)
    d_second = jnp.einsum("tf,df->td", d_gate, gate_full[0], preferred_element_type=f32)
    d_second = d_second + jnp.einsum("tf,df->td", d_up, gate_full[1], preferred_element_type=f32)
    d_resid = cot_rows + norm_back(d_second * norm_scale[1], normed_two, spread_two)
    d_branch_low = d_resid.astype(bf16)
    g_out = jnp.einsum("tm,tn->mn", mix_in, d_branch_low, preferred_element_type=f32)
    d_mix_in = jnp.einsum("tn,mn->tm", d_branch_low, out_full, preferred_element_type=f32)
    d_mixed = norm_back(d_mix_in * head_part[3], mix_hat, spread_mix).astype(bf16)
    vector_grads = jnp.concatenate(
        [
            jnp.zeros((width,), f32),
            jnp.zeros((width,), f32),
            column_sum(d_mix_in),
            column_sum(d_mix_in * mix_hat),
            jnp.zeros((width,), f32),
            column_sum(d_second * normed_two),
            jnp.zeros((width,), f32),
            column_sum(d_second),
            column_sum(d_branch_low),
            column_sum(cot_block),
            column_sum(d_gate),
            column_sum(d_up),
            column_sum(d_down_in),
            column_sum(d_down_in * hidden_hat),
        ]
    ).reshape(-1, 128)
    vector_grads = pad_to(vector_grads, 0, round_up(vector_grads.shape[0], 16))
    half = hidden_here // 2
    heads_rows = heads_here * head_size
    grad_jobs = (
        (0, ROW, 0, 64, 32), (0, ROW, 64, 64, 32), (1, ROW, 0, 64, 32), (1, ROW, 64, 64, 32),
        (2, COL, 0, half, half // 2), (2, COL, half, half, half // 2),
        (3, COL, 0, heads_rows, heads_rows // 2),
    )
    late_jobs = (
        (0, 0, 64, 32, 0, 0), (0, 64, 64, 32, 1, 0),
        (1, 0, 64, 32, 0, heads_rows), (1, 64, 64, 32, 1, heads_rows),
        (2, 0, 64, 32, 2, 0), (2, 64, 64, 32, 3, 0),
    )
    back_grads = (
        (ROW, g_gate), (ROW, g_up), (COL, g_down.astype(bf16)), (COL, g_out.astype(bf16))
    )
    (
        gate_piece, up_piece, down_piece, out_piece, query_piece, key_piece, value_piece,
        vector_grads, d_tokens, *unused,
    ) = back(
        layers, 1, head_size, rows, grad_jobs, late_jobs, back_grads,
        (queries, keys, values, d_mixed, mixed, first_in, token_block, d_resid, qkv_full),
        (stats, count, cos, sin, vec), vector_grads,
    )
    d_tokens = d_tokens[:, :rows]
    vector_grads = vector_grads.reshape(-1)
    head_sums = vector_grads[: 4 * width].reshape(4, heads, head_size)
    head_sums = lax.dynamic_slice(
        head_sums, (0, y * heads_here, s * dims_here), (4, heads_here, dims_here)
    )
    width_sums = vector_grads[4 * width : 10 * width].reshape(6, width)
    width_sums = lax.dynamic_slice(width_sums, (0, s * 128), (6, width // shards))
    hidden_sums = vector_grads[10 * width : 10 * width + 4 * hidden_size]
    hidden_sums = hidden_sums.reshape(4, hidden_size)
    hidden_sums = lax.dynamic_slice(hidden_sums, (0, y * hidden_here), (4, hidden_here))
    hidden_sums = hidden_sums[:, :real_here]

    return (
        result,
        d_tokens.astype(f32),
        jnp.stack([query_piece, key_piece, value_piece]),
        head_sums[:3],
        head_sums[3],
        out_piece,
        width_sums[:2],
        width_sums[2:],
        jnp.stack([gate_piece[:, :real_here], up_piece[:, :real_here]]),
        hidden_sums[:3],
        hidden_sums[3],
        down_piece[:real_here],
    )


def solution(mesh):
    small = mesh.shape[CTX] == 2 and mesh.shape[TP] == 2
    body = functools.partial(image_per_chip, mesh.shape[SHARD] // 2) if small else general_plan

    return jax.shard_map(
        body,
        mesh=mesh,
        in_specs=(
            P(SHARD, CTX, None),
            P(SHARD, CTX, None),
            P(SHARD, None),
            P(None, SHARD, CTX),
            P(None, SHARD, TP),
            P(None, TP, SHARD),
            P(TP, SHARD),
            P(TP, SHARD),
            P(None, SHARD),
            P(None, SHARD),
            P(None, SHARD, TP),
            P(None, TP),
            P(TP),
            P(TP, SHARD),
        ),
        out_specs=(
            P(SHARD, CTX, None),
            P(SHARD, CTX, None),
            P(None, SHARD, TP),
            P(None, TP, SHARD),
            P(TP, SHARD),
            P(TP, SHARD),
            P(None, SHARD),
            P(None, SHARD),
            P(None, SHARD, TP),
            P(None, TP),
            P(TP),
            P(TP, SHARD),
        ),
        check_vma=False,
    )
```

```python
import functools
import math

import jax
import jax.numpy as jnp
from jax import lax
from jax.experimental import pallas as pl
from jax.experimental.pallas import tpu as pltpu
from jax.sharding import PartitionSpec as P

SHARD, CTX, TP = "shard", "ctx", "tp"


EPS = 1e-06


def standardize(values):
    average = jnp.mean(values, axis=-1, keepdims=True)
    centred = values - average
    spread = lax.rsqrt(jnp.mean(centred * centred, axis=-1, keepdims=True) + EPS)
    return (centred * spread, spread)


def norm_back(grad_hat, normed, spread):
    mean_one = jnp.mean(grad_hat, axis=-1, keepdims=True)
    mean_two = jnp.mean(grad_hat * normed, axis=-1, keepdims=True)
    return (grad_hat - mean_one - normed * mean_two) * spread


def angle_table(row_ids, col_ids, head_size):
    quarter = head_size // 4
    frequency = 10000.0 ** (-jnp.arange(quarter, dtype=jnp.float32) / quarter)
    row_part = row_ids.astype(jnp.float32)[:, None] * frequency[None, :]
    col_part = col_ids.astype(jnp.float32)[:, None] * frequency[None, :]
    return jnp.concatenate([row_part, row_part, col_part, col_part], axis=1)


def turn_half(values):
    quarter = values.shape[-1] // 4
    part_one = values[..., :quarter]
    part_two = values[..., quarter : 2 * quarter]
    part_three = values[..., 2 * quarter : 3 * quarter]
    part_four = values[..., 3 * quarter :]
    return jnp.concatenate([-part_two, part_one, -part_four, part_three], axis=-1)


def rotate(values, angles):
    return values * jnp.cos(angles)[None, :, :] + turn_half(values) * jnp.sin(angles)[None, :, :]


def unrotate(values, angles):
    return values * jnp.cos(angles)[None, :, :] - turn_half(values) * jnp.sin(angles)[None, :, :]


def head_major(values, heads, head_size):
    return values.reshape(values.shape[0], heads, head_size).transpose(1, 0, 2)


def column_sum(values):
    return jnp.sum(values.astype(jnp.float32), axis=0)


def general_plan(
    tokens,
    cotangent,
    valid_tokens,
    places,
    qkv_weight,
    head_biases,
    head_gain,
    out_weight,
    norm_gains,
    width_biases,
    gate_up,
    hidden_biases,
    hidden_gain,
    down_weight,
):
    micro = tokens.shape[0]
    width = tokens.shape[2]
    local_dim = qkv_weight.shape[2]
    local_heads = head_biases.shape[1]
    head_size = local_dim // local_heads
    local_hidden = hidden_gain.shape[0]
    FF = local_hidden * lax.axis_size(TP)
    score_scale = 1.0 / math.sqrt(head_size)
    f32 = jnp.float32
    bf16 = jnp.bfloat16

    def one_batch(batch_idx, carried):
        gathered = (
            lax.all_gather(qkv_weight, SHARD, axis=1, tiled=True),
            lax.all_gather(head_biases, SHARD, axis=2, tiled=True),
            lax.all_gather(head_gain, SHARD, axis=1, tiled=True),
            lax.all_gather(out_weight, SHARD, axis=1, tiled=True),
            lax.all_gather(norm_gains, SHARD, axis=1, tiled=True),
            lax.all_gather(width_biases, SHARD, axis=1, tiled=True),
            lax.all_gather(gate_up, SHARD, axis=1, tiled=True),
            lax.all_gather(down_weight, SHARD, axis=1, tiled=True),
        )
        qkv_full, head_bias, head_scale, out_full, norm_scale, width_bias, gate_full, down_full = (
            gathered
        )
        head_bias_f = head_bias.astype(f32)
        head_scale_f = head_scale.astype(f32)[:, None, :]
        norm_scale = norm_scale.astype(f32)
        width_bias = width_bias.astype(f32)
        hidden_bias = hidden_biases.astype(f32)
        hidden_scale = hidden_gain.astype(f32)
        out_heads = out_full.reshape(local_heads, head_size, width)
        token_rows = lax.dynamic_index_in_dim(tokens, batch_idx, 0, keepdims=False).astype(f32)
        cot_rows = lax.dynamic_index_in_dim(cotangent, batch_idx, 0, keepdims=False).astype(f32)
        valid_row = lax.dynamic_index_in_dim(valid_tokens, batch_idx, 0, keepdims=False) > 0
        row_ids = lax.dynamic_index_in_dim(places[0], batch_idx, 0, keepdims=False)
        col_ids = lax.dynamic_index_in_dim(places[1], batch_idx, 0, keepdims=False)
        angles = angle_table(row_ids, col_ids, head_size)
        normed_one, spread_one = standardize(token_rows)
        first_in = (normed_one * norm_scale[0] + width_bias[0]).astype(bf16)
        query_flat = jnp.dot(first_in, qkv_full[0], preferred_element_type=f32)
        key_flat = jnp.dot(first_in, qkv_full[1], preferred_element_type=f32)
        value_flat = jnp.dot(first_in, qkv_full[2], preferred_element_type=f32)
        query_pre = head_major(query_flat, local_heads, head_size) + head_bias_f[0][:, None, :]
        key_pre = head_major(key_flat, local_heads, head_size)
        value_local = (
            head_major(value_flat, local_heads, head_size) + head_bias_f[1][:, None, :]
        ).astype(bf16)
        queries = rotate(query_pre, angles).astype(bf16)
        key_local = rotate(key_pre, angles).astype(bf16)
        key_heads, value_heads = (
            lax.all_gather(key_local, CTX, axis=1, tiled=True),
            lax.all_gather(value_local, CTX, axis=1, tiled=True),
        )

        def score_block():
            raw = (
                jnp.einsum("htd,hsd->hts", queries, key_heads, preferred_element_type=f32)
                * score_scale
            )
            return jnp.where(valid_row[None, None, :], raw, -1e30)

        scores = score_block()
        row_top = jnp.max(scores, axis=-1, keepdims=True)
        row_total = jnp.sum(jnp.exp(scores - row_top), axis=-1, keepdims=True)
        soft_low = (jnp.exp(scores - row_top) / row_total).astype(bf16)
        mixed = jnp.einsum("hts,hsd->htd", soft_low, value_heads, preferred_element_type=f32)
        mix_sums = lax.psum(
            (
                jnp.sum(mixed, axis=(0, 2), keepdims=True),
                jnp.sum(mixed * mixed, axis=(0, 2), keepdims=True),
            ),
            TP,
        )
        mix_mean = mix_sums[0] / width
        spread_mix = lax.rsqrt(mix_sums[1] / width - mix_mean * mix_mean + EPS)
        mix_hat = (mixed - mix_mean) * spread_mix
        mix_in = (mix_hat * head_scale_f + head_bias_f[2][:, None, :]).astype(bf16)
        branch = lax.psum(
            jnp.einsum("htd,hdn->tn", mix_in, out_heads, preferred_element_type=f32), TP
        )
        resid = token_rows + (branch + width_bias[2])
        normed_two, spread_two = standardize(resid)
        second_in = (normed_two * norm_scale[1] + width_bias[1]).astype(bf16)
        gate_pre = jnp.dot(second_in, gate_full[0], preferred_element_type=f32) + hidden_bias[0]
        up_pre = jnp.dot(second_in, gate_full[1], preferred_element_type=f32) + hidden_bias[1]
        sigmoid_gate = jax.nn.sigmoid(gate_pre)
        silu_gate = gate_pre * sigmoid_gate
        hidden = silu_gate * up_pre
        hidden_sums = lax.psum(
            (
                jnp.sum(hidden, axis=-1, keepdims=True),
                jnp.sum(hidden * hidden, axis=-1, keepdims=True),
            ),
            TP,
        )
        hidden_mean = hidden_sums[0] / FF
        spread_hid = lax.rsqrt(hidden_sums[1] / FF - hidden_mean * hidden_mean + EPS)
        hidden_hat = (hidden - hidden_mean) * spread_hid
        down_in = (hidden_hat * hidden_scale + hidden_bias[2]).astype(bf16)
        ffn_out = lax.psum(
            jnp.dot(down_in, down_full, preferred_element_type=f32).astype(jnp.bfloat16), TP
        ).astype(jnp.float32)
        result = (resid + (ffn_out + width_bias[3])).astype(bf16)
        d_ffn_low = cot_rows.astype(bf16)
        g_down = jnp.einsum("tf,td->fd", down_in, d_ffn_low, preferred_element_type=f32)
        d_down_in = jnp.einsum("td,fd->tf", d_ffn_low, down_full, preferred_element_type=f32)
        grad_hid = d_down_in * hidden_scale
        hid_back = lax.psum(
            (
                jnp.sum(grad_hid, axis=-1, keepdims=True),
                jnp.sum(grad_hid * hidden_hat, axis=-1, keepdims=True),
            ),
            TP,
        )
        d_hidden = (grad_hid - hid_back[0] / FF - hidden_hat * (hid_back[1] / FF)) * spread_hid
        d_gate = (
            d_hidden * up_pre * sigmoid_gate * (1.0 + gate_pre * (1.0 - sigmoid_gate))
        ).astype(bf16)
        d_up = (d_hidden * silu_gate).astype(bf16)
        g_gate_one = jnp.einsum("td,tf->df", second_in, d_gate, preferred_element_type=f32)
        g_up_one = jnp.einsum("td,tf->df", second_in, d_up, preferred_element_type=f32)
        d_second_part = jnp.einsum(
            "tf,df->td", d_gate, gate_full[0], preferred_element_type=f32
        ) + jnp.einsum("tf,df->td", d_up, gate_full[1], preferred_element_type=f32)
        d_second = lax.psum(d_second_part, TP)
        d_resid = cot_rows + norm_back(d_second * norm_scale[1], normed_two, spread_two)
        d_branch_low = d_resid.astype(bf16)
        g_out = jnp.einsum("htd,tn->hdn", mix_in, d_branch_low, preferred_element_type=f32).reshape(
            local_dim, width
        )
        d_mix_in = jnp.einsum("tn,hdn->htd", d_branch_low, out_heads, preferred_element_type=f32)
        grad_mix = d_mix_in * head_scale_f
        mix_back = lax.psum(
            (
                jnp.sum(grad_mix, axis=(0, 2), keepdims=True),
                jnp.sum(grad_mix * mix_hat, axis=(0, 2), keepdims=True),
            ),
            TP,
        )
        d_mixed = (
            (grad_mix - mix_back[0] / width - mix_hat * (mix_back[1] / width)) * spread_mix
        ).astype(bf16)
        again = score_block()
        weights_soft = jnp.exp(again - row_top) / row_total
        d_soft = jnp.einsum("htd,hsd->hts", d_mixed, value_heads, preferred_element_type=f32)
        row_dot = jnp.sum(weights_soft * d_soft, axis=-1, keepdims=True)
        d_scores = (weights_soft * (d_soft - row_dot)).astype(bf16)
        d_query = (
            jnp.einsum("hts,hsd->htd", d_scores, key_heads, preferred_element_type=f32)
            * score_scale
        )
        soft_again = weights_soft.astype(bf16)
        d_key_all = (
            jnp.einsum("hts,htd->hsd", d_scores, queries, preferred_element_type=f32) * score_scale
        )
        d_value_all = jnp.einsum("hts,htd->hsd", soft_again, d_mixed, preferred_element_type=f32)
        d_key_heads, d_value_loc = (
            lax.psum_scatter(
                d_key_all.astype(jnp.bfloat16), CTX, scatter_dimension=1, tiled=True
            ).astype(jnp.float32),
            lax.psum_scatter(
                d_value_all.astype(jnp.bfloat16), CTX, scatter_dimension=1, tiled=True
            ).astype(jnp.float32),
        )
        d_query_low = unrotate(d_query, angles).astype(bf16)
        d_key_low = unrotate(d_key_heads, angles).astype(bf16)
        d_value_low = d_value_loc.astype(bf16)
        g_query = jnp.einsum(
            "tn,htd->nhd", first_in, d_query_low, preferred_element_type=f32
        ).reshape(width, local_dim)
        g_key = jnp.einsum("tn,htd->nhd", first_in, d_key_low, preferred_element_type=f32).reshape(
            width, local_dim
        )
        g_value = jnp.einsum(
            "tn,htd->nhd", first_in, d_value_low, preferred_element_type=f32
        ).reshape(width, local_dim)
        d_first_part = jnp.einsum(
            "htd,nhd->tn",
            d_query_low,
            qkv_full[0].reshape(width, local_heads, head_size),
            preferred_element_type=f32,
        )
        d_first_part = d_first_part + jnp.einsum(
            "htd,nhd->tn",
            d_key_low,
            qkv_full[1].reshape(width, local_heads, head_size),
            preferred_element_type=f32,
        )
        d_first_part = d_first_part + jnp.einsum(
            "htd,nhd->tn",
            d_value_low,
            qkv_full[2].reshape(width, local_heads, head_size),
            preferred_element_type=f32,
        )
        d_first = lax.psum(d_first_part.astype(jnp.bfloat16), TP).astype(jnp.float32)
        d_tokens = d_resid + norm_back(d_first * norm_scale[0], normed_one, spread_one)
        g_head_bias = jnp.stack(
            [
                jnp.sum(d_query_low.astype(f32), axis=1),
                jnp.sum(d_value_low.astype(f32), axis=1),
                jnp.sum(d_mix_in, axis=1),
            ]
        )
        g_head_scale = jnp.sum(d_mix_in * mix_hat, axis=1)
        g_norm = jnp.stack([column_sum(d_first * normed_one), column_sum(d_second * normed_two)])
        g_width = jnp.stack(
            [
                column_sum(d_first),
                column_sum(d_second),
                column_sum(d_branch_low),
                column_sum(d_ffn_low),
            ]
        )
        g_hidden_bias = jnp.stack([column_sum(d_gate), column_sum(d_up), column_sum(d_down_in)])
        g_hidden_scale = column_sum(d_down_in * hidden_hat)
        out_all = lax.dynamic_update_index_in_dim(carried[0], result, batch_idx, 0)
        grad_all = lax.dynamic_update_index_in_dim(carried[1], d_tokens, batch_idx, 0)
        updates = (
            g_query,
            g_key,
            g_value,
            g_head_bias,
            g_head_scale,
            g_out,
            g_norm,
            g_width,
            g_gate_one,
            g_up_one,
            g_down,
            g_hidden_bias,
            g_hidden_scale,
        )
        return (
            out_all,
            grad_all,
            tuple((before + added for before, added in zip(carried[2], updates))),
        )

    zeros_acc = (
        jnp.zeros((width, local_dim), f32),
        jnp.zeros((width, local_dim), f32),
        jnp.zeros((width, local_dim), f32),
        jnp.zeros((3, local_heads, head_size), f32),
        jnp.zeros((local_heads, head_size), f32),
        jnp.zeros((local_dim, width), f32),
        jnp.zeros((2, width), f32),
        jnp.zeros((4, width), f32),
        jnp.zeros((width, local_hidden), f32),
        jnp.zeros((width, local_hidden), f32),
        jnp.zeros((local_hidden, width), f32),
        jnp.zeros((3, local_hidden), f32),
        jnp.zeros((local_hidden,), f32),
    )
    start = (jnp.zeros(tokens.shape, bf16), jnp.zeros(tokens.shape, f32), zeros_acc)
    out_all, grad_all, summed = lax.fori_loop(0, micro, one_batch, start)
    (
        acc_query,
        acc_key,
        acc_value,
        acc_head_bias,
        acc_head_scale,
        acc_out,
        acc_norm,
        acc_width,
        acc_gate_one,
        acc_up_one,
        acc_down,
        acc_hidden_bias,
        acc_hidden_scale,
    ) = summed
    acc_qkv = jnp.stack([acc_query, acc_key, acc_value])
    acc_gate = jnp.stack([acc_gate_one, acc_up_one])
    sharded = (
        acc_qkv,
        acc_head_bias,
        acc_head_scale,
        acc_out,
        acc_norm,
        acc_width,
        acc_gate,
        acc_down,
    )
    hidden_done = lax.psum((acc_hidden_bias, acc_hidden_scale), (SHARD, CTX))
    return (
        out_all,
        grad_all,
        lax.psum_scatter(
            lax.psum(sharded[0].astype(jnp.bfloat16), CTX),
            SHARD,
            scatter_dimension=1,
            tiled=True,
        ).astype(jnp.float32),
        lax.psum_scatter(
            lax.psum(sharded[1].astype(jnp.bfloat16), CTX),
            SHARD,
            scatter_dimension=2,
            tiled=True,
        ).astype(jnp.float32),
        lax.psum_scatter(
            lax.psum(sharded[2].astype(jnp.bfloat16), CTX),
            SHARD,
            scatter_dimension=1,
            tiled=True,
        ).astype(jnp.float32),
        lax.psum_scatter(
            lax.psum(sharded[3].astype(jnp.bfloat16), CTX),
            SHARD,
            scatter_dimension=1,
            tiled=True,
        ).astype(jnp.float32),
        lax.psum_scatter(
            lax.psum(sharded[4].astype(jnp.bfloat16), CTX),
            SHARD,
            scatter_dimension=1,
            tiled=True,
        ).astype(jnp.float32),
        lax.psum_scatter(
            lax.psum(sharded[5].astype(jnp.bfloat16), CTX),
            SHARD,
            scatter_dimension=1,
            tiled=True,
        ).astype(jnp.float32),
        lax.psum_scatter(
            lax.psum(sharded[6].astype(jnp.bfloat16), CTX),
            SHARD,
            scatter_dimension=1,
            tiled=True,
        ).astype(jnp.float32),
        hidden_done[0],
        hidden_done[1],
        lax.psum_scatter(
            lax.psum(sharded[7].astype(jnp.bfloat16), CTX),
            SHARD,
            scatter_dimension=1,
            tiled=True,
        ).astype(jnp.float32),
    )


MESH = pl.DeviceIdType.MESH
LIMIT = 56 * 1024 * 1024
ANY = pl.BlockSpec(memory_space=pl.ANY)
IN_VMEM = pl.BlockSpec(memory_space=pltpu.VMEM)
CORE, ACROSS, BESIDE, UP, DOWN, SWAP, FAR = range(7)
ROW, COL = range(2)


def place_of():
    index = lax.axis_index(SHARD)
    return (lax.div(index, 2), lax.rem(index, 2), lax.axis_index(CTX), lax.axis_index(TP))


def when(condition, action):
    if condition is None:
        action()
    else:
        pl.when(condition)(action)


def both(first, second):
    return jnp.logical_and(first, second)


def device(place, way):
    z, k, x, y = place
    return {
        CORE: {SHARD: 2 * z + 1 - k},
        ACROSS: {CTX: 1 - x},
        BESIDE: {TP: 1 - y},
        UP: {SHARD: 2 * z + 2 + k},
        DOWN: {SHARD: 2 * z - 2 + k},
        SWAP: {SHARD: 2 * z + 1 - k, CTX: 1 - x},
        FAR: {SHARD: 2 * z + 1 - k, CTX: 1 - x, TP: 1 - y},
    }[way]


def greet(layers, place, diagonals):
    z, k, x, y = place
    barrier = pltpu.get_barrier_semaphore()

    def hello(way):
        pl.semaphore_signal(barrier, inc=1, device_id=device(place, way), device_id_type=MESH)

    hello(CORE)
    hello(ACROSS)
    hello(BESIDE)
    pl.when(z > 0)(lambda: hello(DOWN))
    pl.when(z < layers - 1)(lambda: hello(UP))
    count = 3 + jnp.where(z > 0, 1, 0) + jnp.where(z < layers - 1, 1, 0)
    for way in diagonals:
        pl.when(k != x)(lambda way=way: hello(way))
        count = count + jnp.where(k != x, 1, 0)
    pl.semaphore_wait(barrier, count)


class Links:
    def __init__(self, place, send_sem, recv_sem):
        self.place, self.send_sem, self.recv_sem = place, send_sem, recv_sem
        self.used = 0
        self.sent = []
        self.noted = None

    def take(self, count):
        first = self.used
        self.used += count
        return first

    def copy(self, way, at, source, target):
        return pltpu.make_async_remote_copy(
            src_ref=source,
            dst_ref=target,
            send_sem=self.send_sem.at[at],
            recv_sem=self.recv_sem.at[at],
            device_id=device(self.place, way),
            device_id_type=MESH,
        )

    def do(self, condition, action):
        if self.noted is None:
            when(condition, action)
        else:
            self.noted.append((condition, action))

    def record(self, actions):
        self.noted = []
        for action in actions:
            action()
        found, self.noted = self.noted, None
        return found

    def send(self, condition, copy):
        self.do(condition, copy.start)
        self.sent.append((condition, copy))

    def finish(self):
        for condition, copy in self.sent:
            when(condition, copy.wait_send)


def run(noted):
    for condition, action in noted:
        when(condition, action)


def piece_view(kind, rows, cols, ref, y, s, first, size):
    if kind == ROW:
        at_row, at_col = s * rows + first, y * cols
    else:
        at_row, at_col = y * rows + first, s * cols
    at_row, at_col = pl.multiple_of(at_row, 16), pl.multiple_of(at_col, 128)
    return ref.at[pl.ds(at_row, size), pl.ds(at_col, cols)]


def cut_rows(ref, first, size):
    return ref.at[pl.ds(pl.multiple_of(first, 16), size), :]


class Gather:
    def __init__(self, layers, links, kind, own, full, low, rows, split, local_sem):
        self.layers, self.links, self.kind, self.own, self.full = layers, links, kind, own, full
        self.piece_rows, self.cols = own.shape
        self.low, self.rows = low, rows
        self.split, self.half = split, split // 2
        self.local_sem = local_sem
        n = layers
        self.z_a = links.take(2 * n)
        self.z_b = links.take(2 * n)
        self.x_a, self.x_b = links.take(n), links.take(n)
        self.y_a, self.y_b = links.take(n), links.take(1)
        self.core = links.take(2 * n)

    @staticmethod
    def sem_count(layers):
        return 9 * layers + 1

    def copy(self, way, at, y, z, first, size, from_own=False, other_core=False):
        k = self.links.place[1]
        s = 2 * z + (1 - k if other_core else k)
        first = first + self.low
        there = piece_view(self.kind, self.piece_rows, self.cols, self.full, y, s, first, size)
        here = cut_rows(self.own, first, size) if from_own else there
        return self.links.copy(way, at, here, there)

    def half_a(self, way, at, y, z, which, from_own=False):
        return self.copy(way, at, y, z, which * self.half, self.half, from_own)

    def part_a(self, way, at, y, z, from_own=False):
        return self.copy(way, at, y, z, 0, self.split, from_own)

    def part_b(self, way, at, y, z, from_own=False):
        return self.copy(way, at, y, z, self.split, self.rows - self.split, from_own)

    def to_core(self, y, z, from_own=False, other_core=False):
        return self.copy(CORE, self.core + 2 * z + y, y, z, 0, self.rows, from_own, other_core)

    def z_at(self, base, way, z):
        return base + (0 if way == UP else self.layers) + z

    def begin(self):
        z, k, x, y = self.links.place
        send = self.links.send
        low, high = z > 0, z < self.layers - 1
        own_view = piece_view(
            self.kind, self.piece_rows, self.cols, self.full, y, 2 * z + k, self.low, self.rows
        )
        own = cut_rows(self.own, self.low, self.rows)
        self.local = pltpu.make_async_copy(own, own_view, self.local_sem)
        if self.split < self.rows:
            send(None, self.part_b(BESIDE, self.y_b, y, z, True))
            same = x == y
            send(both(same, high), self.part_b(UP, self.z_at(self.z_b, UP, z), y, z, True))
            send(both(same, low), self.part_b(DOWN, self.z_at(self.z_b, DOWN, z), y, z, True))
        if self.split:
            send(high, self.half_a(UP, self.z_at(self.z_a, UP, z), y, z, x, True))
            send(low, self.half_a(DOWN, self.z_at(self.z_a, DOWN, z), y, z, x, True))
            send(None, self.part_a(BESIDE, self.y_a + z, y, z, True))
        send(None, self.to_core(y, z, True))
        self.links.do(None, self.local.start)

    def cross_y(self):
        if self.split == self.rows:
            return
        z, k, x, y = self.links.place
        send = self.links.send
        self.links.do(None, self.part_b(BESIDE, self.y_b, 1 - y, z).wait_recv)
        other = x != y
        low, high = z > 0, z < self.layers - 1
        send(both(other, high), self.part_b(UP, self.z_at(self.z_b, UP, z), 1 - y, z))
        send(both(other, low), self.part_b(DOWN, self.z_at(self.z_b, DOWN, z), 1 - y, z))

    def steps(self, step):
        z = self.links.place[0]
        below, above = z - 1 - step, z + 1 + step
        return (
            (UP, below, below >= 0, z < self.layers - 1),
            (DOWN, above, above <= self.layers - 1, z > 0),
        )

    def along_z(self, step):
        z, k, x, y = self.links.place
        send = self.links.send
        for way, origin, there, further in self.steps(step):
            if self.split < self.rows:
                came = self.part_b(way, self.z_at(self.z_b, way, origin), x, origin)
                self.links.do(there, came.wait_recv)
                send(both(there, further), came)
                send(there, self.part_b(ACROSS, self.x_b + origin, x, origin))
            if self.split:
                came = self.half_a(way, self.z_at(self.z_a, way, origin), y, origin, x)
                self.links.do(there, came.wait_recv)
                send(both(there, further), came)
                send(there, self.half_a(ACROSS, self.x_a + origin, y, origin, x))

    def along_x(self, step):
        z, k, x, y = self.links.place
        send = self.links.send
        for way, origin, there, further in self.steps(step):
            if self.split:
                self.links.do(there, self.half_a(ACROSS, self.x_a + origin, y, origin, 1 - x).wait_recv)
                send(there, self.part_a(BESIDE, self.y_a + origin, y, origin))
            if self.split < self.rows:
                self.links.do(there, self.part_b(ACROSS, self.x_b + origin, 1 - x, origin).wait_recv)
            send(there, self.to_core(y, origin))

    def along_y(self, step):
        z, k, x, y = self.links.place
        todo = ((None, z, None, None),) if step < 0 else self.steps(step)
        for way, origin, there, further in todo:
            if self.split:
                self.links.do(there, self.part_a(BESIDE, self.y_a + origin, 1 - y, origin).wait_recv)
            self.links.send(there, self.to_core(1 - y, origin))

    def stages(self):
        found = [[self.begin], [self.cross_y]]
        for step in range(self.layers + 1):
            now = []
            if step < self.layers - 1:
                now.append(functools.partial(self.along_z, step))
            if step == 0:
                now.append(functools.partial(self.along_y, -1))
            if 0 <= step - 1 < self.layers - 1:
                now.append(functools.partial(self.along_x, step - 1))
            if 0 <= step - 2 < self.layers - 1:
                now.append(functools.partial(self.along_y, step - 2))
            found.append(now)
        return found

    def arrived(self):
        self.links.do(None, self.local.wait)
        for layer in range(self.layers):
            for y in range(2):
                self.links.do(None, self.to_core(y, layer, other_core=True).wait_recv)


def ticks_of(links, jobs, starts, begins):
    plans = [job.stages() for job in jobs]
    ticks = [[] for _ in range(max([at + len(plan) for at, plan in zip(starts, plans)]))]
    for start, begin, plan in zip(starts, begins, plans):
        for stage, actions in enumerate(plan):
            ticks[start + stage if stage else begin] += actions
    return [links.record(tick) for tick in ticks]


class Swap:
    def __init__(self, links, source, target, local_sem):
        z, k, x, y = links.place
        self.same, self.other = k == x, k != x
        self.here = pltpu.make_async_copy(source, target, local_sem)
        self.there = links.copy(SWAP, links.take(1), source, target)

    def begin(self):
        pl.when(self.same)(self.here.start)
        pl.when(self.other)(self.there.start)

    def arrived(self):
        pl.when(self.same)(self.here.wait)
        pl.when(self.other)(self.there.wait)


class Cross:
    def __init__(self, links, source, target, local_sem):
        y = links.place[3]
        at = links.take(1)
        self.here = pltpu.make_async_copy(source, target.at[y], local_sem)
        self.out = links.copy(BESIDE, at, source, target.at[y])
        self.back = links.copy(BESIDE, at, source, target.at[1 - y])

    def begin(self):
        self.here.start()
        self.out.start()

    def arrived(self):
        self.here.wait()
        self.out.wait_send()
        self.back.wait_recv()


class Spread:
    def __init__(self, links, block, both_images, local_sem):
        z, k, x, y = links.place
        self.same, self.other = k == x, k != x
        here, first, second = links.take(1), links.take(1), 0
        target = both_images.at[y]
        self.keep = pltpu.make_async_copy(block, target, local_sem)
        self.beside = links.copy(BESIDE, here, block, target)
        self.swap = links.copy(SWAP, first, block, target)
        self.far = links.copy(FAR, here, block, target)
        self.came = links.copy(BESIDE, here, block, both_images.at[1 - y])

    def begin(self):
        def same():
            self.keep.start()
            self.beside.start()

        def other():
            self.swap.start()
            self.far.start()

        pl.when(self.same)(same)
        pl.when(self.other)(other)

    def arrived(self):
        def same():
            self.keep.wait()
            self.beside.wait_send()

        def other():
            self.swap.wait()
            self.far.wait_send()

        pl.when(self.same)(same)
        pl.when(self.other)(other)
        self.came.wait_recv()


def full_shape(layers, kind, piece):
    if kind == ROW:
        return piece[:-2] + (piece[-2] * layers * 2, piece[-1] * 2)
    return (piece[-2] * 2, piece[-1] * layers * 2)


def by_chunks(shape, body):
    rows, cols = shape
    chunk = 16
    while rows % (2 * chunk) == 0 and 2 * chunk * cols <= 16384:
        chunk *= 2

    def step(i, nothing):
        body((pl.ds(pl.multiple_of(i * chunk, 16), chunk), slice(None)))
        return nothing

    lax.fori_loop(0, rows // chunk, step, 0)


def add_into(target, term):
    def body(where):
        target[where] = target[where] + term[where]

    by_chunks(target.shape, body)


def store_sum(out, *terms):
    def body(where):
        total = terms[0][where].astype(jnp.float32)
        for term in terms[1:]:
            total = total + term[where].astype(jnp.float32)
        out[where] = total

    by_chunks(out.shape, body)


class Reduce:
    def __init__(self, layers, links, kind, grad, out, low, split, scratch, local_sem, local_base):
        self.layers, self.links, self.kind, self.grad = layers, links, kind, grad
        self.mine, self.load, self.y_in, self.x_in, self.z_in, self.last = scratch
        self.sent = []
        self.rows, self.cols = self.mine.shape[-2:]
        self.low, self.piece_rows = low, out.shape[0]
        self.out = cut_rows(out, low, self.rows)
        self.split = split
        self.local_sem, self.local_base = local_sem, local_base
        n = layers
        self.core = links.take(2 * n)
        self.y_a, self.x_b = links.take(n), links.take(n)
        self.z_a, self.z_b = links.take(2 * n), links.take(2 * n)
        self.end_a, self.end_b, self.end_c = links.take(1), links.take(1), links.take(1)
        self.order = []
        low, high = 0, layers - 1
        while low <= high:
            self.order.append(high)
            if low < high:
                self.order.append(low)
            low, high = low + 1, high - 1

    @staticmethod
    def sem_count(layers):
        return 8 * layers + 3

    def part_a(self, ref):
        return cut_rows(ref, 0, self.split)

    def part_b(self, ref):
        return cut_rows(ref, self.split, self.rows - self.split)

    def send(self, condition, copy):
        self.links.do(condition, copy.start)
        self.sent.append((condition, copy))

    def finish(self):
        for condition, copy in self.sent:
            when(condition, copy.wait_send)

    def add(self, condition, target, term):
        self.links.do(condition, functools.partial(add_into, target, term))

    def grad_piece(self, y, s):
        return piece_view(
            self.kind, self.piece_rows, self.cols, self.grad, y, s, self.low, self.rows
        )

    def local(self, number):
        k = self.links.place[1]
        layer, y = self.order[number // 2], number % 2
        return pltpu.make_async_copy(
            self.grad_piece(y, 2 * layer + k),
            self.load.at[number % 2],
            self.local_sem.at[self.local_base + number],
        )

    def to_core(self, y, layer):
        k = self.links.place[1]
        return self.links.copy(
            CORE,
            self.core + 2 * layer + y,
            self.grad_piece(y, 2 * layer + 1 - k),
            self.mine.at[y, layer],
        )

    def begin(self):
        for layer in self.order:
            for y in range(2):
                self.send(None, self.to_core(y, layer))
        for number in range(2):
            self.links.do(None, self.local(number).start)

    def to_y(self, layer):
        y = self.links.place[3]
        source = self.part_a(self.mine.at[1 - y, layer])
        return self.links.copy(BESIDE, self.y_a + layer, source, self.y_in.at[layer])

    def to_x(self, layer):
        x = self.links.place[2]
        source = self.part_b(self.mine.at[1 - x, layer])
        return self.links.copy(ACROSS, self.x_b + layer, source, self.x_in.at[layer])

    def chip_sum(self):
        for number in range(2 * self.layers):
            layer, side = self.order[number // 2], number % 2
            self.links.do(None, self.local(number).wait)
            self.links.do(None, self.to_core(side, layer).wait_recv)
            self.add(None, self.mine.at[side, layer], self.load.at[number % 2])
            if number + 2 < 2 * self.layers:
                self.links.do(None, self.local(number + 2).start)
            if side:
                self.send(None, self.to_y(layer))
                self.send(None, self.to_x(layer))

    def plane_sum(self):
        z, k, x, y = self.links.place
        for layer in self.order:
            self.links.do(None, self.to_y(layer).wait_recv)
            self.add(None, self.part_a(self.mine.at[y, layer]), self.y_in.at[layer])
            self.links.do(None, self.to_x(layer).wait_recv)
            self.add(None, self.part_b(self.mine.at[x, layer]), self.x_in.at[layer])

    def chain(self, way, layer, receiver):
        z, k, x, y = self.links.place
        slot = layer if way == UP else jnp.where(receiver == layer, self.layers, layer)
        add = 0 if way == UP else self.layers
        found = []
        for base, part, side in ((self.z_a, self.part_a, y), (self.z_b, self.part_b, x)):
            total, box = part(self.mine.at[side, layer]), part(self.z_in.at[slot])
            found.append((total, box, self.links.copy(way, base + add + layer, total, box)))
        return found

    def take(self, condition, way, layer):
        for total, box, copy in self.chain(way, layer, self.links.place[0]):
            self.links.do(condition, copy.wait_recv)
            self.add(condition, total, box)

    def along_z(self, depth):
        z = self.links.place[0]
        top = self.layers - 1
        for way, here, goals in (
            (UP, z == depth, range(top, depth, -1)),
            (DOWN, z == top - depth, range(0, top - depth)),
        ):
            for layer in goals:
                if depth:
                    self.take(here, way, layer)
                for total, box, copy in self.chain(way, layer, z + 1 if way == UP else z - 1):
                    self.send(here, copy)

    def ending(self):
        z, k, x, y = self.links.place
        self.take(z > 0, UP, z)
        self.take(z < self.layers - 1, DOWN, z)
        self.sum_a, self.sum_b = self.part_a(self.mine.at[y, z]), self.part_b(self.mine.at[x, z])
        self.got_a, self.got_b = self.part_a(self.last.at[0]), self.part_b(self.last.at[0])
        self.got_y = self.part_b(self.last.at[1])
        self.x_end = self.links.copy(ACROSS, self.end_a, self.sum_a, self.got_a)
        self.y_end = self.links.copy(BESIDE, self.end_b, self.sum_b, self.got_y)
        self.x_last = self.links.copy(ACROSS, self.end_c, self.sum_b, self.got_b)
        self.send(y != x, self.y_end)
        self.send(None, self.x_end)

    def owner(self):
        z, k, x, y = self.links.place

        self.links.do(y == x, self.y_end.wait_recv)
        self.add(y == x, self.sum_b, self.got_y)
        self.send(y == x, self.x_last)
        self.links.do(None, self.x_end.wait_recv)
        out_a = self.part_a(self.out)
        self.links.do(None, functools.partial(store_sum, out_a, self.sum_a, self.got_a))

    def write(self):
        z, k, x, y = self.links.place
        out_b = self.part_b(self.out)

        self.links.do(y != x, self.x_last.wait_recv)
        self.links.do(y != x, functools.partial(store_sum, out_b, self.got_b))
        self.links.do(y == x, functools.partial(store_sum, out_b, self.sum_b))

    def stages(self):
        chains = [[functools.partial(self.along_z, depth)] for depth in range(self.layers - 1)]
        return [
            [self.begin], [self.chip_sum], [self.plane_sum], *chains,
            [self.ending], [self.owner], [self.write],
        ]


class Total:
    def __init__(self, layers, links, given, out, boxes, layer_boxes):
        self.layers, self.links, self.given, self.out = layers, links, given, out
        self.boxes, self.layer_boxes = boxes, layer_boxes
        self.pair = [links.take(1) for _ in range(3)]
        self.z_up, self.z_down = links.take(layers), links.take(layers)

    @staticmethod
    def sem_count(layers):
        return 3 + 2 * layers

    def exchange(self, number):
        way = (CORE, ACROSS, BESIDE)[number]
        source = self.given if number == 0 else self.boxes.at[2 + number]
        return self.links.copy(way, self.pair[number], source, self.boxes.at[number])

    def begin(self):
        self.links.send(None, self.exchange(0))

    def join(self, number):
        z = self.links.place[0]
        self.links.do(None, self.exchange(number).wait_recv)
        mine = self.given if number == 0 else self.boxes.at[2 + number]
        result = self.layer_boxes.at[z] if number == 2 else self.boxes.at[3 + number]
        self.links.do(None, functools.partial(store_sum, result, mine, self.boxes.at[number]))
        if number < 2:
            self.links.send(None, self.exchange(number + 1))
        else:
            self.links.send(z < self.layers - 1, self.pass_on(UP, z))
            self.links.send(z > 0, self.pass_on(DOWN, z))

    def pass_on(self, way, layer):
        box = self.layer_boxes.at[layer]
        return self.links.copy(way, (self.z_up if way == UP else self.z_down) + layer, box, box)

    def along_z(self, step):
        z = self.links.place[0]
        top = self.layers - 1
        below, above = z - 1 - step, z + 1 + step
        for way, origin, there, further in (
            (UP, below, below >= 0, z < top),
            (DOWN, above, above <= top, z > 0),
        ):
            copy = self.pass_on(way, origin)
            self.links.do(there, copy.wait_recv)
            self.links.send(both(there, further), copy)

    def write(self):
        layers = [self.layer_boxes.at[layer] for layer in range(self.layers)]
        self.links.do(None, functools.partial(store_sum, self.out, *layers))

    def stages(self):
        joins = [[functools.partial(self.join, number)] for number in range(3)]
        moves = [[functools.partial(self.along_z, step)] for step in range(self.layers - 1)]
        return [[self.begin], *joins, *moves, [self.write]]


def reduce_jobs(layers, links, jobs, grads, outs, scratch, local_sem):
    todo = []
    for number, (mat, kind, low, rows, split) in enumerate(jobs):
        own = scratch[6 * number : 6 * number + 6]
        at = number * 2 * layers
        grad, out = grads[mat], outs[mat]
        todo.append(Reduce(layers, links, kind, grad, out, low, split, own, local_sem, at))
    return todo


def reduce_shapes(layers, rows, cols, split):
    return [
        (2, layers, rows, cols), (2, rows, cols), (layers, split, cols),
        (layers, rows - split, cols), (layers + 1, rows, cols), (2, rows, cols),
    ]


def piece_shape(layers, kind, full):
    if kind == ROW:
        return full[:-2] + (full[-2] // (2 * layers), full[-1] // 2)
    return (full[-2] // 2, full[-1] // (2 * layers))


def pair_lanes(shape, head_size):
    lane = lax.broadcasted_iota(jnp.int32, shape, len(shape) - 1)
    return lane < head_size


def dot_last(left, right):
    return lax.dot_general(left, right, (((1,), (1,)), ((), ())), preferred_element_type=jnp.float32)


def dot_first(left, right):
    return lax.dot_general(left, right, (((0,), (0,)), ((), ())), preferred_element_type=jnp.float32)


def dot(left, right):
    return lax.dot_general(left, right, (((1,), (0,)), ((), ())), preferred_element_type=jnp.float32)


def only_head(values, head, head_size):
    lane = lax.broadcasted_iota(jnp.int32, (1, values.shape[1]), 1)
    keep = (lane < head_size) if head == 0 else (lane >= head_size)
    return values * jnp.where(keep, 1.0, 0.0).astype(values.dtype)


LOG2_E = 1.4426950408889634


def turn_lanes(values, quarter):
    width = values.shape[-1]
    lane = lax.broadcasted_iota(jnp.int32, (1, width), 1)
    even = lax.rem(lax.div(lane, quarter), 2) == 0
    after = pltpu.roll(values, width - quarter, 1)
    before = pltpu.roll(values, quarter, 1)
    return jnp.where(even, -after, before)


def slot_bias(shape, axis, rows, tokens_here, count):
    slot = lax.broadcasted_iota(jnp.int32, shape, axis)
    second = slot >= rows
    within = jnp.where(second, slot - rows, slot)
    token = jnp.where(second, within + tokens_here, within).astype(jnp.float32)
    return jnp.where(jnp.logical_and(within < tokens_here, token < count), 0.0, -1e30)


def front_kernel(layers, head_size, grid_side, *refs):
    (
        vec_own, qkv_own, out_own, gate_own, down_own, tokens, cot, valid, hidden_own,
        vec_full, qkv_full, out_full, gate_full, down_full, hidden_full, cot_out,
        x_out, n_out, q_out, k_out, v_out, o_out, stat_out, vec_out, count_out, cos, sin,
        x, valid_both, vec, weight, hat, normed, q, keys, values, bias,
        send_sem, recv_sem, local_sem,
    ) = refs
    f32, bf16 = jnp.float32, jnp.bfloat16
    place = place_of()
    z, k, me_x, y = place
    greet(layers, place, (SWAP,))
    links = Links(place, send_sem, recv_sem)
    rows, width = x.shape
    tokens_here = valid.shape[1] // 2
    tile = weight.shape[2]
    quarter = head_size // 4
    lanes = 2 * head_size
    locals_used = [0]

    def local_at():
        locals_used[0] += 1
        return local_sem.at[locals_used[0] - 1]

    block = Swap(links, tokens.at[y], x, local_at())
    cot_block = Swap(links, cot.at[y], cot_out, local_at())
    valid_swap = Swap(links, valid, valid_both, local_at())
    cross = Cross(links, hidden_own, hidden_full, local_at())
    out_rows, down_rows = out_own.shape[0], down_own.shape[0] // 2
    todo = [
        (ROW, vec_own, vec_full, 0, vec_own.shape[0], 0),
        (ROW, qkv_own.at[0], qkv_full.at[0], 0, 128, 64),
        (ROW, qkv_own.at[1], qkv_full.at[1], 0, 128, 64),
        (ROW, qkv_own.at[2], qkv_full.at[2], 0, 128, 64),
        (ROW, gate_own.at[0], gate_full.at[0], 0, 64, 32),
        (ROW, gate_own.at[0], gate_full.at[0], 64, 64, 32),
        (ROW, gate_own.at[1], gate_full.at[1], 0, 64, 32),
        (ROW, gate_own.at[1], gate_full.at[1], 64, 64, 32),
        (COL, down_own, down_full, 0, down_rows, 448),
        (COL, down_own, down_full, down_rows, down_rows, 448),
        (COL, out_own, out_full, 0, out_rows, 320),
    ]
    starts = (0, 1, 2, 3, 4, 5, 6, 7, 8, 9, 10)
    begins = (0, 0, 1, 2, 3, 4, 5, 6, 7, 8, 9)
    jobs = [
        Gather(layers, links, kind, own, full, low, size, split, local_at())
        for kind, own, full, low, size, split in todo
    ]
    ticks = ticks_of(links, jobs, starts, begins)
    weight_loads = []
    for mat in range(3):
        for part in range(width // tile):
            slot = len(weight_loads) % 2
            weight_loads.append(
                pltpu.make_async_copy(
                    qkv_full.at[mat, :, pl.ds(part * tile, tile)], weight.at[slot], local_at()
                )
            )
    vec_load = pltpu.make_async_copy(vec_full, vec, local_at())
    keeps = [
        pltpu.make_async_copy(source, target, local_at())
        for source, target in ((x, x_out), (normed, n_out), (q, q_out), (keys, k_out), (values, v_out))
    ]
    shares = []
    my_rows = pl.ds(pl.multiple_of(k * rows, 16), rows)
    other_rows = pl.ds(pl.multiple_of((1 - k) * rows, 16), rows)
    for store in (keys, values):
        for part in range(width // tile):
            at = links.take(1)
            cols = pl.ds(part * tile, tile)
            out_going = links.copy(CORE, at, store.at[my_rows, cols], store.at[my_rows, cols])
            coming = links.copy(CORE, at, store.at[other_rows, cols], store.at[other_rows, cols])
            shares.append((out_going, coming))

    block.begin()
    valid_swap.begin()
    run(ticks[0])
    cot_block.begin()
    cross.begin()
    run(ticks[1])

    block.arrived()
    valid_swap.arrived()
    keeps[0].start()
    chunk = rows // 3

    def normalise(i, nothing):
        at = pl.ds(pl.multiple_of(i * chunk, 16), chunk)
        value, spread = standardize(x[at, :].astype(f32))
        hat[at, :] = value
        return nothing

    lax.fori_loop(0, 3, normalise, 0)
    flags = jnp.where(y == 0, valid_both[0:1, :], valid_both[1:2, :]).astype(f32)
    count = jnp.sum(flags, axis=1, keepdims=True)
    count_out[...] = jnp.broadcast_to(count, count_out.shape)
    columns = (count - 1.0) * (1.0 / grid_side)
    token = lax.broadcasted_iota(jnp.int32, (rows, lanes), 0).astype(f32)
    token = token + (k * tokens_here).astype(f32)
    lane = lax.broadcasted_iota(jnp.int32, (rows, lanes), 1)
    live = jnp.logical_and(token >= 1.0, token < count)
    row_id = jnp.floor((token - 0.5) / columns)
    col_id = token - 1.0 - row_id * columns
    where_at = jnp.where(lax.rem(lane, head_size) < 2 * quarter, row_id, col_id)
    where_at = jnp.where(live, where_at, 0.0)
    power = lax.rem(lane, quarter).astype(f32) * (-math.log(10000.0) / quarter)
    angle = where_at * jnp.exp(power)
    cos[...] = jnp.cos(angle)
    sin[...] = jnp.sin(angle)
    bias[...] = slot_bias(bias.shape, 1, rows, tokens_here, count)

    for tick in ticks[2:8]:
        run(tick)
    jobs[0].arrived()
    vec_load.start()
    vec_load.wait()
    piece_rows = vec_own.shape[0]
    summed = vec[0:piece_rows, :].astype(f32)
    for s in range(1, 2 * layers):
        summed = summed + vec[s * piece_rows : (s + 1) * piece_rows, :].astype(f32)
    vec_out[...] = summed

    def scale(i, nothing):
        at = pl.ds(pl.multiple_of(i * chunk, 16), chunk)
        normed[at, :] = (hat[at, :] * vec_out[4:5, :] + vec_out[6:7, :]).astype(bf16)
        return nothing

    lax.fori_loop(0, 3, scale, 0)
    keeps[1].start()
    repeat = tile // lanes
    per = width // tile
    for mat in range(3):
        run(ticks[8 + mat])
        jobs[1 + mat].arrived()
        for part in range(per):
            weight_loads[mat * per + part].start()
        for part in range(per):
            load = weight_loads[mat * per + part]
            load.wait()
            cols = pl.ds(part * tile, tile)
            raw = dot(normed[...], weight[(mat * per + part) % 2])
            if mat != 1:
                raw = raw + vec_out[0 if mat == 0 else 1 : 1 if mat == 0 else 2, cols]
            if mat < 2:
                turned = turn_lanes(raw, quarter)
                wide_cos = jnp.concatenate([cos[...]] * repeat, axis=1)
                wide_sin = jnp.concatenate([sin[...]] * repeat, axis=1)
                raw = raw * wide_cos + turned * wide_sin
            if mat == 0:
                q[:, cols] = raw.astype(bf16)
            else:
                (keys if mat == 1 else values)[my_rows, cols] = raw.astype(bf16)
                shares[(mat - 1) * per + part][0].start()
    keeps[2].start()
    for out_going, coming in shares:
        out_going.wait_send()
        coming.wait_recv()
    keeps[3].start()
    keeps[4].start()

    late = ticks[11:]
    score_scale = LOG2_E / math.sqrt(head_size)
    pairs = width // lanes

    def mix(i, nothing):
        for number, tick in enumerate(late):
            pl.when(i == number)(functools.partial(run, tick))
        cols = pl.ds(pl.multiple_of(i * lanes, lanes), lanes)
        queries, near_keys, near_values = q[:, cols], keys[:, cols], values[:, cols]
        parts = []
        for head in range(2):
            s = dot_last(only_head(queries, head, head_size), near_keys) * score_scale + bias[...]
            top = jnp.max(s, axis=1, keepdims=True)
            e = jnp.exp2(s - top)
            total = jnp.sum(e, axis=1, keepdims=True)
            parts.append(dot(e.astype(bf16), near_values) * (1.0 / total))
            level = jnp.broadcast_to(top + jnp.log2(total), (rows, 128))
            stat_out[i, head : head + 1, :] = jnp.transpose(level)[0:1, :]
        o_out[:, cols] = jnp.where(pair_lanes((rows, lanes), head_size), parts[0], parts[1])
        return nothing

    lax.fori_loop(0, pairs, mix, 0)
    for tick in late[8:]:
        run(tick)
    for job in jobs[4:]:
        job.arrived()
    cross.arrived()
    cot_block.arrived()
    for keep in keeps:
        keep.wait()
    links.finish()


def front(
    layers, number, head_size, grid_side, vec, qkv, out, gate, down, tokens, cot, valid, hidden
):
    bf16, f32 = jnp.bfloat16, jnp.float32
    rows, width = tokens.shape[1:]
    pairs = width // (2 * head_size)
    tile = 512
    fulls = [
        full_shape(layers, kind, piece.shape)
        for kind, piece in ((ROW, vec), (ROW, qkv), (COL, out), (ROW, gate), (COL, down))
    ]
    shapes = [jax.ShapeDtypeStruct(shape, bf16) for shape in fulls]
    shapes += [jax.ShapeDtypeStruct((2,) + hidden.shape, bf16)]
    shapes += [jax.ShapeDtypeStruct((n * rows, width), bf16) for n in (1, 1, 1, 1, 2, 2)]
    shapes += [
        jax.ShapeDtypeStruct((rows, width), f32),
        jax.ShapeDtypeStruct((pairs, 2, rows), f32),
        jax.ShapeDtypeStruct((vec.shape[0], width), f32),
        jax.ShapeDtypeStruct((8, 128), f32),
        jax.ShapeDtypeStruct((rows, 2 * head_size), f32),
        jax.ShapeDtypeStruct((rows, 2 * head_size), f32),
    ]
    sems = 11 * Gather.sem_count(layers) + 8
    return pl.pallas_call(
        functools.partial(front_kernel, layers, head_size, grid_side),
        out_shape=shapes,
        in_specs=[ANY] * 9,
        out_specs=[ANY] * 12 + [IN_VMEM] * 6,
        scratch_shapes=[
            pltpu.VMEM((rows, width), bf16),
            pltpu.VMEM(valid.shape, valid.dtype),
            pltpu.VMEM(fulls[0], bf16),
            pltpu.VMEM((2, width, tile), bf16),
            pltpu.VMEM((rows, width), f32),
            pltpu.VMEM((rows, width), bf16),
            pltpu.VMEM((rows, width), bf16),
            pltpu.VMEM((2 * rows, width), bf16),
            pltpu.VMEM((2 * rows, width), bf16),
            pltpu.VMEM((1, 2 * rows), f32),
            pltpu.SemaphoreType.DMA((sems,)),
            pltpu.SemaphoreType.DMA((sems,)),
            pltpu.SemaphoreType.DMA((32,)),
        ],
        compiler_params=pltpu.CompilerParams(
            collective_id=number, has_side_effects=True, vmem_limit_bytes=LIMIT
        ),
    )(vec, qkv, out, gate, down, tokens, cot, valid, hidden)


def back_kernel(layers, head_size, tokens_here, jobs, late_jobs, mats, *refs):
    grads, refs = refs[:mats], refs[mats:]
    given_arrays, refs = refs[:9], refs[9:]
    q_in, keys_in, values_in, do_in, mixed_in, n_in, x_in, resid_in, weights = given_arrays
    stats, count, cos, sin, vec, total_in = refs[:6]
    outs, refs = refs[6 : 6 + mats], refs[6 + mats :]
    late_outs, total_out, tokens_out, late_grads = refs[:3], refs[3], refs[4], refs[5:8]
    scratch, refs = refs[8 : 8 + 6 * len(jobs)], refs[8 + 6 * len(jobs) :]
    (
        q, keys, values, do, mixed, k_sum, v_sum, dq_low, dk_low, dv_low, normed_t, d_first,
        d_tokens, bias, total, boxes, layer_boxes, send_sem, recv_sem, local_sem, ready,
    ) = refs
    f32, bf16 = jnp.float32, jnp.bfloat16
    place = place_of()
    z, k, x, y = place
    greet(layers, place, (SWAP, FAR))
    links = Links(place, send_sem, recv_sem)
    first_jobs = reduce_jobs(layers, links, jobs, grads, outs, scratch, local_sem)
    locals_used = [len(jobs) * 2 * layers]

    def local_at():
        locals_used[0] += 1
        return local_sem.at[locals_used[0] - 1]

    second_jobs = []
    for mat, low, rows_here, split, host, first_col in late_jobs:
        cols_here = pl.ds(first_col, late_outs[mat].shape[-1])
        own = []
        for ref in scratch[6 * host : 6 * host + 6]:
            own.append(ref.at[(slice(None),) * (len(ref.shape) - 1) + (cols_here,)])
        second_jobs.append(
            Reduce(
                layers, links, ROW, late_grads[mat], late_outs[mat], low, split, own,
                local_sem, locals_used[0],
            )
        )
        locals_used[0] += 2 * layers
    sums = Total(layers, links, total, total_out, boxes, layer_boxes)
    early, n_late = len(jobs), len(second_jobs)
    handover = early + 5
    late_starts = [handover + number // 2 for number in range(n_late)]
    starts = list(range(early)) + late_starts + [handover + 3]
    begins = [max(0, number - 1) for number in range(early)] + late_starts + [handover + 3]
    ticks = ticks_of(links, first_jobs + second_jobs + [sums], starts, begins)
    spread = Spread(links, d_tokens, tokens_out, local_at())

    rows, width = q.shape
    lanes = 2 * head_size
    pairs = width // lanes
    scale = 1.0 / math.sqrt(head_size)
    quarter = head_size // 4
    my_rows = pl.ds(pl.multiple_of(k * rows, 16), rows)
    other_rows = pl.ds(pl.multiple_of((1 - k) * rows, 16), rows)
    first = links.take(2 * pairs)

    def share(i):
        cols = pl.ds(pl.multiple_of(i * lanes, lanes), lanes)
        return (
            links.copy(CORE, first + 2 * i, k_sum.at[other_rows, cols], dk_low.at[:, cols]),
            links.copy(CORE, first + 2 * i + 1, v_sum.at[other_rows, cols], dv_low.at[:, cols]),
        )

    def turn_back(grad):
        return grad * cos[...] - turn_lanes(grad, quarter) * sin[...]

    def load(source, target):
        copy = pltpu.make_async_copy(source, target, local_at())
        copy.start()
        return copy

    run(ticks[0])
    loads = [
        load(source, target)
        for source, target in (
            (q_in, q), (keys_in, keys), (values_in, values), (do_in, do), (mixed_in, mixed)
        )
    ]
    bias[...] = slot_bias(bias.shape, 0, rows, tokens_here, count[0:1, 0:1])
    total[...] = total_in[...]
    run(ticks[1])
    for copy in loads:
        copy.wait()
    beside = ticks[2 : 2 + pairs]

    def step(i, nothing):
        for number, tick in enumerate(beside):
            pl.when(i == number)(functools.partial(run, tick))
        cols = pl.ds(pl.multiple_of(i * lanes, lanes), lanes)
        queries, near_keys, near_values, grad = q[:, cols], keys[:, cols], values[:, cols], do[:, cols]
        products = jnp.transpose(grad.astype(f32) * mixed[:, cols])
        found = []
        for head in range(2):
            row_dot = products[head * head_size : (head + 1) * head_size]
            row_dot = jnp.sum(row_dot, axis=0, keepdims=True)
            s = dot_last(near_keys, only_head(queries, head, head_size)) * (scale * LOG2_E)
            p = jnp.exp2(s + bias[...] - stats[i, head : head + 1, :])
            dp = dot_last(near_values, only_head(grad, head, head_size))
            ds = (p * (dp - row_dot)).astype(bf16)
            found.append(
                (dot_first(near_keys, ds) * scale, dot(ds, queries) * scale, dot(p.astype(bf16), grad))
            )
        dq = jnp.concatenate([found[0][0][:head_size], found[1][0][head_size:]], axis=0)
        dq = turn_back(jnp.transpose(dq)).astype(bf16)
        dq_low[:, cols] = dq
        total[pl.ds(i, 1), :] = jnp.sum(dq.astype(f32), axis=0, keepdims=True)
        in_first = pair_lanes((2 * rows, lanes), head_size)
        k_sum[:, cols] = jnp.where(in_first, found[0][1], found[1][1]).astype(bf16)
        v_sum[:, cols] = jnp.where(in_first, found[0][2], found[1][2]).astype(bf16)
        for copy in share(i):
            copy.start()
        return nothing

    lax.fori_loop(0, pairs, step, 0)
    normed_load = load(n_in, q)
    loads = [load(weights.at[0], keys.at[pl.ds(0, width)]), load(weights.at[1], values.at[pl.ds(0, width)])]
    loads += [load(x_in, do), load(resid_in, mixed)]
    at_tick = [2 + pairs]

    def advance():
        run(ticks[at_tick[0]])
        at_tick[0] += 1

    def join(i, nothing):
        cols = pl.ds(pl.multiple_of(i * lanes, lanes), lanes)
        for copy in share(i):
            copy.wait()
        dk = k_sum[my_rows, cols].astype(f32) + dk_low[:, cols].astype(f32)
        dk_low[:, cols] = turn_back(dk).astype(bf16)
        dv = v_sum[my_rows, cols].astype(f32) + dv_low[:, cols].astype(f32)
        dv = dv.astype(bf16)
        dv_low[:, cols] = dv
        total[pl.ds(pairs + i, 1), :] = jnp.sum(dv.astype(f32), axis=0, keepdims=True)
        return nothing

    advance()
    lax.fori_loop(0, pairs, join, 0)
    normed_load.wait()
    last_weight = load(weights.at[2], k_sum.at[pl.ds(0, width)])

    def flip(i, nothing):
        at = pl.ds(pl.multiple_of(i * lanes, lanes), lanes)
        normed_t[at, :] = jnp.transpose(q[:, at])
        return nothing

    lax.fori_loop(0, width // lanes, flip, 0)
    while at_tick[0] < handover:
        advance()
    tile = 256
    stores = []

    def weight_grad(mat):
        low_grad = (dq_low, dk_low, dv_low)[mat]
        def part(i, nothing):
            at = pl.ds(pl.multiple_of(i * tile, tile), tile)
            v_sum[at, :] = dot(normed_t[at, :], low_grad[...]).astype(bf16)
            return nothing

        lax.fori_loop(0, width // tile, part, 0)
        stores.append(load(v_sum.at[pl.ds(0, width)], late_grads[mat]))

    weight_grad(0)
    for job in first_jobs[:4]:
        job.finish()
    near = [(None, CORE), (None, ACROSS), (None, BESIDE), (z > 0, DOWN), (z < layers - 1, UP)]
    for condition, way in near:

        def hello(way=way):
            pl.semaphore_signal(
                ready, inc=1, device_id=device(place, way), device_id_type=MESH
            )

        when(condition, hello)
    expected = 3 + jnp.where(z > 0, 1, 0) + jnp.where(z < layers - 1, 1, 0)
    pl.semaphore_wait(ready, expected)
    stores[-1].wait()
    advance()
    for mat in (1, 2):
        weight_grad(mat)
        stores[-1].wait()
        advance()
    for copy in loads + [last_weight]:
        copy.wait()

    def project_back(i, nothing):
        at = pl.ds(pl.multiple_of(i * tile, tile), tile)
        result = dot_last(dq_low[...], keys[at, :])
        result = result + dot_last(dk_low[...], values[at, :])
        d_first[:, at] = result + dot_last(dv_low[...], k_sum[at, :])
        return nothing

    lax.fori_loop(0, width // tile, project_back, 0)
    chunk = rows // 3
    gain = vec[4:5, :]
    gain_sum = jnp.zeros((1, width), f32)
    bias_sum = jnp.zeros((1, width), f32)
    for number in range(3):
        at = pl.ds(number * chunk, chunk)
        hat, inverse = standardize(do[at, :].astype(f32))
        dn = d_first[at, :]
        d_tokens[at, :] = (mixed[at, :] + norm_back(dn * gain, hat, inverse)).astype(bf16)
        gain_sum = gain_sum + jnp.sum(dn * hat, axis=0, keepdims=True)
        bias_sum = bias_sum + jnp.sum(dn, axis=0, keepdims=True)
    for i in range(width // 128):
        cols = slice(i * 128, (i + 1) * 128)
        at = 4 * width // 128 + i
        total[at : at + 1, :] = gain_sum[:, cols]
        at = 6 * width // 128 + i
        total[at : at + 1, :] = bias_sum[:, cols]
    spread.begin()
    while at_tick[0] < len(ticks):
        advance()
    spread.arrived()
    for job in first_jobs[4:] + second_jobs:
        job.finish()
    links.finish()


def back(layers, number, head_size, tokens_here, jobs, late_jobs, grads, given, small, total):
    bf16, f32 = jnp.bfloat16, jnp.float32
    pieces = [piece_shape(layers, kind, g.shape) for kind, g in grads]
    rows, width = given[0].shape
    pairs = width // (2 * head_size)
    sems = (len(jobs) + len(late_jobs)) * Reduce.sem_count(layers) + 2 * pairs
    sems += Total.sem_count(layers) + 2
    late_piece = (width // (2 * layers), width // 2)
    scratch = []
    for mat, kind, low, job_rows, split in jobs:
        shapes = reduce_shapes(layers, job_rows, pieces[mat][-1], split)
        scratch += [pltpu.VMEM(shape, bf16) for shape in shapes]
    half, whole = (rows, width), (2 * rows, width)
    buffers = [(half, bf16), (whole, bf16), (whole, bf16), (half, bf16), (half, f32)]
    buffers += [(whole, bf16)] * 2 + [(half, bf16)] * 3 + [((width, rows), bf16), (half, f32)]
    buffers += [(half, bf16), ((2 * rows, 1), f32), (total.shape, f32)]
    buffers += [((5,) + total.shape, f32), ((layers,) + total.shape, f32)]
    return pl.pallas_call(
        functools.partial(
            back_kernel, layers, head_size, tokens_here, jobs, late_jobs, len(grads)
        ),
        out_shape=[jax.ShapeDtypeStruct(piece, f32) for piece in pieces]
        + [jax.ShapeDtypeStruct(late_piece, f32)] * 3
        + [jax.ShapeDtypeStruct(total.shape, f32)]
        + [jax.ShapeDtypeStruct((2, rows, width), bf16)]
        + [jax.ShapeDtypeStruct((width, width), bf16)] * 3,
        in_specs=[ANY] * (len(grads) + len(given)) + [IN_VMEM] * (len(small) + 1),
        out_specs=[IN_VMEM] * (len(pieces) + 4) + [ANY] * 4,
        scratch_shapes=scratch
        + [pltpu.VMEM(shape, dtype) for shape, dtype in buffers]
        + [
            pltpu.SemaphoreType.DMA((sems,)),
            pltpu.SemaphoreType.DMA((sems,)),
            pltpu.SemaphoreType.DMA(((len(jobs) + len(late_jobs)) * 2 * layers + 16,)),
            pltpu.SemaphoreType.REGULAR,
        ],
        compiler_params=pltpu.CompilerParams(
            collective_id=number, has_side_effects=True, vmem_limit_bytes=62 * 1024 * 1024
        ),
    )(*[g for kind, g in grads], *given, *small, total)


def pad_to(values, axis, size):
    pads = [(0, 0)] * values.ndim
    pads[axis] = (0, size - values.shape[axis])
    return jnp.pad(values, pads)


def round_up(size, step):
    return (size + step - 1) // step * step


def image_per_chip(
    layers,
    tokens,
    cotangent,
    valid_tokens,
    places,
    qkv_weight,
    head_biases,
    head_gain,
    out_weight,
    norm_gains,
    width_biases,
    gate_up,
    hidden_biases,
    hidden_gain,
    down_weight,
):
    f32 = jnp.float32
    bf16 = jnp.bfloat16
    z, k, x, y = place_of()
    s = 2 * z + k
    shards = 2 * layers
    width = tokens.shape[2]
    rows = tokens.shape[1]
    heads_here = head_gain.shape[0]
    heads = 2 * heads_here
    dims_here = head_gain.shape[1]
    head_size = dims_here * shards
    real_here = hidden_gain.shape[0]
    hidden_here = round_up(real_here, 128)
    real = 2 * real_here
    hidden_size = 2 * hidden_here
    score_scale = 1.0 / math.sqrt(head_size)

    padded = round_up(rows, 16)
    heads_own = jnp.concatenate([head_biases, head_gain[None]], axis=0)
    spot = jnp.zeros((4, heads_here, head_size), bf16)
    spot = lax.dynamic_update_slice(spot, heads_own, (0, 0, s * dims_here)).reshape(4, -1)
    width_own = jnp.concatenate([norm_gains, width_biases], axis=0)
    lane_at = s * width_own.shape[1] - y * spot.shape[1]
    inside = both(lane_at >= 0, lane_at < spot.shape[1])
    width_own = jnp.where(inside, width_own, jnp.zeros_like(width_own))
    at = jnp.where(inside, lane_at, 0)
    lanes_own = lax.dynamic_update_slice(jnp.zeros((6, spot.shape[1]), bf16), width_own, (0, at))
    vectors = pad_to(jnp.concatenate([spot, lanes_own], axis=0), 0, 16)
    hidden_vectors = jnp.concatenate([hidden_biases, hidden_gain[None]], axis=0)
    hidden_vectors = pad_to(pad_to(hidden_vectors, 1, hidden_here), 0, 16)
    gate_pad = pad_to(gate_up, 2, hidden_here)
    down_pad = pad_to(down_weight, 0, hidden_here)
    swaps, others = [], []
    for layer in range(layers):
        swaps += [(4 * layer + 1, 4 * layer + 2), (4 * layer + 2, 4 * layer + 1)]
        for spot, far in ((0, 0), (1, 2), (2, 1), (3, 3)):
            for side in range(2):
                others.append((2 * (4 * layer + spot) + side, 2 * (4 * layer + far) + 1 - side))
    (
        vec_full, qkv_full, out_full, gate_full, down_full, hidden_full, cot_block,
        token_block, first_in, queries, keys, values, mixed, stats, vec, count, cos, sin,
    ) = front(
        layers, 0, head_size, 32, vectors, qkv_weight, out_weight, gate_pad, down_pad,
        pad_to(tokens, 1, padded), pad_to(cotangent, 1, padded), valid_tokens, hidden_vectors,
    )
    head_part, norm_scale, width_bias = vec[0:4], vec[4:6], vec[6:10]
    hidden_part = jnp.concatenate([hidden_full[0, :4], hidden_full[1, :4]], axis=1).astype(f32)
    token_rows = token_block.astype(f32)
    cot_rows = cot_block.astype(f32)
    mix_hat, spread_mix = standardize(mixed)
    mix_in = (mix_hat * head_part[3] + head_part[2]).astype(bf16)
    branch = jnp.dot(mix_in, out_full, preferred_element_type=f32)
    resid = token_rows + (branch + width_bias[2])
    normed_two, spread_two = standardize(resid)
    second_in = (normed_two * norm_scale[1] + width_bias[1]).astype(bf16)
    gate_pre = jnp.dot(second_in, gate_full[0], preferred_element_type=f32) + hidden_part[0]
    up_pre = jnp.dot(second_in, gate_full[1], preferred_element_type=f32) + hidden_part[1]
    sigmoid_gate = jax.nn.sigmoid(gate_pre)
    silu_gate = gate_pre * sigmoid_gate
    hidden = silu_gate * up_pre
    hidden_mean = jnp.sum(hidden, axis=-1, keepdims=True) / real
    centred = hidden - hidden_mean
    extra = (hidden_size - real) * hidden_mean * hidden_mean
    hidden_var = (jnp.sum(centred * centred, axis=-1, keepdims=True) - extra) / real
    spread_hid = lax.rsqrt(jnp.maximum(hidden_var, 0.0) + EPS)
    hidden_hat = centred * spread_hid
    down_in = (hidden_hat * hidden_part[3] + hidden_part[2]).astype(bf16)
    ffn_out = jnp.dot(down_in, down_full, preferred_element_type=f32)
    result = (resid + (ffn_out + width_bias[3])).astype(bf16)[:rows]
    result_other = lax.ppermute(result, (SHARD, CTX, TP), others)
    results = (result, result_other, lax.ppermute(result, (SHARD, CTX), swaps))

    g_down = jnp.einsum("tf,td->fd", down_in, cot_block, preferred_element_type=f32)
    d_down_in = jnp.einsum("td,fd->tf", cot_block, down_full, preferred_element_type=f32)
    grad_hid = d_down_in * hidden_part[3]
    hid_back_one = jnp.sum(grad_hid, axis=-1, keepdims=True) / real
    hid_back_two = jnp.sum(grad_hid * hidden_hat, axis=-1, keepdims=True) / real
    d_hidden = (grad_hid - hid_back_one - hidden_hat * hid_back_two) * spread_hid
    d_gate = (d_hidden * up_pre * sigmoid_gate * (1.0 + gate_pre * (1.0 - sigmoid_gate))).astype(
        bf16
    )
    d_up = (d_hidden * silu_gate).astype(bf16)
    g_gate = jnp.einsum("td,tf->df", second_in, d_gate, preferred_element_type=f32).astype(bf16)
    g_up = jnp.einsum("td,tf->df", second_in, d_up, preferred_element_type=f32).astype(bf16)
    d_second = jnp.einsum("tf,df->td", d_gate, gate_full[0], preferred_element_type=f32)
    d_second = d_second + jnp.einsum("tf,df->td", d_up, gate_full[1], preferred_element_type=f32)
    d_resid = cot_rows + norm_back(d_second * norm_scale[1], normed_two, spread_two)
    d_branch_low = d_resid.astype(bf16)
    g_out = jnp.einsum("tm,tn->mn", mix_in, d_branch_low, preferred_element_type=f32)
    d_mix_in = jnp.einsum("tn,mn->tm", d_branch_low, out_full, preferred_element_type=f32)
    d_mixed = norm_back(d_mix_in * head_part[3], mix_hat, spread_mix).astype(bf16)
    vector_grads = jnp.concatenate(
        [
            jnp.zeros((width,), f32),
            jnp.zeros((width,), f32),
            column_sum(d_mix_in),
            column_sum(d_mix_in * mix_hat),
            jnp.zeros((width,), f32),
            column_sum(d_second * normed_two),
            jnp.zeros((width,), f32),
            column_sum(d_second),
            column_sum(d_branch_low),
            column_sum(cot_block),
            column_sum(d_gate),
            column_sum(d_up),
            column_sum(d_down_in),
            column_sum(d_down_in * hidden_hat),
        ]
    ).reshape(-1, 128)
    vector_grads = pad_to(vector_grads, 0, round_up(vector_grads.shape[0], 16))
    result, result_other, swapped, d_mixed = lax.optimization_barrier((*results, d_mixed))
    result = jnp.where(k == x, result, swapped)
    result = jnp.stack(
        [jnp.where(y == 0, result, result_other), jnp.where(y == 0, result_other, result)], axis=1
    ).transpose(1, 0, 2)
    half = hidden_here // 2
    heads_rows = heads_here * head_size
    grad_jobs = (
        (0, ROW, 0, 64, 32), (0, ROW, 64, 64, 32), (1, ROW, 0, 64, 32), (1, ROW, 64, 64, 32),
        (2, COL, 0, half, half // 2), (2, COL, half, half, half // 2),
        (3, COL, 0, heads_rows, heads_rows // 2),
    )
    late_jobs = (
        (0, 0, 64, 32, 0, 0), (0, 64, 64, 32, 1, 0),
        (1, 0, 64, 32, 0, heads_rows), (1, 64, 64, 32, 1, heads_rows),
        (2, 0, 64, 32, 2, 0), (2, 64, 64, 32, 3, 0),
    )
    back_grads = (
        (ROW, g_gate), (ROW, g_up), (COL, g_down.astype(bf16)), (COL, g_out.astype(bf16))
    )
    (
        gate_piece, up_piece, down_piece, out_piece, query_piece, key_piece, value_piece,
        vector_grads, d_tokens, *unused,
    ) = back(
        layers, 1, head_size, rows, grad_jobs, late_jobs, back_grads,
        (queries, keys, values, d_mixed, mixed, first_in, token_block, d_resid, qkv_full),
        (stats, count, cos, sin, vec), vector_grads,
    )
    d_tokens = jnp.stack([d_tokens[0, :rows], d_tokens[1, :rows]], axis=1).transpose(1, 0, 2)
    vector_grads = vector_grads.reshape(-1)
    head_sums = vector_grads[: 4 * width].reshape(4, heads, head_size)
    head_sums = lax.dynamic_slice(
        head_sums, (0, y * heads_here, s * dims_here), (4, heads_here, dims_here)
    )
    width_sums = vector_grads[4 * width : 10 * width].reshape(6, width)
    width_sums = lax.dynamic_slice(width_sums, (0, s * 128), (6, width // shards))
    hidden_sums = vector_grads[10 * width : 10 * width + 4 * hidden_size]
    hidden_sums = hidden_sums.reshape(4, hidden_size)
    hidden_sums = lax.dynamic_slice(hidden_sums, (0, y * hidden_here), (4, hidden_here))
    hidden_sums = hidden_sums[:, :real_here]

    return (
        result,
        d_tokens.astype(f32),
        jnp.stack([query_piece, key_piece, value_piece]),
        head_sums[:3],
        head_sums[3],
        out_piece,
        width_sums[:2],
        width_sums[2:],
        jnp.stack([gate_piece[:, :real_here], up_piece[:, :real_here]]),
        hidden_sums[:3],
        hidden_sums[3],
        down_piece[:real_here],
    )


def solution(mesh):
    small = mesh.shape[CTX] == 2 and mesh.shape[TP] == 2
    body = functools.partial(image_per_chip, mesh.shape[SHARD] // 2) if small else general_plan

    return jax.shard_map(
        body,
        mesh=mesh,
        in_specs=(
            P(SHARD, CTX, None),
            P(SHARD, CTX, None),
            P(SHARD, None),
            P(None, SHARD, CTX),
            P(None, SHARD, TP),
            P(None, TP, SHARD),
            P(TP, SHARD),
            P(TP, SHARD),
            P(None, SHARD),
            P(None, SHARD),
            P(None, SHARD, TP),
            P(None, TP),
            P(TP),
            P(TP, SHARD),
        ),
        out_specs=(
            P(SHARD, CTX, None),
            P(SHARD, CTX, None),
            P(None, SHARD, TP),
            P(None, TP, SHARD),
            P(TP, SHARD),
            P(TP, SHARD),
            P(None, SHARD),
            P(None, SHARD),
            P(None, SHARD, TP),
            P(None, TP),
            P(TP),
            P(TP, SHARD),
        ),
        check_vma=False,
    )
```

```python
import functools
import math

import jax
import jax.numpy as jnp
from jax import lax
from jax.experimental import pallas as pl
from jax.experimental.pallas import tpu as pltpu
from jax.sharding import PartitionSpec as P

SHARD, CTX, TP = "shard", "ctx", "tp"


EPS = 1e-06


def standardize(values):
    average = jnp.mean(values, axis=-1, keepdims=True)
    centred = values - average
    spread = lax.rsqrt(jnp.mean(centred * centred, axis=-1, keepdims=True) + EPS)
    return (centred * spread, spread)


def norm_back(grad_hat, normed, spread):
    mean_one = jnp.mean(grad_hat, axis=-1, keepdims=True)
    mean_two = jnp.mean(grad_hat * normed, axis=-1, keepdims=True)
    return (grad_hat - mean_one - normed * mean_two) * spread


def angle_table(row_ids, col_ids, head_size):
    quarter = head_size // 4
    frequency = 10000.0 ** (-jnp.arange(quarter, dtype=jnp.float32) / quarter)
    row_part = row_ids.astype(jnp.float32)[:, None] * frequency[None, :]
    col_part = col_ids.astype(jnp.float32)[:, None] * frequency[None, :]
    return jnp.concatenate([row_part, row_part, col_part, col_part], axis=1)


def turn_half(values):
    quarter = values.shape[-1] // 4
    part_one = values[..., :quarter]
    part_two = values[..., quarter : 2 * quarter]
    part_three = values[..., 2 * quarter : 3 * quarter]
    part_four = values[..., 3 * quarter :]
    return jnp.concatenate([-part_two, part_one, -part_four, part_three], axis=-1)


def rotate(values, angles):
    return values * jnp.cos(angles)[None, :, :] + turn_half(values) * jnp.sin(angles)[None, :, :]


def unrotate(values, angles):
    return values * jnp.cos(angles)[None, :, :] - turn_half(values) * jnp.sin(angles)[None, :, :]


def head_major(values, heads, head_size):
    return values.reshape(values.shape[0], heads, head_size).transpose(1, 0, 2)


def column_sum(values):
    return jnp.sum(values.astype(jnp.float32), axis=0)


def general_plan(
    tokens,
    cotangent,
    valid_tokens,
    places,
    qkv_weight,
    head_biases,
    head_gain,
    out_weight,
    norm_gains,
    width_biases,
    gate_up,
    hidden_biases,
    hidden_gain,
    down_weight,
):
    micro = tokens.shape[0]
    width = tokens.shape[2]
    local_dim = qkv_weight.shape[2]
    local_heads = head_biases.shape[1]
    head_size = local_dim // local_heads
    local_hidden = hidden_gain.shape[0]
    FF = local_hidden * lax.axis_size(TP)
    score_scale = 1.0 / math.sqrt(head_size)
    f32 = jnp.float32
    bf16 = jnp.bfloat16

    def one_batch(batch_idx, carried):
        gathered = (
            lax.all_gather(qkv_weight, SHARD, axis=1, tiled=True),
            lax.all_gather(head_biases, SHARD, axis=2, tiled=True),
            lax.all_gather(head_gain, SHARD, axis=1, tiled=True),
            lax.all_gather(out_weight, SHARD, axis=1, tiled=True),
            lax.all_gather(norm_gains, SHARD, axis=1, tiled=True),
            lax.all_gather(width_biases, SHARD, axis=1, tiled=True),
            lax.all_gather(gate_up, SHARD, axis=1, tiled=True),
            lax.all_gather(down_weight, SHARD, axis=1, tiled=True),
        )
        qkv_full, head_bias, head_scale, out_full, norm_scale, width_bias, gate_full, down_full = (
            gathered
        )
        head_bias_f = head_bias.astype(f32)
        head_scale_f = head_scale.astype(f32)[:, None, :]
        norm_scale = norm_scale.astype(f32)
        width_bias = width_bias.astype(f32)
        hidden_bias = hidden_biases.astype(f32)
        hidden_scale = hidden_gain.astype(f32)
        out_heads = out_full.reshape(local_heads, head_size, width)
        token_rows = lax.dynamic_index_in_dim(tokens, batch_idx, 0, keepdims=False).astype(f32)
        cot_rows = lax.dynamic_index_in_dim(cotangent, batch_idx, 0, keepdims=False).astype(f32)
        valid_row = lax.dynamic_index_in_dim(valid_tokens, batch_idx, 0, keepdims=False) > 0
        row_ids = lax.dynamic_index_in_dim(places[0], batch_idx, 0, keepdims=False)
        col_ids = lax.dynamic_index_in_dim(places[1], batch_idx, 0, keepdims=False)
        angles = angle_table(row_ids, col_ids, head_size)
        normed_one, spread_one = standardize(token_rows)
        first_in = (normed_one * norm_scale[0] + width_bias[0]).astype(bf16)
        query_flat = jnp.dot(first_in, qkv_full[0], preferred_element_type=f32)
        key_flat = jnp.dot(first_in, qkv_full[1], preferred_element_type=f32)
        value_flat = jnp.dot(first_in, qkv_full[2], preferred_element_type=f32)
        query_pre = head_major(query_flat, local_heads, head_size) + head_bias_f[0][:, None, :]
        key_pre = head_major(key_flat, local_heads, head_size)
        value_local = (
            head_major(value_flat, local_heads, head_size) + head_bias_f[1][:, None, :]
        ).astype(bf16)
        queries = rotate(query_pre, angles).astype(bf16)
        key_local = rotate(key_pre, angles).astype(bf16)
        key_heads, value_heads = (
            lax.all_gather(key_local, CTX, axis=1, tiled=True),
            lax.all_gather(value_local, CTX, axis=1, tiled=True),
        )

        def score_block():
            raw = (
                jnp.einsum("htd,hsd->hts", queries, key_heads, preferred_element_type=f32)
                * score_scale
            )
            return jnp.where(valid_row[None, None, :], raw, -1e30)

        scores = score_block()
        row_top = jnp.max(scores, axis=-1, keepdims=True)
        row_total = jnp.sum(jnp.exp(scores - row_top), axis=-1, keepdims=True)
        soft_low = (jnp.exp(scores - row_top) / row_total).astype(bf16)
        mixed = jnp.einsum("hts,hsd->htd", soft_low, value_heads, preferred_element_type=f32)
        mix_sums = lax.psum(
            (
                jnp.sum(mixed, axis=(0, 2), keepdims=True),
                jnp.sum(mixed * mixed, axis=(0, 2), keepdims=True),
            ),
            TP,
        )
        mix_mean = mix_sums[0] / width
        spread_mix = lax.rsqrt(mix_sums[1] / width - mix_mean * mix_mean + EPS)
        mix_hat = (mixed - mix_mean) * spread_mix
        mix_in = (mix_hat * head_scale_f + head_bias_f[2][:, None, :]).astype(bf16)
        branch = lax.psum(
            jnp.einsum("htd,hdn->tn", mix_in, out_heads, preferred_element_type=f32), TP
        )
        resid = token_rows + (branch + width_bias[2])
        normed_two, spread_two = standardize(resid)
        second_in = (normed_two * norm_scale[1] + width_bias[1]).astype(bf16)
        gate_pre = jnp.dot(second_in, gate_full[0], preferred_element_type=f32) + hidden_bias[0]
        up_pre = jnp.dot(second_in, gate_full[1], preferred_element_type=f32) + hidden_bias[1]
        sigmoid_gate = jax.nn.sigmoid(gate_pre)
        silu_gate = gate_pre * sigmoid_gate
        hidden = silu_gate * up_pre
        hidden_sums = lax.psum(
            (
                jnp.sum(hidden, axis=-1, keepdims=True),
                jnp.sum(hidden * hidden, axis=-1, keepdims=True),
            ),
            TP,
        )
        hidden_mean = hidden_sums[0] / FF
        spread_hid = lax.rsqrt(hidden_sums[1] / FF - hidden_mean * hidden_mean + EPS)
        hidden_hat = (hidden - hidden_mean) * spread_hid
        down_in = (hidden_hat * hidden_scale + hidden_bias[2]).astype(bf16)
        ffn_out = lax.psum(
            jnp.dot(down_in, down_full, preferred_element_type=f32).astype(jnp.bfloat16), TP
        ).astype(jnp.float32)
        result = (resid + (ffn_out + width_bias[3])).astype(bf16)
        d_ffn_low = cot_rows.astype(bf16)
        g_down = jnp.einsum("tf,td->fd", down_in, d_ffn_low, preferred_element_type=f32)
        d_down_in = jnp.einsum("td,fd->tf", d_ffn_low, down_full, preferred_element_type=f32)
        grad_hid = d_down_in * hidden_scale
        hid_back = lax.psum(
            (
                jnp.sum(grad_hid, axis=-1, keepdims=True),
                jnp.sum(grad_hid * hidden_hat, axis=-1, keepdims=True),
            ),
            TP,
        )
        d_hidden = (grad_hid - hid_back[0] / FF - hidden_hat * (hid_back[1] / FF)) * spread_hid
        d_gate = (
            d_hidden * up_pre * sigmoid_gate * (1.0 + gate_pre * (1.0 - sigmoid_gate))
        ).astype(bf16)
        d_up = (d_hidden * silu_gate).astype(bf16)
        g_gate_one = jnp.einsum("td,tf->df", second_in, d_gate, preferred_element_type=f32)
        g_up_one = jnp.einsum("td,tf->df", second_in, d_up, preferred_element_type=f32)
        d_second_part = jnp.einsum(
            "tf,df->td", d_gate, gate_full[0], preferred_element_type=f32
        ) + jnp.einsum("tf,df->td", d_up, gate_full[1], preferred_element_type=f32)
        d_second = lax.psum(d_second_part, TP)
        d_resid = cot_rows + norm_back(d_second * norm_scale[1], normed_two, spread_two)
        d_branch_low = d_resid.astype(bf16)
        g_out = jnp.einsum("htd,tn->hdn", mix_in, d_branch_low, preferred_element_type=f32).reshape(
            local_dim, width
        )
        d_mix_in = jnp.einsum("tn,hdn->htd", d_branch_low, out_heads, preferred_element_type=f32)
        grad_mix = d_mix_in * head_scale_f
        mix_back = lax.psum(
            (
                jnp.sum(grad_mix, axis=(0, 2), keepdims=True),
                jnp.sum(grad_mix * mix_hat, axis=(0, 2), keepdims=True),
            ),
            TP,
        )
        d_mixed = (
            (grad_mix - mix_back[0] / width - mix_hat * (mix_back[1] / width)) * spread_mix
        ).astype(bf16)
        again = score_block()
        weights_soft = jnp.exp(again - row_top) / row_total
        d_soft = jnp.einsum("htd,hsd->hts", d_mixed, value_heads, preferred_element_type=f32)
        row_dot = jnp.sum(weights_soft * d_soft, axis=-1, keepdims=True)
        d_scores = (weights_soft * (d_soft - row_dot)).astype(bf16)
        d_query = (
            jnp.einsum("hts,hsd->htd", d_scores, key_heads, preferred_element_type=f32)
            * score_scale
        )
        soft_again = weights_soft.astype(bf16)
        d_key_all = (
            jnp.einsum("hts,htd->hsd", d_scores, queries, preferred_element_type=f32) * score_scale
        )
        d_value_all = jnp.einsum("hts,htd->hsd", soft_again, d_mixed, preferred_element_type=f32)
        d_key_heads, d_value_loc = (
            lax.psum_scatter(
                d_key_all.astype(jnp.bfloat16), CTX, scatter_dimension=1, tiled=True
            ).astype(jnp.float32),
            lax.psum_scatter(
                d_value_all.astype(jnp.bfloat16), CTX, scatter_dimension=1, tiled=True
            ).astype(jnp.float32),
        )
        d_query_low = unrotate(d_query, angles).astype(bf16)
        d_key_low = unrotate(d_key_heads, angles).astype(bf16)
        d_value_low = d_value_loc.astype(bf16)
        g_query = jnp.einsum(
            "tn,htd->nhd", first_in, d_query_low, preferred_element_type=f32
        ).reshape(width, local_dim)
        g_key = jnp.einsum("tn,htd->nhd", first_in, d_key_low, preferred_element_type=f32).reshape(
            width, local_dim
        )
        g_value = jnp.einsum(
            "tn,htd->nhd", first_in, d_value_low, preferred_element_type=f32
        ).reshape(width, local_dim)
        d_first_part = jnp.einsum(
            "htd,nhd->tn",
            d_query_low,
            qkv_full[0].reshape(width, local_heads, head_size),
            preferred_element_type=f32,
        )
        d_first_part = d_first_part + jnp.einsum(
            "htd,nhd->tn",
            d_key_low,
            qkv_full[1].reshape(width, local_heads, head_size),
            preferred_element_type=f32,
        )
        d_first_part = d_first_part + jnp.einsum(
            "htd,nhd->tn",
            d_value_low,
            qkv_full[2].reshape(width, local_heads, head_size),
            preferred_element_type=f32,
        )
        d_first = lax.psum(d_first_part.astype(jnp.bfloat16), TP).astype(jnp.float32)
        d_tokens = d_resid + norm_back(d_first * norm_scale[0], normed_one, spread_one)
        g_head_bias = jnp.stack(
            [
                jnp.sum(d_query_low.astype(f32), axis=1),
                jnp.sum(d_value_low.astype(f32), axis=1),
                jnp.sum(d_mix_in, axis=1),
            ]
        )
        g_head_scale = jnp.sum(d_mix_in * mix_hat, axis=1)
        g_norm = jnp.stack([column_sum(d_first * normed_one), column_sum(d_second * normed_two)])
        g_width = jnp.stack(
            [
                column_sum(d_first),
                column_sum(d_second),
                column_sum(d_branch_low),
                column_sum(d_ffn_low),
            ]
        )
        g_hidden_bias = jnp.stack([column_sum(d_gate), column_sum(d_up), column_sum(d_down_in)])
        g_hidden_scale = column_sum(d_down_in * hidden_hat)
        out_all = lax.dynamic_update_index_in_dim(carried[0], result, batch_idx, 0)
        grad_all = lax.dynamic_update_index_in_dim(carried[1], d_tokens, batch_idx, 0)
        updates = (
            g_query,
            g_key,
            g_value,
            g_head_bias,
            g_head_scale,
            g_out,
            g_norm,
            g_width,
            g_gate_one,
            g_up_one,
            g_down,
            g_hidden_bias,
            g_hidden_scale,
        )
        return (
            out_all,
            grad_all,
            tuple((before + added for before, added in zip(carried[2], updates))),
        )

    zeros_acc = (
        jnp.zeros((width, local_dim), f32),
        jnp.zeros((width, local_dim), f32),
        jnp.zeros((width, local_dim), f32),
        jnp.zeros((3, local_heads, head_size), f32),
        jnp.zeros((local_heads, head_size), f32),
        jnp.zeros((local_dim, width), f32),
        jnp.zeros((2, width), f32),
        jnp.zeros((4, width), f32),
        jnp.zeros((width, local_hidden), f32),
        jnp.zeros((width, local_hidden), f32),
        jnp.zeros((local_hidden, width), f32),
        jnp.zeros((3, local_hidden), f32),
        jnp.zeros((local_hidden,), f32),
    )
    start = (jnp.zeros(tokens.shape, bf16), jnp.zeros(tokens.shape, f32), zeros_acc)
    out_all, grad_all, summed = lax.fori_loop(0, micro, one_batch, start)
    (
        acc_query,
        acc_key,
        acc_value,
        acc_head_bias,
        acc_head_scale,
        acc_out,
        acc_norm,
        acc_width,
        acc_gate_one,
        acc_up_one,
        acc_down,
        acc_hidden_bias,
        acc_hidden_scale,
    ) = summed
    acc_qkv = jnp.stack([acc_query, acc_key, acc_value])
    acc_gate = jnp.stack([acc_gate_one, acc_up_one])
    sharded = (
        acc_qkv,
        acc_head_bias,
        acc_head_scale,
        acc_out,
        acc_norm,
        acc_width,
        acc_gate,
        acc_down,
    )
    hidden_done = lax.psum((acc_hidden_bias, acc_hidden_scale), (SHARD, CTX))
    return (
        out_all,
        grad_all,
        lax.psum_scatter(
            lax.psum(sharded[0].astype(jnp.bfloat16), CTX),
            SHARD,
            scatter_dimension=1,
            tiled=True,
        ).astype(jnp.float32),
        lax.psum_scatter(
            lax.psum(sharded[1].astype(jnp.bfloat16), CTX),
            SHARD,
            scatter_dimension=2,
            tiled=True,
        ).astype(jnp.float32),
        lax.psum_scatter(
            lax.psum(sharded[2].astype(jnp.bfloat16), CTX),
            SHARD,
            scatter_dimension=1,
            tiled=True,
        ).astype(jnp.float32),
        lax.psum_scatter(
            lax.psum(sharded[3].astype(jnp.bfloat16), CTX),
            SHARD,
            scatter_dimension=1,
            tiled=True,
        ).astype(jnp.float32),
        lax.psum_scatter(
            lax.psum(sharded[4].astype(jnp.bfloat16), CTX),
            SHARD,
            scatter_dimension=1,
            tiled=True,
        ).astype(jnp.float32),
        lax.psum_scatter(
            lax.psum(sharded[5].astype(jnp.bfloat16), CTX),
            SHARD,
            scatter_dimension=1,
            tiled=True,
        ).astype(jnp.float32),
        lax.psum_scatter(
            lax.psum(sharded[6].astype(jnp.bfloat16), CTX),
            SHARD,
            scatter_dimension=1,
            tiled=True,
        ).astype(jnp.float32),
        hidden_done[0],
        hidden_done[1],
        lax.psum_scatter(
            lax.psum(sharded[7].astype(jnp.bfloat16), CTX),
            SHARD,
            scatter_dimension=1,
            tiled=True,
        ).astype(jnp.float32),
    )


MESH = pl.DeviceIdType.MESH
LIMIT = 56 * 1024 * 1024
ANY = pl.BlockSpec(memory_space=pl.ANY)
IN_VMEM = pl.BlockSpec(memory_space=pltpu.VMEM)
CORE, ACROSS, BESIDE, UP, DOWN, SWAP, FAR = range(7)
ROW, COL = range(2)


def place_of():
    index = lax.axis_index(SHARD)
    return (lax.div(index, 2), lax.rem(index, 2), lax.axis_index(CTX), lax.axis_index(TP))


def when(condition, action):
    if condition is None:
        action()
    else:
        pl.when(condition)(action)


def both(first, second):
    return jnp.logical_and(first, second)


def device(place, way):
    z, k, x, y = place
    return {
        CORE: {SHARD: 2 * z + 1 - k},
        ACROSS: {CTX: 1 - x},
        BESIDE: {TP: 1 - y},
        UP: {SHARD: 2 * z + 2 + k},
        DOWN: {SHARD: 2 * z - 2 + k},
        SWAP: {SHARD: 2 * z + 1 - k, CTX: 1 - x},
        FAR: {SHARD: 2 * z + 1 - k, CTX: 1 - x, TP: 1 - y},
    }[way]


def greet(layers, place, diagonals):
    z, k, x, y = place
    barrier = pltpu.get_barrier_semaphore()

    def hello(way):
        pl.semaphore_signal(barrier, inc=1, device_id=device(place, way), device_id_type=MESH)

    hello(CORE)
    hello(ACROSS)
    hello(BESIDE)
    pl.when(z > 0)(lambda: hello(DOWN))
    pl.when(z < layers - 1)(lambda: hello(UP))
    count = 3 + jnp.where(z > 0, 1, 0) + jnp.where(z < layers - 1, 1, 0)
    for way in diagonals:
        pl.when(k != x)(lambda way=way: hello(way))
        count = count + jnp.where(k != x, 1, 0)
    pl.semaphore_wait(barrier, count)


class Links:
    def __init__(self, place, send_sem, recv_sem):
        self.place, self.send_sem, self.recv_sem = place, send_sem, recv_sem
        self.used = 0
        self.sent = []
        self.noted = None

    def take(self, count):
        first = self.used
        self.used += count
        return first

    def copy(self, way, at, source, target):
        return pltpu.make_async_remote_copy(
            src_ref=source,
            dst_ref=target,
            send_sem=self.send_sem.at[at],
            recv_sem=self.recv_sem.at[at],
            device_id=device(self.place, way),
            device_id_type=MESH,
        )

    def do(self, condition, action):
        if self.noted is None:
            when(condition, action)
        else:
            self.noted.append((condition, action))

    def record(self, actions):
        self.noted = []
        for action in actions:
            action()
        found, self.noted = self.noted, None
        return found

    def send(self, condition, copy):
        self.do(condition, copy.start)
        self.sent.append((condition, copy))

    def finish(self):
        for condition, copy in self.sent:
            when(condition, copy.wait_send)


def run(noted):
    for condition, action in noted:
        when(condition, action)


def piece_view(kind, rows, cols, ref, y, s, first, size):
    if kind == ROW:
        at_row, at_col = s * rows + first, y * cols
    else:
        at_row, at_col = y * rows + first, s * cols
    at_row, at_col = pl.multiple_of(at_row, 16), pl.multiple_of(at_col, 128)
    return ref.at[pl.ds(at_row, size), pl.ds(at_col, cols)]


def cut_rows(ref, first, size):
    return ref.at[pl.ds(pl.multiple_of(first, 16), size), :]


class Gather:
    def __init__(self, layers, links, kind, own, full, low, rows, split, local_sem):
        self.layers, self.links, self.kind, self.own, self.full = layers, links, kind, own, full
        self.piece_rows, self.cols = own.shape
        self.low, self.rows = low, rows
        self.split, self.half = split, split // 2
        self.local_sem = local_sem
        n = layers
        self.z_a = links.take(2 * n)
        self.z_b = links.take(2 * n)
        self.x_a, self.x_b = links.take(n), links.take(n)
        self.y_a, self.y_b = links.take(n), links.take(1)
        self.core = links.take(2 * n)

    @staticmethod
    def sem_count(layers):
        return 9 * layers + 1

    def copy(self, way, at, y, z, first, size, from_own=False, other_core=False):
        k = self.links.place[1]
        s = 2 * z + (1 - k if other_core else k)
        first = first + self.low
        there = piece_view(self.kind, self.piece_rows, self.cols, self.full, y, s, first, size)
        here = cut_rows(self.own, first, size) if from_own else there
        return self.links.copy(way, at, here, there)

    def half_a(self, way, at, y, z, which, from_own=False):
        return self.copy(way, at, y, z, which * self.half, self.half, from_own)

    def part_a(self, way, at, y, z, from_own=False):
        return self.copy(way, at, y, z, 0, self.split, from_own)

    def part_b(self, way, at, y, z, from_own=False):
        return self.copy(way, at, y, z, self.split, self.rows - self.split, from_own)

    def to_core(self, y, z, from_own=False, other_core=False):
        return self.copy(CORE, self.core + 2 * z + y, y, z, 0, self.rows, from_own, other_core)

    def z_at(self, base, way, z):
        return base + (0 if way == UP else self.layers) + z

    def begin(self):
        z, k, x, y = self.links.place
        send = self.links.send
        low, high = z > 0, z < self.layers - 1
        own_view = piece_view(
            self.kind, self.piece_rows, self.cols, self.full, y, 2 * z + k, self.low, self.rows
        )
        own = cut_rows(self.own, self.low, self.rows)
        self.local = pltpu.make_async_copy(own, own_view, self.local_sem)
        if self.split < self.rows:
            send(None, self.part_b(BESIDE, self.y_b, y, z, True))
            same = x == y
            send(both(same, high), self.part_b(UP, self.z_at(self.z_b, UP, z), y, z, True))
            send(both(same, low), self.part_b(DOWN, self.z_at(self.z_b, DOWN, z), y, z, True))
        if self.split:
            send(high, self.half_a(UP, self.z_at(self.z_a, UP, z), y, z, x, True))
            send(low, self.half_a(DOWN, self.z_at(self.z_a, DOWN, z), y, z, x, True))
            send(None, self.part_a(BESIDE, self.y_a + z, y, z, True))
        send(None, self.to_core(y, z, True))
        self.links.do(None, self.local.start)

    def cross_y(self):
        if self.split == self.rows:
            return
        z, k, x, y = self.links.place
        send = self.links.send
        self.links.do(None, self.part_b(BESIDE, self.y_b, 1 - y, z).wait_recv)
        other = x != y
        low, high = z > 0, z < self.layers - 1
        send(both(other, high), self.part_b(UP, self.z_at(self.z_b, UP, z), 1 - y, z))
        send(both(other, low), self.part_b(DOWN, self.z_at(self.z_b, DOWN, z), 1 - y, z))

    def steps(self, step):
        z = self.links.place[0]
        below, above = z - 1 - step, z + 1 + step
        return (
            (UP, below, below >= 0, z < self.layers - 1),
            (DOWN, above, above <= self.layers - 1, z > 0),
        )

    def along_z(self, step):
        z, k, x, y = self.links.place
        send = self.links.send
        for way, origin, there, further in self.steps(step):
            if self.split < self.rows:
                came = self.part_b(way, self.z_at(self.z_b, way, origin), x, origin)
                self.links.do(there, came.wait_recv)
                send(both(there, further), came)
                send(there, self.part_b(ACROSS, self.x_b + origin, x, origin))
            if self.split:
                came = self.half_a(way, self.z_at(self.z_a, way, origin), y, origin, x)
                self.links.do(there, came.wait_recv)
                send(both(there, further), came)
                send(there, self.half_a(ACROSS, self.x_a + origin, y, origin, x))

    def along_x(self, step):
        z, k, x, y = self.links.place
        send = self.links.send
        for way, origin, there, further in self.steps(step):
            if self.split:
                self.links.do(there, self.half_a(ACROSS, self.x_a + origin, y, origin, 1 - x).wait_recv)
                send(there, self.part_a(BESIDE, self.y_a + origin, y, origin))
            if self.split < self.rows:
                self.links.do(there, self.part_b(ACROSS, self.x_b + origin, 1 - x, origin).wait_recv)
            send(there, self.to_core(y, origin))

    def along_y(self, step):
        z, k, x, y = self.links.place
        todo = ((None, z, None, None),) if step < 0 else self.steps(step)
        for way, origin, there, further in todo:
            if self.split:
                self.links.do(there, self.part_a(BESIDE, self.y_a + origin, 1 - y, origin).wait_recv)
            self.links.send(there, self.to_core(1 - y, origin))

    def stages(self):
        found = [[self.begin], [self.cross_y]]
        for step in range(self.layers + 1):
            now = []
            if step < self.layers - 1:
                now.append(functools.partial(self.along_z, step))
            if step == 0:
                now.append(functools.partial(self.along_y, -1))
            if 0 <= step - 1 < self.layers - 1:
                now.append(functools.partial(self.along_x, step - 1))
            if 0 <= step - 2 < self.layers - 1:
                now.append(functools.partial(self.along_y, step - 2))
            found.append(now)
        return found

    def arrived(self):
        self.links.do(None, self.local.wait)
        for layer in range(self.layers):
            for y in range(2):
                self.links.do(None, self.to_core(y, layer, other_core=True).wait_recv)


def ticks_of(links, jobs, starts, begins):
    plans = [job.stages() for job in jobs]
    ticks = [[] for _ in range(max([at + len(plan) for at, plan in zip(starts, plans)]))]
    for start, begin, plan in zip(starts, begins, plans):
        for stage, actions in enumerate(plan):
            ticks[start + stage if stage else begin] += actions
    return [links.record(tick) for tick in ticks]


class Swap:
    def __init__(self, links, source, target, local_sem):
        z, k, x, y = links.place
        self.same, self.other = k == x, k != x
        self.here = pltpu.make_async_copy(source, target, local_sem)
        self.there = links.copy(SWAP, links.take(1), source, target)

    def begin(self):
        pl.when(self.same)(self.here.start)
        pl.when(self.other)(self.there.start)

    def arrived(self):
        pl.when(self.same)(self.here.wait)
        pl.when(self.other)(self.there.wait)


class Cross:
    def __init__(self, links, source, target, local_sem):
        y = links.place[3]
        at = links.take(1)
        self.here = pltpu.make_async_copy(source, target.at[y], local_sem)
        self.out = links.copy(BESIDE, at, source, target.at[y])
        self.back = links.copy(BESIDE, at, source, target.at[1 - y])

    def begin(self):
        self.here.start()
        self.out.start()

    def arrived(self):
        self.here.wait()
        self.out.wait_send()
        self.back.wait_recv()


class Spread:
    def __init__(self, links, block, both_images, local_sem):
        z, k, x, y = links.place
        self.same, self.other = k == x, k != x
        here, first, second = links.take(1), links.take(1), 0
        target = both_images.at[y]
        self.keep = pltpu.make_async_copy(block, target, local_sem)
        self.beside = links.copy(BESIDE, here, block, target)
        self.swap = links.copy(SWAP, first, block, target)
        self.far = links.copy(FAR, here, block, target)
        self.came = links.copy(BESIDE, here, block, both_images.at[1 - y])

    def begin(self):
        def same():
            self.keep.start()
            self.beside.start()

        def other():
            self.swap.start()
            self.far.start()

        pl.when(self.same)(same)
        pl.when(self.other)(other)

    def arrived(self):
        def same():
            self.keep.wait()
            self.beside.wait_send()

        def other():
            self.swap.wait()
            self.far.wait_send()

        pl.when(self.same)(same)
        pl.when(self.other)(other)
        self.came.wait_recv()


def full_shape(layers, kind, piece):
    if kind == ROW:
        return piece[:-2] + (piece[-2] * layers * 2, piece[-1] * 2)
    return (piece[-2] * 2, piece[-1] * layers * 2)


def by_chunks(shape, body):
    rows, cols = shape
    chunk = 16
    while rows % (2 * chunk) == 0 and 2 * chunk * cols <= 16384:
        chunk *= 2

    def step(i, nothing):
        body((pl.ds(pl.multiple_of(i * chunk, 16), chunk), slice(None)))
        return nothing

    lax.fori_loop(0, rows // chunk, step, 0)


def add_into(target, term):
    def body(where):
        target[where] = target[where] + term[where]

    by_chunks(target.shape, body)


def store_sum(out, *terms):
    def body(where):
        total = terms[0][where].astype(jnp.float32)
        for term in terms[1:]:
            total = total + term[where].astype(jnp.float32)
        out[where] = total

    by_chunks(out.shape, body)


class Reduce:
    def __init__(self, layers, links, kind, grad, out, low, split, scratch, local_sem, local_base):
        self.layers, self.links, self.kind, self.grad = layers, links, kind, grad
        self.mine, self.load, self.y_in, self.x_in, self.z_in, self.last = scratch
        self.sent = []
        self.rows, self.cols = self.mine.shape[-2:]
        self.low, self.piece_rows = low, out.shape[0]
        self.out = cut_rows(out, low, self.rows)
        self.split = split
        self.local_sem, self.local_base = local_sem, local_base
        n = layers
        self.core = links.take(2 * n)
        self.y_a, self.x_b = links.take(n), links.take(n)
        self.z_a, self.z_b = links.take(2 * n), links.take(2 * n)
        self.end_a, self.end_b, self.end_c = links.take(1), links.take(1), links.take(1)
        self.order = []
        low, high = 0, layers - 1
        while low <= high:
            self.order.append(high)
            if low < high:
                self.order.append(low)
            low, high = low + 1, high - 1

    @staticmethod
    def sem_count(layers):
        return 8 * layers + 3

    def part_a(self, ref):
        return cut_rows(ref, 0, self.split)

    def part_b(self, ref):
        return cut_rows(ref, self.split, self.rows - self.split)

    def send(self, condition, copy):
        self.links.do(condition, copy.start)
        self.sent.append((condition, copy))

    def finish(self):
        for condition, copy in self.sent:
            when(condition, copy.wait_send)

    def add(self, condition, target, term):
        self.links.do(condition, functools.partial(add_into, target, term))

    def grad_piece(self, y, s):
        return piece_view(
            self.kind, self.piece_rows, self.cols, self.grad, y, s, self.low, self.rows
        )

    def local(self, number):
        k = self.links.place[1]
        layer, y = self.order[number // 2], number % 2
        return pltpu.make_async_copy(
            self.grad_piece(y, 2 * layer + k),
            self.load.at[number % 2],
            self.local_sem.at[self.local_base + number],
        )

    def to_core(self, y, layer):
        k = self.links.place[1]
        return self.links.copy(
            CORE,
            self.core + 2 * layer + y,
            self.grad_piece(y, 2 * layer + 1 - k),
            self.mine.at[y, layer],
        )

    def begin(self):
        for layer in self.order:
            for y in range(2):
                self.send(None, self.to_core(y, layer))
        for number in range(2):
            self.links.do(None, self.local(number).start)

    def to_y(self, layer):
        y = self.links.place[3]
        source = self.part_a(self.mine.at[1 - y, layer])
        return self.links.copy(BESIDE, self.y_a + layer, source, self.y_in.at[layer])

    def to_x(self, layer):
        x = self.links.place[2]
        source = self.part_b(self.mine.at[1 - x, layer])
        return self.links.copy(ACROSS, self.x_b + layer, source, self.x_in.at[layer])

    def chip_sum(self):
        for number in range(2 * self.layers):
            layer, side = self.order[number // 2], number % 2
            self.links.do(None, self.local(number).wait)
            self.links.do(None, self.to_core(side, layer).wait_recv)
            self.add(None, self.mine.at[side, layer], self.load.at[number % 2])
            if number + 2 < 2 * self.layers:
                self.links.do(None, self.local(number + 2).start)
            if side:
                self.send(None, self.to_y(layer))
                self.send(None, self.to_x(layer))

    def plane_sum(self):
        z, k, x, y = self.links.place
        for layer in self.order:
            self.links.do(None, self.to_y(layer).wait_recv)
            self.add(None, self.part_a(self.mine.at[y, layer]), self.y_in.at[layer])
            self.links.do(None, self.to_x(layer).wait_recv)
            self.add(None, self.part_b(self.mine.at[x, layer]), self.x_in.at[layer])

    def chain(self, way, layer, receiver):
        z, k, x, y = self.links.place
        slot = layer if way == UP else jnp.where(receiver == layer, self.layers, layer)
        add = 0 if way == UP else self.layers
        found = []
        for base, part, side in ((self.z_a, self.part_a, y), (self.z_b, self.part_b, x)):
            total, box = part(self.mine.at[side, layer]), part(self.z_in.at[slot])
            found.append((total, box, self.links.copy(way, base + add + layer, total, box)))
        return found

    def take(self, condition, way, layer):
        for total, box, copy in self.chain(way, layer, self.links.place[0]):
            self.links.do(condition, copy.wait_recv)
            self.add(condition, total, box)

    def along_z(self, depth):
        z = self.links.place[0]
        top = self.layers - 1
        for way, here, goals in (
            (UP, z == depth, range(top, depth, -1)),
            (DOWN, z == top - depth, range(0, top - depth)),
        ):
            for layer in goals:
                if depth:
                    self.take(here, way, layer)
                for total, box, copy in self.chain(way, layer, z + 1 if way == UP else z - 1):
                    self.send(here, copy)

    def ending(self):
        z, k, x, y = self.links.place
        self.take(z > 0, UP, z)
        self.take(z < self.layers - 1, DOWN, z)
        self.sum_a, self.sum_b = self.part_a(self.mine.at[y, z]), self.part_b(self.mine.at[x, z])
        self.got_a, self.got_b = self.part_a(self.last.at[0]), self.part_b(self.last.at[0])
        self.got_y = self.part_b(self.last.at[1])
        self.x_end = self.links.copy(ACROSS, self.end_a, self.sum_a, self.got_a)
        self.y_end = self.links.copy(BESIDE, self.end_b, self.sum_b, self.got_y)
        self.x_last = self.links.copy(ACROSS, self.end_c, self.sum_b, self.got_b)
        self.send(y != x, self.y_end)
        self.send(None, self.x_end)

    def owner(self):
        z, k, x, y = self.links.place

        self.links.do(y == x, self.y_end.wait_recv)
        self.add(y == x, self.sum_b, self.got_y)
        self.send(y == x, self.x_last)
        self.links.do(None, self.x_end.wait_recv)
        out_a = self.part_a(self.out)
        self.links.do(None, functools.partial(store_sum, out_a, self.sum_a, self.got_a))

    def write(self):
        z, k, x, y = self.links.place
        out_b = self.part_b(self.out)

        self.links.do(y != x, self.x_last.wait_recv)
        self.links.do(y != x, functools.partial(store_sum, out_b, self.got_b))
        self.links.do(y == x, functools.partial(store_sum, out_b, self.sum_b))

    def stages(self):
        chains = [[functools.partial(self.along_z, depth)] for depth in range(self.layers - 1)]
        return [
            [self.begin], [self.chip_sum], [self.plane_sum], *chains,
            [self.ending], [self.owner], [self.write],
        ]


class Total:
    def __init__(self, layers, links, given, out, boxes, layer_boxes):
        self.layers, self.links, self.given, self.out = layers, links, given, out
        self.boxes, self.layer_boxes = boxes, layer_boxes
        self.pair = [links.take(1) for _ in range(3)]
        self.z_up, self.z_down = links.take(layers), links.take(layers)

    @staticmethod
    def sem_count(layers):
        return 3 + 2 * layers

    def exchange(self, number):
        way = (CORE, ACROSS, BESIDE)[number]
        source = self.given if number == 0 else self.boxes.at[2 + number]
        return self.links.copy(way, self.pair[number], source, self.boxes.at[number])

    def begin(self):
        self.links.send(None, self.exchange(0))

    def join(self, number):
        z = self.links.place[0]
        self.links.do(None, self.exchange(number).wait_recv)
        mine = self.given if number == 0 else self.boxes.at[2 + number]
        result = self.layer_boxes.at[z] if number == 2 else self.boxes.at[3 + number]
        self.links.do(None, functools.partial(store_sum, result, mine, self.boxes.at[number]))
        if number < 2:
            self.links.send(None, self.exchange(number + 1))
        else:
            self.links.send(z < self.layers - 1, self.pass_on(UP, z))
            self.links.send(z > 0, self.pass_on(DOWN, z))

    def pass_on(self, way, layer):
        box = self.layer_boxes.at[layer]
        return self.links.copy(way, (self.z_up if way == UP else self.z_down) + layer, box, box)

    def along_z(self, step):
        z = self.links.place[0]
        top = self.layers - 1
        below, above = z - 1 - step, z + 1 + step
        for way, origin, there, further in (
            (UP, below, below >= 0, z < top),
            (DOWN, above, above <= top, z > 0),
        ):
            copy = self.pass_on(way, origin)
            self.links.do(there, copy.wait_recv)
            self.links.send(both(there, further), copy)

    def write(self):
        layers = [self.layer_boxes.at[layer] for layer in range(self.layers)]
        self.links.do(None, functools.partial(store_sum, self.out, *layers))

    def stages(self):
        joins = [[functools.partial(self.join, number)] for number in range(3)]
        moves = [[functools.partial(self.along_z, step)] for step in range(self.layers - 1)]
        return [[self.begin], *joins, *moves, [self.write]]


def reduce_jobs(layers, links, jobs, grads, outs, scratch, local_sem):
    todo = []
    for number, (mat, kind, low, rows, split) in enumerate(jobs):
        own = scratch[6 * number : 6 * number + 6]
        at = number * 2 * layers
        grad, out = grads[mat], outs[mat]
        todo.append(Reduce(layers, links, kind, grad, out, low, split, own, local_sem, at))
    return todo


def reduce_shapes(layers, rows, cols, split):
    return [
        (2, layers, rows, cols), (2, rows, cols), (layers, split, cols),
        (layers, rows - split, cols), (layers + 1, rows, cols), (2, rows, cols),
    ]


def piece_shape(layers, kind, full):
    if kind == ROW:
        return full[:-2] + (full[-2] // (2 * layers), full[-1] // 2)
    return (full[-2] // 2, full[-1] // (2 * layers))


def pair_lanes(shape, head_size):
    lane = lax.broadcasted_iota(jnp.int32, shape, len(shape) - 1)
    return lane < head_size


def dot_last(left, right):
    return lax.dot_general(left, right, (((1,), (1,)), ((), ())), preferred_element_type=jnp.float32)


def dot_first(left, right):
    return lax.dot_general(left, right, (((0,), (0,)), ((), ())), preferred_element_type=jnp.float32)


def dot(left, right):
    return lax.dot_general(left, right, (((1,), (0,)), ((), ())), preferred_element_type=jnp.float32)


def only_head(values, head, head_size):
    lane = lax.broadcasted_iota(jnp.int32, (1, values.shape[1]), 1)
    keep = (lane < head_size) if head == 0 else (lane >= head_size)
    return values * jnp.where(keep, 1.0, 0.0).astype(values.dtype)


LOG2_E = 1.4426950408889634


def turn_lanes(values, quarter):
    width = values.shape[-1]
    lane = lax.broadcasted_iota(jnp.int32, (1, width), 1)
    even = lax.rem(lax.div(lane, quarter), 2) == 0
    after = pltpu.roll(values, width - quarter, 1)
    before = pltpu.roll(values, quarter, 1)
    return jnp.where(even, -after, before)


def slot_bias(shape, axis, rows, tokens_here, count):
    slot = lax.broadcasted_iota(jnp.int32, shape, axis)
    second = slot >= rows
    within = jnp.where(second, slot - rows, slot)
    token = jnp.where(second, within + tokens_here, within).astype(jnp.float32)
    return jnp.where(jnp.logical_and(within < tokens_here, token < count), 0.0, -1e30)


def front_kernel(layers, head_size, grid_side, *refs):
    (
        vec_own, qkv_own, out_own, gate_own, down_own, tokens, cot, valid, hidden_own,
        vec_full, qkv_full, out_full, gate_full, down_full, hidden_full, cot_out,
        x_out, n_out, q_out, k_out, v_out, o_out, stat_out, vec_out, count_out, cos, sin,
        x, valid_both, vec, weight, hat, normed, q, keys, values, bias,
        send_sem, recv_sem, local_sem,
    ) = refs
    f32, bf16 = jnp.float32, jnp.bfloat16
    place = place_of()
    z, k, me_x, y = place
    greet(layers, place, (SWAP,))
    links = Links(place, send_sem, recv_sem)
    rows, width = x.shape
    tokens_here = valid.shape[1] // 2
    tile = weight.shape[2]
    quarter = head_size // 4
    lanes = 2 * head_size
    locals_used = [0]

    def local_at():
        locals_used[0] += 1
        return local_sem.at[locals_used[0] - 1]

    block = Swap(links, tokens.at[y], x, local_at())
    cot_block = Swap(links, cot.at[y], cot_out, local_at())
    valid_swap = Swap(links, valid, valid_both, local_at())
    cross = Cross(links, hidden_own, hidden_full, local_at())
    out_rows, down_rows = out_own.shape[0], down_own.shape[0] // 2
    todo = [
        (ROW, vec_own, vec_full, 0, vec_own.shape[0], 0),
        (ROW, qkv_own.at[0], qkv_full.at[0], 0, 128, 64),
        (ROW, qkv_own.at[1], qkv_full.at[1], 0, 128, 64),
        (ROW, qkv_own.at[2], qkv_full.at[2], 0, 128, 64),
        (ROW, gate_own.at[0], gate_full.at[0], 0, 64, 32),
        (ROW, gate_own.at[0], gate_full.at[0], 64, 64, 32),
        (ROW, gate_own.at[1], gate_full.at[1], 0, 64, 32),
        (ROW, gate_own.at[1], gate_full.at[1], 64, 64, 32),
        (COL, down_own, down_full, 0, down_rows, 448),
        (COL, down_own, down_full, down_rows, down_rows, 448),
        (COL, out_own, out_full, 0, out_rows, 320),
    ]
    starts = (0, 1, 2, 3, 4, 5, 6, 7, 8, 9, 10)
    begins = (0, 0, 1, 2, 3, 4, 5, 6, 7, 8, 9)
    jobs = [
        Gather(layers, links, kind, own, full, low, size, split, local_at())
        for kind, own, full, low, size, split in todo
    ]
    ticks = ticks_of(links, jobs, starts, begins)
    weight_loads = []
    for mat in range(3):
        for part in range(width // tile):
            slot = len(weight_loads) % 2
            weight_loads.append(
                pltpu.make_async_copy(
                    qkv_full.at[mat, :, pl.ds(part * tile, tile)], weight.at[slot], local_at()
                )
            )
    vec_load = pltpu.make_async_copy(vec_full, vec, local_at())
    keeps = [
        pltpu.make_async_copy(source, target, local_at())
        for source, target in ((x, x_out), (normed, n_out), (q, q_out), (keys, k_out), (values, v_out))
    ]
    shares = []
    my_rows = pl.ds(pl.multiple_of(k * rows, 16), rows)
    other_rows = pl.ds(pl.multiple_of((1 - k) * rows, 16), rows)
    for store in (keys, values):
        for part in range(width // tile):
            at = links.take(1)
            cols = pl.ds(part * tile, tile)
            out_going = links.copy(CORE, at, store.at[my_rows, cols], store.at[my_rows, cols])
            coming = links.copy(CORE, at, store.at[other_rows, cols], store.at[other_rows, cols])
            shares.append((out_going, coming))

    block.begin()
    valid_swap.begin()
    run(ticks[0])
    cot_block.begin()
    cross.begin()
    run(ticks[1])

    block.arrived()
    valid_swap.arrived()
    keeps[0].start()
    chunk = rows // 3

    def normalise(i, nothing):
        at = pl.ds(pl.multiple_of(i * chunk, 16), chunk)
        value, spread = standardize(x[at, :].astype(f32))
        hat[at, :] = value
        return nothing

    lax.fori_loop(0, 3, normalise, 0)
    flags = jnp.where(y == 0, valid_both[0:1, :], valid_both[1:2, :]).astype(f32)
    count = jnp.sum(flags, axis=1, keepdims=True)
    count_out[...] = jnp.broadcast_to(count, count_out.shape)
    columns = (count - 1.0) * (1.0 / grid_side)
    token = lax.broadcasted_iota(jnp.int32, (rows, lanes), 0).astype(f32)
    token = token + (k * tokens_here).astype(f32)
    lane = lax.broadcasted_iota(jnp.int32, (rows, lanes), 1)
    live = jnp.logical_and(token >= 1.0, token < count)
    row_id = jnp.floor((token - 0.5) / columns)
    col_id = token - 1.0 - row_id * columns
    where_at = jnp.where(lax.rem(lane, head_size) < 2 * quarter, row_id, col_id)
    where_at = jnp.where(live, where_at, 0.0)
    power = lax.rem(lane, quarter).astype(f32) * (-math.log(10000.0) / quarter)
    angle = where_at * jnp.exp(power)
    cos[...] = jnp.cos(angle)
    sin[...] = jnp.sin(angle)
    bias[...] = slot_bias(bias.shape, 1, rows, tokens_here, count)

    for tick in ticks[2:8]:
        run(tick)
    jobs[0].arrived()
    vec_load.start()
    vec_load.wait()
    piece_rows = vec_own.shape[0]
    summed = vec[0:piece_rows, :].astype(f32)
    for s in range(1, 2 * layers):
        summed = summed + vec[s * piece_rows : (s + 1) * piece_rows, :].astype(f32)
    vec_out[...] = summed

    def scale(i, nothing):
        at = pl.ds(pl.multiple_of(i * chunk, 16), chunk)
        normed[at, :] = (hat[at, :] * vec_out[4:5, :] + vec_out[6:7, :]).astype(bf16)
        return nothing

    lax.fori_loop(0, 3, scale, 0)
    keeps[1].start()
    repeat = tile // lanes
    per = width // tile
    for mat in range(3):
        run(ticks[8 + mat])
        jobs[1 + mat].arrived()
        for part in range(per):
            weight_loads[mat * per + part].start()
        for part in range(per):
            load = weight_loads[mat * per + part]
            load.wait()
            cols = pl.ds(part * tile, tile)
            raw = dot(normed[...], weight[(mat * per + part) % 2])
            if mat != 1:
                raw = raw + vec_out[0 if mat == 0 else 1 : 1 if mat == 0 else 2, cols]
            if mat < 2:
                turned = turn_lanes(raw, quarter)
                wide_cos = jnp.concatenate([cos[...]] * repeat, axis=1)
                wide_sin = jnp.concatenate([sin[...]] * repeat, axis=1)
                raw = raw * wide_cos + turned * wide_sin
            if mat == 0:
                q[:, cols] = raw.astype(bf16)
            else:
                (keys if mat == 1 else values)[my_rows, cols] = raw.astype(bf16)
                shares[(mat - 1) * per + part][0].start()
    keeps[2].start()
    for out_going, coming in shares:
        out_going.wait_send()
        coming.wait_recv()
    keeps[3].start()
    keeps[4].start()

    late = ticks[11:]
    score_scale = LOG2_E / math.sqrt(head_size)
    pairs = width // lanes

    def mix(i, nothing):
        for number, tick in enumerate(late):
            pl.when(i == number)(functools.partial(run, tick))
        cols = pl.ds(pl.multiple_of(i * lanes, lanes), lanes)
        queries, near_keys, near_values = q[:, cols], keys[:, cols], values[:, cols]
        parts = []
        for head in range(2):
            s = dot_last(only_head(queries, head, head_size), near_keys) * score_scale + bias[...]
            top = jnp.max(s, axis=1, keepdims=True)
            e = jnp.exp2(s - top)
            total = jnp.sum(e, axis=1, keepdims=True)
            parts.append(dot(e.astype(bf16), near_values) * (1.0 / total))
            level = jnp.broadcast_to(top + jnp.log2(total), (rows, 128))
            stat_out[i, head : head + 1, :] = jnp.transpose(level)[0:1, :]
        o_out[:, cols] = jnp.where(pair_lanes((rows, lanes), head_size), parts[0], parts[1])
        return nothing

    lax.fori_loop(0, pairs, mix, 0)
    for tick in late[8:]:
        run(tick)
    for job in jobs[4:]:
        job.arrived()
    cross.arrived()
    cot_block.arrived()
    for keep in keeps:
        keep.wait()
    links.finish()


def front(
    layers, number, head_size, grid_side, vec, qkv, out, gate, down, tokens, cot, valid, hidden
):
    bf16, f32 = jnp.bfloat16, jnp.float32
    rows, width = tokens.shape[1:]
    pairs = width // (2 * head_size)
    tile = 512
    fulls = [
        full_shape(layers, kind, piece.shape)
        for kind, piece in ((ROW, vec), (ROW, qkv), (COL, out), (ROW, gate), (COL, down))
    ]
    shapes = [jax.ShapeDtypeStruct(shape, bf16) for shape in fulls]
    shapes += [jax.ShapeDtypeStruct((2,) + hidden.shape, bf16)]
    shapes += [jax.ShapeDtypeStruct((n * rows, width), bf16) for n in (1, 1, 1, 1, 2, 2)]
    shapes += [
        jax.ShapeDtypeStruct((rows, width), f32),
        jax.ShapeDtypeStruct((pairs, 2, rows), f32),
        jax.ShapeDtypeStruct((vec.shape[0], width), f32),
        jax.ShapeDtypeStruct((8, 128), f32),
        jax.ShapeDtypeStruct((rows, 2 * head_size), f32),
        jax.ShapeDtypeStruct((rows, 2 * head_size), f32),
    ]
    sems = 11 * Gather.sem_count(layers) + 8
    return pl.pallas_call(
        functools.partial(front_kernel, layers, head_size, grid_side),
        out_shape=shapes,
        in_specs=[ANY] * 9,
        out_specs=[ANY] * 12 + [IN_VMEM] * 6,
        scratch_shapes=[
            pltpu.VMEM((rows, width), bf16),
            pltpu.VMEM(valid.shape, valid.dtype),
            pltpu.VMEM(fulls[0], bf16),
            pltpu.VMEM((2, width, tile), bf16),
            pltpu.VMEM((rows, width), f32),
            pltpu.VMEM((rows, width), bf16),
            pltpu.VMEM((rows, width), bf16),
            pltpu.VMEM((2 * rows, width), bf16),
            pltpu.VMEM((2 * rows, width), bf16),
            pltpu.VMEM((1, 2 * rows), f32),
            pltpu.SemaphoreType.DMA((sems,)),
            pltpu.SemaphoreType.DMA((sems,)),
            pltpu.SemaphoreType.DMA((32,)),
        ],
        compiler_params=pltpu.CompilerParams(
            collective_id=number, has_side_effects=True, vmem_limit_bytes=LIMIT
        ),
    )(vec, qkv, out, gate, down, tokens, cot, valid, hidden)


def back_kernel(layers, head_size, tokens_here, jobs, late_jobs, mats, *refs):
    grads, refs = refs[:mats], refs[mats:]
    given_arrays, refs = refs[:9], refs[9:]
    q_in, keys_in, values_in, do_in, mixed_in, n_in, x_in, resid_in, weights = given_arrays
    stats, count, cos, sin, vec, total_in = refs[:6]
    outs, refs = refs[6 : 6 + mats], refs[6 + mats :]
    late_outs, total_out, tokens_out, late_grads = refs[:3], refs[3], refs[4], refs[5:8]
    scratch, refs = refs[8 : 8 + 6 * len(jobs)], refs[8 + 6 * len(jobs) :]
    (
        q, keys, values, do, mixed, k_sum, v_sum, dq_low, dk_low, dv_low, normed_t, d_first,
        d_tokens, bias, total, boxes, layer_boxes, send_sem, recv_sem, local_sem, ready,
    ) = refs
    f32, bf16 = jnp.float32, jnp.bfloat16
    place = place_of()
    z, k, x, y = place
    greet(layers, place, (SWAP, FAR))
    links = Links(place, send_sem, recv_sem)
    first_jobs = reduce_jobs(layers, links, jobs, grads, outs, scratch, local_sem)
    locals_used = [len(jobs) * 2 * layers]

    def local_at():
        locals_used[0] += 1
        return local_sem.at[locals_used[0] - 1]

    second_jobs = []
    for mat, low, rows_here, split, host, first_col in late_jobs:
        cols_here = pl.ds(first_col, late_outs[mat].shape[-1])
        own = []
        for ref in scratch[6 * host : 6 * host + 6]:
            own.append(ref.at[(slice(None),) * (len(ref.shape) - 1) + (cols_here,)])
        second_jobs.append(
            Reduce(
                layers, links, ROW, late_grads[mat], late_outs[mat], low, split, own,
                local_sem, locals_used[0],
            )
        )
        locals_used[0] += 2 * layers
    sums = Total(layers, links, total, total_out, boxes, layer_boxes)
    early, n_late = len(jobs), len(second_jobs)
    handover = early + 5
    late_starts = [handover + number // 2 for number in range(n_late)]
    starts = list(range(early)) + late_starts + [handover + 3]
    begins = [max(0, number - 1) for number in range(early)] + late_starts + [handover + 3]
    ticks = ticks_of(links, first_jobs + second_jobs + [sums], starts, begins)
    spread = Spread(links, d_tokens, tokens_out, local_at())

    rows, width = q.shape
    lanes = 2 * head_size
    pairs = width // lanes
    scale = 1.0 / math.sqrt(head_size)
    quarter = head_size // 4
    my_rows = pl.ds(pl.multiple_of(k * rows, 16), rows)
    other_rows = pl.ds(pl.multiple_of((1 - k) * rows, 16), rows)
    first = links.take(2 * pairs)

    def share(i):
        cols = pl.ds(pl.multiple_of(i * lanes, lanes), lanes)
        return (
            links.copy(CORE, first + 2 * i, k_sum.at[other_rows, cols], dk_low.at[:, cols]),
            links.copy(CORE, first + 2 * i + 1, v_sum.at[other_rows, cols], dv_low.at[:, cols]),
        )

    def turn_back(grad):
        return grad * cos[...] - turn_lanes(grad, quarter) * sin[...]

    def load(source, target):
        copy = pltpu.make_async_copy(source, target, local_at())
        copy.start()
        return copy

    run(ticks[0])
    loads = [
        load(source, target)
        for source, target in (
            (q_in, q), (keys_in, keys), (values_in, values), (do_in, do), (mixed_in, mixed)
        )
    ]
    bias[...] = slot_bias(bias.shape, 0, rows, tokens_here, count[0:1, 0:1])
    total[...] = total_in[...]
    run(ticks[1])
    for copy in loads:
        copy.wait()
    beside = ticks[2 : 2 + pairs]

    def step(i, nothing):
        for number, tick in enumerate(beside):
            pl.when(i == number)(functools.partial(run, tick))
        cols = pl.ds(pl.multiple_of(i * lanes, lanes), lanes)
        queries, near_keys, near_values, grad = q[:, cols], keys[:, cols], values[:, cols], do[:, cols]
        products = jnp.transpose(grad.astype(f32) * mixed[:, cols])
        found = []
        for head in range(2):
            row_dot = products[head * head_size : (head + 1) * head_size]
            row_dot = jnp.sum(row_dot, axis=0, keepdims=True)
            s = dot_last(near_keys, only_head(queries, head, head_size)) * (scale * LOG2_E)
            p = jnp.exp2(s + bias[...] - stats[i, head : head + 1, :])
            dp = dot_last(near_values, only_head(grad, head, head_size))
            ds = (p * (dp - row_dot)).astype(bf16)
            found.append(
                (dot_first(near_keys, ds) * scale, dot(ds, queries) * scale, dot(p.astype(bf16), grad))
            )
        dq = jnp.concatenate([found[0][0][:head_size], found[1][0][head_size:]], axis=0)
        dq = turn_back(jnp.transpose(dq)).astype(bf16)
        dq_low[:, cols] = dq
        total[pl.ds(i, 1), :] = jnp.sum(dq.astype(f32), axis=0, keepdims=True)
        in_first = pair_lanes((2 * rows, lanes), head_size)
        k_sum[:, cols] = jnp.where(in_first, found[0][1], found[1][1]).astype(bf16)
        v_sum[:, cols] = jnp.where(in_first, found[0][2], found[1][2]).astype(bf16)
        for copy in share(i):
            copy.start()
        return nothing

    lax.fori_loop(0, pairs, step, 0)
    normed_load = load(n_in, q)
    loads = [load(weights.at[0], keys.at[pl.ds(0, width)]), load(weights.at[1], values.at[pl.ds(0, width)])]
    loads += [load(x_in, do), load(resid_in, mixed)]
    at_tick = [2 + pairs]

    def advance():
        run(ticks[at_tick[0]])
        at_tick[0] += 1

    def join(i, nothing):
        cols = pl.ds(pl.multiple_of(i * lanes, lanes), lanes)
        for copy in share(i):
            copy.wait()
        dk = k_sum[my_rows, cols].astype(f32) + dk_low[:, cols].astype(f32)
        dk_low[:, cols] = turn_back(dk).astype(bf16)
        dv = v_sum[my_rows, cols].astype(f32) + dv_low[:, cols].astype(f32)
        dv = dv.astype(bf16)
        dv_low[:, cols] = dv
        total[pl.ds(pairs + i, 1), :] = jnp.sum(dv.astype(f32), axis=0, keepdims=True)
        return nothing

    advance()
    lax.fori_loop(0, pairs, join, 0)
    normed_load.wait()
    last_weight = load(weights.at[2], k_sum.at[pl.ds(0, width)])

    def flip(i, nothing):
        at = pl.ds(pl.multiple_of(i * lanes, lanes), lanes)
        normed_t[at, :] = jnp.transpose(q[:, at])
        return nothing

    lax.fori_loop(0, width // lanes, flip, 0)
    while at_tick[0] < handover:
        advance()
    tile = 256
    stores = []

    def weight_grad(mat):
        low_grad = (dq_low, dk_low, dv_low)[mat]
        def part(i, nothing):
            at = pl.ds(pl.multiple_of(i * tile, tile), tile)
            v_sum[at, :] = dot(normed_t[at, :], low_grad[...]).astype(bf16)
            return nothing

        lax.fori_loop(0, width // tile, part, 0)
        stores.append(load(v_sum.at[pl.ds(0, width)], late_grads[mat]))

    weight_grad(0)
    for job in first_jobs[:4]:
        job.finish()
    near = [(None, CORE), (None, ACROSS), (None, BESIDE), (z > 0, DOWN), (z < layers - 1, UP)]
    for condition, way in near:

        def hello(way=way):
            pl.semaphore_signal(
                ready, inc=1, device_id=device(place, way), device_id_type=MESH
            )

        when(condition, hello)
    expected = 3 + jnp.where(z > 0, 1, 0) + jnp.where(z < layers - 1, 1, 0)
    pl.semaphore_wait(ready, expected)
    stores[-1].wait()
    advance()
    for mat in (1, 2):
        weight_grad(mat)
        stores[-1].wait()
        advance()
    for copy in loads + [last_weight]:
        copy.wait()

    def project_back(i, nothing):
        at = pl.ds(pl.multiple_of(i * tile, tile), tile)
        result = dot_last(dq_low[...], keys[at, :])
        result = result + dot_last(dk_low[...], values[at, :])
        d_first[:, at] = result + dot_last(dv_low[...], k_sum[at, :])
        return nothing

    lax.fori_loop(0, width // tile, project_back, 0)
    chunk = rows // 3
    gain = vec[4:5, :]
    gain_sum = jnp.zeros((1, width), f32)
    bias_sum = jnp.zeros((1, width), f32)
    for number in range(3):
        at = pl.ds(number * chunk, chunk)
        hat, inverse = standardize(do[at, :].astype(f32))
        dn = d_first[at, :]
        d_tokens[at, :] = (mixed[at, :] + norm_back(dn * gain, hat, inverse)).astype(bf16)
        gain_sum = gain_sum + jnp.sum(dn * hat, axis=0, keepdims=True)
        bias_sum = bias_sum + jnp.sum(dn, axis=0, keepdims=True)
    for i in range(width // 128):
        cols = slice(i * 128, (i + 1) * 128)
        at = 4 * width // 128 + i
        total[at : at + 1, :] = gain_sum[:, cols]
        at = 6 * width // 128 + i
        total[at : at + 1, :] = bias_sum[:, cols]
    spread.begin()
    while at_tick[0] < len(ticks):
        advance()
    spread.arrived()
    for job in first_jobs[4:] + second_jobs:
        job.finish()
    links.finish()


def back(layers, number, head_size, tokens_here, jobs, late_jobs, grads, given, small, total):
    bf16, f32 = jnp.bfloat16, jnp.float32
    pieces = [piece_shape(layers, kind, g.shape) for kind, g in grads]
    rows, width = given[0].shape
    pairs = width // (2 * head_size)
    sems = (len(jobs) + len(late_jobs)) * Reduce.sem_count(layers) + 2 * pairs
    sems += Total.sem_count(layers) + 2
    late_piece = (width // (2 * layers), width // 2)
    scratch = []
    for mat, kind, low, job_rows, split in jobs:
        shapes = reduce_shapes(layers, job_rows, pieces[mat][-1], split)
        scratch += [pltpu.VMEM(shape, bf16) for shape in shapes]
    half, whole = (rows, width), (2 * rows, width)
    buffers = [(half, bf16), (whole, bf16), (whole, bf16), (half, bf16), (half, f32)]
    buffers += [(whole, bf16)] * 2 + [(half, bf16)] * 3 + [((width, rows), bf16), (half, f32)]
    buffers += [(half, bf16), ((2 * rows, 1), f32), (total.shape, f32)]
    buffers += [((5,) + total.shape, f32), ((layers,) + total.shape, f32)]
    return pl.pallas_call(
        functools.partial(
            back_kernel, layers, head_size, tokens_here, jobs, late_jobs, len(grads)
        ),
        out_shape=[jax.ShapeDtypeStruct(piece, f32) for piece in pieces]
        + [jax.ShapeDtypeStruct(late_piece, f32)] * 3
        + [jax.ShapeDtypeStruct(total.shape, f32)]
        + [jax.ShapeDtypeStruct((2, rows, width), bf16)]
        + [jax.ShapeDtypeStruct((width, width), bf16)] * 3,
        in_specs=[ANY] * (len(grads) + len(given)) + [IN_VMEM] * (len(small) + 1),
        out_specs=[IN_VMEM] * (len(pieces) + 4) + [ANY] * 4,
        scratch_shapes=scratch
        + [pltpu.VMEM(shape, dtype) for shape, dtype in buffers]
        + [
            pltpu.SemaphoreType.DMA((sems,)),
            pltpu.SemaphoreType.DMA((sems,)),
            pltpu.SemaphoreType.DMA(((len(jobs) + len(late_jobs)) * 2 * layers + 16,)),
            pltpu.SemaphoreType.REGULAR,
        ],
        compiler_params=pltpu.CompilerParams(
            collective_id=number, has_side_effects=True, vmem_limit_bytes=62 * 1024 * 1024
        ),
    )(*[g for kind, g in grads], *given, *small, total)


def pad_to(values, axis, size):
    pads = [(0, 0)] * values.ndim
    pads[axis] = (0, size - values.shape[axis])
    return jnp.pad(values, pads)


def round_up(size, step):
    return (size + step - 1) // step * step


def image_per_chip(
    layers,
    tokens,
    cotangent,
    valid_tokens,
    places,
    qkv_weight,
    head_biases,
    head_gain,
    out_weight,
    norm_gains,
    width_biases,
    gate_up,
    hidden_biases,
    hidden_gain,
    down_weight,
):
    f32 = jnp.float32
    bf16 = jnp.bfloat16
    z, k, x, y = place_of()
    s = 2 * z + k
    shards = 2 * layers
    width = tokens.shape[2]
    rows = tokens.shape[1]
    heads_here = head_gain.shape[0]
    heads = 2 * heads_here
    dims_here = head_gain.shape[1]
    head_size = dims_here * shards
    real_here = hidden_gain.shape[0]
    hidden_here = round_up(real_here, 128)
    real = 2 * real_here
    hidden_size = 2 * hidden_here
    score_scale = 1.0 / math.sqrt(head_size)

    padded = round_up(rows, 16)
    heads_own = jnp.concatenate([head_biases, head_gain[None]], axis=0)
    spot = jnp.zeros((4, heads_here, head_size), bf16)
    spot = lax.dynamic_update_slice(spot, heads_own, (0, 0, s * dims_here)).reshape(4, -1)
    width_own = jnp.concatenate([norm_gains, width_biases], axis=0)
    lane_at = s * width_own.shape[1] - y * spot.shape[1]
    inside = both(lane_at >= 0, lane_at < spot.shape[1])
    width_own = jnp.where(inside, width_own, jnp.zeros_like(width_own))
    at = jnp.where(inside, lane_at, 0)
    lanes_own = lax.dynamic_update_slice(jnp.zeros((6, spot.shape[1]), bf16), width_own, (0, at))
    vectors = pad_to(jnp.concatenate([spot, lanes_own], axis=0), 0, 16)
    hidden_vectors = jnp.concatenate([hidden_biases, hidden_gain[None]], axis=0)
    hidden_vectors = pad_to(pad_to(hidden_vectors, 1, hidden_here), 0, 16)
    gate_pad = pad_to(gate_up, 2, hidden_here)
    down_pad = pad_to(down_weight, 0, hidden_here)
    swaps, others = [], []
    for layer in range(layers):
        swaps += [(4 * layer + 1, 4 * layer + 2), (4 * layer + 2, 4 * layer + 1)]
        for spot, far in ((0, 0), (1, 2), (2, 1), (3, 3)):
            for side in range(2):
                others.append((2 * (4 * layer + spot) + side, 2 * (4 * layer + far) + 1 - side))
    (
        vec_full, qkv_full, out_full, gate_full, down_full, hidden_full, cot_block,
        token_block, first_in, queries, keys, values, mixed, stats, vec, count, cos, sin,
    ) = front(
        layers, 0, head_size, 32, vectors, qkv_weight, out_weight, gate_pad, down_pad,
        pad_to(tokens, 1, padded), pad_to(cotangent, 1, padded), valid_tokens, hidden_vectors,
    )
    head_part, norm_scale, width_bias = vec[0:4], vec[4:6], vec[6:10]
    hidden_part = jnp.concatenate([hidden_full[0, :4], hidden_full[1, :4]], axis=1).astype(f32)
    token_rows = token_block.astype(f32)
    cot_rows = cot_block.astype(f32)
    mix_hat, spread_mix = standardize(mixed)
    mix_in = (mix_hat * head_part[3] + head_part[2]).astype(bf16)
    branch = jnp.dot(mix_in, out_full, preferred_element_type=f32)
    resid = token_rows + (branch + width_bias[2])
    normed_two, spread_two = standardize(resid)
    second_in = (normed_two * norm_scale[1] + width_bias[1]).astype(bf16)
    gate_pre = jnp.dot(second_in, gate_full[0], preferred_element_type=f32) + hidden_part[0]
    up_pre = jnp.dot(second_in, gate_full[1], preferred_element_type=f32) + hidden_part[1]
    sigmoid_gate = jax.nn.sigmoid(gate_pre)
    silu_gate = gate_pre * sigmoid_gate
    hidden = silu_gate * up_pre
    hidden_mean = jnp.sum(hidden, axis=-1, keepdims=True) / real
    centred = hidden - hidden_mean
    extra = (hidden_size - real) * hidden_mean * hidden_mean
    hidden_var = (jnp.sum(centred * centred, axis=-1, keepdims=True) - extra) / real
    spread_hid = lax.rsqrt(jnp.maximum(hidden_var, 0.0) + EPS)
    hidden_hat = centred * spread_hid
    down_in = (hidden_hat * hidden_part[3] + hidden_part[2]).astype(bf16)
    down_in = lax.optimization_barrier(down_in)
    ffn_out = jnp.dot(down_in, down_full, preferred_element_type=f32)
    result = (resid + (ffn_out + width_bias[3])).astype(bf16)[:rows]
    result_other = lax.ppermute(result, (SHARD, CTX, TP), others)
    results = (result, result_other, lax.ppermute(result, (SHARD, CTX), swaps))

    g_down = jnp.einsum("tf,td->fd", down_in, cot_block, preferred_element_type=f32)
    d_down_in = jnp.einsum("td,fd->tf", cot_block, down_full, preferred_element_type=f32)
    grad_hid = d_down_in * hidden_part[3]
    hid_back_one = jnp.sum(grad_hid, axis=-1, keepdims=True) / real
    hid_back_two = jnp.sum(grad_hid * hidden_hat, axis=-1, keepdims=True) / real
    d_hidden = (grad_hid - hid_back_one - hidden_hat * hid_back_two) * spread_hid
    d_gate = (d_hidden * up_pre * sigmoid_gate * (1.0 + gate_pre * (1.0 - sigmoid_gate))).astype(
        bf16
    )
    d_up = (d_hidden * silu_gate).astype(bf16)
    g_gate = jnp.einsum("td,tf->df", second_in, d_gate, preferred_element_type=f32).astype(bf16)
    g_up = jnp.einsum("td,tf->df", second_in, d_up, preferred_element_type=f32).astype(bf16)
    d_second = jnp.einsum("tf,df->td", d_gate, gate_full[0], preferred_element_type=f32)
    d_second = d_second + jnp.einsum("tf,df->td", d_up, gate_full[1], preferred_element_type=f32)
    d_resid = cot_rows + norm_back(d_second * norm_scale[1], normed_two, spread_two)
    d_branch_low = d_resid.astype(bf16)
    g_out = jnp.einsum("tm,tn->mn", mix_in, d_branch_low, preferred_element_type=f32)
    d_mix_in = jnp.einsum("tn,mn->tm", d_branch_low, out_full, preferred_element_type=f32)
    d_mixed = norm_back(d_mix_in * head_part[3], mix_hat, spread_mix).astype(bf16)
    vector_grads = jnp.concatenate(
        [
            jnp.zeros((width,), f32),
            jnp.zeros((width,), f32),
            column_sum(d_mix_in),
            column_sum(d_mix_in * mix_hat),
            jnp.zeros((width,), f32),
            column_sum(d_second * normed_two),
            jnp.zeros((width,), f32),
            column_sum(d_second),
            column_sum(d_branch_low),
            column_sum(cot_block),
            column_sum(d_gate),
            column_sum(d_up),
            column_sum(d_down_in),
            column_sum(d_down_in * hidden_hat),
        ]
    ).reshape(-1, 128)
    vector_grads = pad_to(vector_grads, 0, round_up(vector_grads.shape[0], 16))
    result, result_other, swapped, d_mixed = lax.optimization_barrier((*results, d_mixed))
    result = jnp.where(k == x, result, swapped)
    result = jnp.stack(
        [jnp.where(y == 0, result, result_other), jnp.where(y == 0, result_other, result)], axis=1
    ).transpose(1, 0, 2)
    half = hidden_here // 2
    heads_rows = heads_here * head_size
    grad_jobs = (
        (0, ROW, 0, 64, 32), (0, ROW, 64, 64, 32), (1, ROW, 0, 64, 32), (1, ROW, 64, 64, 32),
        (2, COL, 0, half, half // 2), (2, COL, half, half, half // 2),
        (3, COL, 0, heads_rows, heads_rows // 2),
    )
    late_jobs = (
        (0, 0, 64, 32, 0, 0), (0, 64, 64, 32, 1, 0),
        (1, 0, 64, 32, 0, heads_rows), (1, 64, 64, 32, 1, heads_rows),
        (2, 0, 64, 32, 2, 0), (2, 64, 64, 32, 3, 0),
    )
    back_grads = (
        (ROW, g_gate), (ROW, g_up), (COL, g_down.astype(bf16)), (COL, g_out.astype(bf16))
    )
    (
        gate_piece, up_piece, down_piece, out_piece, query_piece, key_piece, value_piece,
        vector_grads, d_tokens, *unused,
    ) = back(
        layers, 1, head_size, rows, grad_jobs, late_jobs, back_grads,
        (queries, keys, values, d_mixed, mixed, first_in, token_block, d_resid, qkv_full),
        (stats, count, cos, sin, vec), vector_grads,
    )
    d_tokens = jnp.stack([d_tokens[0, :rows], d_tokens[1, :rows]], axis=1).transpose(1, 0, 2)
    vector_grads = vector_grads.reshape(-1)
    head_sums = vector_grads[: 4 * width].reshape(4, heads, head_size)
    head_sums = lax.dynamic_slice(
        head_sums, (0, y * heads_here, s * dims_here), (4, heads_here, dims_here)
    )
    width_sums = vector_grads[4 * width : 10 * width].reshape(6, width)
    width_sums = lax.dynamic_slice(width_sums, (0, s * 128), (6, width // shards))
    hidden_sums = vector_grads[10 * width : 10 * width + 4 * hidden_size]
    hidden_sums = hidden_sums.reshape(4, hidden_size)
    hidden_sums = lax.dynamic_slice(hidden_sums, (0, y * hidden_here), (4, hidden_here))
    hidden_sums = hidden_sums[:, :real_here]

    return (
        result,
        d_tokens.astype(f32),
        jnp.stack([query_piece, key_piece, value_piece]),
        head_sums[:3],
        head_sums[3],
        out_piece,
        width_sums[:2],
        width_sums[2:],
        jnp.stack([gate_piece[:, :real_here], up_piece[:, :real_here]]),
        hidden_sums[:3],
        hidden_sums[3],
        down_piece[:real_here],
    )


def solution(mesh):
    small = mesh.shape[CTX] == 2 and mesh.shape[TP] == 2
    body = functools.partial(image_per_chip, mesh.shape[SHARD] // 2) if small else general_plan

    return jax.shard_map(
        body,
        mesh=mesh,
        in_specs=(
            P(SHARD, CTX, None),
            P(SHARD, CTX, None),
            P(SHARD, None),
            P(None, SHARD, CTX),
            P(None, SHARD, TP),
            P(None, TP, SHARD),
            P(TP, SHARD),
            P(TP, SHARD),
            P(None, SHARD),
            P(None, SHARD),
            P(None, SHARD, TP),
            P(None, TP),
            P(TP),
            P(TP, SHARD),
        ),
        out_specs=(
            P(SHARD, CTX, None),
            P(SHARD, CTX, None),
            P(None, SHARD, TP),
            P(None, TP, SHARD),
            P(TP, SHARD),
            P(TP, SHARD),
            P(None, SHARD),
            P(None, SHARD),
            P(None, SHARD, TP),
            P(None, TP),
            P(TP),
            P(TP, SHARD),
        ),
        check_vma=False,
    )
```

```python
import functools
import math

import jax
import jax.numpy as jnp
from jax import lax
from jax.experimental import pallas as pl
from jax.experimental.pallas import tpu as pltpu
from jax.sharding import PartitionSpec as P

SHARD, CTX, TP = "shard", "ctx", "tp"


EPS = 1e-06


def standardize(values):
    average = jnp.mean(values, axis=-1, keepdims=True)
    centred = values - average
    spread = lax.rsqrt(jnp.mean(centred * centred, axis=-1, keepdims=True) + EPS)
    return (centred * spread, spread)


def norm_back(grad_hat, normed, spread):
    mean_one = jnp.mean(grad_hat, axis=-1, keepdims=True)
    mean_two = jnp.mean(grad_hat * normed, axis=-1, keepdims=True)
    return (grad_hat - mean_one - normed * mean_two) * spread


def angle_table(row_ids, col_ids, head_size):
    quarter = head_size // 4
    frequency = 10000.0 ** (-jnp.arange(quarter, dtype=jnp.float32) / quarter)
    row_part = row_ids.astype(jnp.float32)[:, None] * frequency[None, :]
    col_part = col_ids.astype(jnp.float32)[:, None] * frequency[None, :]
    return jnp.concatenate([row_part, row_part, col_part, col_part], axis=1)


def turn_half(values):
    quarter = values.shape[-1] // 4
    part_one = values[..., :quarter]
    part_two = values[..., quarter : 2 * quarter]
    part_three = values[..., 2 * quarter : 3 * quarter]
    part_four = values[..., 3 * quarter :]
    return jnp.concatenate([-part_two, part_one, -part_four, part_three], axis=-1)


def rotate(values, angles):
    return values * jnp.cos(angles)[None, :, :] + turn_half(values) * jnp.sin(angles)[None, :, :]


def unrotate(values, angles):
    return values * jnp.cos(angles)[None, :, :] - turn_half(values) * jnp.sin(angles)[None, :, :]


def head_major(values, heads, head_size):
    return values.reshape(values.shape[0], heads, head_size).transpose(1, 0, 2)


def column_sum(values):
    return jnp.sum(values.astype(jnp.float32), axis=0)


def general_plan(
    tokens,
    cotangent,
    valid_tokens,
    places,
    qkv_weight,
    head_biases,
    head_gain,
    out_weight,
    norm_gains,
    width_biases,
    gate_up,
    hidden_biases,
    hidden_gain,
    down_weight,
):
    micro = tokens.shape[0]
    width = tokens.shape[2]
    local_dim = qkv_weight.shape[2]
    local_heads = head_biases.shape[1]
    head_size = local_dim // local_heads
    local_hidden = hidden_gain.shape[0]
    FF = local_hidden * lax.axis_size(TP)
    score_scale = 1.0 / math.sqrt(head_size)
    f32 = jnp.float32
    bf16 = jnp.bfloat16

    def one_batch(batch_idx, carried):
        gathered = (
            lax.all_gather(qkv_weight, SHARD, axis=1, tiled=True),
            lax.all_gather(head_biases, SHARD, axis=2, tiled=True),
            lax.all_gather(head_gain, SHARD, axis=1, tiled=True),
            lax.all_gather(out_weight, SHARD, axis=1, tiled=True),
            lax.all_gather(norm_gains, SHARD, axis=1, tiled=True),
            lax.all_gather(width_biases, SHARD, axis=1, tiled=True),
            lax.all_gather(gate_up, SHARD, axis=1, tiled=True),
            lax.all_gather(down_weight, SHARD, axis=1, tiled=True),
        )
        qkv_full, head_bias, head_scale, out_full, norm_scale, width_bias, gate_full, down_full = (
            gathered
        )
        head_bias_f = head_bias.astype(f32)
        head_scale_f = head_scale.astype(f32)[:, None, :]
        norm_scale = norm_scale.astype(f32)
        width_bias = width_bias.astype(f32)
        hidden_bias = hidden_biases.astype(f32)
        hidden_scale = hidden_gain.astype(f32)
        out_heads = out_full.reshape(local_heads, head_size, width)
        token_rows = lax.dynamic_index_in_dim(tokens, batch_idx, 0, keepdims=False).astype(f32)
        cot_rows = lax.dynamic_index_in_dim(cotangent, batch_idx, 0, keepdims=False).astype(f32)
        valid_row = lax.dynamic_index_in_dim(valid_tokens, batch_idx, 0, keepdims=False) > 0
        row_ids = lax.dynamic_index_in_dim(places[0], batch_idx, 0, keepdims=False)
        col_ids = lax.dynamic_index_in_dim(places[1], batch_idx, 0, keepdims=False)
        angles = angle_table(row_ids, col_ids, head_size)
        normed_one, spread_one = standardize(token_rows)
        first_in = (normed_one * norm_scale[0] + width_bias[0]).astype(bf16)
        query_flat = jnp.dot(first_in, qkv_full[0], preferred_element_type=f32)
        key_flat = jnp.dot(first_in, qkv_full[1], preferred_element_type=f32)
        value_flat = jnp.dot(first_in, qkv_full[2], preferred_element_type=f32)
        query_pre = head_major(query_flat, local_heads, head_size) + head_bias_f[0][:, None, :]
        key_pre = head_major(key_flat, local_heads, head_size)
        value_local = (
            head_major(value_flat, local_heads, head_size) + head_bias_f[1][:, None, :]
        ).astype(bf16)
        queries = rotate(query_pre, angles).astype(bf16)
        key_local = rotate(key_pre, angles).astype(bf16)
        key_heads, value_heads = (
            lax.all_gather(key_local, CTX, axis=1, tiled=True),
            lax.all_gather(value_local, CTX, axis=1, tiled=True),
        )

        def score_block():
            raw = (
                jnp.einsum("htd,hsd->hts", queries, key_heads, preferred_element_type=f32)
                * score_scale
            )
            return jnp.where(valid_row[None, None, :], raw, -1e30)

        scores = score_block()
        row_top = jnp.max(scores, axis=-1, keepdims=True)
        row_total = jnp.sum(jnp.exp(scores - row_top), axis=-1, keepdims=True)
        soft_low = (jnp.exp(scores - row_top) / row_total).astype(bf16)
        mixed = jnp.einsum("hts,hsd->htd", soft_low, value_heads, preferred_element_type=f32)
        mix_sums = lax.psum(
            (
                jnp.sum(mixed, axis=(0, 2), keepdims=True),
                jnp.sum(mixed * mixed, axis=(0, 2), keepdims=True),
            ),
            TP,
        )
        mix_mean = mix_sums[0] / width
        spread_mix = lax.rsqrt(mix_sums[1] / width - mix_mean * mix_mean + EPS)
        mix_hat = (mixed - mix_mean) * spread_mix
        mix_in = (mix_hat * head_scale_f + head_bias_f[2][:, None, :]).astype(bf16)
        branch = lax.psum(
            jnp.einsum("htd,hdn->tn", mix_in, out_heads, preferred_element_type=f32), TP
        )
        resid = token_rows + (branch + width_bias[2])
        normed_two, spread_two = standardize(resid)
        second_in = (normed_two * norm_scale[1] + width_bias[1]).astype(bf16)
        gate_pre = jnp.dot(second_in, gate_full[0], preferred_element_type=f32) + hidden_bias[0]
        up_pre = jnp.dot(second_in, gate_full[1], preferred_element_type=f32) + hidden_bias[1]
        sigmoid_gate = jax.nn.sigmoid(gate_pre)
        silu_gate = gate_pre * sigmoid_gate
        hidden = silu_gate * up_pre
        hidden_sums = lax.psum(
            (
                jnp.sum(hidden, axis=-1, keepdims=True),
                jnp.sum(hidden * hidden, axis=-1, keepdims=True),
            ),
            TP,
        )
        hidden_mean = hidden_sums[0] / FF
        spread_hid = lax.rsqrt(hidden_sums[1] / FF - hidden_mean * hidden_mean + EPS)
        hidden_hat = (hidden - hidden_mean) * spread_hid
        down_in = (hidden_hat * hidden_scale + hidden_bias[2]).astype(bf16)
        ffn_out = lax.psum(
            jnp.dot(down_in, down_full, preferred_element_type=f32).astype(jnp.bfloat16), TP
        ).astype(jnp.float32)
        result = (resid + (ffn_out + width_bias[3])).astype(bf16)
        d_ffn_low = cot_rows.astype(bf16)
        g_down = jnp.einsum("tf,td->fd", down_in, d_ffn_low, preferred_element_type=f32)
        d_down_in = jnp.einsum("td,fd->tf", d_ffn_low, down_full, preferred_element_type=f32)
        grad_hid = d_down_in * hidden_scale
        hid_back = lax.psum(
            (
                jnp.sum(grad_hid, axis=-1, keepdims=True),
                jnp.sum(grad_hid * hidden_hat, axis=-1, keepdims=True),
            ),
            TP,
        )
        d_hidden = (grad_hid - hid_back[0] / FF - hidden_hat * (hid_back[1] / FF)) * spread_hid
        d_gate = (
            d_hidden * up_pre * sigmoid_gate * (1.0 + gate_pre * (1.0 - sigmoid_gate))
        ).astype(bf16)
        d_up = (d_hidden * silu_gate).astype(bf16)
        g_gate_one = jnp.einsum("td,tf->df", second_in, d_gate, preferred_element_type=f32)
        g_up_one = jnp.einsum("td,tf->df", second_in, d_up, preferred_element_type=f32)
        d_second_part = jnp.einsum(
            "tf,df->td", d_gate, gate_full[0], preferred_element_type=f32
        ) + jnp.einsum("tf,df->td", d_up, gate_full[1], preferred_element_type=f32)
        d_second = lax.psum(d_second_part, TP)
        d_resid = cot_rows + norm_back(d_second * norm_scale[1], normed_two, spread_two)
        d_branch_low = d_resid.astype(bf16)
        g_out = jnp.einsum("htd,tn->hdn", mix_in, d_branch_low, preferred_element_type=f32).reshape(
            local_dim, width
        )
        d_mix_in = jnp.einsum("tn,hdn->htd", d_branch_low, out_heads, preferred_element_type=f32)
        grad_mix = d_mix_in * head_scale_f
        mix_back = lax.psum(
            (
                jnp.sum(grad_mix, axis=(0, 2), keepdims=True),
                jnp.sum(grad_mix * mix_hat, axis=(0, 2), keepdims=True),
            ),
            TP,
        )
        d_mixed = (
            (grad_mix - mix_back[0] / width - mix_hat * (mix_back[1] / width)) * spread_mix
        ).astype(bf16)
        again = score_block()
        weights_soft = jnp.exp(again - row_top) / row_total
        d_soft = jnp.einsum("htd,hsd->hts", d_mixed, value_heads, preferred_element_type=f32)
        row_dot = jnp.sum(weights_soft * d_soft, axis=-1, keepdims=True)
        d_scores = (weights_soft * (d_soft - row_dot)).astype(bf16)
        d_query = (
            jnp.einsum("hts,hsd->htd", d_scores, key_heads, preferred_element_type=f32)
            * score_scale
        )
        soft_again = weights_soft.astype(bf16)
        d_key_all = (
            jnp.einsum("hts,htd->hsd", d_scores, queries, preferred_element_type=f32) * score_scale
        )
        d_value_all = jnp.einsum("hts,htd->hsd", soft_again, d_mixed, preferred_element_type=f32)
        d_key_heads, d_value_loc = (
            lax.psum_scatter(
                d_key_all.astype(jnp.bfloat16), CTX, scatter_dimension=1, tiled=True
            ).astype(jnp.float32),
            lax.psum_scatter(
                d_value_all.astype(jnp.bfloat16), CTX, scatter_dimension=1, tiled=True
            ).astype(jnp.float32),
        )
        d_query_low = unrotate(d_query, angles).astype(bf16)
        d_key_low = unrotate(d_key_heads, angles).astype(bf16)
        d_value_low = d_value_loc.astype(bf16)
        g_query = jnp.einsum(
            "tn,htd->nhd", first_in, d_query_low, preferred_element_type=f32
        ).reshape(width, local_dim)
        g_key = jnp.einsum("tn,htd->nhd", first_in, d_key_low, preferred_element_type=f32).reshape(
            width, local_dim
        )
        g_value = jnp.einsum(
            "tn,htd->nhd", first_in, d_value_low, preferred_element_type=f32
        ).reshape(width, local_dim)
        d_first_part = jnp.einsum(
            "htd,nhd->tn",
            d_query_low,
            qkv_full[0].reshape(width, local_heads, head_size),
            preferred_element_type=f32,
        )
        d_first_part = d_first_part + jnp.einsum(
            "htd,nhd->tn",
            d_key_low,
            qkv_full[1].reshape(width, local_heads, head_size),
            preferred_element_type=f32,
        )
        d_first_part = d_first_part + jnp.einsum(
            "htd,nhd->tn",
            d_value_low,
            qkv_full[2].reshape(width, local_heads, head_size),
            preferred_element_type=f32,
        )
        d_first = lax.psum(d_first_part.astype(jnp.bfloat16), TP).astype(jnp.float32)
        d_tokens = d_resid + norm_back(d_first * norm_scale[0], normed_one, spread_one)
        g_head_bias = jnp.stack(
            [
                jnp.sum(d_query_low.astype(f32), axis=1),
                jnp.sum(d_value_low.astype(f32), axis=1),
                jnp.sum(d_mix_in, axis=1),
            ]
        )
        g_head_scale = jnp.sum(d_mix_in * mix_hat, axis=1)
        g_norm = jnp.stack([column_sum(d_first * normed_one), column_sum(d_second * normed_two)])
        g_width = jnp.stack(
            [
                column_sum(d_first),
                column_sum(d_second),
                column_sum(d_branch_low),
                column_sum(d_ffn_low),
            ]
        )
        g_hidden_bias = jnp.stack([column_sum(d_gate), column_sum(d_up), column_sum(d_down_in)])
        g_hidden_scale = column_sum(d_down_in * hidden_hat)
        out_all = lax.dynamic_update_index_in_dim(carried[0], result, batch_idx, 0)
        grad_all = lax.dynamic_update_index_in_dim(carried[1], d_tokens, batch_idx, 0)
        updates = (
            g_query,
            g_key,
            g_value,
            g_head_bias,
            g_head_scale,
            g_out,
            g_norm,
            g_width,
            g_gate_one,
            g_up_one,
            g_down,
            g_hidden_bias,
            g_hidden_scale,
        )
        return (
            out_all,
            grad_all,
            tuple((before + added for before, added in zip(carried[2], updates))),
        )

    zeros_acc = (
        jnp.zeros((width, local_dim), f32),
        jnp.zeros((width, local_dim), f32),
        jnp.zeros((width, local_dim), f32),
        jnp.zeros((3, local_heads, head_size), f32),
        jnp.zeros((local_heads, head_size), f32),
        jnp.zeros((local_dim, width), f32),
        jnp.zeros((2, width), f32),
        jnp.zeros((4, width), f32),
        jnp.zeros((width, local_hidden), f32),
        jnp.zeros((width, local_hidden), f32),
        jnp.zeros((local_hidden, width), f32),
        jnp.zeros((3, local_hidden), f32),
        jnp.zeros((local_hidden,), f32),
    )
    start = (jnp.zeros(tokens.shape, bf16), jnp.zeros(tokens.shape, f32), zeros_acc)
    out_all, grad_all, summed = lax.fori_loop(0, micro, one_batch, start)
    (
        acc_query,
        acc_key,
        acc_value,
        acc_head_bias,
        acc_head_scale,
        acc_out,
        acc_norm,
        acc_width,
        acc_gate_one,
        acc_up_one,
        acc_down,
        acc_hidden_bias,
        acc_hidden_scale,
    ) = summed
    acc_qkv = jnp.stack([acc_query, acc_key, acc_value])
    acc_gate = jnp.stack([acc_gate_one, acc_up_one])
    sharded = (
        acc_qkv,
        acc_head_bias,
        acc_head_scale,
        acc_out,
        acc_norm,
        acc_width,
        acc_gate,
        acc_down,
    )
    hidden_done = lax.psum((acc_hidden_bias, acc_hidden_scale), (SHARD, CTX))
    return (
        out_all,
        grad_all,
        lax.psum_scatter(
            lax.psum(sharded[0].astype(jnp.bfloat16), CTX),
            SHARD,
            scatter_dimension=1,
            tiled=True,
        ).astype(jnp.float32),
        lax.psum_scatter(
            lax.psum(sharded[1].astype(jnp.bfloat16), CTX),
            SHARD,
            scatter_dimension=2,
            tiled=True,
        ).astype(jnp.float32),
        lax.psum_scatter(
            lax.psum(sharded[2].astype(jnp.bfloat16), CTX),
            SHARD,
            scatter_dimension=1,
            tiled=True,
        ).astype(jnp.float32),
        lax.psum_scatter(
            lax.psum(sharded[3].astype(jnp.bfloat16), CTX),
            SHARD,
            scatter_dimension=1,
            tiled=True,
        ).astype(jnp.float32),
        lax.psum_scatter(
            lax.psum(sharded[4].astype(jnp.bfloat16), CTX),
            SHARD,
            scatter_dimension=1,
            tiled=True,
        ).astype(jnp.float32),
        lax.psum_scatter(
            lax.psum(sharded[5].astype(jnp.bfloat16), CTX),
            SHARD,
            scatter_dimension=1,
            tiled=True,
        ).astype(jnp.float32),
        lax.psum_scatter(
            lax.psum(sharded[6].astype(jnp.bfloat16), CTX),
            SHARD,
            scatter_dimension=1,
            tiled=True,
        ).astype(jnp.float32),
        hidden_done[0],
        hidden_done[1],
        lax.psum_scatter(
            lax.psum(sharded[7].astype(jnp.bfloat16), CTX),
            SHARD,
            scatter_dimension=1,
            tiled=True,
        ).astype(jnp.float32),
    )


MESH = pl.DeviceIdType.MESH
LIMIT = 56 * 1024 * 1024
ANY = pl.BlockSpec(memory_space=pl.ANY)
IN_VMEM = pl.BlockSpec(memory_space=pltpu.VMEM)
CORE, ACROSS, BESIDE, UP, DOWN, SWAP, FAR = range(7)
ROW, COL = range(2)


def place_of():
    index = lax.axis_index(SHARD)
    return (lax.div(index, 2), lax.rem(index, 2), lax.axis_index(CTX), lax.axis_index(TP))


def when(condition, action):
    if condition is None:
        action()
    else:
        pl.when(condition)(action)


def both(first, second):
    return jnp.logical_and(first, second)


def device(place, way):
    z, k, x, y = place
    return {
        CORE: {SHARD: 2 * z + 1 - k},
        ACROSS: {CTX: 1 - x},
        BESIDE: {TP: 1 - y},
        UP: {SHARD: 2 * z + 2 + k},
        DOWN: {SHARD: 2 * z - 2 + k},
        SWAP: {SHARD: 2 * z + 1 - k, CTX: 1 - x},
        FAR: {SHARD: 2 * z + 1 - k, CTX: 1 - x, TP: 1 - y},
    }[way]


def greet(layers, place, diagonals):
    z, k, x, y = place
    barrier = pltpu.get_barrier_semaphore()

    def hello(way):
        pl.semaphore_signal(barrier, inc=1, device_id=device(place, way), device_id_type=MESH)

    hello(CORE)
    hello(ACROSS)
    hello(BESIDE)
    pl.when(z > 0)(lambda: hello(DOWN))
    pl.when(z < layers - 1)(lambda: hello(UP))
    count = 3 + jnp.where(z > 0, 1, 0) + jnp.where(z < layers - 1, 1, 0)
    for way in diagonals:
        pl.when(k != x)(lambda way=way: hello(way))
        count = count + jnp.where(k != x, 1, 0)
    pl.semaphore_wait(barrier, count)


class Links:
    def __init__(self, place, send_sem, recv_sem):
        self.place, self.send_sem, self.recv_sem = place, send_sem, recv_sem
        self.used = 0
        self.sent = []
        self.noted = None

    def take(self, count):
        first = self.used
        self.used += count
        return first

    def copy(self, way, at, source, target):
        return pltpu.make_async_remote_copy(
            src_ref=source,
            dst_ref=target,
            send_sem=self.send_sem.at[at],
            recv_sem=self.recv_sem.at[at],
            device_id=device(self.place, way),
            device_id_type=MESH,
        )

    def do(self, condition, action):
        if self.noted is None:
            when(condition, action)
        else:
            self.noted.append((condition, action))

    def record(self, actions):
        self.noted = []
        for action in actions:
            action()
        found, self.noted = self.noted, None
        return found

    def send(self, condition, copy):
        self.do(condition, copy.start)
        self.sent.append((condition, copy))

    def finish(self):
        for condition, copy in self.sent:
            when(condition, copy.wait_send)


def run(noted):
    for condition, action in noted:
        when(condition, action)


def piece_view(kind, rows, cols, ref, y, s, first, size):
    if kind == ROW:
        at_row, at_col = s * rows + first, y * cols
    else:
        at_row, at_col = y * rows + first, s * cols
    at_row, at_col = pl.multiple_of(at_row, 16), pl.multiple_of(at_col, 128)
    return ref.at[pl.ds(at_row, size), pl.ds(at_col, cols)]


def cut_rows(ref, first, size):
    return ref.at[pl.ds(pl.multiple_of(first, 16), size), :]


class Gather:
    def __init__(self, layers, links, kind, own, full, low, rows, split, local_sem):
        self.layers, self.links, self.kind, self.own, self.full = layers, links, kind, own, full
        self.piece_rows, self.cols = own.shape
        self.low, self.rows = low, rows
        self.split, self.half = split, split // 2
        self.local_sem = local_sem
        n = layers
        self.z_a = links.take(2 * n)
        self.z_b = links.take(2 * n)
        self.x_a, self.x_b = links.take(n), links.take(n)
        self.y_a, self.y_b = links.take(n), links.take(1)
        self.core = links.take(2 * n)

    @staticmethod
    def sem_count(layers):
        return 9 * layers + 1

    def copy(self, way, at, y, z, first, size, from_own=False, other_core=False):
        k = self.links.place[1]
        s = 2 * z + (1 - k if other_core else k)
        first = first + self.low
        there = piece_view(self.kind, self.piece_rows, self.cols, self.full, y, s, first, size)
        here = cut_rows(self.own, first, size) if from_own else there
        return self.links.copy(way, at, here, there)

    def half_a(self, way, at, y, z, which, from_own=False):
        return self.copy(way, at, y, z, which * self.half, self.half, from_own)

    def part_a(self, way, at, y, z, from_own=False):
        return self.copy(way, at, y, z, 0, self.split, from_own)

    def part_b(self, way, at, y, z, from_own=False):
        return self.copy(way, at, y, z, self.split, self.rows - self.split, from_own)

    def to_core(self, y, z, from_own=False, other_core=False):
        return self.copy(CORE, self.core + 2 * z + y, y, z, 0, self.rows, from_own, other_core)

    def z_at(self, base, way, z):
        return base + (0 if way == UP else self.layers) + z

    def begin(self):
        z, k, x, y = self.links.place
        send = self.links.send
        low, high = z > 0, z < self.layers - 1
        own_view = piece_view(
            self.kind, self.piece_rows, self.cols, self.full, y, 2 * z + k, self.low, self.rows
        )
        own = cut_rows(self.own, self.low, self.rows)
        self.local = pltpu.make_async_copy(own, own_view, self.local_sem)
        if self.split < self.rows:
            send(None, self.part_b(BESIDE, self.y_b, y, z, True))
            same = x == y
            send(both(same, high), self.part_b(UP, self.z_at(self.z_b, UP, z), y, z, True))
            send(both(same, low), self.part_b(DOWN, self.z_at(self.z_b, DOWN, z), y, z, True))
        if self.split:
            send(high, self.half_a(UP, self.z_at(self.z_a, UP, z), y, z, x, True))
            send(low, self.half_a(DOWN, self.z_at(self.z_a, DOWN, z), y, z, x, True))
            send(None, self.part_a(BESIDE, self.y_a + z, y, z, True))
        send(None, self.to_core(y, z, True))
        self.links.do(None, self.local.start)

    def cross_y(self):
        if self.split == self.rows:
            return
        z, k, x, y = self.links.place
        send = self.links.send
        self.links.do(None, self.part_b(BESIDE, self.y_b, 1 - y, z).wait_recv)
        other = x != y
        low, high = z > 0, z < self.layers - 1
        send(both(other, high), self.part_b(UP, self.z_at(self.z_b, UP, z), 1 - y, z))
        send(both(other, low), self.part_b(DOWN, self.z_at(self.z_b, DOWN, z), 1 - y, z))

    def steps(self, step):
        z = self.links.place[0]
        below, above = z - 1 - step, z + 1 + step
        return (
            (UP, below, below >= 0, z < self.layers - 1),
            (DOWN, above, above <= self.layers - 1, z > 0),
        )

    def along_z(self, step):
        z, k, x, y = self.links.place
        send = self.links.send
        for way, origin, there, further in self.steps(step):
            if self.split < self.rows:
                came = self.part_b(way, self.z_at(self.z_b, way, origin), x, origin)
                self.links.do(there, came.wait_recv)
                send(both(there, further), came)
                send(there, self.part_b(ACROSS, self.x_b + origin, x, origin))
            if self.split:
                came = self.half_a(way, self.z_at(self.z_a, way, origin), y, origin, x)
                self.links.do(there, came.wait_recv)
                send(both(there, further), came)
                send(there, self.half_a(ACROSS, self.x_a + origin, y, origin, x))

    def along_x(self, step):
        z, k, x, y = self.links.place
        send = self.links.send
        for way, origin, there, further in self.steps(step):
            if self.split:
                self.links.do(there, self.half_a(ACROSS, self.x_a + origin, y, origin, 1 - x).wait_recv)
                send(there, self.part_a(BESIDE, self.y_a + origin, y, origin))
            if self.split < self.rows:
                self.links.do(there, self.part_b(ACROSS, self.x_b + origin, 1 - x, origin).wait_recv)
            send(there, self.to_core(y, origin))

    def along_y(self, step):
        z, k, x, y = self.links.place
        todo = ((None, z, None, None),) if step < 0 else self.steps(step)
        for way, origin, there, further in todo:
            if self.split:
                self.links.do(there, self.part_a(BESIDE, self.y_a + origin, 1 - y, origin).wait_recv)
            self.links.send(there, self.to_core(1 - y, origin))

    def stages(self):
        found = [[self.begin], [self.cross_y]]
        for step in range(self.layers + 1):
            now = []
            if step < self.layers - 1:
                now.append(functools.partial(self.along_z, step))
            if step == 0:
                now.append(functools.partial(self.along_y, -1))
            if 0 <= step - 1 < self.layers - 1:
                now.append(functools.partial(self.along_x, step - 1))
            if 0 <= step - 2 < self.layers - 1:
                now.append(functools.partial(self.along_y, step - 2))
            found.append(now)
        return found

    def arrived(self):
        self.links.do(None, self.local.wait)
        for layer in range(self.layers):
            for y in range(2):
                self.links.do(None, self.to_core(y, layer, other_core=True).wait_recv)


def ticks_of(links, jobs, starts, begins):
    plans = [job.stages() for job in jobs]
    ticks = [[] for _ in range(max([at + len(plan) for at, plan in zip(starts, plans)]))]
    for start, begin, plan in zip(starts, begins, plans):
        for stage, actions in enumerate(plan):
            ticks[start + stage if stage else begin] += actions
    return [links.record(tick) for tick in ticks]


class Swap:
    def __init__(self, links, source, target, local_sem):
        z, k, x, y = links.place
        self.same, self.other = k == x, k != x
        self.here = pltpu.make_async_copy(source, target, local_sem)
        self.there = links.copy(SWAP, links.take(1), source, target)

    def begin(self):
        pl.when(self.same)(self.here.start)
        pl.when(self.other)(self.there.start)

    def arrived(self):
        pl.when(self.same)(self.here.wait)
        pl.when(self.other)(self.there.wait)


class Cross:
    def __init__(self, links, source, target, local_sem):
        y = links.place[3]
        at = links.take(1)
        self.here = pltpu.make_async_copy(source, target.at[y], local_sem)
        self.out = links.copy(BESIDE, at, source, target.at[y])
        self.back = links.copy(BESIDE, at, source, target.at[1 - y])

    def begin(self):
        self.here.start()
        self.out.start()

    def arrived(self):
        self.here.wait()
        self.out.wait_send()
        self.back.wait_recv()


class Spread:
    def __init__(self, links, block, both_images, local_sem):
        z, k, x, y = links.place
        self.same, self.other = k == x, k != x
        here, first, second = links.take(1), links.take(1), 0
        target = both_images.at[y]
        self.keep = pltpu.make_async_copy(block, target, local_sem)
        self.beside = links.copy(BESIDE, here, block, target)
        self.swap = links.copy(SWAP, first, block, target)
        self.far = links.copy(FAR, here, block, target)
        self.came = links.copy(BESIDE, here, block, both_images.at[1 - y])

    def begin(self):
        def same():
            self.keep.start()
            self.beside.start()

        def other():
            self.swap.start()
            self.far.start()

        pl.when(self.same)(same)
        pl.when(self.other)(other)

    def arrived(self):
        def same():
            self.keep.wait()
            self.beside.wait_send()

        def other():
            self.swap.wait()
            self.far.wait_send()

        pl.when(self.same)(same)
        pl.when(self.other)(other)
        self.came.wait_recv()


def full_shape(layers, kind, piece):
    if kind == ROW:
        return piece[:-2] + (piece[-2] * layers * 2, piece[-1] * 2)
    return (piece[-2] * 2, piece[-1] * layers * 2)


def by_chunks(shape, body):
    rows, cols = shape
    chunk = 16
    while rows % (2 * chunk) == 0 and 2 * chunk * cols <= 16384:
        chunk *= 2

    def step(i, nothing):
        body((pl.ds(pl.multiple_of(i * chunk, 16), chunk), slice(None)))
        return nothing

    lax.fori_loop(0, rows // chunk, step, 0)


def add_into(target, term):
    def body(where):
        target[where] = target[where] + term[where]

    by_chunks(target.shape, body)


def store_sum(out, *terms):
    def body(where):
        total = terms[0][where].astype(jnp.float32)
        for term in terms[1:]:
            total = total + term[where].astype(jnp.float32)
        out[where] = total

    by_chunks(out.shape, body)


class Reduce:
    def __init__(self, layers, links, kind, grad, out, low, split, scratch, local_sem, local_base):
        self.layers, self.links, self.kind, self.grad = layers, links, kind, grad
        self.mine, self.load, self.y_in, self.x_in, self.z_in, self.last = scratch
        self.sent = []
        self.rows, self.cols = self.mine.shape[-2:]
        self.low, self.piece_rows = low, out.shape[0]
        self.out = cut_rows(out, low, self.rows)
        self.split = split
        self.local_sem, self.local_base = local_sem, local_base
        n = layers
        self.core = links.take(2 * n)
        self.y_a, self.x_b = links.take(n), links.take(n)
        self.z_a, self.z_b = links.take(2 * n), links.take(2 * n)
        self.end_a, self.end_b, self.end_c = links.take(1), links.take(1), links.take(1)
        self.order = []
        low, high = 0, layers - 1
        while low <= high:
            self.order.append(high)
            if low < high:
                self.order.append(low)
            low, high = low + 1, high - 1

    @staticmethod
    def sem_count(layers):
        return 8 * layers + 3

    def part_a(self, ref):
        return cut_rows(ref, 0, self.split)

    def part_b(self, ref):
        return cut_rows(ref, self.split, self.rows - self.split)

    def send(self, condition, copy):
        self.links.do(condition, copy.start)
        self.sent.append((condition, copy))

    def finish(self):
        for condition, copy in self.sent:
            when(condition, copy.wait_send)

    def add(self, condition, target, term):
        self.links.do(condition, functools.partial(add_into, target, term))

    def grad_piece(self, y, s):
        return piece_view(
            self.kind, self.piece_rows, self.cols, self.grad, y, s, self.low, self.rows
        )

    def local(self, number):
        k = self.links.place[1]
        layer, y = self.order[number // 2], number % 2
        return pltpu.make_async_copy(
            self.grad_piece(y, 2 * layer + k),
            self.load.at[number % 2],
            self.local_sem.at[self.local_base + number],
        )

    def to_core(self, y, layer):
        k = self.links.place[1]
        return self.links.copy(
            CORE,
            self.core + 2 * layer + y,
            self.grad_piece(y, 2 * layer + 1 - k),
            self.mine.at[y, layer],
        )

    def begin(self):
        for layer in self.order:
            for y in range(2):
                self.send(None, self.to_core(y, layer))
        for number in range(2):
            self.links.do(None, self.local(number).start)

    def to_y(self, layer):
        y = self.links.place[3]
        source = self.part_a(self.mine.at[1 - y, layer])
        return self.links.copy(BESIDE, self.y_a + layer, source, self.y_in.at[layer])

    def to_x(self, layer):
        x = self.links.place[2]
        source = self.part_b(self.mine.at[1 - x, layer])
        return self.links.copy(ACROSS, self.x_b + layer, source, self.x_in.at[layer])

    def chip_sum(self):
        for number in range(2 * self.layers):
            layer, side = self.order[number // 2], number % 2
            self.links.do(None, self.local(number).wait)
            self.links.do(None, self.to_core(side, layer).wait_recv)
            self.add(None, self.mine.at[side, layer], self.load.at[number % 2])
            if number + 2 < 2 * self.layers:
                self.links.do(None, self.local(number + 2).start)
            if side:
                self.send(None, self.to_y(layer))
                self.send(None, self.to_x(layer))

    def plane_sum(self):
        z, k, x, y = self.links.place
        for layer in self.order:
            self.links.do(None, self.to_y(layer).wait_recv)
            self.add(None, self.part_a(self.mine.at[y, layer]), self.y_in.at[layer])
            self.links.do(None, self.to_x(layer).wait_recv)
            self.add(None, self.part_b(self.mine.at[x, layer]), self.x_in.at[layer])

    def chain(self, way, layer, receiver):
        z, k, x, y = self.links.place
        slot = layer if way == UP else jnp.where(receiver == layer, self.layers, layer)
        add = 0 if way == UP else self.layers
        found = []
        for base, part, side in ((self.z_a, self.part_a, y), (self.z_b, self.part_b, x)):
            total, box = part(self.mine.at[side, layer]), part(self.z_in.at[slot])
            found.append((total, box, self.links.copy(way, base + add + layer, total, box)))
        return found

    def take(self, condition, way, layer):
        for total, box, copy in self.chain(way, layer, self.links.place[0]):
            self.links.do(condition, copy.wait_recv)
            self.add(condition, total, box)

    def along_z(self, depth):
        z = self.links.place[0]
        top = self.layers - 1
        for way, here, goals in (
            (UP, z == depth, range(top, depth, -1)),
            (DOWN, z == top - depth, range(0, top - depth)),
        ):
            for layer in goals:
                if depth:
                    self.take(here, way, layer)
                for total, box, copy in self.chain(way, layer, z + 1 if way == UP else z - 1):
                    self.send(here, copy)

    def ending(self):
        z, k, x, y = self.links.place
        self.take(z > 0, UP, z)
        self.take(z < self.layers - 1, DOWN, z)
        self.sum_a, self.sum_b = self.part_a(self.mine.at[y, z]), self.part_b(self.mine.at[x, z])
        self.got_a, self.got_b = self.part_a(self.last.at[0]), self.part_b(self.last.at[0])
        self.got_y = self.part_b(self.last.at[1])
        self.x_end = self.links.copy(ACROSS, self.end_a, self.sum_a, self.got_a)
        self.y_end = self.links.copy(BESIDE, self.end_b, self.sum_b, self.got_y)
        self.x_last = self.links.copy(ACROSS, self.end_c, self.sum_b, self.got_b)
        self.send(y != x, self.y_end)
        self.send(None, self.x_end)

    def owner(self):
        z, k, x, y = self.links.place

        self.links.do(y == x, self.y_end.wait_recv)
        self.add(y == x, self.sum_b, self.got_y)
        self.send(y == x, self.x_last)
        self.links.do(None, self.x_end.wait_recv)
        out_a = self.part_a(self.out)
        self.links.do(None, functools.partial(store_sum, out_a, self.sum_a, self.got_a))

    def write(self):
        z, k, x, y = self.links.place
        out_b = self.part_b(self.out)

        self.links.do(y != x, self.x_last.wait_recv)
        self.links.do(y != x, functools.partial(store_sum, out_b, self.got_b))
        self.links.do(y == x, functools.partial(store_sum, out_b, self.sum_b))

    def stages(self):
        chains = [[functools.partial(self.along_z, depth)] for depth in range(self.layers - 1)]
        return [
            [self.begin], [self.chip_sum], [self.plane_sum], *chains,
            [self.ending], [self.owner], [self.write],
        ]


class Total:
    def __init__(self, layers, links, given, out, boxes, layer_boxes):
        self.layers, self.links, self.given, self.out = layers, links, given, out
        self.boxes, self.layer_boxes = boxes, layer_boxes
        self.pair = [links.take(1) for _ in range(3)]
        self.z_up, self.z_down = links.take(layers), links.take(layers)

    @staticmethod
    def sem_count(layers):
        return 3 + 2 * layers

    def exchange(self, number):
        way = (CORE, ACROSS, BESIDE)[number]
        source = self.given if number == 0 else self.boxes.at[2 + number]
        return self.links.copy(way, self.pair[number], source, self.boxes.at[number])

    def begin(self):
        self.links.send(None, self.exchange(0))

    def join(self, number):
        z = self.links.place[0]
        self.links.do(None, self.exchange(number).wait_recv)
        mine = self.given if number == 0 else self.boxes.at[2 + number]
        result = self.layer_boxes.at[z] if number == 2 else self.boxes.at[3 + number]
        self.links.do(None, functools.partial(store_sum, result, mine, self.boxes.at[number]))
        if number < 2:
            self.links.send(None, self.exchange(number + 1))
        else:
            self.links.send(z < self.layers - 1, self.pass_on(UP, z))
            self.links.send(z > 0, self.pass_on(DOWN, z))

    def pass_on(self, way, layer):
        box = self.layer_boxes.at[layer]
        return self.links.copy(way, (self.z_up if way == UP else self.z_down) + layer, box, box)

    def along_z(self, step):
        z = self.links.place[0]
        top = self.layers - 1
        below, above = z - 1 - step, z + 1 + step
        for way, origin, there, further in (
            (UP, below, below >= 0, z < top),
            (DOWN, above, above <= top, z > 0),
        ):
            copy = self.pass_on(way, origin)
            self.links.do(there, copy.wait_recv)
            self.links.send(both(there, further), copy)

    def write(self):
        layers = [self.layer_boxes.at[layer] for layer in range(self.layers)]
        self.links.do(None, functools.partial(store_sum, self.out, *layers))

    def stages(self):
        joins = [[functools.partial(self.join, number)] for number in range(3)]
        moves = [[functools.partial(self.along_z, step)] for step in range(self.layers - 1)]
        return [[self.begin], *joins, *moves, [self.write]]


def reduce_jobs(layers, links, jobs, grads, outs, scratch, local_sem):
    todo = []
    for number, (mat, kind, low, rows, split) in enumerate(jobs):
        own = scratch[6 * number : 6 * number + 6]
        at = number * 2 * layers
        grad, out = grads[mat], outs[mat]
        todo.append(Reduce(layers, links, kind, grad, out, low, split, own, local_sem, at))
    return todo


def reduce_shapes(layers, rows, cols, split):
    return [
        (2, layers, rows, cols), (2, rows, cols), (layers, split, cols),
        (layers, rows - split, cols), (layers + 1, rows, cols), (2, rows, cols),
    ]


def piece_shape(layers, kind, full):
    if kind == ROW:
        return full[:-2] + (full[-2] // (2 * layers), full[-1] // 2)
    return (full[-2] // 2, full[-1] // (2 * layers))


def pair_lanes(shape, head_size):
    lane = lax.broadcasted_iota(jnp.int32, shape, len(shape) - 1)
    return lane < head_size


def dot_last(left, right):
    return lax.dot_general(left, right, (((1,), (1,)), ((), ())), preferred_element_type=jnp.float32)


def dot_first(left, right):
    return lax.dot_general(left, right, (((0,), (0,)), ((), ())), preferred_element_type=jnp.float32)


def dot(left, right):
    return lax.dot_general(left, right, (((1,), (0,)), ((), ())), preferred_element_type=jnp.float32)


def only_head(values, head, head_size):
    lane = lax.broadcasted_iota(jnp.int32, (1, values.shape[1]), 1)
    keep = (lane < head_size) if head == 0 else (lane >= head_size)
    return values * jnp.where(keep, 1.0, 0.0).astype(values.dtype)


LOG2_E = 1.4426950408889634


def turn_lanes(values, quarter):
    width = values.shape[-1]
    lane = lax.broadcasted_iota(jnp.int32, (1, width), 1)
    even = lax.rem(lax.div(lane, quarter), 2) == 0
    after = pltpu.roll(values, width - quarter, 1)
    before = pltpu.roll(values, quarter, 1)
    return jnp.where(even, -after, before)


def slot_bias(shape, axis, rows, tokens_here, count):
    slot = lax.broadcasted_iota(jnp.int32, shape, axis)
    second = slot >= rows
    within = jnp.where(second, slot - rows, slot)
    token = jnp.where(second, within + tokens_here, within).astype(jnp.float32)
    return jnp.where(jnp.logical_and(within < tokens_here, token < count), 0.0, -1e30)


def front_kernel(layers, head_size, grid_side, *refs):
    (
        vec_own, qkv_own, out_own, gate_own, down_own, tokens, cot, valid, hidden_own,
        vec_full, qkv_full, out_full, gate_full, down_full, hidden_full, cot_out,
        x_out, n_out, q_out, k_out, v_out, o_out, stat_out, vec_out, count_out, cos, sin,
        x, valid_both, vec, weight, hat, normed, q, keys, values, bias,
        send_sem, recv_sem, local_sem,
    ) = refs
    f32, bf16 = jnp.float32, jnp.bfloat16
    place = place_of()
    z, k, me_x, y = place
    greet(layers, place, (SWAP,))
    links = Links(place, send_sem, recv_sem)
    rows, width = x.shape
    tokens_here = valid.shape[1] // 2
    tile = weight.shape[2]
    quarter = head_size // 4
    lanes = 2 * head_size
    locals_used = [0]

    def local_at():
        locals_used[0] += 1
        return local_sem.at[locals_used[0] - 1]

    block = Swap(links, tokens.at[y], x, local_at())
    cot_block = Swap(links, cot.at[y], cot_out, local_at())
    valid_swap = Swap(links, valid, valid_both, local_at())
    cross = Cross(links, hidden_own, hidden_full, local_at())
    out_rows, down_rows = out_own.shape[0], down_own.shape[0] // 2
    todo = [
        (ROW, vec_own, vec_full, 0, vec_own.shape[0], 0),
        (ROW, qkv_own.at[0], qkv_full.at[0], 0, 128, 64),
        (ROW, qkv_own.at[1], qkv_full.at[1], 0, 128, 64),
        (ROW, qkv_own.at[2], qkv_full.at[2], 0, 128, 64),
        (ROW, gate_own.at[0], gate_full.at[0], 0, 64, 32),
        (ROW, gate_own.at[0], gate_full.at[0], 64, 64, 32),
        (ROW, gate_own.at[1], gate_full.at[1], 0, 64, 32),
        (ROW, gate_own.at[1], gate_full.at[1], 64, 64, 32),
        (COL, down_own, down_full, 0, down_rows, 448),
        (COL, down_own, down_full, down_rows, down_rows, 448),
        (COL, out_own, out_full, 0, out_rows, 320),
    ]
    starts = (0, 1, 2, 3, 4, 5, 6, 7, 8, 9, 10)
    begins = (0, 0, 0, 1, 2, 3, 4, 5, 6, 7, 8)
    jobs = [
        Gather(layers, links, kind, own, full, low, size, split, local_at())
        for kind, own, full, low, size, split in todo
    ]
    ticks = ticks_of(links, jobs, starts, begins)
    weight_loads = []
    for mat in range(3):
        for part in range(width // tile):
            slot = len(weight_loads) % 2
            weight_loads.append(
                pltpu.make_async_copy(
                    qkv_full.at[mat, :, pl.ds(part * tile, tile)], weight.at[slot], local_at()
                )
            )
    vec_load = pltpu.make_async_copy(vec_full, vec, local_at())
    keeps = [
        pltpu.make_async_copy(source, target, local_at())
        for source, target in ((x, x_out), (normed, n_out), (q, q_out), (keys, k_out), (values, v_out))
    ]
    shares = []
    my_rows = pl.ds(pl.multiple_of(k * rows, 16), rows)
    other_rows = pl.ds(pl.multiple_of((1 - k) * rows, 16), rows)
    for store in (keys, values):
        for part in range(width // tile):
            at = links.take(1)
            cols = pl.ds(part * tile, tile)
            out_going = links.copy(CORE, at, store.at[my_rows, cols], store.at[my_rows, cols])
            coming = links.copy(CORE, at, store.at[other_rows, cols], store.at[other_rows, cols])
            shares.append((out_going, coming))

    block.begin()
    valid_swap.begin()
    run(ticks[0])
    cot_block.begin()
    cross.begin()
    run(ticks[1])

    block.arrived()
    valid_swap.arrived()
    keeps[0].start()
    chunk = rows // 3

    def normalise(i, nothing):
        at = pl.ds(pl.multiple_of(i * chunk, 16), chunk)
        value, spread = standardize(x[at, :].astype(f32))
        hat[at, :] = value
        return nothing

    lax.fori_loop(0, 3, normalise, 0)
    flags = jnp.where(y == 0, valid_both[0:1, :], valid_both[1:2, :]).astype(f32)
    count = jnp.sum(flags, axis=1, keepdims=True)
    count_out[...] = jnp.broadcast_to(count, count_out.shape)
    columns = (count - 1.0) * (1.0 / grid_side)
    token = lax.broadcasted_iota(jnp.int32, (rows, lanes), 0).astype(f32)
    token = token + (k * tokens_here).astype(f32)
    lane = lax.broadcasted_iota(jnp.int32, (rows, lanes), 1)
    live = jnp.logical_and(token >= 1.0, token < count)
    row_id = jnp.floor((token - 0.5) / columns)
    col_id = token - 1.0 - row_id * columns
    where_at = jnp.where(lax.rem(lane, head_size) < 2 * quarter, row_id, col_id)
    where_at = jnp.where(live, where_at, 0.0)
    power = lax.rem(lane, quarter).astype(f32) * (-math.log(10000.0) / quarter)
    angle = where_at * jnp.exp(power)
    cos[...] = jnp.cos(angle)
    sin[...] = jnp.sin(angle)
    bias[...] = slot_bias(bias.shape, 1, rows, tokens_here, count)

    for tick in ticks[2:8]:
        run(tick)
    jobs[0].arrived()
    vec_load.start()
    vec_load.wait()
    piece_rows = vec_own.shape[0]
    summed = vec[0:piece_rows, :].astype(f32)
    for s in range(1, 2 * layers):
        summed = summed + vec[s * piece_rows : (s + 1) * piece_rows, :].astype(f32)
    vec_out[...] = summed

    def scale(i, nothing):
        at = pl.ds(pl.multiple_of(i * chunk, 16), chunk)
        normed[at, :] = (hat[at, :] * vec_out[4:5, :] + vec_out[6:7, :]).astype(bf16)
        return nothing

    lax.fori_loop(0, 3, scale, 0)
    keeps[1].start()
    repeat = tile // lanes
    per = width // tile
    for mat in range(3):
        run(ticks[8 + mat])
        jobs[1 + mat].arrived()
        for part in range(per):
            weight_loads[mat * per + part].start()
        for part in range(per):
            load = weight_loads[mat * per + part]
            load.wait()
            cols = pl.ds(part * tile, tile)
            raw = dot(normed[...], weight[(mat * per + part) % 2])
            if mat != 1:
                raw = raw + vec_out[0 if mat == 0 else 1 : 1 if mat == 0 else 2, cols]
            if mat < 2:
                turned = turn_lanes(raw, quarter)
                wide_cos = jnp.concatenate([cos[...]] * repeat, axis=1)
                wide_sin = jnp.concatenate([sin[...]] * repeat, axis=1)
                raw = raw * wide_cos + turned * wide_sin
            if mat == 0:
                q[:, cols] = raw.astype(bf16)
            else:
                (keys if mat == 1 else values)[my_rows, cols] = raw.astype(bf16)
                shares[(mat - 1) * per + part][0].start()
    keeps[2].start()
    for out_going, coming in shares:
        out_going.wait_send()
        coming.wait_recv()
    keeps[3].start()
    keeps[4].start()

    late = ticks[11:]
    score_scale = LOG2_E / math.sqrt(head_size)
    pairs = width // lanes

    def mix(i, nothing):
        for number, tick in enumerate(late):
            pl.when(i == number)(functools.partial(run, tick))
        cols = pl.ds(pl.multiple_of(i * lanes, lanes), lanes)
        queries, near_keys, near_values = q[:, cols], keys[:, cols], values[:, cols]
        parts = []
        for head in range(2):
            s = dot_last(only_head(queries, head, head_size), near_keys) * score_scale + bias[...]
            top = jnp.max(s, axis=1, keepdims=True)
            e = jnp.exp2(s - top)
            total = jnp.sum(e, axis=1, keepdims=True)
            parts.append(dot(e.astype(bf16), near_values) * (1.0 / total))
            level = jnp.broadcast_to(top + jnp.log2(total), (rows, 128))
            stat_out[i, head : head + 1, :] = jnp.transpose(level)[0:1, :]
        o_out[:, cols] = jnp.where(pair_lanes((rows, lanes), head_size), parts[0], parts[1])
        return nothing

    lax.fori_loop(0, pairs, mix, 0)
    for tick in late[8:]:
        run(tick)
    for job in jobs[4:]:
        job.arrived()
    cross.arrived()
    cot_block.arrived()
    for keep in keeps:
        keep.wait()
    links.finish()


def front(
    layers, number, head_size, grid_side, vec, qkv, out, gate, down, tokens, cot, valid, hidden
):
    bf16, f32 = jnp.bfloat16, jnp.float32
    rows, width = tokens.shape[1:]
    pairs = width // (2 * head_size)
    tile = 512
    fulls = [
        full_shape(layers, kind, piece.shape)
        for kind, piece in ((ROW, vec), (ROW, qkv), (COL, out), (ROW, gate), (COL, down))
    ]
    shapes = [jax.ShapeDtypeStruct(shape, bf16) for shape in fulls]
    shapes += [jax.ShapeDtypeStruct((2,) + hidden.shape, bf16)]
    shapes += [jax.ShapeDtypeStruct((n * rows, width), bf16) for n in (1, 1, 1, 1, 2, 2)]
    shapes += [
        jax.ShapeDtypeStruct((rows, width), f32),
        jax.ShapeDtypeStruct((pairs, 2, rows), f32),
        jax.ShapeDtypeStruct((vec.shape[0], width), f32),
        jax.ShapeDtypeStruct((8, 128), f32),
        jax.ShapeDtypeStruct((rows, 2 * head_size), f32),
        jax.ShapeDtypeStruct((rows, 2 * head_size), f32),
    ]
    sems = 11 * Gather.sem_count(layers) + 8
    return pl.pallas_call(
        functools.partial(front_kernel, layers, head_size, grid_side),
        out_shape=shapes,
        in_specs=[ANY] * 9,
        out_specs=[ANY] * 12 + [IN_VMEM] * 6,
        scratch_shapes=[
            pltpu.VMEM((rows, width), bf16),
            pltpu.VMEM(valid.shape, valid.dtype),
            pltpu.VMEM(fulls[0], bf16),
            pltpu.VMEM((2, width, tile), bf16),
            pltpu.VMEM((rows, width), f32),
            pltpu.VMEM((rows, width), bf16),
            pltpu.VMEM((rows, width), bf16),
            pltpu.VMEM((2 * rows, width), bf16),
            pltpu.VMEM((2 * rows, width), bf16),
            pltpu.VMEM((1, 2 * rows), f32),
            pltpu.SemaphoreType.DMA((sems,)),
            pltpu.SemaphoreType.DMA((sems,)),
            pltpu.SemaphoreType.DMA((32,)),
        ],
        compiler_params=pltpu.CompilerParams(
            collective_id=number, has_side_effects=True, vmem_limit_bytes=LIMIT
        ),
    )(vec, qkv, out, gate, down, tokens, cot, valid, hidden)


def back_kernel(layers, head_size, tokens_here, jobs, late_jobs, mats, *refs):
    grads, refs = refs[:mats], refs[mats:]
    given_arrays, refs = refs[:9], refs[9:]
    q_in, keys_in, values_in, do_in, mixed_in, n_in, x_in, resid_in, weights = given_arrays
    stats, count, cos, sin, vec, total_in = refs[:6]
    outs, refs = refs[6 : 6 + mats], refs[6 + mats :]
    late_outs, total_out, tokens_out, late_grads = refs[:3], refs[3], refs[4], refs[5:8]
    scratch, refs = refs[8 : 8 + 6 * len(jobs)], refs[8 + 6 * len(jobs) :]
    (
        q, keys, values, do, mixed, k_sum, v_sum, dq_low, dk_low, dv_low, normed_t, d_first,
        d_tokens, bias, total, boxes, layer_boxes, send_sem, recv_sem, local_sem, ready,
    ) = refs
    f32, bf16 = jnp.float32, jnp.bfloat16
    place = place_of()
    z, k, x, y = place
    greet(layers, place, (SWAP, FAR))
    links = Links(place, send_sem, recv_sem)
    first_jobs = reduce_jobs(layers, links, jobs, grads, outs, scratch, local_sem)
    locals_used = [len(jobs) * 2 * layers]

    def local_at():
        locals_used[0] += 1
        return local_sem.at[locals_used[0] - 1]

    second_jobs = []
    for mat, low, rows_here, split, host, first_col in late_jobs:
        cols_here = pl.ds(first_col, late_outs[mat].shape[-1])
        own = []
        for ref in scratch[6 * host : 6 * host + 6]:
            own.append(ref.at[(slice(None),) * (len(ref.shape) - 1) + (cols_here,)])
        second_jobs.append(
            Reduce(
                layers, links, ROW, late_grads[mat], late_outs[mat], low, split, own,
                local_sem, locals_used[0],
            )
        )
        locals_used[0] += 2 * layers
    sums = Total(layers, links, total, total_out, boxes, layer_boxes)
    early, n_late = len(jobs), len(second_jobs)
    handover = early + 5
    late_starts = [handover + number // 2 for number in range(n_late)]
    starts = list(range(early)) + late_starts + [handover + 3]
    begins = [max(0, number - 1) for number in range(early)] + late_starts + [handover + 3]
    ticks = ticks_of(links, first_jobs + second_jobs + [sums], starts, begins)
    spread = Spread(links, d_tokens, tokens_out, local_at())

    rows, width = q.shape
    lanes = 2 * head_size
    pairs = width // lanes
    scale = 1.0 / math.sqrt(head_size)
    quarter = head_size // 4
    my_rows = pl.ds(pl.multiple_of(k * rows, 16), rows)
    other_rows = pl.ds(pl.multiple_of((1 - k) * rows, 16), rows)
    first = links.take(2 * pairs)

    def share(i):
        cols = pl.ds(pl.multiple_of(i * lanes, lanes), lanes)
        return (
            links.copy(CORE, first + 2 * i, k_sum.at[other_rows, cols], dk_low.at[:, cols]),
            links.copy(CORE, first + 2 * i + 1, v_sum.at[other_rows, cols], dv_low.at[:, cols]),
        )

    def turn_back(grad):
        return grad * cos[...] - turn_lanes(grad, quarter) * sin[...]

    def load(source, target):
        copy = pltpu.make_async_copy(source, target, local_at())
        copy.start()
        return copy

    run(ticks[0])
    loads = [
        load(source, target)
        for source, target in (
            (q_in, q), (keys_in, keys), (values_in, values), (do_in, do), (mixed_in, mixed)
        )
    ]
    bias[...] = slot_bias(bias.shape, 0, rows, tokens_here, count[0:1, 0:1])
    total[...] = total_in[...]
    run(ticks[1])
    for copy in loads:
        copy.wait()
    beside = ticks[2 : 2 + pairs]

    def step(i, nothing):
        for number, tick in enumerate(beside):
            pl.when(i == number)(functools.partial(run, tick))
        cols = pl.ds(pl.multiple_of(i * lanes, lanes), lanes)
        queries, near_keys, near_values, grad = q[:, cols], keys[:, cols], values[:, cols], do[:, cols]
        products = jnp.transpose(grad.astype(f32) * mixed[:, cols])
        found = []
        for head in range(2):
            row_dot = products[head * head_size : (head + 1) * head_size]
            row_dot = jnp.sum(row_dot, axis=0, keepdims=True)
            s = dot_last(near_keys, only_head(queries, head, head_size)) * (scale * LOG2_E)
            p = jnp.exp2(s + bias[...] - stats[i, head : head + 1, :])
            dp = dot_last(near_values, only_head(grad, head, head_size))
            ds = (p * (dp - row_dot)).astype(bf16)
            found.append(
                (dot_first(near_keys, ds) * scale, dot(ds, queries) * scale, dot(p.astype(bf16), grad))
            )
        dq = jnp.concatenate([found[0][0][:head_size], found[1][0][head_size:]], axis=0)
        dq = turn_back(jnp.transpose(dq)).astype(bf16)
        dq_low[:, cols] = dq
        total[pl.ds(i, 1), :] = jnp.sum(dq.astype(f32), axis=0, keepdims=True)
        in_first = pair_lanes((2 * rows, lanes), head_size)
        k_sum[:, cols] = jnp.where(in_first, found[0][1], found[1][1]).astype(bf16)
        v_sum[:, cols] = jnp.where(in_first, found[0][2], found[1][2]).astype(bf16)
        for copy in share(i):
            copy.start()
        return nothing

    lax.fori_loop(0, pairs, step, 0)
    normed_load = load(n_in, q)
    loads = [load(weights.at[0], keys.at[pl.ds(0, width)]), load(weights.at[1], values.at[pl.ds(0, width)])]
    loads += [load(x_in, do), load(resid_in, mixed)]
    at_tick = [2 + pairs]

    def advance():
        run(ticks[at_tick[0]])
        at_tick[0] += 1

    def join(i, nothing):
        cols = pl.ds(pl.multiple_of(i * lanes, lanes), lanes)
        for copy in share(i):
            copy.wait()
        dk = k_sum[my_rows, cols].astype(f32) + dk_low[:, cols].astype(f32)
        dk_low[:, cols] = turn_back(dk).astype(bf16)
        dv = v_sum[my_rows, cols].astype(f32) + dv_low[:, cols].astype(f32)
        dv = dv.astype(bf16)
        dv_low[:, cols] = dv
        total[pl.ds(pairs + i, 1), :] = jnp.sum(dv.astype(f32), axis=0, keepdims=True)
        return nothing

    advance()
    lax.fori_loop(0, pairs, join, 0)
    normed_load.wait()
    last_weight = load(weights.at[2], k_sum.at[pl.ds(0, width)])

    def flip(i, nothing):
        at = pl.ds(pl.multiple_of(i * lanes, lanes), lanes)
        normed_t[at, :] = jnp.transpose(q[:, at])
        return nothing

    lax.fori_loop(0, width // lanes, flip, 0)
    while at_tick[0] < handover:
        advance()
    tile = 256
    stores = []

    def weight_grad(mat):
        low_grad = (dq_low, dk_low, dv_low)[mat]
        def part(i, nothing):
            at = pl.ds(pl.multiple_of(i * tile, tile), tile)
            v_sum[at, :] = dot(normed_t[at, :], low_grad[...]).astype(bf16)
            return nothing

        lax.fori_loop(0, width // tile, part, 0)
        stores.append(load(v_sum.at[pl.ds(0, width)], late_grads[mat]))

    weight_grad(0)
    for job in first_jobs[:4]:
        job.finish()
    near = [(None, CORE), (None, ACROSS), (None, BESIDE), (z > 0, DOWN), (z < layers - 1, UP)]
    for condition, way in near:

        def hello(way=way):
            pl.semaphore_signal(
                ready, inc=1, device_id=device(place, way), device_id_type=MESH
            )

        when(condition, hello)
    expected = 3 + jnp.where(z > 0, 1, 0) + jnp.where(z < layers - 1, 1, 0)
    pl.semaphore_wait(ready, expected)
    stores[-1].wait()
    advance()
    for mat in (1, 2):
        weight_grad(mat)
        stores[-1].wait()
        advance()
    for copy in loads + [last_weight]:
        copy.wait()

    def project_back(i, nothing):
        at = pl.ds(pl.multiple_of(i * tile, tile), tile)
        result = dot_last(dq_low[...], keys[at, :])
        result = result + dot_last(dk_low[...], values[at, :])
        d_first[:, at] = result + dot_last(dv_low[...], k_sum[at, :])
        return nothing

    lax.fori_loop(0, width // tile, project_back, 0)
    chunk = rows // 3
    gain = vec[4:5, :]
    gain_sum = jnp.zeros((1, width), f32)
    bias_sum = jnp.zeros((1, width), f32)
    for number in range(3):
        at = pl.ds(number * chunk, chunk)
        hat, inverse = standardize(do[at, :].astype(f32))
        dn = d_first[at, :]
        d_tokens[at, :] = (mixed[at, :] + norm_back(dn * gain, hat, inverse)).astype(bf16)
        gain_sum = gain_sum + jnp.sum(dn * hat, axis=0, keepdims=True)
        bias_sum = bias_sum + jnp.sum(dn, axis=0, keepdims=True)
    for i in range(width // 128):
        cols = slice(i * 128, (i + 1) * 128)
        at = 4 * width // 128 + i
        total[at : at + 1, :] = gain_sum[:, cols]
        at = 6 * width // 128 + i
        total[at : at + 1, :] = bias_sum[:, cols]
    spread.begin()
    while at_tick[0] < len(ticks):
        advance()
    spread.arrived()
    for job in first_jobs[4:] + second_jobs:
        job.finish()
    links.finish()


def back(layers, number, head_size, tokens_here, jobs, late_jobs, grads, given, small, total):
    bf16, f32 = jnp.bfloat16, jnp.float32
    pieces = [piece_shape(layers, kind, g.shape) for kind, g in grads]
    rows, width = given[0].shape
    pairs = width // (2 * head_size)
    sems = (len(jobs) + len(late_jobs)) * Reduce.sem_count(layers) + 2 * pairs
    sems += Total.sem_count(layers) + 2
    late_piece = (width // (2 * layers), width // 2)
    scratch = []
    for mat, kind, low, job_rows, split in jobs:
        shapes = reduce_shapes(layers, job_rows, pieces[mat][-1], split)
        scratch += [pltpu.VMEM(shape, bf16) for shape in shapes]
    half, whole = (rows, width), (2 * rows, width)
    buffers = [(half, bf16), (whole, bf16), (whole, bf16), (half, bf16), (half, f32)]
    buffers += [(whole, bf16)] * 2 + [(half, bf16)] * 3 + [((width, rows), bf16), (half, f32)]
    buffers += [(half, bf16), ((2 * rows, 1), f32), (total.shape, f32)]
    buffers += [((5,) + total.shape, f32), ((layers,) + total.shape, f32)]
    return pl.pallas_call(
        functools.partial(
            back_kernel, layers, head_size, tokens_here, jobs, late_jobs, len(grads)
        ),
        out_shape=[jax.ShapeDtypeStruct(piece, f32) for piece in pieces]
        + [jax.ShapeDtypeStruct(late_piece, f32)] * 3
        + [jax.ShapeDtypeStruct(total.shape, f32)]
        + [jax.ShapeDtypeStruct((2, rows, width), bf16)]
        + [jax.ShapeDtypeStruct((width, width), bf16)] * 3,
        in_specs=[ANY] * (len(grads) + len(given)) + [IN_VMEM] * (len(small) + 1),
        out_specs=[IN_VMEM] * (len(pieces) + 4) + [ANY] * 4,
        scratch_shapes=scratch
        + [pltpu.VMEM(shape, dtype) for shape, dtype in buffers]
        + [
            pltpu.SemaphoreType.DMA((sems,)),
            pltpu.SemaphoreType.DMA((sems,)),
            pltpu.SemaphoreType.DMA(((len(jobs) + len(late_jobs)) * 2 * layers + 16,)),
            pltpu.SemaphoreType.REGULAR,
        ],
        compiler_params=pltpu.CompilerParams(
            collective_id=number, has_side_effects=True, vmem_limit_bytes=62 * 1024 * 1024
        ),
    )(*[g for kind, g in grads], *given, *small, total)


def pad_to(values, axis, size):
    pads = [(0, 0)] * values.ndim
    pads[axis] = (0, size - values.shape[axis])
    return jnp.pad(values, pads)


def round_up(size, step):
    return (size + step - 1) // step * step


def image_per_chip(
    layers,
    tokens,
    cotangent,
    valid_tokens,
    places,
    qkv_weight,
    head_biases,
    head_gain,
    out_weight,
    norm_gains,
    width_biases,
    gate_up,
    hidden_biases,
    hidden_gain,
    down_weight,
):
    f32 = jnp.float32
    bf16 = jnp.bfloat16
    z, k, x, y = place_of()
    s = 2 * z + k
    shards = 2 * layers
    width = tokens.shape[2]
    rows = tokens.shape[1]
    heads_here = head_gain.shape[0]
    heads = 2 * heads_here
    dims_here = head_gain.shape[1]
    head_size = dims_here * shards
    real_here = hidden_gain.shape[0]
    hidden_here = round_up(real_here, 128)
    real = 2 * real_here
    hidden_size = 2 * hidden_here
    score_scale = 1.0 / math.sqrt(head_size)

    padded = round_up(rows, 16)
    heads_own = jnp.concatenate([head_biases, head_gain[None]], axis=0)
    spot = jnp.zeros((4, heads_here, head_size), bf16)
    spot = lax.dynamic_update_slice(spot, heads_own, (0, 0, s * dims_here)).reshape(4, -1)
    width_own = jnp.concatenate([norm_gains, width_biases], axis=0)
    lane_at = s * width_own.shape[1] - y * spot.shape[1]
    inside = both(lane_at >= 0, lane_at < spot.shape[1])
    width_own = jnp.where(inside, width_own, jnp.zeros_like(width_own))
    at = jnp.where(inside, lane_at, 0)
    lanes_own = lax.dynamic_update_slice(jnp.zeros((6, spot.shape[1]), bf16), width_own, (0, at))
    vectors = pad_to(jnp.concatenate([spot, lanes_own], axis=0), 0, 16)
    hidden_vectors = jnp.concatenate([hidden_biases, hidden_gain[None]], axis=0)
    hidden_vectors = pad_to(pad_to(hidden_vectors, 1, hidden_here), 0, 16)
    gate_pad = pad_to(gate_up, 2, hidden_here)
    down_pad = pad_to(down_weight, 0, hidden_here)
    swaps, others = [], []
    for layer in range(layers):
        swaps += [(4 * layer + 1, 4 * layer + 2), (4 * layer + 2, 4 * layer + 1)]
        for spot, far in ((0, 0), (1, 2), (2, 1), (3, 3)):
            for side in range(2):
                others.append((2 * (4 * layer + spot) + side, 2 * (4 * layer + far) + 1 - side))
    (
        vec_full, qkv_full, out_full, gate_full, down_full, hidden_full, cot_block,
        token_block, first_in, queries, keys, values, mixed, stats, vec, count, cos, sin,
    ) = front(
        layers, 0, head_size, 32, vectors, qkv_weight, out_weight, gate_pad, down_pad,
        pad_to(tokens, 1, padded), pad_to(cotangent, 1, padded), valid_tokens, hidden_vectors,
    )
    head_part, norm_scale, width_bias = vec[0:4], vec[4:6], vec[6:10]
    hidden_part = jnp.concatenate([hidden_full[0, :4], hidden_full[1, :4]], axis=1).astype(f32)
    token_rows = token_block.astype(f32)
    cot_rows = cot_block.astype(f32)
    mix_hat, spread_mix = standardize(mixed)
    mix_in = (mix_hat * head_part[3] + head_part[2]).astype(bf16)
    branch = jnp.dot(mix_in, out_full, preferred_element_type=f32)
    resid = token_rows + (branch + width_bias[2])
    normed_two, spread_two = standardize(resid)
    second_in = (normed_two * norm_scale[1] + width_bias[1]).astype(bf16)
    gate_pre = jnp.dot(second_in, gate_full[0], preferred_element_type=f32) + hidden_part[0]
    up_pre = jnp.dot(second_in, gate_full[1], preferred_element_type=f32) + hidden_part[1]
    sigmoid_gate = jax.nn.sigmoid(gate_pre)
    silu_gate = gate_pre * sigmoid_gate
    hidden = silu_gate * up_pre
    hidden_mean = jnp.sum(hidden, axis=-1, keepdims=True) / real
    centred = hidden - hidden_mean
    extra = (hidden_size - real) * hidden_mean * hidden_mean
    hidden_var = (jnp.sum(centred * centred, axis=-1, keepdims=True) - extra) / real
    spread_hid = lax.rsqrt(jnp.maximum(hidden_var, 0.0) + EPS)
    hidden_hat = centred * spread_hid
    down_in = (hidden_hat * hidden_part[3] + hidden_part[2]).astype(bf16)
    down_in = lax.optimization_barrier(down_in)
    ffn_out = jnp.dot(down_in, down_full, preferred_element_type=f32)
    result = (resid + (ffn_out + width_bias[3])).astype(bf16)[:rows]
    result_other = lax.ppermute(result, (SHARD, CTX, TP), others)
    results = (result, result_other, lax.ppermute(result, (SHARD, CTX), swaps))

    g_down = jnp.einsum("tf,td->fd", down_in, cot_block, preferred_element_type=f32)
    d_down_in = jnp.einsum("td,fd->tf", cot_block, down_full, preferred_element_type=f32)
    grad_hid = d_down_in * hidden_part[3]
    hid_back_one = jnp.sum(grad_hid, axis=-1, keepdims=True) / real
    hid_back_two = jnp.sum(grad_hid * hidden_hat, axis=-1, keepdims=True) / real
    d_hidden = (grad_hid - hid_back_one - hidden_hat * hid_back_two) * spread_hid
    d_gate = (d_hidden * up_pre * sigmoid_gate * (1.0 + gate_pre * (1.0 - sigmoid_gate))).astype(
        bf16
    )
    d_up = (d_hidden * silu_gate).astype(bf16)
    g_gate = jnp.einsum("td,tf->df", second_in, d_gate, preferred_element_type=f32).astype(bf16)
    g_up = jnp.einsum("td,tf->df", second_in, d_up, preferred_element_type=f32).astype(bf16)
    d_second = jnp.einsum("tf,df->td", d_gate, gate_full[0], preferred_element_type=f32)
    d_second = d_second + jnp.einsum("tf,df->td", d_up, gate_full[1], preferred_element_type=f32)
    d_resid = cot_rows + norm_back(d_second * norm_scale[1], normed_two, spread_two)
    d_branch_low = d_resid.astype(bf16)
    g_out = jnp.einsum("tm,tn->mn", mix_in, d_branch_low, preferred_element_type=f32)
    d_mix_in = jnp.einsum("tn,mn->tm", d_branch_low, out_full, preferred_element_type=f32)
    d_mixed = norm_back(d_mix_in * head_part[3], mix_hat, spread_mix).astype(bf16)
    vector_grads = jnp.concatenate(
        [
            jnp.zeros((width,), f32),
            jnp.zeros((width,), f32),
            column_sum(d_mix_in),
            column_sum(d_mix_in * mix_hat),
            jnp.zeros((width,), f32),
            column_sum(d_second * normed_two),
            jnp.zeros((width,), f32),
            column_sum(d_second),
            column_sum(d_branch_low),
            column_sum(cot_block),
            column_sum(d_gate),
            column_sum(d_up),
            column_sum(d_down_in),
            column_sum(d_down_in * hidden_hat),
        ]
    ).reshape(-1, 128)
    vector_grads = pad_to(vector_grads, 0, round_up(vector_grads.shape[0], 16))
    result, result_other, swapped, d_mixed = lax.optimization_barrier((*results, d_mixed))
    result = jnp.where(k == x, result, swapped)
    result = jnp.stack(
        [jnp.where(y == 0, result, result_other), jnp.where(y == 0, result_other, result)], axis=1
    ).transpose(1, 0, 2)
    half = hidden_here // 2
    heads_rows = heads_here * head_size
    grad_jobs = (
        (0, ROW, 0, 64, 32), (0, ROW, 64, 64, 32), (1, ROW, 0, 64, 32), (1, ROW, 64, 64, 32),
        (2, COL, 0, half, half // 2), (2, COL, half, half, half // 2),
        (3, COL, 0, heads_rows, heads_rows // 2),
    )
    late_jobs = (
        (0, 0, 64, 32, 0, 0), (0, 64, 64, 32, 1, 0),
        (1, 0, 64, 32, 0, heads_rows), (1, 64, 64, 32, 1, heads_rows),
        (2, 0, 64, 32, 2, 0), (2, 64, 64, 32, 3, 0),
    )
    back_grads = (
        (ROW, g_gate), (ROW, g_up), (COL, g_down.astype(bf16)), (COL, g_out.astype(bf16))
    )
    (
        gate_piece, up_piece, down_piece, out_piece, query_piece, key_piece, value_piece,
        vector_grads, d_tokens, *unused,
    ) = back(
        layers, 1, head_size, rows, grad_jobs, late_jobs, back_grads,
        (queries, keys, values, d_mixed, mixed, first_in, token_block, d_resid, qkv_full),
        (stats, count, cos, sin, vec), vector_grads,
    )
    d_tokens = jnp.stack([d_tokens[0, :rows], d_tokens[1, :rows]], axis=1).transpose(1, 0, 2)
    vector_grads = vector_grads.reshape(-1)
    head_sums = vector_grads[: 4 * width].reshape(4, heads, head_size)
    head_sums = lax.dynamic_slice(
        head_sums, (0, y * heads_here, s * dims_here), (4, heads_here, dims_here)
    )
    width_sums = vector_grads[4 * width : 10 * width].reshape(6, width)
    width_sums = lax.dynamic_slice(width_sums, (0, s * 128), (6, width // shards))
    hidden_sums = vector_grads[10 * width : 10 * width + 4 * hidden_size]
    hidden_sums = hidden_sums.reshape(4, hidden_size)
    hidden_sums = lax.dynamic_slice(hidden_sums, (0, y * hidden_here), (4, hidden_here))
    hidden_sums = hidden_sums[:, :real_here]

    return (
        result,
        d_tokens.astype(f32),
        jnp.stack([query_piece, key_piece, value_piece]),
        head_sums[:3],
        head_sums[3],
        out_piece,
        width_sums[:2],
        width_sums[2:],
        jnp.stack([gate_piece[:, :real_here], up_piece[:, :real_here]]),
        hidden_sums[:3],
        hidden_sums[3],
        down_piece[:real_here],
    )


def solution(mesh):
    small = mesh.shape[CTX] == 2 and mesh.shape[TP] == 2
    body = functools.partial(image_per_chip, mesh.shape[SHARD] // 2) if small else general_plan

    return jax.shard_map(
        body,
        mesh=mesh,
        in_specs=(
            P(SHARD, CTX, None),
            P(SHARD, CTX, None),
            P(SHARD, None),
            P(None, SHARD, CTX),
            P(None, SHARD, TP),
            P(None, TP, SHARD),
            P(TP, SHARD),
            P(TP, SHARD),
            P(None, SHARD),
            P(None, SHARD),
            P(None, SHARD, TP),
            P(None, TP),
            P(TP),
            P(TP, SHARD),
        ),
        out_specs=(
            P(SHARD, CTX, None),
            P(SHARD, CTX, None),
            P(None, SHARD, TP),
            P(None, TP, SHARD),
            P(TP, SHARD),
            P(TP, SHARD),
            P(None, SHARD),
            P(None, SHARD),
            P(None, SHARD, TP),
            P(None, TP),
            P(TP),
            P(TP, SHARD),
        ),
        check_vma=False,
    )
```
